32 devices in a mesh: expert: 8 (over z, x), tensor: 4 (over y, core).
Axes of the slice: x: 2, y: 2, z: 4, core: 2. Of those that a mesh axis runs over, the one named last changes fastest.
Arguments:
- tokens: bfloat16 [4096, 2048], P('expert'), may hold values from -6 to 6
- cotangent: bfloat16 [4096, 2048], P('expert'), may hold values from -6 to 6
- attn_gain: bfloat16 [2048], replicated, may hold values from 0.5 to 1.5
- ffn_gain: bfloat16 [2048], replicated, may hold values from 0.5 to 1.5
- query_gain: bfloat16 [2048], P('tensor'), may hold values from 0.5 to 1.5
- key_gain: bfloat16 [2048], P('tensor'), may hold values from 0.5 to 1.5
- query_weight: bfloat16 [2048, 2048], P(None, 'tensor'), may hold values from -0.125 to 0.125
- key_weight: bfloat16 [2048, 2048], P(None, 'tensor'), may hold values from -0.125 to 0.125
- value_weight: bfloat16 [2048, 2048], P(None, 'tensor'), may hold values from -0.125 to 0.125
- output_weight: bfloat16 [2048, 2048], P('tensor'), may hold values from -0.5 to 0.5
- expert_gate: bfloat16 [32, 2048, 1024], P('expert', None, 'tensor'), may hold values from -0.125 to 0.125
- expert_up: bfloat16 [32, 2048, 1024], P('expert', None, 'tensor'), may hold values from -0.125 to 0.125
- expert_down: bfloat16 [32, 1024, 2048], P('expert', 'tensor'), may hold values from -0.5 to 0.5
- adapt_in: bfloat16 [3, 2048, 128], replicated, may hold values from -0.125 to 0.125
- adapt_out: bfloat16 [3, 128, 2048], P(None, None, 'tensor'), may hold values from -1.5 to 1.5
- adapt_in_out: bfloat16 [2048, 128], P('tensor'), may hold values from -0.5 to 0.5
- adapt_out_out: bfloat16 [128, 2048], replicated, may hold values from -1.5 to 1.5
- routes: int32 [4096, 8], P('expert'), may hold values from 0 to 31, all different within a row; in each aligned block of 512 rows (0 to 511, 512 to 1023, ...) at most 160 rows name the same one
- gate_weights: float32 [4096, 8], P('expert'), may hold values from 0.1 to 0.25
- block_parent: int32 [32], P('expert'), may hold values from 0 to 2, as said below
- adapter_pick: int32 [8, 8], P('expert'), may hold values from 0 to 1, as said below
Outputs:
- layer_out: bfloat16 [4096, 2048], P('expert', 'tensor')
- input_grad: float32 [4096, 2048], P('expert')
- grad_adapt_in: float32 [3, 2048, 128], replicated
- grad_adapt_out: float32 [3, 128, 2048], P(None, None, 'tensor')
- grad_adapt_in_out: float32 [2048, 128], P('tensor')
- grad_adapt_out_out: float32 [128, 2048], replicated
The draws below stay inside these ranges and needn't reach their ends.
Inputs may be any that keep to these rules, and one draw needn't show every extreme that they name: `routes`: in the rows of one tree's 512 tokens no expert is named more than 160 times, a bound that some block reaches. `block_parent`: each entry is the index, within its tree of 4 blocks, of the block directly above it on its path; it is below the block's own index, except for each tree's first block, which names itself; each tree's last block names the block before it. `adapter_pick`: each row holds a single 1.
All inputs are finite; a program needn't handle non-finite values.
Results may differ from the reference program's by a relative error of at most 0.02.
Values may be sent and summed in bfloat16 or wider, within the bound.
No kernel may reach another device: no remote copies, remote signals or barrier semaphores. Data moves between devices by JAX's collectives and lax.ppermute only.
A program may use at most 256 MiB of HBM per device.

```python
import math
import jax
import jax.numpy as jnp
import numpy as np
from jax import lax

D = 2048
HEADS = 16
HD = 128
FF = 1024
TOP = 8
RANK = 16
ADAPTERS = 8
BLOCK = 128
TREE_BLOCKS = 4
EXPERTS = 32
AR = 128
TOK_DEV = 512
TOKENS = 4096
TREES = 8
NBLK = 32
CAP = 160
N_EXPERT = 8


def draw_block_parent(key, part):
    key = jax.random.fold_in(key, 11)
    places = jnp.arange(TREE_BLOCKS, dtype=jnp.int32)
    raw_bits = jax.random.randint(key, (NBLK // TREE_BLOCKS, TREE_BLOCKS), 0, 1 << 20, dtype=jnp.int32)
    parents = raw_bits % jnp.maximum(places, 1)[None, :]
    parents = jnp.where(places[None, :] == TREE_BLOCKS - 1, TREE_BLOCKS - 2, parents)
    return parents.reshape(NBLK).astype(jnp.int32)


def draw_adapter_pick(key, part):
    key = jax.random.fold_in(key, 12)
    chosen = jax.random.randint(key, (TREES,), 0, ADAPTERS, dtype=jnp.int32)
    return (chosen[:, None] == jnp.arange(ADAPTERS, dtype=jnp.int32)[None, :]).astype(jnp.int32)


def steps_of(stream_key, shape, shards, smallest, largest):
    gain, own = 1.0, jax.random.fold_in(stream_key, 6)
    for dim, parts in shards:
        heights = jnp.exp(jax.random.uniform(jax.random.fold_in(own, dim), (parts,), jnp.float32, smallest / len(shards), largest / len(shards)))
        gain = gain * jnp.repeat(heights, shape[dim] // parts).reshape([-1 if axis == dim else 1 for axis in range(len(shape))])
    return gain


def assign_block(rng, own, number, rows, count, top, bound, slope):
    order = jax.random.permutation(rng, count)
    packed, usual = portions_of(count, rows * top, bound, slope, True), portions_of(count, rows * top, bound, slope, False)
    places = jnp.arange(count)

    def named(sizes, offset_by):
        used = int((sizes > 0).sum())
        fixed = max(1, used // 4)
        passed = fixed + (places - fixed + offset_by * (used - fixed)) % max(1, count - fixed)
        return jnp.zeros((count,), jnp.int32).at[order[jnp.where(places < fixed, places, passed)]].set(jnp.asarray(sizes, jnp.int32))

    sizes = jnp.where(number % 4 == 0, named(packed, number // 4), named(usual, number - number // 4 - 1))
    mixed = jax.random.permutation(jax.random.fold_in(own, 3), count)
    source_of, receiver = mixed[0:count // 2 * 2:2], mixed[1:count // 2 * 2:2]
    margin = jnp.minimum(sizes[source_of] - 1, bound - sizes[receiver]) // 2
    margin = jnp.where((source_of == order[0]) | (receiver == order[0]) | (sizes[receiver] == 0), 0, jnp.maximum(margin, 0))
    passed = jax.random.randint(jax.random.fold_in(own, 4), (count // 2,), 0, 1 << 20) % (margin + 1)
    sizes = sizes.at[source_of].add(-passed).at[receiver].add(passed)
    items = jnp.searchsorted(jnp.cumsum(sizes), jnp.arange(rows * top), side="right").astype(jnp.int32)
    listing = items.reshape(top, rows).T
    listing = listing[jax.random.permutation(jax.random.fold_in(own, 1), rows)]
    offset_by = jax.random.randint(jax.random.fold_in(own, 2), (rows, 1), 0, top)
    return jnp.take_along_axis(listing, (jnp.arange(top)[None, :] + offset_by) % top, axis=1)


def portions_of(count, total, most, slope, full):
    weights = [(1 << 20) // math.isqrt(grade ** slope) + 1 for grade in range(1, count + 1)]
    largest = most if full else min(most, max(-(-total // count), total * weights[0] // sum(weights)))
    least = 1 if total - largest >= count - 1 else 0
    given, spare = [largest] + [least] * (count - 1), total - largest - least * (count - 1)
    while spare > 0:
        candidates = [i for i in range(1, count) if given[i] < largest] or [i for i in range(1, count) if given[i] < most]
        whole, left = sum([weights[i] for i in candidates]), spare
        for i in candidates:
            addition = min(most - given[i], max(1, left * weights[i] // whole), spare)
            given[i] = given[i] + addition
            spare = spare - addition
    return np.array(given)


def bell_draw(rng, extent, scale, most, cuts=(), kind=jnp.bfloat16):
    drawn = scale * jax.random.normal(rng, extent, jnp.float32)
    if cuts:
        drawn = drawn * steps_of(rng, extent, cuts, -0.22, 0.18)
    return jnp.clip(drawn, -most, most).astype(kind)


def setup_inputs(seed: int = 0) -> dict:
    arg_keys = jax.random.split(jax.random.key(seed), 22)
    tokens = bell_draw(arg_keys[0], (TOKENS, D), 1.0, 6.0, ((0, 8),))
    cotangent = bell_draw(arg_keys[1], (TOKENS, D), 1.0, 6.0, ((0, 8),))
    attn_gain = jnp.clip(1.0 + 0.1 * jax.random.normal(arg_keys[2], (D,), jnp.float32), 0.5, 1.5).astype(jnp.bfloat16)
    ffn_gain = jnp.clip(1.0 + 0.1 * jax.random.normal(arg_keys[3], (D,), jnp.float32), 0.5, 1.5).astype(jnp.bfloat16)
    query_gain = jnp.clip(1.0 + 0.1 * jax.random.normal(arg_keys[4], (D,), jnp.float32), 0.5, 1.5).astype(jnp.bfloat16)
    key_gain = jnp.clip(1.0 + 0.1 * jax.random.normal(arg_keys[5], (D,), jnp.float32), 0.5, 1.5).astype(jnp.bfloat16)
    query_weight = bell_draw(arg_keys[6], (D, D), D ** -0.5, 0.125, ((1, 4),))
    key_weight = bell_draw(arg_keys[7], (D, D), D ** -0.5, 0.125, ((1, 4),))
    value_weight = bell_draw(arg_keys[8], (D, D), D ** -0.5, 0.125, ((1, 4),))
    output_weight = bell_draw(arg_keys[9], (D, D), (D // 16) ** -0.5, 0.5, ((0, 4),))
    expert_gate = bell_draw(arg_keys[10], (EXPERTS, D, FF), D ** -0.5, 0.125, ((0, 8), (2, 4)))
    expert_up = bell_draw(arg_keys[11], (EXPERTS, D, FF), D ** -0.5, 0.125, ((0, 8), (2, 4)))
    expert_down = bell_draw(arg_keys[12], (EXPERTS, FF, D), (FF // 8) ** -0.5, 0.5, ((0, 8), (1, 4)))
    adapt_in = bell_draw(arg_keys[13], (3, D, AR), D ** -0.5, 0.125)
    adapt_out = bell_draw(arg_keys[14], (3, AR, D), RANK ** -0.5, 1.5, ((2, 4),))
    adapt_in_out = bell_draw(arg_keys[15], (D, AR), (D // 16) ** -0.5, 0.5, ((0, 4),))
    adapt_out_out = bell_draw(arg_keys[16], (AR, D), RANK ** -0.5, 1.5)
    routes_keys = jax.random.split(jax.random.fold_in(arg_keys[17], 1), TOKENS // TOK_DEV)
    routes_turns = jax.random.permutation(jax.random.fold_in(arg_keys[17], 3), TOKENS // TOK_DEV)
    routes = jax.vmap(lambda own, number: assign_block(jax.random.fold_in(arg_keys[17], 2), own, number, TOK_DEV, EXPERTS, TOP, CAP, 1))(routes_keys, routes_turns).reshape((TOKENS, TOP))
    gate_weights = jnp.clip(jnp.exp(math.log(0.25) - 0.9162907 * jax.random.uniform(arg_keys[18], (TOKENS, TOP), jnp.float32) ** steps_of(arg_keys[18], (TOKENS, TOP), ((0, 8),), -0.2, 0.2)), 0.1, 0.25)
    block_parent = draw_block_parent(jax.random.fold_in(arg_keys[21], 71), 0)
    adapter_pick = draw_adapter_pick(jax.random.fold_in(arg_keys[21], 71), 0)
    return dict(tokens=tokens, cotangent=cotangent, attn_gain=attn_gain, ffn_gain=ffn_gain, query_gain=query_gain, key_gain=key_gain, query_weight=query_weight, key_weight=key_weight, value_weight=value_weight, output_weight=output_weight, expert_gate=expert_gate, expert_up=expert_up, expert_down=expert_down, adapt_in=adapt_in, adapt_out=adapt_out, adapt_in_out=adapt_in_out, adapt_out_out=adapt_out_out, routes=routes, gate_weights=gate_weights, block_parent=block_parent, adapter_pick=adapter_pick)


@jax.custom_vjp
def low(v):
    return lax.optimization_barrier(v.astype(jnp.bfloat16)).astype(jnp.float32)

@jax.custom_vjp
def low_back(v):
    return v

def low_keep(v):
    return (low(v), None)

def low_pass(kept, grad):
    return (grad,)

def back_keep(v):
    return (v, None)

def back_low(kept, grad):
    return (low(grad),)
low.defvjp(low_keep, low_pass)
low_back.defvjp(back_keep, back_low)
EPSILON = 1e-05
ROPE_BASE = 10000.0
MASKED_SCORE = -1e+30
EXACT_PRODUCTS = lax.Precision.HIGHEST

def ancestry(parents):
    blocks = parents.shape[1]
    places = jnp.arange(blocks, dtype=jnp.int32)
    current = jnp.broadcast_to(places[None, :], parents.shape).astype(jnp.int32)

    def climb(climb_step, climb_state):
        walker, reached = climb_state
        walker = jnp.take_along_axis(parents, walker, axis=1).astype(jnp.int32)
        return (walker, reached | (walker[:, :, None] == places[None, None, :]))
    initial = (current, current[:, :, None] == places[None, None, :])
    return lax.fori_loop(0, blocks - 1, climb, initial)[1]

def rope_tables(reached, block_span, head_size):
    depths = lax.optimization_barrier(jnp.sum(reached.astype(jnp.int32), axis=2)) - 1
    offsets = jnp.arange(block_span, dtype=jnp.int32)
    located = (depths[:, :, None] * block_span + offsets[None, None, :]).reshape(-1).astype(jnp.float32)
    halves = head_size // 2
    speeds = ROPE_BASE ** (-2.0 * jnp.arange(halves, dtype=jnp.float32) / head_size)
    angles = located[:, None] * speeds[None, :]
    angles = jnp.concatenate([angles, angles], axis=1)
    return (jnp.cos(angles), jnp.sin(angles))

def rotate(values, cosine_table, sine_table):
    halves = values.shape[-1] // 2
    turned = jnp.concatenate([-values[..., halves:], values[..., :halves]], axis=-1)
    return values * cosine_table[:, None, :] + turned * sine_table[:, None, :]

def token_mask(reached, total_size):
    blocks = reached.shape[0]
    block_span = total_size // blocks
    widened = jnp.broadcast_to(reached[:, None, :, None], (blocks, block_span, blocks, block_span)).reshape(total_size, total_size)
    positions = jnp.arange(total_size, dtype=jnp.int32)
    return widened & (positions[None, :] <= positions[:, None])

def normalize(values):
    return values * lax.rsqrt(lax.optimization_barrier(jnp.mean(values * values, axis=-1, keepdims=True)) + EPSILON)

def tree_attention(tree_item):
    queries, keys, values, reached = tree_item
    key_mask = token_mask(reached, queries.shape[0])
    scores = jnp.einsum('qhd,khd->hqk', queries, keys, precision=EXACT_PRODUCTS) * queries.shape[2] ** (-0.5)
    scores = jnp.where(key_mask[None], low_back(scores), MASKED_SCORE)
    row_max = lax.optimization_barrier(jnp.max(scores, axis=2, keepdims=True))
    raised = jnp.exp(scores - row_max)
    weights = low(raised / lax.optimization_barrier(jnp.sum(raised, axis=2, keepdims=True)))
    return jnp.einsum('hqk,khd->qhd', weights, values, precision=EXACT_PRODUCTS)

def expert_block(expert_item):
    rows_in, gate_matrix, up_matrix, down_matrix = expert_item
    gate_value = low_back(jnp.dot(rows_in, gate_matrix, precision=EXACT_PRODUCTS))
    up_value = low_back(jnp.dot(rows_in, up_matrix, precision=EXACT_PRODUCTS))
    hidden = low(jax.nn.silu(gate_value) * up_value)
    return jnp.dot(hidden, down_matrix, precision=EXACT_PRODUCTS)

def reference(tokens, cotangent, attn_gain, ffn_gain, query_gain, key_gain, query_weight, key_weight, value_weight, output_weight, expert_gate, expert_up, expert_down, adapt_in, adapt_out, adapt_in_out, adapt_out_out, routes, gate_weights, block_parent, adapter_pick):
    first_gain = attn_gain.astype(jnp.float32)
    second_gain = ffn_gain.astype(jnp.float32)
    query_scale = query_gain.astype(jnp.float32)
    key_scale = key_gain.astype(jnp.float32)
    query_matrix = query_weight.astype(jnp.float32)
    key_matrix = key_weight.astype(jnp.float32)
    value_matrix = value_weight.astype(jnp.float32)
    output_matrix = output_weight.astype(jnp.float32)
    gate_all = expert_gate.astype(jnp.float32)
    up_all = expert_up.astype(jnp.float32)
    down_all = expert_down.astype(jnp.float32)
    reached = ancestry(block_parent.reshape(N_EXPERT, TREE_BLOCKS).astype(jnp.int32))
    cosine_table, sine_table = rope_tables(reached, BLOCK, HD)
    select = jnp.repeat(jnp.repeat(adapter_pick.astype(jnp.float32), RANK, axis=1), TOK_DEV, axis=0)
    route_list = routes.reshape(N_EXPERT, TOK_DEV * TOP).astype(jnp.int32)
    route_hits = (route_list[:, :, None] == jnp.arange(EXPERTS, dtype=jnp.int32)[None, None, :]).astype(jnp.int32)
    within = lax.optimization_barrier(jnp.sum(jnp.cumsum(route_hits, axis=1) * route_hits, axis=2)) - 1
    owner_rows = jnp.arange(N_EXPERT, dtype=jnp.int32)[:, None] * CAP
    slot_ids = (route_list * (N_EXPERT * CAP) + owner_rows + within).reshape(TOKENS, TOP).astype(jnp.int32)
    slot_owner = jnp.zeros((EXPERTS * N_EXPERT * CAP,), jnp.int32).at[slot_ids.reshape(-1)].set(jnp.arange(TOKENS * TOP, dtype=jnp.int32) + 1)
    slot_live = (slot_owner > 0)[:, None]
    source_token = (jnp.maximum(slot_owner - 1, 0) // TOP).astype(jnp.int32)

    def forward(inputs, adapt_in_f, adapt_out_f, adapt_in_out_f, adapt_out_out_f):
        normed_in = low(normalize(inputs) * first_gain)
        lowrank = low(low_back(jnp.einsum('td,idr->itr', normed_in, adapt_in_f, precision=EXACT_PRODUCTS) * select[None]))

        def project(matrix, projection):
            return low_back(jnp.dot(normed_in, matrix, precision=EXACT_PRODUCTS) + jnp.dot(lowrank[projection], adapt_out_f[projection], precision=EXACT_PRODUCTS))
        query_raw = project(query_matrix, 0)
        key_raw = project(key_matrix, 1)
        value_raw = project(value_matrix, 2)
        queries = low(rotate((normalize(query_raw) * query_scale).reshape(TOKENS, HEADS, HD), cosine_table, sine_table))
        keys = low(rotate((normalize(key_raw) * key_scale).reshape(TOKENS, HEADS, HD), cosine_table, sine_table))
        values = low(value_raw).reshape(TOKENS, HEADS, HD)
        attended = lax.map(jax.checkpoint(tree_attention), (queries.reshape(N_EXPERT, TOK_DEV, HEADS, HD), keys.reshape(N_EXPERT, TOK_DEV, HEADS, HD), values.reshape(N_EXPERT, TOK_DEV, HEADS, HD), reached))
        attended = low(low_back(attended.reshape(TOKENS, D)))
        mixed = low(low_back(jnp.dot(attended, adapt_in_out_f, precision=EXACT_PRODUCTS) * select))
        resid = inputs + low_back(jnp.dot(attended, output_matrix, precision=EXACT_PRODUCTS) + jnp.dot(mixed, adapt_out_out_f, precision=EXACT_PRODUCTS))
        normed_ffn = low(normalize(resid) * second_gain)
        rows_in = low_back(jnp.where(slot_live, normed_ffn[source_token], 0.0)).reshape(EXPERTS, N_EXPERT * CAP, D)
        expert_rows = lax.map(jax.checkpoint(expert_block), (rows_in, gate_all, up_all, down_all))
        expert_rows = low(low_back(expert_rows)).reshape(EXPERTS * N_EXPERT * CAP, D)
        mixture = jnp.zeros((TOKENS, D), jnp.float32)
        for chosen in range(TOP):
            mixture = mixture + gate_weights[:, chosen:chosen + 1] * expert_rows[slot_ids[:, chosen]]
        return resid + mixture
    result, pullback = jax.vjp(forward, tokens.astype(jnp.float32), adapt_in.astype(jnp.float32), adapt_out.astype(jnp.float32), adapt_in_out.astype(jnp.float32), adapt_out_out.astype(jnp.float32))
    grads = pullback(cotangent.astype(jnp.float32))
    return (result.astype(jnp.bfloat16), grads[0], grads[1], grads[2], grads[3], grads[4])
```

```python
import jax
import jax.numpy as jnp
from jax import lax
from jax.sharding import PartitionSpec as P

HD = 128
RANK = 16


EPSILON = 1e-05
ROPE_BASE = 10000.0
MASKED_SCORE = -1e30


def ancestry(parents):
    blocks = parents.shape[1]
    places = jnp.arange(blocks, dtype=jnp.int32)
    current = places[None, :]

    def climb(climb_step, climb_state):
        walker, reached = climb_state
        walker = jnp.take_along_axis(parents, walker, axis=1)
        return (walker, reached | (walker[:, :, None] == places[None, None, :]))

    initial = (current, current[:, :, None] == places[None, None, :])
    return lax.fori_loop(0, blocks - 1, climb, initial)[1]


def rope_tables(reached, block_span, head_size):
    depths = jnp.sum(reached.astype(jnp.int32), axis=2) - 1
    offsets = jnp.arange(block_span, dtype=jnp.int32)
    located = (
        (depths[:, :, None] * block_span + offsets[None, None, :]).reshape(-1).astype(jnp.float32)
    )
    halves = head_size // 2
    speeds = ROPE_BASE ** (-2.0 * jnp.arange(halves, dtype=jnp.float32) / head_size)
    angles = located[:, None] * speeds[None, :]
    angles = jnp.concatenate([angles, angles], axis=1)
    return (jnp.cos(angles), jnp.sin(angles))


def rotate(values, cosine_table, sine_table):
    halves = values.shape[-1] // 2
    turned = jnp.concatenate([-values[..., halves:], values[..., :halves]], axis=-1)
    return values * cosine_table[:, None, :] + turned * sine_table[:, None, :]


def unrotate(values, cosine_table, sine_table):
    halves = values.shape[-1] // 2
    sined = values * sine_table[:, None, :]
    return values * cosine_table[:, None, :] + jnp.concatenate(
        [sined[..., halves:], -sined[..., :halves]], axis=-1
    )


def token_mask(reached, total_size):
    blocks = reached.shape[0]
    block_span = total_size // blocks
    widened = jnp.broadcast_to(
        reached[:, None, :, None], (blocks, block_span, blocks, block_span)
    ).reshape(total_size, total_size)
    positions = jnp.arange(total_size, dtype=jnp.int32)
    return widened & (positions[None, :] <= positions[:, None])


def norm_back(scaled_grad, values, inverse, model_width, inner_sum):
    return inverse * scaled_grad - values * inverse**3 * (inner_sum / model_width)


def divide_axes(owners, tensor_count):
    outer = 4
    return {
        "z": ("expert", outer, owners // outer, owners),
        "x": ("expert", owners // outer, 1, owners),
        "y": ("tensor", tensor_count // 2, 2, tensor_count),
        "c": ("tensor", 2, 1, tensor_count),
    }


def turn(array, axes, name, step):
    axis, length, stride, total = axes[name]
    pairs = []
    for index in range(total):
        place = (index // stride) % length
        moved = index + ((place + step) % length - place) * stride
        pairs.append((index, moved))
    return lax.ppermute(array, axis, pairs)


def ring_gather(array, axes, name):
    held = [array]
    for _ in range(axes[name][1] - 1):
        held.append(turn(held[-1], axes, name, 1))
    return jnp.concatenate(held, axis=0)


def add_low(left, right):
    return (left.astype(jnp.float32) + right.astype(jnp.float32)).astype(jnp.bfloat16)


def ring_scatter(array, axes, name):
    length = axes[name][1]
    parts = jnp.split(array, length, axis=0)
    total = parts[-1]
    for index in range(length - 2, -1, -1):
        total = add_low(turn(total, axes, name, -1), parts[index])
    return total


def gather_plane(rows, axes):
    half = rows.shape[0] // 2
    first = ring_gather(ring_gather(rows[:half], axes, "x"), axes, "y")
    second = ring_gather(ring_gather(rows[half:], axes, "y"), axes, "x")
    return ring_gather(jnp.concatenate([first, second], axis=0), axes, "c")


def scatter_plane(rows, axes):
    rows = ring_scatter(rows, axes, "c")
    half = rows.shape[0] // 2
    first = ring_scatter(ring_scatter(rows[:half], axes, "y"), axes, "x")
    second = ring_scatter(ring_scatter(rows[half:], axes, "x"), axes, "y")
    return jnp.concatenate([first, second], axis=0)


def gather_all(rows, axes):
    planes = [rows]
    for _ in range(axes["z"][1] - 1):
        planes.append(turn(planes[-1], axes, "z", 1))
    return [gather_plane(plane, axes) for plane in planes]


def place_tensor(rows, axes, kind):
    rank = lax.axis_index("tensor")
    count = lax.axis_size("tensor")
    size = rows.shape[0]
    span = axes["y"][1]
    held = [rows]
    for _ in range(span - 1):
        held.append(turn(held[-1], axes, "y", 1))
    other = [turn(piece, axes, "c", 1) for piece in held]
    whole = jnp.zeros((count * size, rows.shape[1]), kind)
    core = rank % 2
    for step in range(span):
        level = (rank // 2 + span - step) % span
        whole = lax.dynamic_update_slice_in_dim(
            whole, held[step].astype(kind), (level * 2 + core) * size, 0
        )
        whole = lax.dynamic_update_slice_in_dim(
            whole, other[step].astype(kind), (level * 2 + 1 - core) * size, 0
        )
    return whole


def scatter_tensor(rows, axes):
    rank = lax.axis_index("tensor")
    count = lax.axis_size("tensor")
    size = rows.shape[0] // count
    span = axes["y"][1]
    blocks = rows.reshape(span, 2, size, rows.shape[1])
    core = rank % 2
    mine = lax.dynamic_index_in_dim(blocks, core, 1, keepdims=False)
    theirs = lax.dynamic_index_in_dim(blocks, 1 - core, 1, keepdims=False)
    mine = add_low(mine, turn(theirs, axes, "c", 1))
    total = None
    for step in range(span - 1, -1, -1):
        level = (rank // 2 + span - step) % span
        part = lax.dynamic_index_in_dim(mine, level, 0, keepdims=False)
        total = part if total is None else add_low(turn(total, axes, "y", -1), part)
    return total


def swap_columns(rows, axes):
    rank = lax.axis_index("tensor")
    count = lax.axis_size("tensor")
    size, width = rows.shape
    span = axes["y"][1]
    share = width // count
    level, core = rank // 2, rank % 2
    whole = jnp.zeros((count * size, share), rows.dtype)
    for step in range(span):
        toward = (level + step) % span
        piece = lax.dynamic_slice_in_dim(rows, toward * 2 * share, 2 * share, 1)
        if step:
            piece = turn(piece, axes, "y", step)
        mine = lax.dynamic_slice_in_dim(piece, core * share, share, 1)
        theirs = lax.dynamic_slice_in_dim(piece, (1 - core) * share, share, 1)
        theirs = turn(theirs, axes, "c", 1)
        source = (level + span - step) % span
        whole = lax.dynamic_update_slice_in_dim(whole, mine, (source * 2 + core) * size, 0)
        whole = lax.dynamic_update_slice_in_dim(whole, theirs, (source * 2 + 1 - core) * size, 0)
    return whole


def sum_tensor(array, axes):
    total = add_low(array, turn(array, axes, "c", 1))
    moving = total
    result = total.astype(jnp.float32)
    for _ in range(axes["y"][1] - 1):
        moving = turn(moving, axes, "y", 1)
        result = result + moving.astype(jnp.float32)
    return result


def body(
    tokens,
    cotangent,
    attn_gain,
    ffn_gain,
    query_gain,
    key_gain,
    query_weight,
    key_weight,
    value_weight,
    output_weight,
    expert_gate,
    expert_up,
    expert_down,
    adapt_in,
    adapt_out,
    adapt_in_out,
    adapt_out_out,
    routes,
    gate_weights,
    block_parent,
    adapter_pick,
):
    rows_here, model_width = tokens.shape
    local_width = query_weight.shape[1]
    heads_here = local_width // HD
    tensor_rank = lax.axis_index("tensor")
    tensor_count = lax.axis_size("tensor")
    owners = lax.axis_size("expert")
    owner_rank = lax.axis_index("expert")
    axes = divide_axes(owners, tensor_count)
    experts_here, _, hidden_here = expert_gate.shape
    experts_all = experts_here * owners
    column_share = model_width // tensor_count
    row_share = rows_here // tensor_count
    float_kind = jnp.float32
    half_kind = jnp.bfloat16

    def own_rows(array):
        return lax.dynamic_slice_in_dim(array, tensor_rank * row_share, row_share, 0)

    def matmul(left, right):
        return jnp.dot(left, right, preferred_element_type=float_kind)

    def matmul_t(left, right):
        return lax.dot_general(
            left, right, (((1,), (1,)), ((), ())), preferred_element_type=float_kind
        )

    def t_matmul(left, right):
        return lax.dot_general(
            left, right, (((0,), (0,)), ((), ())), preferred_element_type=float_kind
        )

    cotangent_rows = own_rows(cotangent)
    routes_rows = own_rows(routes)
    weights_rows = own_rows(gate_weights)
    route_weights = jnp.sum(
        jnp.where(
            routes_rows[:, :, None] == jnp.arange(experts_all, dtype=jnp.int32)[None, None, :],
            weights_rows[:, :, None],
            0.0,
        ),
        axis=1,
    )
    weights_high = route_weights.astype(half_kind)
    weights_low = (route_weights - weights_high.astype(float_kind)).astype(half_kind)
    side_width = -(-2 * experts_all // 128) * 128
    side_pad = jnp.zeros((row_share, side_width - 2 * experts_all), half_kind)
    cotangent_sent = jnp.concatenate(
        [cotangent_rows, weights_high, weights_low, side_pad], axis=1
    )
    cotangent_planes = gather_all(cotangent_sent, axes)
    side_index = jnp.arange(side_width, dtype=jnp.int32)
    hidden_owner = owner_rank * experts_here + jnp.arange(
        experts_here * hidden_here, dtype=jnp.int32
    ) // hidden_here
    spread = (
        (side_index[:, None] % experts_all == hidden_owner[None, :])
        & (side_index[:, None] < 2 * experts_all)
    ).astype(half_kind)
    gate_wide = jnp.swapaxes(expert_gate, 0, 1).reshape(model_width, -1)
    up_wide = jnp.swapaxes(expert_up, 0, 1).reshape(model_width, -1)
    down_tall = expert_down.reshape(-1, model_width)

    inputs = tokens.astype(float_kind)
    first_gain = attn_gain.astype(float_kind)
    second_gain = ffn_gain.astype(float_kind)
    first_inverse = lax.rsqrt(jnp.mean(inputs * inputs, axis=1, keepdims=True) + EPSILON)
    normed_in = (inputs * first_inverse * first_gain).astype(half_kind)
    reached = ancestry(block_parent.reshape(1, -1))
    cosine_table, sine_table = rope_tables(reached, rows_here // block_parent.shape[0], HD)
    key_mask = token_mask(reached[0], rows_here)
    picked = jnp.argmax(adapter_pick[0]) * RANK
    adapt_in_used = lax.dynamic_slice_in_dim(adapt_in, picked, RANK, 2)
    adapt_out_used = lax.dynamic_slice_in_dim(adapt_out, picked, RANK, 1)
    mix_in_used = lax.dynamic_slice_in_dim(adapt_in_out, picked, RANK, 1)
    mix_out_used = lax.dynamic_slice_in_dim(adapt_out_out, picked, RANK, 0)
    picks = lax.all_gather(adapter_pick.astype(float_kind), "expert", axis=0, tiled=True)
    lowrank = jnp.einsum(
        "td,idr->itr", normed_in, adapt_in_used, preferred_element_type=float_kind
    ).astype(half_kind)
    matrices = (query_weight, key_weight, value_weight)
    raw_list = [
        matmul(normed_in, matrices[projection])
        + matmul(lowrank[projection], adapt_out_used[projection])
        for projection in range(3)
    ]
    query_raw, key_raw, value_raw = raw_list
    query_squares, key_squares = lax.psum(
        (jnp.sum(query_raw * query_raw, axis=1), jnp.sum(key_raw * key_raw, axis=1)), "tensor"
    )
    query_inverse = lax.rsqrt(query_squares / model_width + EPSILON)[:, None]
    key_inverse = lax.rsqrt(key_squares / model_width + EPSILON)[:, None]
    query_scale = query_gain.astype(float_kind)
    key_scale = key_gain.astype(float_kind)
    queries = rotate(
        (query_raw * query_inverse * query_scale).reshape(rows_here, heads_here, HD),
        cosine_table,
        sine_table,
    ).astype(half_kind)
    keys = rotate(
        (key_raw * key_inverse * key_scale).reshape(rows_here, heads_here, HD),
        cosine_table,
        sine_table,
    ).astype(half_kind)
    values = value_raw.astype(half_kind).reshape(rows_here, heads_here, HD)
    score_scale = HD ** (-0.5)
    scores = (
        jnp.einsum("qhd,khd->hqk", queries, keys, preferred_element_type=float_kind) * score_scale
    )
    scores = jnp.where(key_mask[None], scores, MASKED_SCORE)
    row_max = jnp.max(scores, axis=2, keepdims=True)
    raised = jnp.exp(scores - row_max)
    row_total = jnp.sum(raised, axis=2, keepdims=True)
    weights_half = (raised / row_total).astype(half_kind)
    log_total = row_max + jnp.log(row_total)
    attended = (
        jnp.einsum("hqk,khd->qhd", weights_half, values, preferred_element_type=float_kind)
        .reshape(rows_here, local_width)
        .astype(half_kind)
    )
    output_part = matmul(attended, output_weight).astype(half_kind)
    mixing_part = matmul(attended, mix_in_used).astype(half_kind)
    mixing_pad = jnp.zeros((rows_here, 128 - RANK), half_kind)
    branch_rows = scatter_tensor(
        jnp.concatenate([output_part, mixing_part, mixing_pad], axis=1), axes
    )
    mixed_rows = branch_rows[:, model_width : model_width + RANK]
    resid_rows = (
        own_rows(tokens).astype(float_kind)
        + branch_rows[:, :model_width].astype(float_kind)
        + matmul(mixed_rows, mix_out_used)
    )
    second_inverse = lax.rsqrt(
        jnp.mean(resid_rows * resid_rows, axis=1, keepdims=True) + EPSILON
    )
    normed_rows = (resid_rows * second_inverse * second_gain).astype(half_kind)
    normed_planes = gather_all(normed_rows, axes)

    kept_states = []
    for plane, beside in zip(normed_planes, cotangent_planes):
        gate_value = matmul(plane, gate_wide)
        up_value = matmul(plane, up_wide)
        sigmoid_gate = jax.nn.sigmoid(gate_value)
        weight_wide = matmul(beside[:, model_width:], spread)
        hidden_grad = matmul_t(beside[:, :model_width], down_tall) * weight_wide
        gate_grad = (
            hidden_grad * up_value * sigmoid_gate * (1.0 + gate_value * (1.0 - sigmoid_gate))
        ).astype(half_kind)
        up_grad = (hidden_grad * gate_value * sigmoid_gate).astype(half_kind)
        hidden = (gate_value * sigmoid_gate * up_value * weight_wide).astype(half_kind)
        kept_states.append((gate_grad, up_grad, hidden))
    total = None
    for gate_grad, up_grad, _ in reversed(kept_states):
        part = (matmul_t(gate_grad, gate_wide) + matmul_t(up_grad, up_wide)).astype(half_kind)
        part = scatter_plane(part, axes)
        total = part if total is None else add_low(turn(total, axes, "z", -1), part)
    ffn_rows_grad = total.astype(float_kind)
    total = None
    for _, _, hidden in reversed(kept_states):
        part = scatter_plane(matmul(hidden, down_tall).astype(half_kind), axes)
        total = part if total is None else add_low(turn(total, axes, "z", -1), part)
    layer_rows = (resid_rows + total.astype(float_kind)).astype(half_kind)
    layer_out = swap_columns(layer_rows, axes)

    second_scaled = ffn_rows_grad * second_gain
    resid_grad_rows = cotangent_rows.astype(float_kind) + norm_back(
        second_scaled,
        resid_rows,
        second_inverse,
        model_width,
        jnp.sum(second_scaled * resid_rows, axis=1, keepdims=True),
    )
    branch_sent = jnp.concatenate(
        [resid_grad_rows.astype(half_kind), mixed_rows, jnp.zeros((row_share, 128 - RANK), half_kind)],
        axis=1,
    )
    branch_whole = place_tensor(branch_sent, axes, half_kind)
    branch_grad = branch_whole[:, :model_width]
    mixed = branch_whole[:, model_width : model_width + RANK]
    mixed_grad = matmul_t(branch_grad, mix_out_used).astype(half_kind)
    attended_grad = (
        matmul_t(branch_grad, output_weight) + matmul_t(mixed_grad, mix_in_used)
    ).astype(half_kind)
    attended_grad = attended_grad.reshape(rows_here, heads_here, HD)
    scores = (
        jnp.einsum("qhd,khd->hqk", queries, keys, preferred_element_type=float_kind) * score_scale
    )
    softmax_full = jnp.where(key_mask[None], jnp.exp(scores - log_total), 0.0)
    softmax_half = softmax_full.astype(half_kind)
    value_grad = jnp.einsum(
        "hqk,qhd->khd", softmax_half, attended_grad, preferred_element_type=float_kind
    ).astype(half_kind)
    prob_grad = jnp.einsum("qhd,khd->hqk", attended_grad, values, preferred_element_type=float_kind)
    score_grad = (
        softmax_full * (prob_grad - jnp.sum(softmax_full * prob_grad, axis=2, keepdims=True))
    ).astype(half_kind)
    query_grad = (
        jnp.einsum("hqk,khd->qhd", score_grad, keys, preferred_element_type=float_kind)
        * score_scale
    )
    key_grad = (
        jnp.einsum("hqk,qhd->khd", score_grad, queries, preferred_element_type=float_kind)
        * score_scale
    )
    query_scaled = (
        unrotate(query_grad, cosine_table, sine_table).reshape(rows_here, local_width) * query_scale
    )
    key_scaled = (
        unrotate(key_grad, cosine_table, sine_table).reshape(rows_here, local_width) * key_scale
    )
    query_inner, key_inner = lax.psum(
        (jnp.sum(query_scaled * query_raw, axis=1), jnp.sum(key_scaled * key_raw, axis=1)), "tensor"
    )
    query_raw_grad = norm_back(
        query_scaled, query_raw, query_inverse, model_width, query_inner[:, None]
    ).astype(half_kind)
    key_raw_grad = norm_back(
        key_scaled, key_raw, key_inverse, model_width, key_inner[:, None]
    ).astype(half_kind)
    value_raw_grad = value_grad.reshape(rows_here, local_width)
    raw_grads = (query_raw_grad, key_raw_grad, value_raw_grad)
    lowrank_part = jnp.concatenate(
        [matmul_t(raw_grads[projection], adapt_out_used[projection]) for projection in range(3)],
        axis=1,
    )
    lowrank_grad = sum_tensor(lowrank_part.astype(half_kind), axes).astype(half_kind)
    normed_part = (
        matmul_t(query_raw_grad, query_weight)
        + matmul_t(key_raw_grad, key_weight)
        + matmul_t(value_raw_grad, value_weight)
    )
    normed_grad_rows = scatter_tensor(normed_part.astype(half_kind), axes).astype(float_kind)
    lowrank_rows = own_rows(lowrank_grad)
    for projection in range(3):
        normed_grad_rows = normed_grad_rows + matmul_t(
            lowrank_rows[:, projection * RANK : (projection + 1) * RANK], adapt_in_used[projection]
        )
    first_scaled = normed_grad_rows * first_gain
    inputs_rows = own_rows(inputs)
    input_grad_rows = resid_grad_rows + norm_back(
        first_scaled,
        inputs_rows,
        own_rows(first_inverse),
        model_width,
        jnp.sum(first_scaled * inputs_rows, axis=1, keepdims=True),
    )
    input_grad = place_tensor(input_grad_rows.astype(half_kind), axes, float_kind)

    normed_share = lax.dynamic_slice_in_dim(
        normed_in, tensor_rank * column_share, column_share, 1
    )
    branch_share = lax.dynamic_slice_in_dim(
        branch_grad, tensor_rank * column_share, column_share, 1
    )
    compact = jnp.concatenate(
        [t_matmul(lowrank_grad, normed_share), t_matmul(mixed, branch_share)]
        + [t_matmul(lowrank[projection], raw_grads[projection]) for projection in range(3)]
        + [t_matmul(mixed_grad, attended)],
        axis=0,
    ).astype(half_kind)
    kinds = compact.shape[0] // RANK
    trees = ring_gather(ring_gather(compact, axes, "x"), axes, "z")
    far, near = axes["z"][1], axes["x"][1]
    tree_index = (
        (owner_rank // near + far - jnp.arange(far, dtype=jnp.int32)[:, None]) % far * near
        + (owner_rank % near + near - jnp.arange(near, dtype=jnp.int32)[None, :]) % near
    ).reshape(-1)
    tree_picks = matmul(
        (tree_index[:, None] == jnp.arange(owners, dtype=jnp.int32)[None, :]).astype(float_kind),
        picks,
    ).astype(half_kind)
    trees = trees.reshape(owners, kinds, RANK, column_share)
    grad_adapt_out = jnp.einsum(
        "sa,skrc->karc", tree_picks, trees[:, 4:7], preferred_element_type=float_kind
    ).reshape(3, -1, column_share)
    grad_adapt_in_out = jnp.einsum(
        "sa,src->car", tree_picks, trees[:, 7], preferred_element_type=float_kind
    ).reshape(column_share, -1)
    shared = place_tensor(
        trees[:, :4].reshape(owners * 4 * RANK, column_share), axes, half_kind
    ).reshape(tensor_count, owners, 4, RANK, column_share)
    grad_adapt_in = jnp.einsum(
        "sa,tskrc->ktcar", tree_picks, shared[:, :, :3], preferred_element_type=float_kind
    ).reshape(3, model_width, -1)
    grad_adapt_out_out = jnp.einsum(
        "sa,tsrc->artc", tree_picks, shared[:, :, 3], preferred_element_type=float_kind
    ).reshape(-1, model_width)
    return (
        layer_out,
        input_grad,
        grad_adapt_in,
        grad_adapt_out,
        grad_adapt_in_out,
        grad_adapt_out_out,
    )


def solution(mesh):
    return jax.shard_map(
        body,
        mesh=mesh,
        in_specs=(
            P("expert", None),
            P("expert", None),
            P(),
            P(),
            P("tensor"),
            P("tensor"),
            P(None, "tensor"),
            P(None, "tensor"),
            P(None, "tensor"),
            P("tensor", None),
            P("expert", None, "tensor"),
            P("expert", None, "tensor"),
            P("expert", "tensor", None),
            P(),
            P(None, None, "tensor"),
            P("tensor", None),
            P(),
            P("expert", None),
            P("expert", None),
            P("expert"),
            P("expert", None),
        ),
        out_specs=(
            P("expert", "tensor"),
            P("expert", None),
            P(),
            P(None, None, "tensor"),
            P("tensor", None),
            P(),
        ),
        check_vma=False,
    )
```

```python
import functools

import jax
import jax.numpy as jnp
from jax import lax
from jax.experimental import pallas as pl
from jax.experimental.pallas import tpu as pltpu
from jax.sharding import PartitionSpec as P

HD = 128
RANK = 16


EPSILON = 1e-05
ROPE_BASE = 10000.0
MASKED_SCORE = -1e30
VMEM_LIMIT = 52 * 2**20


def ancestry(parents):
    blocks = parents.shape[0]
    places = jnp.arange(blocks, dtype=jnp.int32)
    walker = places
    reached = walker[:, None] == places[None, :]
    for _ in range(blocks - 1):
        hits = (walker[:, None] == places[None, :]).astype(jnp.int32)
        walker = jnp.sum(hits * parents[None, :], axis=1)
        reached = reached | (walker[:, None] == places[None, :])
    return reached[None]


def rope_tables(reached, block_span, head_size):
    depths = jnp.sum(reached.astype(jnp.int32), axis=2) - 1
    offsets = jnp.arange(block_span, dtype=jnp.int32)
    located = (
        (depths[:, :, None] * block_span + offsets[None, None, :]).reshape(-1).astype(jnp.float32)
    )
    halves = head_size // 2
    speeds = ROPE_BASE ** (-2.0 * jnp.arange(halves, dtype=jnp.float32) / head_size)
    angles = located[:, None] * speeds[None, :]
    angles = jnp.concatenate([angles, angles], axis=1)
    return (jnp.cos(angles), jnp.sin(angles))


def rotate(values, cosine_table, sine_table):
    halves = values.shape[-1] // 2
    turned = jnp.concatenate([-values[..., halves:], values[..., :halves]], axis=-1)
    return values * cosine_table[:, None, :] + turned * sine_table[:, None, :]


def unrotate(values, cosine_table, sine_table):
    halves = values.shape[-1] // 2
    sined = values * sine_table[:, None, :]
    return values * cosine_table[:, None, :] + jnp.concatenate(
        [sined[..., halves:], -sined[..., :halves]], axis=-1
    )


def token_mask(reached, total_size):
    blocks = reached.shape[0]
    block_span = total_size // blocks
    widened = jnp.broadcast_to(
        reached[:, None, :, None], (blocks, block_span, blocks, block_span)
    ).reshape(total_size, total_size)
    positions = jnp.arange(total_size, dtype=jnp.int32)
    return widened & (positions[None, :] <= positions[:, None])


def norm_back(scaled_grad, values, inverse, model_width, inner_sum):
    return inverse * scaled_grad - values * inverse**3 * (inner_sum / model_width)


def divide_axes(owners, tensor_count):
    outer = 4
    return {
        "z": ("expert", outer, owners // outer, owners),
        "x": ("expert", owners // outer, 1, owners),
        "y": ("tensor", tensor_count // 2, 2, tensor_count),
        "c": ("tensor", 2, 1, tensor_count),
    }


def turn(array, axes, name, step):
    axis, length, stride, total = axes[name]
    pairs = []
    for index in range(total):
        place = (index // stride) % length
        moved = index + ((place + step) % length - place) * stride
        pairs.append((index, moved))
    return lax.ppermute(array, axis, pairs)


def ring(array, axes, name):
    held = [array]
    for _ in range(axes[name][1] - 1):
        held.append(turn(held[-1], axes, name, 1))
    return held


def wide(array):
    return array.astype(jnp.float32)


def low(array):
    return array.astype(jnp.bfloat16)


def gather_first(rows, axes):
    half = rows.shape[0] // 2
    return (
        jnp.concatenate(ring(rows[:half], axes, "x"), axis=0),
        jnp.concatenate(ring(rows[half:], axes, "y"), axis=0),
    )


def gather_second(pair, axes):
    return ring(pair[0], axes, "y") + ring(pair[1], axes, "x")


def send_sum(parts, axes, name):
    total = parts[-1]
    for part in parts[-2:0:-1]:
        total = low(wide(turn(total, axes, name, -1)) + wide(part))
    return turn(total, axes, name, -1)


def scatter_first(pieces, axes):
    span = axes["y"][1]
    return send_sum(pieces[:span], axes, "y"), send_sum(pieces[span:], axes, "x")


def scatter_second(pieces, came, axes):
    span = axes["y"][1]
    first = wide(pieces[0]) + wide(came[0])
    second = wide(pieces[span]) + wide(came[1])
    first = jnp.split(first, axes["x"][1], axis=0)
    second = jnp.split(second, axes["y"][1], axis=0)
    first_came = send_sum([low(part) for part in first], axes, "x")
    second_came = send_sum([low(part) for part in second], axes, "y")
    return (first[0], second[0]), (first_came, second_came)


def scatter_last(kept, came):
    return jnp.concatenate([kept[0] + wide(came[0]), kept[1] + wide(came[1])], axis=0)


def place_tensor(rows, axes, kind):
    rank = lax.axis_index("tensor")
    count = lax.axis_size("tensor")
    size = rows.shape[0]
    span = axes["y"][1]
    held = ring(rows, axes, "y")
    other = [turn(piece, axes, "c", 1) for piece in held]
    whole = jnp.zeros((count * size, rows.shape[1]), kind)
    core = rank % 2
    for step in range(span):
        level = (rank // 2 + span - step) % span
        whole = lax.dynamic_update_slice_in_dim(
            whole, held[step].astype(kind), (level * 2 + core) * size, 0
        )
        whole = lax.dynamic_update_slice_in_dim(
            whole, other[step].astype(kind), (level * 2 + 1 - core) * size, 0
        )
    return whole


def scatter_tensor(rows, axes):
    rank = lax.axis_index("tensor")
    count = lax.axis_size("tensor")
    size = rows.shape[0] // count
    span = axes["y"][1]
    blocks = rows.reshape(span, 2, size, rows.shape[1])
    core = rank % 2
    mine = lax.dynamic_index_in_dim(blocks, core, 1, keepdims=False)
    theirs = lax.dynamic_index_in_dim(blocks, 1 - core, 1, keepdims=False)
    mine = wide(mine) + wide(turn(theirs, axes, "c", 1))
    total = None
    for step in range(span - 1, -1, -1):
        level = (rank // 2 + span - step) % span
        part = lax.dynamic_index_in_dim(mine, level, 0, keepdims=False)
        total = part if total is None else wide(turn(low(total), axes, "y", -1)) + part
    return total


def swap_columns(rows, axes):
    rank = lax.axis_index("tensor")
    count = lax.axis_size("tensor")
    size, width = rows.shape
    span = axes["y"][1]
    share = width // count
    level, core = rank // 2, rank % 2
    whole = jnp.zeros((count * size, share), rows.dtype)
    for step in range(span):
        toward = (level + step) % span
        piece = lax.dynamic_slice_in_dim(rows, toward * 2 * share, 2 * share, 1)
        if step:
            piece = turn(piece, axes, "y", step)
        mine = lax.dynamic_slice_in_dim(piece, core * share, share, 1)
        theirs = lax.dynamic_slice_in_dim(piece, (1 - core) * share, share, 1)
        theirs = turn(theirs, axes, "c", 1)
        source = (level + span - step) % span
        whole = lax.dynamic_update_slice_in_dim(whole, mine, (source * 2 + core) * size, 0)
        whole = lax.dynamic_update_slice_in_dim(whole, theirs, (source * 2 + 1 - core) * size, 0)
    return whole


def sum_tensor(array, axes):
    total = wide(array) + wide(turn(array, axes, "c", 1))
    moving = low(total)
    result = total
    for _ in range(axes["y"][1] - 1):
        moving = turn(moving, axes, "y", 1)
        result = result + wide(moving)
    return result


def dot(left, right):
    return jnp.dot(left, right, preferred_element_type=jnp.float32)


def dot_t(left, right):
    return lax.dot_general(
        left, right, (((1,), (1,)), ((), ())), preferred_element_type=jnp.float32
    )


def t_dot(left, right):
    return lax.dot_general(
        left, right, (((0,), (0,)), ((), ())), preferred_element_type=jnp.float32
    )


def kernel_call(kernel, grid, ins, outs, operands, flops):
    moved = sum(array.size * array.dtype.itemsize for array in operands)
    return pl.pallas_call(
        kernel,
        grid=(grid,),
        in_specs=[pl.BlockSpec(block, index) for block, index in ins],
        out_specs=[pl.BlockSpec(block, index) for _, _, block, index in outs],
        out_shape=[jax.ShapeDtypeStruct(shape, kind) for shape, kind, _, _ in outs],
        compiler_params=pltpu.CompilerParams(vmem_limit_bytes=VMEM_LIMIT),
        cost_estimate=pl.CostEstimate(flops=flops, bytes_accessed=moved, transcendentals=0),
    )(*operands)


def stack_rows(refs, columns):
    return jnp.concatenate([ref[:, columns] for ref in refs], axis=0)


def hidden_kernel(count, width, *refs):
    pieces, (down_own, down_other, spread), (out, side_out) = (
        refs[:count],
        refs[count : count + 3],
        refs[count + 3 :],
    )
    side = stack_rows(pieces, slice(width, None))
    rows = stack_rows(pieces, slice(0, width))
    weight = dot(side, spread[...])
    out[0] = low(dot_t(rows, down_own[...]) * weight)
    out[1] = low(dot_t(rows, down_other[...]) * weight)
    side_out[...] = side


def hidden_call(pieces, down_own, down_other, spread, experts):
    width = down_own.shape[1]
    rows = sum(piece.shape[0] for piece in pieces)
    hidden = down_own.shape[0]
    part = hidden // experts
    side = spread.shape[0]
    whole = lambda e: (0, 0)
    ins = [(piece.shape, whole) for piece in pieces]
    ins += [((part, width), lambda e: (e, 0))] * 2
    ins += [((side, part), lambda e: (0, e))]
    outs = [
        ((2, rows, hidden), jnp.bfloat16, (2, rows, part), lambda e: (0, 0, e)),
        ((rows, side), jnp.bfloat16, (rows, side), whole),
    ]
    return kernel_call(
        functools.partial(hidden_kernel, len(pieces), width),
        experts,
        ins,
        outs,
        [*pieces, down_own, down_other, spread],
        4 * rows * hidden * width,
    )


def gate_kernel(count, *refs):
    pieces = refs[:count]
    gate_own, gate_other, up_own, up_other, spread, side, back = refs[count : count + 7]
    gate_out, up_out, hidden_out = refs[count + 7 :]
    rows = stack_rows(pieces, slice(None))
    weight = dot(side[...], spread[...])
    for half, (gate, up) in enumerate(((gate_own, up_own), (gate_other, up_other))):
        gate_value = dot(rows, gate[0])
        up_value = dot(rows, up[0])
        sigmoid = jax.nn.sigmoid(gate_value)
        silu = gate_value * sigmoid
        grad = wide(back[half])
        gate_out[half] = low(grad * up_value * (sigmoid + silu * (1.0 - sigmoid)))
        up_out[half] = low(grad * silu)
        hidden_out[half] = low(silu * up_value * weight)


def gate_call(pieces, gates, ups, spread, side, back):
    experts, width, part = gates[0].shape
    rows = side.shape[0]
    whole = lambda e: (0, 0)
    ins = [(piece.shape, whole) for piece in pieces]
    ins += [((1, width, part), lambda e: (e, 0, 0))] * 4
    ins += [((spread.shape[0], part), lambda e: (0, e)), (side.shape, whole)]
    ins += [((2, rows, part), lambda e: (0, 0, e))]
    out = (back.shape, jnp.bfloat16, (2, rows, part), lambda e: (0, 0, e))
    return kernel_call(
        functools.partial(gate_kernel, len(pieces)),
        experts,
        ins,
        [out] * 3,
        [*pieces, *gates, *ups, spread, side, back],
        8 * rows * experts * part * width,
    )


def rows_kernel(gate_grad, up_grad, gate_own, gate_other, up_own, up_other, *outs):
    total = None
    pairs = ((gate_grad, gate_own, gate_other), (up_grad, up_own, up_other))
    for grad, *weights in pairs:
        for half, weight in enumerate(weights):
            joined = jnp.concatenate([weight[e] for e in range(weight.shape[0])], axis=1)
            term = dot_t(grad[half], joined)
            total = term if total is None else total + term
    size = outs[0].shape[0]
    for index, out in enumerate(outs):
        out[...] = low(total[index * size : (index + 1) * size])


def rows_call(gate_grad, up_grad, gates, ups, count):
    experts, width, part = gates[0].shape
    rows = gate_grad.shape[1]
    tile = min(width, 512)
    ins = [(gate_grad.shape, lambda n: (0, 0, 0))] * 2
    ins += [((experts, tile, part), lambda n: (0, n, 0))] * 4
    size = rows // count
    out = ((size, width), jnp.bfloat16, (size, tile), lambda n: (0, n))
    return kernel_call(
        rows_kernel,
        width // tile,
        ins,
        [out] * count,
        [gate_grad, up_grad, *gates, *ups],
        8 * rows * experts * part * width,
    )


def down_kernel(hidden, down_own, down_other, *outs):
    total = dot(hidden[0], down_own[...]) + dot(hidden[1], down_other[...])
    size = outs[0].shape[0]
    for index, out in enumerate(outs):
        out[...] = low(total[index * size : (index + 1) * size])


def down_call(hidden, downs, count):
    _, rows, part = hidden.shape
    width = downs[0].shape[1]
    tile = min(width, 512)
    ins = [(hidden.shape, lambda n: (0, 0, 0))] + [((part, tile), lambda n: (0, n))] * 2
    size = rows // count
    out = ((size, width), jnp.bfloat16, (size, tile), lambda n: (0, n))
    return kernel_call(
        down_kernel,
        width // tile,
        ins,
        [out] * count,
        [hidden, *downs],
        4 * rows * part * width,
    )


def body(
    tokens,
    cotangent,
    attn_gain,
    ffn_gain,
    query_gain,
    key_gain,
    query_weight,
    key_weight,
    value_weight,
    output_weight,
    expert_gate,
    expert_up,
    expert_down,
    adapt_in,
    adapt_out,
    adapt_in_out,
    adapt_out_out,
    routes,
    gate_weights,
    block_parent,
    adapter_pick,
):
    rows_here, model_width = tokens.shape
    local_width = query_weight.shape[1]
    heads_here = local_width // HD
    tensor_rank = lax.axis_index("tensor")
    tensor_count = lax.axis_size("tensor")
    owners = lax.axis_size("expert")
    owner_rank = lax.axis_index("expert")
    axes = divide_axes(owners, tensor_count)
    far, near, span = axes["z"][1], axes["x"][1], axes["y"][1]
    experts_here, _, hidden_here = expert_gate.shape
    experts_all = experts_here * owners
    column_share = model_width // tensor_count
    row_share = rows_here // tensor_count
    float_kind = jnp.float32
    half_kind = jnp.bfloat16
    hold = lax.optimization_barrier

    def own_rows(array):
        return lax.dynamic_slice_in_dim(array, tensor_rank * row_share, row_share, 0)

    cotangent_rows = own_rows(cotangent)
    routes_rows = own_rows(routes)
    weights_rows = own_rows(gate_weights)
    route_weights = jnp.sum(
        jnp.where(
            routes_rows[:, :, None] == jnp.arange(experts_all, dtype=jnp.int32)[None, None, :],
            weights_rows[:, :, None],
            0.0,
        ),
        axis=1,
    )
    weights_high = low(route_weights)
    weights_low = low(route_weights - wide(weights_high))
    side_width = -(-2 * experts_all // 128) * 128
    side_pad = jnp.zeros((row_share, side_width - 2 * experts_all), half_kind)
    cot_plane = jnp.concatenate([cotangent_rows, weights_high, weights_low, side_pad], axis=1)
    side_index = jnp.arange(side_width, dtype=jnp.int32)
    hidden_owner = (
        owner_rank * experts_here
        + jnp.arange(experts_here * hidden_here, dtype=jnp.int32) // hidden_here
    )
    spread = low(
        (side_index[:, None] % experts_all == hidden_owner[None, :])
        & (side_index[:, None] < 2 * experts_all)
    )

    cot_next = turn(cot_plane, axes, "z", 1)
    cot_first = gather_first(cot_plane, axes)
    inputs = wide(tokens)
    first_gain = wide(attn_gain)
    second_gain = wide(ffn_gain)
    first_inverse = lax.rsqrt(jnp.mean(inputs * inputs, axis=1, keepdims=True) + EPSILON)
    normed_in = low(inputs * first_inverse * first_gain)
    reached = ancestry(block_parent)
    cosine_table, sine_table = rope_tables(reached, rows_here // block_parent.shape[0], HD)
    key_mask = token_mask(reached[0], rows_here)
    picked = jnp.argmax(adapter_pick[0]) * RANK
    adapt_in_used = lax.dynamic_slice_in_dim(adapt_in, picked, RANK, 2)
    adapt_out_used = lax.dynamic_slice_in_dim(adapt_out, picked, RANK, 1)
    mix_in_used = lax.dynamic_slice_in_dim(adapt_in_out, picked, RANK, 1)
    mix_out_used = lax.dynamic_slice_in_dim(adapt_out_out, picked, RANK, 0)
    lowrank = low(
        jnp.einsum("td,idr->itr", normed_in, adapt_in_used, preferred_element_type=float_kind)
    )
    matrices = (query_weight, key_weight, value_weight)
    query_raw, key_raw, value_raw = [
        dot(normed_in, matrices[projection]) + dot(lowrank[projection], adapt_out_used[projection])
        for projection in range(3)
    ]

    cot_planes = [None] * far
    cot_next, cot_first, query_raw, key_raw, value_raw = hold(
        (cot_next, cot_first, query_raw, key_raw, value_raw)
    )
    cot_later = turn(cot_next, axes, "z", 1)
    cot_planes[0] = gather_second(cot_first, axes)
    cot_first = gather_first(cot_next, axes)
    query_squares, key_squares = lax.psum(
        (jnp.sum(query_raw * query_raw, axis=1), jnp.sum(key_raw * key_raw, axis=1)), "tensor"
    )
    query_inverse = lax.rsqrt(query_squares / model_width + EPSILON)[:, None]
    key_inverse = lax.rsqrt(key_squares / model_width + EPSILON)[:, None]
    query_scale = wide(query_gain)
    key_scale = wide(key_gain)
    queries = low(
        rotate(
            (query_raw * query_inverse * query_scale).reshape(rows_here, heads_here, HD),
            cosine_table,
            sine_table,
        )
    )
    keys = low(
        rotate(
            (key_raw * key_inverse * key_scale).reshape(rows_here, heads_here, HD),
            cosine_table,
            sine_table,
        )
    )
    values = low(value_raw).reshape(rows_here, heads_here, HD)
    score_scale = HD ** (-0.5)
    scores = (
        jnp.einsum("qhd,khd->hqk", queries, keys, preferred_element_type=float_kind) * score_scale
    )
    scores = jnp.where(key_mask[None], scores, MASKED_SCORE)
    row_max = jnp.max(scores, axis=2, keepdims=True)
    raised = jnp.exp(scores - row_max)
    row_total = jnp.sum(raised, axis=2, keepdims=True)
    weights_half = low(raised / row_total)
    log_total = row_max + jnp.log(row_total)
    attended = low(
        jnp.einsum(
            "hqk,khd->qhd", weights_half, values, preferred_element_type=float_kind
        ).reshape(rows_here, local_width)
    )

    cot_next, cot_first, cot_planes[0], attended = hold(
        (cot_later, cot_first, cot_planes[0], attended)
    )
    cot_later = turn(cot_next, axes, "z", 1)
    cot_planes[1] = gather_second(cot_first, axes)
    cot_first = gather_first(cot_next, axes)
    gates = (expert_gate, turn(expert_gate, axes, "c", 1))
    ups = (expert_up, turn(expert_up, axes, "c", 1))
    down_tall = expert_down.reshape(-1, model_width)
    downs = (down_tall, turn(down_tall, axes, "c", 1))
    picks = lax.all_gather(adapter_pick.astype(float_kind), "expert", axis=0, tiled=True)
    mixing_pad = jnp.zeros((local_width, 128 - RANK), half_kind)
    output_used = jnp.concatenate([output_weight, mix_in_used, mixing_pad], axis=1)
    branch_rows = scatter_tensor(low(dot(attended, output_used)), axes)
    mixed_rows = low(branch_rows[:, model_width : model_width + RANK])
    resid_rows = (
        wide(own_rows(tokens)) + branch_rows[:, :model_width] + dot(mixed_rows, mix_out_used)
    )
    second_inverse = lax.rsqrt(
        jnp.mean(resid_rows * resid_rows, axis=1, keepdims=True) + EPSILON
    )
    norm_plane = low(resid_rows * second_inverse * second_gain)

    cot_next, cot_first, cot_planes[1], norm_plane, gates, ups, downs = hold(
        (cot_later, cot_first, cot_planes[1], norm_plane, gates, ups, downs)
    )
    norm_next = turn(norm_plane, axes, "z", 1)
    norm_first = gather_first(norm_plane, axes)
    cot_planes[2] = gather_second(cot_first, axes)
    cot_first = gather_first(cot_next, axes)
    backs = [None] * far

    def hidden_step(index):
        backs[index] = hidden_call(cot_planes[index], *downs, spread, experts_here)

    hidden_step(0)

    norm_planes = [None] * far
    norm_next, norm_first, cot_planes[2], cot_first, backs[0] = hold(
        (norm_next, norm_first, cot_planes[2], cot_first, backs[0])
    )
    norm_later = turn(norm_next, axes, "z", 1)
    norm_planes[0] = gather_second(norm_first, axes)
    norm_first = gather_first(norm_next, axes)
    cot_planes[3] = gather_second(cot_first, axes)
    hidden_step(1)
    hidden_step(2)

    norm_next, norm_first, norm_planes[0], cot_planes[3], backs[1], backs[2] = hold(
        (norm_later, norm_first, norm_planes[0], cot_planes[3], backs[1], backs[2])
    )
    norm_later = turn(norm_next, axes, "z", 1)
    norm_planes[1] = gather_second(norm_first, axes)
    norm_first = gather_first(norm_next, axes)
    gate_grads, up_grads, hiddens = [None] * far, [None] * far, [None] * far

    def gate_step(index):
        back, side = backs[index]
        gate_grads[index], up_grads[index], hiddens[index] = gate_call(
            norm_planes[index], gates, ups, spread, side, back
        )

    parts = [None] * far

    def rows_step(index):
        parts[index] = rows_call(gate_grads[index], up_grads[index], gates, ups, near + span)

    hidden_step(3)
    gate_step(0)

    norm_next, norm_first, norm_planes[1], backs[3], gate_grads[0] = hold(
        (norm_later, norm_first, norm_planes[1], backs[3], gate_grads[0])
    )
    norm_planes[2] = gather_second(norm_first, axes)
    norm_first = gather_first(norm_next, axes)
    gate_step(1)
    rows_step(1)

    norm_first, norm_planes[2], parts[1] = hold((norm_first, norm_planes[2], parts[1]))
    norm_planes[3] = gather_second(norm_first, axes)
    came = [None] * far
    kept = [None] * far
    sums = [None] * far
    came[1] = scatter_first(parts[1], axes)
    gate_step(2)
    rows_step(2)

    norm_planes[3], came[1], parts[2] = hold((norm_planes[3], came[1], parts[2]))
    kept[1], came[1] = scatter_second(parts[1], came[1], axes)
    came[2] = scatter_first(parts[2], axes)
    gate_step(3)
    rows_step(3)

    kept[1], came[1], came[2], parts[3] = hold((kept[1], came[1], came[2], parts[3]))
    sums[1] = scatter_last(kept[1], came[1])
    ring_sum = turn(low(sums[1]), axes, "z", 1)
    kept[2], came[2] = scatter_second(parts[2], came[2], axes)
    came[3] = scatter_first(parts[3], axes)
    rows_step(0)

    ring_sum, kept[2], came[2], came[3], parts[0] = hold(
        (ring_sum, kept[2], came[2], came[3], parts[0])
    )
    ring_sum = turn(low(wide(ring_sum) + scatter_last(kept[2], came[2])), axes, "z", 1)
    kept[3], came[3] = scatter_second(parts[3], came[3], axes)
    came[0] = scatter_first(parts[0], axes)
    mixes = [None] * far

    def down_step(index):
        mixes[index] = down_call(hiddens[index], downs, near + span)

    down_step(1)
    down_step(2)

    ring_sum, kept[3], came[3], came[0], mixes[1], mixes[2] = hold(
        (ring_sum, kept[3], came[3], came[0], mixes[1], mixes[2])
    )
    ring_sum = turn(low(wide(ring_sum) + scatter_last(kept[3], came[3])), axes, "z", 1)
    kept[0], came[0] = scatter_second(parts[0], came[0], axes)
    mix_came = [None] * far
    mix_kept = [None] * far
    mix_came[1] = scatter_first(mixes[1], axes)
    down_step(3)
    down_step(0)

    ring_sum, kept[0], came[0], mix_came[1], mixes[3], mixes[0] = hold(
        (ring_sum, kept[0], came[0], mix_came[1], mixes[3], mixes[0])
    )
    ffn_rows_grad = wide(ring_sum) + scatter_last(kept[0], came[0])
    second_scaled = ffn_rows_grad * second_gain
    resid_grad_rows = wide(cotangent_rows) + norm_back(
        second_scaled,
        resid_rows,
        second_inverse,
        model_width,
        jnp.sum(second_scaled * resid_rows, axis=1, keepdims=True),
    )
    branch_sent = jnp.concatenate(
        [low(resid_grad_rows), mixed_rows, jnp.zeros((row_share, 128 - RANK), half_kind)], axis=1
    )
    branch_whole = place_tensor(branch_sent, axes, half_kind)
    mix_kept[1], mix_came[1] = scatter_second(mixes[1], mix_came[1], axes)

    branch_whole, mix_kept[1], mix_came[1] = hold((branch_whole, mix_kept[1], mix_came[1]))
    mix_sum = turn(low(scatter_last(mix_kept[1], mix_came[1])), axes, "z", 1)
    mix_came[2] = scatter_first(mixes[2], axes)
    branch_grad = branch_whole[:, :model_width]
    mixed = branch_whole[:, model_width : model_width + RANK]
    mixed_grad = low(dot_t(branch_grad, mix_out_used))
    attended_grad = low(dot_t(branch_grad, output_weight) + dot_t(mixed_grad, mix_in_used))
    attended_grad = attended_grad.reshape(rows_here, heads_here, HD)
    scores = (
        jnp.einsum("qhd,khd->hqk", queries, keys, preferred_element_type=float_kind) * score_scale
    )
    softmax_full = jnp.where(key_mask[None], jnp.exp(scores - log_total), 0.0)
    softmax_half = low(softmax_full)
    value_grad = low(
        jnp.einsum("hqk,qhd->khd", softmax_half, attended_grad, preferred_element_type=float_kind)
    )
    prob_grad = jnp.einsum("qhd,khd->hqk", attended_grad, values, preferred_element_type=float_kind)
    score_grad = low(
        softmax_full * (prob_grad - jnp.sum(softmax_full * prob_grad, axis=2, keepdims=True))
    )
    query_grad = (
        jnp.einsum("hqk,khd->qhd", score_grad, keys, preferred_element_type=float_kind)
        * score_scale
    )
    key_grad = (
        jnp.einsum("hqk,qhd->khd", score_grad, queries, preferred_element_type=float_kind)
        * score_scale
    )
    query_scaled = (
        unrotate(query_grad, cosine_table, sine_table).reshape(rows_here, local_width) * query_scale
    )
    key_scaled = (
        unrotate(key_grad, cosine_table, sine_table).reshape(rows_here, local_width) * key_scale
    )

    query_scaled, key_scaled, value_grad, mix_sum, mix_came[2] = hold(
        (query_scaled, key_scaled, value_grad, mix_sum, mix_came[2])
    )
    mix_kept[2], mix_came[2] = scatter_second(mixes[2], mix_came[2], axes)
    mix_came[3] = scatter_first(mixes[3], axes)
    query_inner, key_inner = lax.psum(
        (jnp.sum(query_scaled * query_raw, axis=1), jnp.sum(key_scaled * key_raw, axis=1)), "tensor"
    )
    query_raw_grad = low(
        norm_back(query_scaled, query_raw, query_inverse, model_width, query_inner[:, None])
    )
    key_raw_grad = low(
        norm_back(key_scaled, key_raw, key_inverse, model_width, key_inner[:, None])
    )
    value_raw_grad = value_grad.reshape(rows_here, local_width)
    raw_grads = (query_raw_grad, key_raw_grad, value_raw_grad)
    lowrank_part = low(
        jnp.concatenate(
            [dot_t(raw_grads[projection], adapt_out_used[projection]) for projection in range(3)],
            axis=1,
        )
    )
    normed_part = low(
        dot_t(query_raw_grad, query_weight)
        + dot_t(key_raw_grad, key_weight)
        + dot_t(value_raw_grad, value_weight)
    )

    normed_part, lowrank_part, mix_kept[2], mix_came[2], mix_came[3] = hold(
        (normed_part, lowrank_part, mix_kept[2], mix_came[2], mix_came[3])
    )
    mix_sum = turn(low(wide(mix_sum) + scatter_last(mix_kept[2], mix_came[2])), axes, "z", 1)
    mix_kept[3], mix_came[3] = scatter_second(mixes[3], mix_came[3], axes)
    mix_came[0] = scatter_first(mixes[0], axes)
    lowrank_grad = low(sum_tensor(lowrank_part, axes))
    normed_grad_rows = scatter_tensor(normed_part, axes)
    lowrank_rows = own_rows(lowrank_grad)
    for projection in range(3):
        normed_grad_rows = normed_grad_rows + dot_t(
            lowrank_rows[:, projection * RANK : (projection + 1) * RANK], adapt_in_used[projection]
        )
    first_scaled = normed_grad_rows * first_gain
    inputs_rows = own_rows(inputs)
    input_grad_rows = resid_grad_rows + norm_back(
        first_scaled,
        inputs_rows,
        own_rows(first_inverse),
        model_width,
        jnp.sum(first_scaled * inputs_rows, axis=1, keepdims=True),
    )
    normed_share = lax.dynamic_slice_in_dim(
        normed_in, tensor_rank * column_share, column_share, 1
    )
    branch_share = lax.dynamic_slice_in_dim(
        branch_grad, tensor_rank * column_share, column_share, 1
    )
    compact = low(
        jnp.concatenate(
            [t_dot(lowrank_grad, normed_share), t_dot(mixed, branch_share)]
            + [t_dot(lowrank[projection], raw_grads[projection]) for projection in range(3)]
            + [t_dot(mixed_grad, attended)],
            axis=0,
        )
    )

    input_grad_rows, compact, mix_sum, mix_kept[3], mix_came[3], mix_came[0] = hold(
        (low(input_grad_rows), compact, mix_sum, mix_kept[3], mix_came[3], mix_came[0])
    )
    input_grad = place_tensor(input_grad_rows, axes, float_kind)
    mix_sum = turn(low(wide(mix_sum) + scatter_last(mix_kept[3], mix_came[3])), axes, "z", 1)
    mix_kept[0], mix_came[0] = scatter_second(mixes[0], mix_came[0], axes)
    layer_rows = low(resid_rows + wide(mix_sum) + scatter_last(mix_kept[0], mix_came[0]))
    layer_out = swap_columns(layer_rows, axes)

    kinds = compact.shape[0] // RANK
    trees = jnp.concatenate(
        ring(jnp.concatenate(ring(compact, axes, "x"), axis=0), axes, "z"), axis=0
    )
    tree_index = (
        (owner_rank // near + far - jnp.arange(far, dtype=jnp.int32)[:, None]) % far * near
        + (owner_rank % near + near - jnp.arange(near, dtype=jnp.int32)[None, :]) % near
    ).reshape(-1)
    tree_picks = low(
        dot(
            (tree_index[:, None] == jnp.arange(owners, dtype=jnp.int32)[None, :]).astype(
                float_kind
            ),
            picks,
        )
    )
    trees = trees.reshape(owners, kinds, RANK, column_share)
    grad_adapt_out = jnp.einsum(
        "sa,skrc->karc", tree_picks, trees[:, 4:7], preferred_element_type=float_kind
    ).reshape(3, -1, column_share)
    grad_adapt_in_out = jnp.einsum(
        "sa,src->car", tree_picks, trees[:, 7], preferred_element_type=float_kind
    ).reshape(column_share, -1)
    shared = place_tensor(
        trees[:, :4].reshape(owners * 4 * RANK, column_share), axes, half_kind
    ).reshape(tensor_count, owners, 4, RANK, column_share)
    grad_adapt_in = jnp.einsum(
        "sa,tskrc->ktcar", tree_picks, shared[:, :, :3], preferred_element_type=float_kind
    ).reshape(3, model_width, -1)
    grad_adapt_out_out = jnp.einsum(
        "sa,tsrc->artc", tree_picks, shared[:, :, 3], preferred_element_type=float_kind
    ).reshape(-1, model_width)
    return (
        layer_out,
        input_grad,
        grad_adapt_in,
        grad_adapt_out,
        grad_adapt_in_out,
        grad_adapt_out_out,
    )


def solution(mesh):
    return jax.shard_map(
        body,
        mesh=mesh,
        in_specs=(
            P("expert", None),
            P("expert", None),
            P(),
            P(),
            P("tensor"),
            P("tensor"),
            P(None, "tensor"),
            P(None, "tensor"),
            P(None, "tensor"),
            P("tensor", None),
            P("expert", None, "tensor"),
            P("expert", None, "tensor"),
            P("expert", "tensor", None),
            P(),
            P(None, None, "tensor"),
            P("tensor", None),
            P(),
            P("expert", None),
            P("expert", None),
            P("expert"),
            P("expert", None),
        ),
        out_specs=(
            P("expert", "tensor"),
            P("expert", None),
            P(),
            P(None, None, "tensor"),
            P("tensor", None),
            P(),
        ),
        check_vma=False,
    )
```

```python
import functools

import jax
import jax.numpy as jnp
from jax import lax
from jax.experimental import pallas as pl
from jax.experimental.pallas import tpu as pltpu
from jax.sharding import PartitionSpec as P

HD = 128
RANK = 16


EPSILON = 1e-05
ROPE_BASE = 10000.0
MASKED_SCORE = -1e30
VMEM_LIMIT = 56 * 2**20


def ancestry(parents):
    blocks = parents.shape[0]
    places = jnp.arange(blocks, dtype=jnp.int32)
    walker = places
    reached = walker[:, None] == places[None, :]
    for _ in range(blocks - 1):
        hits = (walker[:, None] == places[None, :]).astype(jnp.int32)
        walker = jnp.sum(hits * parents[None, :], axis=1)
        reached = reached | (walker[:, None] == places[None, :])
    return reached[None]


def rope_tables(reached, block_span, head_size):
    depths = jnp.sum(reached.astype(jnp.int32), axis=2) - 1
    offsets = jnp.arange(block_span, dtype=jnp.int32)
    located = (
        (depths[:, :, None] * block_span + offsets[None, None, :]).reshape(-1).astype(jnp.float32)
    )
    halves = head_size // 2
    speeds = ROPE_BASE ** (-2.0 * jnp.arange(halves, dtype=jnp.float32) / head_size)
    angles = located[:, None] * speeds[None, :]
    angles = jnp.concatenate([angles, angles], axis=1)
    return (jnp.cos(angles), jnp.sin(angles))


def unrotate(values, cosine_table, sine_table):
    halves = values.shape[-1] // 2
    sined = values * sine_table[:, None, :]
    return values * cosine_table[:, None, :] + jnp.concatenate(
        [sined[..., halves:], -sined[..., :halves]], axis=-1
    )


def token_mask(reached, total_size):
    blocks = reached.shape[0]
    block_span = total_size // blocks
    widened = jnp.broadcast_to(
        reached[:, None, :, None], (blocks, block_span, blocks, block_span)
    ).reshape(total_size, total_size)
    positions = jnp.arange(total_size, dtype=jnp.int32)
    return widened & (positions[None, :] <= positions[:, None])


def norm_back(scaled_grad, values, inverse, model_width, inner_sum):
    return inverse * scaled_grad - values * inverse**3 * (inner_sum / model_width)


def divide_axes(owners, tensor_count):
    outer = 4
    return {
        "z": ("expert", outer, owners // outer, owners),
        "x": ("expert", owners // outer, 1, owners),
        "y": ("tensor", tensor_count // 2, 2, tensor_count),
        "c": ("tensor", 2, 1, tensor_count),
    }


def turn(array, axes, name, step):
    axis, length, stride, total = axes[name]
    pairs = []
    for index in range(total):
        place = (index // stride) % length
        moved = index + ((place + step) % length - place) * stride
        pairs.append((index, moved))
    return lax.ppermute(array, axis, pairs)


def ring(array, axes, name):
    held = [array]
    for _ in range(axes[name][1] - 1):
        held.append(turn(held[-1], axes, name, 1))
    return held


def wide(array):
    return array.astype(jnp.float32)


def low(array):
    return array.astype(jnp.bfloat16)


def gather_first(rows, axes):
    half = rows.shape[0] // 2
    return (
        jnp.concatenate(ring(rows[:half], axes, "x"), axis=0),
        jnp.concatenate(ring(rows[half:], axes, "y"), axis=0),
    )


def gather_second(pair, axes):
    return ring(pair[0], axes, "y") + ring(pair[1], axes, "x")


def send_sum(parts, axes, name):
    total = parts[-1]
    for part in parts[-2:0:-1]:
        total = low(wide(turn(total, axes, name, -1)) + wide(part))
    return turn(total, axes, name, -1)


def scatter_first(pieces, axes):
    span = axes["y"][1]
    return send_sum(pieces[:span], axes, "y"), send_sum(pieces[span:], axes, "x")


def scatter_second(pieces, came, axes):
    span = axes["y"][1]
    first = wide(pieces[0]) + wide(came[0])
    second = wide(pieces[span]) + wide(came[1])
    first = jnp.split(first, axes["x"][1], axis=0)
    second = jnp.split(second, axes["y"][1], axis=0)
    first_came = send_sum([low(part) for part in first], axes, "x")
    second_came = send_sum([low(part) for part in second], axes, "y")
    return (first[0], second[0]), (first_came, second_came)


def scatter_last(kept, came):
    return jnp.concatenate([kept[0] + wide(came[0]), kept[1] + wide(came[1])], axis=0)


def place_tensor(rows, axes, kind):
    rank = lax.axis_index("tensor")
    count = lax.axis_size("tensor")
    size = rows.shape[0]
    span = axes["y"][1]
    held = ring(rows, axes, "y")
    other = [turn(piece, axes, "c", 1) for piece in held]
    whole = jnp.zeros((count * size, rows.shape[1]), kind)
    core = rank % 2
    for step in range(span):
        level = (rank // 2 + span - step) % span
        whole = lax.dynamic_update_slice_in_dim(
            whole, held[step].astype(kind), (level * 2 + core) * size, 0
        )
        whole = lax.dynamic_update_slice_in_dim(
            whole, other[step].astype(kind), (level * 2 + 1 - core) * size, 0
        )
    return whole


def scatter_tensor(mine, theirs, axes):
    rank = lax.axis_index("tensor")
    span = axes["y"][1]
    size = mine.shape[0] // span
    came = turn(theirs, axes, "c", 1)
    total = None
    for step in range(span - 1, -1, -1):
        level = (rank // 2 + span - step) % span
        part = wide(lax.dynamic_slice_in_dim(mine, level * size, size, 0)) + wide(
            lax.dynamic_slice_in_dim(came, level * size, size, 0)
        )
        if step:
            total = turn(low(part if total is None else part + wide(total)), axes, "y", -1)
    return part, total


def swap_columns(rows, axes):
    rank = lax.axis_index("tensor")
    count = lax.axis_size("tensor")
    size, width = rows.shape
    span = axes["y"][1]
    share = width // count
    level, core = rank // 2, rank % 2
    whole = jnp.zeros((count * size, share), rows.dtype)
    for step in range(span):
        toward = (level + step) % span
        piece = lax.dynamic_slice_in_dim(rows, toward * 2 * share, 2 * share, 1)
        if step:
            piece = turn(piece, axes, "y", step)
        mine = lax.dynamic_slice_in_dim(piece, core * share, share, 1)
        theirs = lax.dynamic_slice_in_dim(piece, (1 - core) * share, share, 1)
        theirs = turn(theirs, axes, "c", 1)
        source = (level + span - step) % span
        whole = lax.dynamic_update_slice_in_dim(whole, mine, (source * 2 + core) * size, 0)
        whole = lax.dynamic_update_slice_in_dim(whole, theirs, (source * 2 + 1 - core) * size, 0)
    return whole


def sum_tensor(array, axes):
    total = wide(array) + wide(turn(array, axes, "c", 1))
    moving = low(total)
    result = total
    for _ in range(axes["y"][1] - 1):
        moving = turn(moving, axes, "y", 1)
        result = result + wide(moving)
    return result


def dot(left, right):
    return jnp.dot(left, right, preferred_element_type=jnp.float32)


def dot_t(left, right):
    return lax.dot_general(
        left, right, (((1,), (1,)), ((), ())), preferred_element_type=jnp.float32
    )


def t_dot(left, right):
    return lax.dot_general(
        left, right, (((0,), (0,)), ((), ())), preferred_element_type=jnp.float32
    )


ANY = pl.BlockSpec(memory_space=pl.ANY)


def whole(array):
    shape = array.shape
    return pl.BlockSpec(shape, lambda *_: (0,) * len(shape))


def kernel_call(kernel, grid, in_specs, out_specs, out_shape, operands, flops, scratch=(), scalars=0):
    moved = sum(array.size * array.dtype.itemsize for array in operands)
    return pl.pallas_call(
        kernel,
        grid_spec=pltpu.PrefetchScalarGridSpec(
            num_scalar_prefetch=scalars,
            grid=grid,
            in_specs=in_specs,
            out_specs=out_specs,
            scratch_shapes=list(scratch),
        ),
        out_shape=[jax.ShapeDtypeStruct(shape, kind) for shape, kind in out_shape],
        compiler_params=pltpu.CompilerParams(vmem_limit_bytes=VMEM_LIMIT),
        cost_estimate=pl.CostEstimate(flops=flops, bytes_accessed=moved, transcendentals=0),
    )(*operands)


def project_kernel(
    tokens, gain, query_weight, key_weight, value_weight, adapt_in, adapt_out, select,
    normed_out, lowrank_out, query_out, key_out, value_out, squares_out,
    weights, maps, sems,
):
    copies = [pltpu.make_async_copy(adapt_in, maps, sems.at[3])]
    for index, source in enumerate((query_weight, key_weight, value_weight)):
        copies.append(pltpu.make_async_copy(source, weights.at[index], sems.at[index]))
    for copy in copies:
        copy.start()
    inputs = wide(tokens[...])
    inverse = lax.rsqrt(jnp.mean(inputs * inputs, axis=1, keepdims=True) + EPSILON)
    normed_out[...] = low(inputs * inverse * gain[...])
    copies[0].wait()
    for index in range(3):
        lowrank_out[index] = low(dot(normed_out[...], maps[index]) * select[...])
    squares = []
    for index, out in enumerate((query_out, key_out, value_out)):
        copies[index + 1].wait()
        raw = dot(normed_out[...], weights[index]) + dot(lowrank_out[index], adapt_out[index])
        out[...] = raw
        squares.append(jnp.sum(raw * raw, axis=1, keepdims=True))
    lane = lax.broadcasted_iota(jnp.int32, (tokens.shape[0], 128), 1)
    columns = jnp.where(lane == 0, squares[0], jnp.where(lane == 1, squares[1], 0.0))
    squares_out[...] = jnp.transpose(columns)[:8]


def project_call(tokens, gain, weights, adapt_in, adapt_out, select):
    rows, width = tokens.shape
    local = weights[0].shape[1]
    rank = adapt_in.shape[2]
    out_shape = [((rows, width), jnp.bfloat16), ((3, rows, rank), jnp.bfloat16)]
    out_shape += [((rows, local), jnp.float32)] * 3 + [((8, rows), jnp.float32)]
    operands = [tokens, gain, *weights, adapt_in, adapt_out, select]
    return kernel_call(
        project_kernel,
        (1,),
        [whole(tokens), whole(gain), ANY, ANY, ANY, ANY, whole(adapt_out), whole(select)],
        [pl.BlockSpec(shape, lambda *_, size=len(shape): (0,) * size) for shape, _ in out_shape],
        out_shape,
        operands,
        6 * rows * width * local,
        [
            pltpu.VMEM((3, width, local), jnp.bfloat16),
            pltpu.VMEM(adapt_in.shape, jnp.bfloat16),
            pltpu.SemaphoreType.DMA((4,)),
        ],
    )


def spread_columns(rows):
    return jnp.transpose(jnp.concatenate([rows] * (128 // rows.shape[0]), axis=0))


def turned(values):
    half = values.shape[1] // 2
    return jnp.concatenate([values[:, half:], values[:, :half]], axis=1)


def attend_kernel(
    width, size, core, squares, query_raw, key_raw, value_raw, query_gain, key_gain, cosine, sine,
    mask, output_weight, mix_in, queries, keys, values, attended, mine, theirs, held, weight, sem,
):
    head = pl.program_id(0)
    last = pl.num_programs(0) - 1
    copy = pltpu.make_async_copy(output_weight, weight, sem)

    @pl.when(head == 0)
    def _():
        copy.start()

    inverse = lax.rsqrt(spread_columns(squares[...]) / width + EPSILON)
    query = query_raw[...] * inverse[:, 0:1] * query_gain[...]
    key = key_raw[...] * inverse[:, 1:2] * key_gain[...]
    query = low(query * cosine[...] + turned(query) * sine[...])
    key = low(key * cosine[...] + turned(key) * sine[...])
    value = low(value_raw[...])
    queries[...] = query
    keys[...] = key
    values[...] = value
    scores = dot_t(query, key) * HD ** (-0.5) + mask[...]
    raised = jnp.exp(scores - jnp.max(scores, axis=1, keepdims=True))
    weights = low(raised / jnp.sum(raised, axis=1, keepdims=True))
    result = low(dot(weights, value))
    attended[...] = result
    held[head] = result

    @pl.when(head == last)
    def _():
        copy.wait()
        heads = held.shape[0]
        levels = mine.shape[0] // size
        for out, offset in ((mine, core[0]), (theirs, 1 - core[0])):
            taken = []
            for level in range(levels):
                rows = pl.ds(pl.multiple_of((2 * level + offset) * size, size), size)
                taken.append(
                    jnp.concatenate([held[index, rows, :] for index in range(heads)], axis=1)
                )
            taken = jnp.concatenate(taken, axis=0)
            out[:, :width] = dot(taken, weight[...]).astype(out.dtype)
            out[:, width:] = dot(taken, mix_in[...]).astype(out.dtype)


def attend_call(core, squares, raws, gains, tables, mask, output_weight, mix_in, size):
    rows, local = raws[0].shape
    heads = local // HD
    width = output_weight.shape[1]
    wide_width = width + mix_in.shape[1]
    block = pl.BlockSpec((rows, HD), lambda head, *_: (0, head))
    gain_block = pl.BlockSpec((1, HD), lambda head, *_: (0, head))
    fixed = pl.BlockSpec((rows // 2, wide_width), lambda *_: (0, 0))
    operands = [core, squares, *raws, *gains, *tables, mask, output_weight, mix_in]
    return kernel_call(
        functools.partial(attend_kernel, width, size),
        (heads,),
        [whole(squares)] + [block] * 3 + [gain_block] * 2
        + [whole(tables[0]), whole(tables[1]), whole(mask), ANY, whole(mix_in)],
        [block] * 4 + [fixed] * 2,
        [((rows, local), jnp.bfloat16)] * 4
        + [((rows // 2, wide_width), jnp.float32), ((rows // 2, wide_width), jnp.bfloat16)],
        operands,
        4 * rows * rows * local + 2 * rows * local * width,
        [
            pltpu.VMEM((heads, rows, HD), jnp.bfloat16),
            pltpu.VMEM(output_weight.shape, jnp.bfloat16),
            pltpu.SemaphoreType.DMA,
        ],
        1,
    )


def resid_kernel(
    width, kept, came, tokens, mix_out, select, gain, resid_out, norm_out, mixed_out
):
    mixed = low((kept[:, width:] + wide(came[:, width:])) * select[...])
    mixed_out[...] = mixed
    resid = (
        wide(tokens[...])
        + (kept[:, :width] + wide(came[:, :width]))
        + dot(mixed, mix_out[...])
    )
    resid_out[...] = resid
    inverse = lax.rsqrt(jnp.mean(resid * resid, axis=1, keepdims=True) + EPSILON)
    norm_out[...] = low(resid * inverse * gain[...])


def resid_call(kept, came, tokens, mix_out, select, gain):
    rows, width = tokens.shape
    out_shape = [((rows, width), jnp.float32), ((rows, width), jnp.bfloat16)]
    out_shape += [((rows, mix_out.shape[0]), jnp.bfloat16)]
    operands = [kept, came, tokens, mix_out, select, gain]
    return kernel_call(
        functools.partial(resid_kernel, width),
        (1,),
        [whole(array) for array in operands],
        [pl.BlockSpec(shape, lambda *_: (0, 0)) for shape, _ in out_shape],
        out_shape,
        operands,
        2 * rows * width * mix_out.shape[0],
    )


def hidden_kernel(count, width, *refs):
    pieces, (down_own, down_other, spread), (out, side_out), (rows, side) = (
        refs[:count],
        refs[count : count + 3],
        refs[count + 3 : count + 5],
        refs[count + 5 :],
    )
    step = pl.program_id(0)
    size = pieces[0].shape[0]

    @pl.when(step == 0)
    def _():
        for index, piece in enumerate(pieces):
            place = slice(index * size, (index + 1) * size)
            rows[place] = piece[:, :width]
            side[place] = piece[:, width:]
        side_out[...] = side[...]

    def emit(down):
        grad = dot_t(rows[...], down[...]) * dot(side[...], spread[...])
        part = out.shape[2]
        for index in range(out.shape[0]):
            out[index] = low(grad[:, index * part : (index + 1) * part])

    half = pl.num_programs(0) // 2

    @pl.when(step < half)
    def _():
        emit(down_own)

    @pl.when(step >= half)
    def _():
        emit(down_other)


def hidden_call(pieces, downs, spread, experts):
    hidden, width = downs[0].shape
    rows = sum(piece.shape[0] for piece in pieces)
    part = hidden // experts
    side = spread.shape[0]
    pair = 2 * part
    half = experts // 2
    last = half - 1
    return kernel_call(
        functools.partial(hidden_kernel, len(pieces), width),
        (2 * half,),
        [whole(piece) for piece in pieces]
        + [
            pl.BlockSpec((pair, width), lambda n: (jnp.minimum(n, last), 0)),
            pl.BlockSpec((pair, width), lambda n: (jnp.maximum(n - half, 0), 0)),
            pl.BlockSpec((side, pair), lambda n: (0, lax.rem(n, half))),
        ],
        [
            pl.BlockSpec((2, rows, part), lambda n: (n, 0, 0)),
            pl.BlockSpec((rows, side), lambda n: (0, 0)),
        ],
        [((2 * experts, rows, part), jnp.bfloat16), ((rows, side), jnp.bfloat16)],
        [*pieces, *downs, spread],
        4 * rows * hidden * width,
        [pltpu.VMEM((rows, width), jnp.bfloat16), pltpu.VMEM((rows, side), jnp.bfloat16)],
    )


def expert_kernel(count, offset, *refs):
    pieces = refs[:count]
    gate_own, up_own, gate_other, up_other, spread, side, back = refs[count : count + 7]
    outs, hidden_out = refs[count + 7 : 2 * count + 7], refs[2 * count + 7]
    rows, weights, gate_grad, up_grad, hidden, grads, sems, row_sem, back_sem, out_sem = refs[
        2 * count + 8 :
    ]
    step = pl.program_id(0)
    size = pieces[0].shape[0]
    experts, _, part = gate_own.shape
    total_rows = rows.shape[0]
    sources = (gate_own, up_own, gate_other, up_other)

    def load(expert):
        slot = weights.at[expert]
        return [
            pltpu.make_async_copy(
                source.at[expert], slot.at[:, pl.ds(index * part, part)], sems.at[expert]
            )
            for index, source in enumerate(sources)
        ]

    row_copies = [
        pltpu.make_async_copy(piece, rows.at[pl.ds(index * size, size)], row_sem.at[index])
        for index, piece in enumerate(pieces)
    ]
    back_copy = pltpu.make_async_copy(
        back.at[:, pl.ds(offset, total_rows), :], grads, back_sem
    )
    out_copy = pltpu.make_async_copy(hidden, hidden_out, out_sem)

    @pl.when(step == 0)
    def _():
        for copy in row_copies + load(0) + [back_copy] + load(1):
            copy.start()
        for copy in row_copies:
            copy.wait()
        back_copy.wait()

        def work(expert, carry):
            for ahead in range(2, experts):

                @pl.when(expert == ahead - 2)
                def _():
                    for copy in load(ahead):
                        copy.start()

            for copy in load(expert):
                copy.wait()
            values = dot(rows[...], weights[expert])
            weight = dot(side[...], spread[expert])
            for half in range(2):
                gate_value = values[:, 2 * half * part : (2 * half + 1) * part]
                up_value = values[:, (2 * half + 1) * part : (2 * half + 2) * part]
                sigmoid = jax.nn.sigmoid(gate_value)
                silu = gate_value * sigmoid
                place = half * experts + expert
                grad = wide(grads[place])
                gate_grad[place] = low(grad * up_value * (sigmoid + silu * (1.0 - sigmoid)))
                up_grad[place] = low(grad * silu)
                hidden[place] = low(silu * up_value * weight)
            return carry

        lax.fori_loop(0, experts, work, 0)
        out_copy.start()

    tile = outs[0].shape[1]
    columns = pl.ds(pl.multiple_of(step * tile, tile), tile)
    total = None
    for expert in range(experts):
        for half in range(2):
            place = half * experts + expert
            for index, grad in enumerate((gate_grad, up_grad)):
                first = (2 * half + index) * part
                term = dot_t(grad[place], weights[expert, columns, first : first + part])
                total = term if total is None else total + term
    for index, out in enumerate(outs):
        out[...] = low(total[index * size : (index + 1) * size])

    @pl.when(step == pl.num_programs(0) - 1)
    def _():
        out_copy.wait()


def expert_call(pieces, gates, ups, spread, side, back, offset):
    count = len(pieces)
    experts, width, part = gates[0].shape
    size = pieces[0].shape[0]
    rows = size * count
    tile = min(width, 512)
    shape = (2 * experts, rows, part)
    slots = pltpu.VMEM(shape, jnp.bfloat16)
    side_block = pl.BlockSpec((rows, side.shape[1]), lambda n: (offset // rows, 0))
    return kernel_call(
        functools.partial(expert_kernel, count, offset),
        (width // tile,),
        [ANY] * (count + 4) + [whole(spread), side_block, ANY],
        [pl.BlockSpec((size, tile), lambda n: (0, n))] * count + [ANY],
        [((size, width), jnp.bfloat16)] * count + [(shape, jnp.bfloat16)],
        [*pieces, gates[0], ups[0], gates[1], ups[1], spread, side, back],
        16 * rows * experts * part * width,
        [
            pltpu.VMEM((rows, width), jnp.bfloat16),
            pltpu.VMEM((experts, width, 4 * part), jnp.bfloat16),
            slots,
            slots,
            slots,
            slots,
            pltpu.SemaphoreType.DMA((experts,)),
            pltpu.SemaphoreType.DMA((count,)),
            pltpu.SemaphoreType.DMA,
            pltpu.SemaphoreType.DMA,
        ],
    )


def down_kernel(count, *refs):
    hiddens, (down_own, down_other), outs = refs[:count], refs[count : count + 2], refs[count + 2 :]
    places, _, part = hiddens[0].shape
    pieces = len(outs) // count
    size = outs[0].shape[0]
    for index, hidden in enumerate(hiddens):
        total = None
        for place in range(places):
            down = down_own if place < places // 2 else down_other
            first = place % (places // 2) * part
            term = dot(hidden[place], down[first : first + part, :])
            total = term if total is None else total + term
        for piece in range(pieces):
            outs[index * pieces + piece][...] = low(total[piece * size : (piece + 1) * size])


def down_call(hiddens, downs, pieces):
    places, rows, part = hiddens[0].shape
    hidden, width = downs[0].shape
    tile = min(width, 512)
    count = len(hiddens)
    size = rows // pieces
    down_block = pl.BlockSpec((hidden, tile), lambda n: (0, n))
    outs = kernel_call(
        functools.partial(down_kernel, count),
        (width // tile,),
        [whole(array) for array in hiddens] + [down_block] * 2,
        [pl.BlockSpec((size, tile), lambda n: (0, n))] * (count * pieces),
        [((size, width), jnp.bfloat16)] * (count * pieces),
        [*hiddens, *downs],
        4 * count * rows * hidden * width,
    )
    return [outs[index * pieces : (index + 1) * pieces] for index in range(count)]


def body(
    tokens,
    cotangent,
    attn_gain,
    ffn_gain,
    query_gain,
    key_gain,
    query_weight,
    key_weight,
    value_weight,
    output_weight,
    expert_gate,
    expert_up,
    expert_down,
    adapt_in,
    adapt_out,
    adapt_in_out,
    adapt_out_out,
    routes,
    gate_weights,
    block_parent,
    adapter_pick,
):
    rows_here, model_width = tokens.shape
    local_width = query_weight.shape[1]
    heads_here = local_width // HD
    tensor_rank = lax.axis_index("tensor")
    tensor_count = lax.axis_size("tensor")
    owners = lax.axis_size("expert")
    owner_rank = lax.axis_index("expert")
    axes = divide_axes(owners, tensor_count)
    far, near, span = axes["z"][1], axes["x"][1], axes["y"][1]
    experts_here, _, hidden_here = expert_gate.shape
    experts_all = experts_here * owners
    column_share = model_width // tensor_count
    row_share = rows_here // tensor_count
    float_kind = jnp.float32
    half_kind = jnp.bfloat16
    hold = lax.optimization_barrier

    def own_rows(array):
        return lax.dynamic_slice_in_dim(array, tensor_rank * row_share, row_share, 0)

    cotangent_rows = own_rows(cotangent)
    routes_rows = own_rows(routes)
    weights_rows = own_rows(gate_weights)
    route_weights = jnp.sum(
        jnp.where(
            routes_rows[:, :, None] == jnp.arange(experts_all, dtype=jnp.int32)[None, None, :],
            weights_rows[:, :, None],
            0.0,
        ),
        axis=1,
    )
    weights_high = low(route_weights)
    weights_low = low(route_weights - wide(weights_high))
    side_width = -(-2 * experts_all // 128) * 128
    side_pad = jnp.zeros((row_share, side_width - 2 * experts_all), half_kind)
    cot_plane = jnp.concatenate([cotangent_rows, weights_high, weights_low, side_pad], axis=1)
    side_index = jnp.arange(side_width, dtype=jnp.int32)
    hidden_owner = (
        owner_rank * experts_here
        + jnp.arange(experts_here * hidden_here, dtype=jnp.int32) // hidden_here
    )
    spread_flat = low(
        (side_index[:, None] % experts_all == hidden_owner[None, :])
        & (side_index[:, None] < 2 * experts_all)
    )
    spread = jnp.swapaxes(spread_flat.reshape(side_width, experts_here, hidden_here), 0, 1)

    cot_next = turn(cot_plane, axes, "z", 1)
    cot_first = gather_first(cot_plane, axes)
    inputs = wide(tokens)
    first_gain = wide(attn_gain)[None, :]
    second_gain = wide(ffn_gain)[None, :]
    query_scale = wide(query_gain)[None, :]
    key_scale = wide(key_gain)[None, :]
    reached = ancestry(block_parent)
    cosine_table, sine_table = rope_tables(reached, rows_here // block_parent.shape[0], HD)
    signs = jnp.where(jnp.arange(HD) < HD // 2, -1.0, 1.0)[None, :]
    key_mask = token_mask(reached[0], rows_here)
    mask_added = jnp.where(key_mask, 0.0, MASKED_SCORE)
    select = jnp.repeat(wide(adapter_pick), RANK, axis=1)
    core = jnp.reshape(tensor_rank % 2, (1,)).astype(jnp.int32)
    picked = jnp.argmax(adapter_pick[0]) * RANK
    adapt_in_used = lax.dynamic_slice_in_dim(adapt_in, picked, RANK, 2)
    adapt_out_used = lax.dynamic_slice_in_dim(adapt_out, picked, RANK, 1)
    mix_in_used = lax.dynamic_slice_in_dim(adapt_in_out, picked, RANK, 1)
    mix_out_used = lax.dynamic_slice_in_dim(adapt_out_out, picked, RANK, 0)
    normed_in, lowrank, query_raw, key_raw, value_raw, squares = project_call(
        tokens,
        first_gain,
        (query_weight, key_weight, value_weight),
        adapt_in,
        adapt_out,
        select,
    )

    cot_planes = [None] * far
    cot_next, cot_first, squares = hold((cot_next, cot_first, squares))
    squares = lax.psum(squares, "tensor")
    cot_later = turn(cot_next, axes, "z", 1)
    cot_planes[0] = gather_second(cot_first, axes)
    cot_first = gather_first(cot_next, axes)
    queries, keys, values, attended, mine, theirs = attend_call(
        core,
        squares,
        (query_raw, key_raw, value_raw),
        (query_scale, key_scale),
        (cosine_table, sine_table * signs),
        mask_added,
        output_weight,
        adapt_in_out,
        row_share,
    )

    cot_next, cot_first, mine, theirs = hold((cot_later, cot_first, mine, theirs))
    cot_later = turn(cot_next, axes, "z", 1)
    gates = (expert_gate, turn(expert_gate, axes, "c", 1))
    ups = (expert_up, turn(expert_up, axes, "c", 1))
    down_tall = expert_down.reshape(-1, model_width)
    downs = (down_tall, turn(down_tall, axes, "c", 1))
    branch_kept, branch_came = scatter_tensor(mine, theirs, axes)
    branch_came, cot_planes[0] = hold((branch_came, cot_planes[0]))
    cot_planes[1] = gather_second(cot_first, axes)
    cot_first = gather_first(cot_next, axes)
    resid_rows, norm_plane, mixed_rows = resid_call(
        branch_kept, branch_came, own_rows(tokens), adapt_out_out, select, second_gain
    )
    query_squares = squares[0]
    key_squares = squares[1]
    query_inverse = lax.rsqrt(query_squares / model_width + EPSILON)[:, None]
    key_inverse = lax.rsqrt(key_squares / model_width + EPSILON)[:, None]
    second_inverse = lax.rsqrt(
        jnp.mean(resid_rows * resid_rows, axis=1, keepdims=True) + EPSILON
    )
    score_scale = HD ** (-0.5)
    queries = queries.reshape(rows_here, heads_here, HD)
    keys = keys.reshape(rows_here, heads_here, HD)
    values = values.reshape(rows_here, heads_here, HD)

    cot_later, cot_first, cot_planes[1], norm_plane, gates, ups, downs = hold(
        (cot_later, cot_first, cot_planes[1], norm_plane, gates, ups, downs)
    )
    norm_next = turn(norm_plane, axes, "z", 1)
    norm_first = gather_first(norm_plane, axes)
    cot_planes[2] = gather_second(cot_first, axes)
    cot_first = gather_first(cot_later, axes)
    backs, sides = [None] * far, [None] * far

    def hidden_step(first, second):
        pieces = cot_planes[first] + cot_planes[second]
        back, side = hidden_call(pieces, downs, spread_flat, experts_here)
        backs[first], sides[first] = (back, 0), side
        backs[second], sides[second] = (back, side.shape[0] // 2), side
        return back

    back_first = hidden_step(0, 1)

    norm_planes = [None] * far
    norm_next, norm_first, cot_planes[2], cot_first, back_first = hold(
        (norm_next, norm_first, cot_planes[2], cot_first, back_first)
    )
    backs[0], backs[1] = (back_first, backs[0][1]), (back_first, backs[1][1])
    norm_later = turn(norm_next, axes, "z", 1)
    norm_planes[0] = gather_second(norm_first, axes)
    norm_first = gather_first(norm_next, axes)
    cot_planes[3] = gather_second(cot_first, axes)
    parts, hiddens = [None] * far, [None] * far

    def expert_step(index):
        back, offset = backs[index]
        *parts[index], hiddens[index] = expert_call(
            norm_planes[index], gates, ups, spread, sides[index], back, offset
        )

    norm_next, norm_first, norm_planes[0], cot_planes[3] = hold(
        (norm_later, norm_first, norm_planes[0], cot_planes[3])
    )
    norm_later = turn(norm_next, axes, "z", 1)
    norm_planes[1] = gather_second(norm_first, axes)
    norm_first = gather_first(norm_next, axes)
    expert_step(0)
    back_second = hidden_step(2, 3)

    norm_next, norm_first, norm_planes[1], back_second, parts[0] = hold(
        (norm_later, norm_first, norm_planes[1], back_second, parts[0])
    )
    backs[2], backs[3] = (back_second, backs[2][1]), (back_second, backs[3][1])
    norm_planes[2] = gather_second(norm_first, axes)
    norm_first = gather_first(norm_next, axes)
    expert_step(1)

    norm_first, norm_planes[2], parts[1] = hold((norm_first, norm_planes[2], parts[1]))
    norm_planes[3] = gather_second(norm_first, axes)
    came = [None] * far
    kept = [None] * far
    sums = [None] * far
    came[1] = scatter_first(parts[1], axes)
    expert_step(2)

    norm_planes[3], came[1], parts[2] = hold((norm_planes[3], came[1], parts[2]))
    kept[1], came[1] = scatter_second(parts[1], came[1], axes)
    came[2] = scatter_first(parts[2], axes)
    came[0] = scatter_first(parts[0], axes)
    expert_step(3)

    kept[1], came[1], came[2], came[0], parts[3] = hold(
        (kept[1], came[1], came[2], came[0], parts[3])
    )
    sums[1] = scatter_last(kept[1], came[1])
    ring_sum = turn(low(sums[1]), axes, "z", 1)
    kept[2], came[2] = scatter_second(parts[2], came[2], axes)
    came[3] = scatter_first(parts[3], axes)
    kept[0], came[0] = scatter_second(parts[0], came[0], axes)
    mixes = [None] * far
    mixes[1], mixes[2] = down_call([hiddens[1], hiddens[2]], downs, near + span)

    ring_sum, kept[2], came[2], came[3], mixes[1], mixes[2] = hold(
        (ring_sum, kept[2], came[2], came[3], mixes[1], mixes[2])
    )
    ring_sum = turn(low(wide(ring_sum) + scatter_last(kept[2], came[2])), axes, "z", 1)
    kept[3], came[3] = scatter_second(parts[3], came[3], axes)
    mix_came = [None] * far
    mix_kept = [None] * far
    mix_came[1] = scatter_first(mixes[1], axes)
    mixes[3], mixes[0] = down_call([hiddens[3], hiddens[0]], downs, near + span)

    ring_sum, kept[3], came[3], kept[0], came[0], mix_came[1], mixes[3], mixes[0] = hold(
        (ring_sum, kept[3], came[3], kept[0], came[0], mix_came[1], mixes[3], mixes[0])
    )
    ring_sum = turn(low(wide(ring_sum) + scatter_last(kept[3], came[3])), axes, "z", 1)
    mix_kept[1], mix_came[1] = scatter_second(mixes[1], mix_came[1], axes)

    ring_sum, mix_kept[1], mix_came[1] = hold((ring_sum, mix_kept[1], mix_came[1]))
    ffn_rows_grad = wide(ring_sum) + scatter_last(kept[0], came[0])
    second_scaled = ffn_rows_grad * second_gain
    resid_grad_rows = wide(cotangent_rows) + norm_back(
        second_scaled,
        resid_rows,
        second_inverse,
        model_width,
        jnp.sum(second_scaled * resid_rows, axis=1, keepdims=True),
    )
    branch_sent = jnp.concatenate(
        [low(resid_grad_rows), mixed_rows], axis=1
    )
    branch_whole = place_tensor(branch_sent, axes, half_kind)
    mix_sum = turn(low(scatter_last(mix_kept[1], mix_came[1])), axes, "z", 1)
    mix_came[2] = scatter_first(mixes[2], axes)

    branch_whole, mix_came[2] = hold((branch_whole, mix_came[2]))
    branch_grad = branch_whole[:, :model_width]
    mixed = lax.dynamic_slice_in_dim(branch_whole, model_width + picked, RANK, 1)
    mixed_grad = low(dot_t(branch_grad, mix_out_used))
    attended_grad = low(dot_t(branch_grad, output_weight) + dot_t(mixed_grad, mix_in_used))
    attended_grad = attended_grad.reshape(rows_here, heads_here, HD)
    scores = (
        jnp.einsum("qhd,khd->hqk", queries, keys, preferred_element_type=float_kind) * score_scale
    )
    scores = scores + mask_added[None]
    raised = jnp.exp(scores - jnp.max(scores, axis=2, keepdims=True))
    softmax_full = raised / jnp.sum(raised, axis=2, keepdims=True)
    softmax_half = low(softmax_full)
    value_grad = low(
        jnp.einsum("hqk,qhd->khd", softmax_half, attended_grad, preferred_element_type=float_kind)
    )
    prob_grad = jnp.einsum("qhd,khd->hqk", attended_grad, values, preferred_element_type=float_kind)
    score_grad = low(
        softmax_full * (prob_grad - jnp.sum(softmax_full * prob_grad, axis=2, keepdims=True))
    )
    query_grad = (
        jnp.einsum("hqk,khd->qhd", score_grad, keys, preferred_element_type=float_kind)
        * score_scale
    )
    key_grad = (
        jnp.einsum("hqk,qhd->khd", score_grad, queries, preferred_element_type=float_kind)
        * score_scale
    )
    query_scaled = (
        unrotate(query_grad, cosine_table, sine_table).reshape(rows_here, local_width) * query_scale
    )
    key_scaled = (
        unrotate(key_grad, cosine_table, sine_table).reshape(rows_here, local_width) * key_scale
    )

    query_scaled, key_scaled, value_grad, mix_sum, mix_came[2] = hold(
        (query_scaled, key_scaled, value_grad, mix_sum, mix_came[2])
    )
    mix_kept[2], mix_came[2] = scatter_second(mixes[2], mix_came[2], axes)
    mix_came[3] = scatter_first(mixes[3], axes)
    query_inner, key_inner = lax.psum(
        (jnp.sum(query_scaled * query_raw, axis=1), jnp.sum(key_scaled * key_raw, axis=1)), "tensor"
    )
    query_raw_grad = low(
        norm_back(query_scaled, query_raw, query_inverse, model_width, query_inner[:, None])
    )
    key_raw_grad = low(
        norm_back(key_scaled, key_raw, key_inverse, model_width, key_inner[:, None])
    )
    value_raw_grad = value_grad.reshape(rows_here, local_width)
    raw_grads = (query_raw_grad, key_raw_grad, value_raw_grad)
    lowrank_part = low(
        jnp.concatenate(
            [dot_t(raw_grads[projection], adapt_out_used[projection]) for projection in range(3)],
            axis=1,
        )
    )
    normed_part = (
        dot_t(query_raw_grad, query_weight)
        + dot_t(key_raw_grad, key_weight)
        + dot_t(value_raw_grad, value_weight)
    )

    normed_part, lowrank_part, mix_kept[2], mix_came[2], mix_came[3] = hold(
        (normed_part, lowrank_part, mix_kept[2], mix_came[2], mix_came[3])
    )
    mix_sum = turn(low(wide(mix_sum) + scatter_last(mix_kept[2], mix_came[2])), axes, "z", 1)
    mix_kept[3], mix_came[3] = scatter_second(mixes[3], mix_came[3], axes)
    mix_came[0] = scatter_first(mixes[0], axes)
    lowrank_grad = low(sum_tensor(lowrank_part, axes))
    blocks = normed_part.reshape(span, 2, row_share, model_width)
    kept_part, came_part = scatter_tensor(
        lax.dynamic_index_in_dim(blocks, core[0], 1, False).reshape(-1, model_width),
        low(lax.dynamic_index_in_dim(blocks, 1 - core[0], 1, False).reshape(-1, model_width)),
        axes,
    )
    normed_grad_rows = kept_part + wide(came_part)
    lowrank_rows = own_rows(lowrank_grad)
    for projection in range(3):
        normed_grad_rows = normed_grad_rows + dot_t(
            lowrank_rows[:, projection * RANK : (projection + 1) * RANK], adapt_in_used[projection]
        )
    first_scaled = normed_grad_rows * first_gain
    inputs_rows = own_rows(inputs)
    first_inverse = lax.rsqrt(
        jnp.mean(inputs_rows * inputs_rows, axis=1, keepdims=True) + EPSILON
    )
    input_grad_rows = resid_grad_rows + norm_back(
        first_scaled,
        inputs_rows,
        first_inverse,
        model_width,
        jnp.sum(first_scaled * inputs_rows, axis=1, keepdims=True),
    )
    normed_share = lax.dynamic_slice_in_dim(
        normed_in, tensor_rank * column_share, column_share, 1
    )
    branch_share = lax.dynamic_slice_in_dim(
        branch_grad, tensor_rank * column_share, column_share, 1
    )
    compact = low(
        jnp.concatenate(
            [t_dot(lowrank_grad, normed_share), t_dot(mixed, branch_share)]
            + [
                lax.dynamic_slice_in_dim(
                    t_dot(lowrank[projection], raw_grads[projection]), picked, RANK, 0
                )
                for projection in range(3)
            ]
            + [t_dot(mixed_grad, attended)],
            axis=0,
        )
    )

    input_grad_rows, compact, mix_sum, mix_kept[3], mix_came[3], mix_came[0] = hold(
        (low(input_grad_rows), compact, mix_sum, mix_kept[3], mix_came[3], mix_came[0])
    )
    input_grad = place_tensor(input_grad_rows, axes, float_kind)
    mix_sum = turn(low(wide(mix_sum) + scatter_last(mix_kept[3], mix_came[3])), axes, "z", 1)
    mix_kept[0], mix_came[0] = scatter_second(mixes[0], mix_came[0], axes)
    layer_rows = low(resid_rows + wide(mix_sum) + scatter_last(mix_kept[0], mix_came[0]))
    layer_out = swap_columns(layer_rows, axes)

    kinds = compact.shape[0] // RANK
    picks_sent = low(
        jnp.broadcast_to(wide(adapter_pick)[:, :, None], (1, adapter_pick.shape[1], 128))
    ).reshape(-1, 128)
    picks_sent = jnp.concatenate(
        [picks_sent, jnp.zeros((16 - picks_sent.shape[0], 128), half_kind)], axis=0
    )
    picks_sent = jnp.tile(picks_sent, (1, column_share // 128))
    compact = jnp.concatenate([compact, picks_sent], axis=0)
    trees = jnp.concatenate(
        ring(jnp.concatenate(ring(compact, axes, "x"), axis=0), axes, "z"), axis=0
    )
    trees = trees.reshape(owners, kinds + 1, RANK, column_share)
    tree_picks = trees[:, kinds, : adapter_pick.shape[1], 0]
    grad_adapt_out = jnp.einsum(
        "sa,skrc->karc", tree_picks, trees[:, 4:7], preferred_element_type=float_kind
    ).reshape(3, -1, column_share)
    grad_adapt_in_out = jnp.einsum(
        "sa,src->car", tree_picks, trees[:, 7], preferred_element_type=float_kind
    ).reshape(column_share, -1)
    shared = place_tensor(
        trees[:, :4].reshape(owners * 4 * RANK, column_share), axes, half_kind
    ).reshape(tensor_count, owners, 4, RANK, column_share)
    grad_adapt_in = jnp.einsum(
        "sa,tskrc->ktcar", tree_picks, shared[:, :, :3], preferred_element_type=float_kind
    ).reshape(3, model_width, -1)
    grad_adapt_out_out = jnp.einsum(
        "sa,tsrc->artc", tree_picks, shared[:, :, 3], preferred_element_type=float_kind
    ).reshape(-1, model_width)
    return (
        layer_out,
        input_grad,
        grad_adapt_in,
        grad_adapt_out,
        grad_adapt_in_out,
        grad_adapt_out_out,
    )


def solution(mesh):
    return jax.shard_map(
        body,
        mesh=mesh,
        in_specs=(
            P("expert", None),
            P("expert", None),
            P(),
            P(),
            P("tensor"),
            P("tensor"),
            P(None, "tensor"),
            P(None, "tensor"),
            P(None, "tensor"),
            P("tensor", None),
            P("expert", None, "tensor"),
            P("expert", None, "tensor"),
            P("expert", "tensor", None),
            P(),
            P(None, None, "tensor"),
            P("tensor", None),
            P(),
            P("expert", None),
            P("expert", None),
            P("expert"),
            P("expert", None),
        ),
        out_specs=(
            P("expert", "tensor"),
            P("expert", None),
            P(),
            P(None, None, "tensor"),
            P("tensor", None),
            P(),
        ),
        check_vma=False,
    )
```

```python
import functools

import jax
import jax.numpy as jnp
from jax import lax
from jax.experimental import pallas as pl
from jax.experimental.pallas import tpu as pltpu
from jax.sharding import PartitionSpec as P

HD = 128
RANK = 16


EPSILON = 1e-05
ROPE_BASE = 10000.0
MASKED_SCORE = -1e30
VMEM_LIMIT = 56 * 2**20


def ancestry(parents):
    blocks = parents.shape[0]
    places = jnp.arange(blocks, dtype=jnp.int32)
    walker = places
    reached = walker[:, None] == places[None, :]
    for _ in range(blocks - 1):
        hits = (walker[:, None] == places[None, :]).astype(jnp.int32)
        walker = jnp.sum(hits * parents[None, :], axis=1)
        reached = reached | (walker[:, None] == places[None, :])
    return reached[None]


def rope_tables(reached, block_span, head_size):
    depths = jnp.sum(reached.astype(jnp.int32), axis=2) - 1
    offsets = jnp.arange(block_span, dtype=jnp.int32)
    located = (
        (depths[:, :, None] * block_span + offsets[None, None, :]).reshape(-1).astype(jnp.float32)
    )
    halves = head_size // 2
    speeds = ROPE_BASE ** (-2.0 * jnp.arange(halves, dtype=jnp.float32) / head_size)
    angles = located[:, None] * speeds[None, :]
    angles = jnp.concatenate([angles, angles], axis=1)
    return (jnp.cos(angles), jnp.sin(angles))


def token_mask(reached, total_size):
    blocks = reached.shape[0]
    block_span = total_size // blocks
    widened = jnp.broadcast_to(
        reached[:, None, :, None], (blocks, block_span, blocks, block_span)
    ).reshape(total_size, total_size)
    positions = jnp.arange(total_size, dtype=jnp.int32)
    return widened & (positions[None, :] <= positions[:, None])


def norm_back(scaled_grad, values, inverse, model_width, inner_sum):
    return inverse * scaled_grad - values * inverse**3 * (inner_sum / model_width)


def divide_axes(owners, tensor_count):
    outer = 4
    return {
        "z": ("expert", outer, owners // outer, owners),
        "x": ("expert", owners // outer, 1, owners),
        "y": ("tensor", tensor_count // 2, 2, tensor_count),
        "c": ("tensor", 2, 1, tensor_count),
    }


def turn(array, axes, name, step):
    axis, length, stride, total = axes[name]
    pairs = []
    for index in range(total):
        place = (index // stride) % length
        moved = index + ((place + step) % length - place) * stride
        pairs.append((index, moved))
    return lax.ppermute(array, axis, pairs)


def ring(array, axes, name):
    held = [array]
    for _ in range(axes[name][1] - 1):
        held.append(turn(held[-1], axes, name, 1))
    return held


def wide(array):
    return array.astype(jnp.float32)


def low(array):
    return array.astype(jnp.bfloat16)


def gather_first(rows, axes):
    half = rows.shape[0] // 2
    return (
        jnp.concatenate(ring(rows[:half], axes, "x"), axis=0),
        jnp.concatenate(ring(rows[half:], axes, "y"), axis=0),
    )


def gather_second(pair, axes):
    return ring(pair[0], axes, "y") + ring(pair[1], axes, "x")


def send_sum(parts, axes, name):
    total = parts[-1]
    for part in parts[-2:0:-1]:
        total = low(wide(turn(total, axes, name, -1)) + wide(part))
    return turn(total, axes, name, -1)


def scatter_first(pieces, axes):
    span = axes["y"][1]
    return send_sum(pieces[:span], axes, "y"), send_sum(pieces[span:], axes, "x")


def scatter_second(pieces, came, axes):
    span = axes["y"][1]
    first = wide(pieces[0]) + wide(came[0])
    second = wide(pieces[span]) + wide(came[1])
    first = jnp.split(first, axes["x"][1], axis=0)
    second = jnp.split(second, axes["y"][1], axis=0)
    first_came = send_sum([low(part) for part in first], axes, "x")
    second_came = send_sum([low(part) for part in second], axes, "y")
    return (first[0], second[0]), (first_came, second_came)


def scatter_last(kept, came):
    return jnp.concatenate([kept[0] + wide(came[0]), kept[1] + wide(came[1])], axis=0)


def gather_tensor(rows, axes):
    held = ring(rows, axes, "y")
    return held + [turn(piece, axes, "c", 1) for piece in held]


def scatter_tensor(mine, theirs, axes):
    rank = lax.axis_index("tensor")
    span = axes["y"][1]
    size = mine.shape[0] // span
    came = turn(theirs, axes, "c", 1)
    total = None
    for step in range(span - 1, -1, -1):
        level = (rank // 2 + span - step) % span
        part = wide(lax.dynamic_slice_in_dim(mine, level * size, size, 0)) + wide(
            lax.dynamic_slice_in_dim(came, level * size, size, 0)
        )
        if step:
            total = turn(low(part if total is None else part + wide(total)), axes, "y", -1)
    return part, total


def swap_columns(rows, axes):
    rank = lax.axis_index("tensor")
    count = lax.axis_size("tensor")
    size, width = rows.shape
    span = axes["y"][1]
    share = width // count
    level, core = rank // 2, rank % 2
    whole = jnp.zeros((count * size, share), rows.dtype)
    for step in range(span):
        toward = (level + step) % span
        piece = lax.dynamic_slice_in_dim(rows, toward * 2 * share, 2 * share, 1)
        if step:
            piece = turn(piece, axes, "y", step)
        mine = lax.dynamic_slice_in_dim(piece, core * share, share, 1)
        theirs = lax.dynamic_slice_in_dim(piece, (1 - core) * share, share, 1)
        theirs = turn(theirs, axes, "c", 1)
        source = (level + span - step) % span
        whole = lax.dynamic_update_slice_in_dim(whole, mine, (source * 2 + core) * size, 0)
        whole = lax.dynamic_update_slice_in_dim(whole, theirs, (source * 2 + 1 - core) * size, 0)
    return whole


def sum_tensor(array, axes):
    total = wide(array) + wide(turn(array, axes, "c", 1))
    moving = low(total)
    result = total
    for _ in range(axes["y"][1] - 1):
        moving = turn(moving, axes, "y", 1)
        result = result + wide(moving)
    return result


def dot(left, right):
    return jnp.dot(left, right, preferred_element_type=jnp.float32)


def dot_t(left, right):
    return lax.dot_general(
        left, right, (((1,), (1,)), ((), ())), preferred_element_type=jnp.float32
    )


def t_dot(left, right):
    return lax.dot_general(
        left, right, (((0,), (0,)), ((), ())), preferred_element_type=jnp.float32
    )


ANY = pl.BlockSpec(memory_space=pl.ANY)


def whole(array):
    shape = array.shape
    return pl.BlockSpec(shape, lambda *_: (0,) * len(shape))


def kernel_call(kernel, grid, in_specs, out_specs, out_shape, operands, flops, scratch=(), scalars=0):
    moved = sum(array.size * array.dtype.itemsize for array in operands)
    return pl.pallas_call(
        kernel,
        grid_spec=pltpu.PrefetchScalarGridSpec(
            num_scalar_prefetch=scalars,
            grid=grid,
            in_specs=in_specs,
            out_specs=out_specs,
            scratch_shapes=list(scratch),
        ),
        out_shape=[jax.ShapeDtypeStruct(shape, kind) for shape, kind in out_shape],
        compiler_params=pltpu.CompilerParams(vmem_limit_bytes=VMEM_LIMIT),
        cost_estimate=pl.CostEstimate(flops=flops, bytes_accessed=moved, transcendentals=0),
    )(*operands)


def project_kernel(
    tokens, gain, query_weight, key_weight, value_weight, adapt_in, adapt_out, select,
    normed_out, lowrank_out, query_out, key_out, value_out, squares_out,
    weights, maps, sems,
):
    copies = [pltpu.make_async_copy(adapt_in, maps, sems.at[3])]
    for index, source in enumerate((query_weight, key_weight, value_weight)):
        copies.append(pltpu.make_async_copy(source, weights.at[index], sems.at[index]))
    for copy in copies:
        copy.start()
    inputs = wide(tokens[...])
    inverse = lax.rsqrt(jnp.mean(inputs * inputs, axis=1, keepdims=True) + EPSILON)
    normed_out[...] = low(inputs * inverse * wide(gain[...]))
    copies[0].wait()
    for index in range(3):
        lowrank_out[index] = low(dot(normed_out[...], maps[index]) * select[...])
    squares = []
    for index, out in enumerate((query_out, key_out, value_out)):
        copies[index + 1].wait()
        raw = dot(normed_out[...], weights[index]) + dot(lowrank_out[index], adapt_out[index])
        out[...] = raw
        squares.append(jnp.sum(raw * raw, axis=1, keepdims=True))
    lane = lax.broadcasted_iota(jnp.int32, (tokens.shape[0], 128), 1)
    columns = jnp.where(lane == 0, squares[0], jnp.where(lane == 1, squares[1], 0.0))
    squares_out[...] = jnp.transpose(columns)[:8]


def project_call(tokens, gain, weights, adapt_in, adapt_out, select):
    rows, width = tokens.shape
    local = weights[0].shape[1]
    rank = adapt_in.shape[2]
    out_shape = [((rows, width), jnp.bfloat16), ((3, rows, rank), jnp.bfloat16)]
    out_shape += [((rows, local), jnp.float32)] * 3 + [((8, rows), jnp.float32)]
    operands = [tokens, gain, *weights, adapt_in, adapt_out, select]
    return kernel_call(
        project_kernel,
        (1,),
        [whole(tokens), whole(gain), ANY, ANY, ANY, ANY, whole(adapt_out), whole(select)],
        [pl.BlockSpec(shape, lambda *_, size=len(shape): (0,) * size) for shape, _ in out_shape],
        out_shape,
        operands,
        6 * rows * width * local,
        [
            pltpu.VMEM((3, width, local), jnp.bfloat16),
            pltpu.VMEM(adapt_in.shape, jnp.bfloat16),
            pltpu.SemaphoreType.DMA((4,)),
        ],
    )


def spread_columns(rows):
    return jnp.transpose(jnp.concatenate([rows] * (128 // rows.shape[0]), axis=0))


def turned(values):
    half = values.shape[1] // 2
    return jnp.concatenate([values[:, half:], values[:, :half]], axis=1)


def attend_kernel(
    width, size, core, squares, query_raw, key_raw, value_raw, query_gain, key_gain, cosine, sine,
    mask, output_weight, mix_in, queries, keys, values, attended, mine, theirs, held, weight, sem,
):
    head = pl.program_id(0)
    last = pl.num_programs(0) - 1
    copy = pltpu.make_async_copy(output_weight, weight, sem)

    @pl.when(head == 0)
    def _():
        copy.start()

    inverse = lax.rsqrt(spread_columns(squares[...]) / width + EPSILON)
    query = query_raw[...] * inverse[:, 0:1] * wide(query_gain[...])
    key = key_raw[...] * inverse[:, 1:2] * wide(key_gain[...])
    query = low(query * cosine[...] + turned(query) * sine[...])
    key = low(key * cosine[...] + turned(key) * sine[...])
    value = low(value_raw[...])
    queries[...] = query
    keys[...] = key
    values[...] = value
    scores = dot_t(query, key) * HD ** (-0.5) + mask[...]
    raised = jnp.exp(scores - jnp.max(scores, axis=1, keepdims=True))
    weights = low(raised / jnp.sum(raised, axis=1, keepdims=True))
    result = low(dot(weights, value))
    attended[...] = result
    held[head] = result

    @pl.when(head == last)
    def _():
        copy.wait()
        heads = held.shape[0]
        levels = mine.shape[0] // size
        for out, offset in ((mine, core[0]), (theirs, 1 - core[0])):
            taken = []
            for level in range(levels):
                rows = pl.ds(pl.multiple_of((2 * level + offset) * size, size), size)
                taken.append(
                    jnp.concatenate([held[index, rows, :] for index in range(heads)], axis=1)
                )
            taken = jnp.concatenate(taken, axis=0)
            out[:, :width] = dot(taken, weight[...]).astype(out.dtype)
            out[:, width:] = dot(taken, mix_in[...]).astype(out.dtype)


def attend_call(core, squares, raws, gains, tables, mask, output_weight, mix_in, size):
    rows, local = raws[0].shape
    heads = local // HD
    width = output_weight.shape[1]
    wide_width = width + mix_in.shape[1]
    block = pl.BlockSpec((rows, HD), lambda head, *_: (0, head))
    gain_block = pl.BlockSpec((1, HD), lambda head, *_: (0, head))
    fixed = pl.BlockSpec((rows // 2, wide_width), lambda *_: (0, 0))
    operands = [core, squares, *raws, *gains, *tables, mask, output_weight, mix_in]
    return kernel_call(
        functools.partial(attend_kernel, width, size),
        (heads,),
        [whole(squares)] + [block] * 3 + [gain_block] * 2
        + [whole(tables[0]), whole(tables[1]), whole(mask), ANY, whole(mix_in)],
        [block] * 4 + [fixed] * 2,
        [((rows, local), jnp.bfloat16)] * 4
        + [((rows // 2, wide_width), jnp.float32), ((rows // 2, wide_width), jnp.bfloat16)],
        operands,
        4 * rows * rows * local + 2 * rows * local * width,
        [
            pltpu.VMEM((heads, rows, HD), jnp.bfloat16),
            pltpu.VMEM(output_weight.shape, jnp.bfloat16),
            pltpu.SemaphoreType.DMA,
        ],
        1,
    )


def resid_kernel(
    width, kept, came, tokens, mix_out, select, gain, resid_out, norm_out, mixed_out
):
    mixed = low((kept[:, width:] + wide(came[:, width:])) * select[...])
    mixed_out[...] = mixed
    resid = (
        wide(tokens[...])
        + (kept[:, :width] + wide(came[:, :width]))
        + dot(mixed, mix_out[...])
    )
    resid_out[...] = resid
    inverse = lax.rsqrt(jnp.mean(resid * resid, axis=1, keepdims=True) + EPSILON)
    norm_out[...] = low(resid * inverse * wide(gain[...]))


def resid_call(kept, came, tokens, mix_out, select, gain):
    rows, width = tokens.shape
    out_shape = [((rows, width), jnp.float32), ((rows, width), jnp.bfloat16)]
    out_shape += [((rows, mix_out.shape[0]), jnp.bfloat16)]
    operands = [kept, came, tokens, mix_out, select, gain]
    return kernel_call(
        functools.partial(resid_kernel, width),
        (1,),
        [whole(array) for array in operands],
        [pl.BlockSpec(shape, lambda *_: (0, 0)) for shape, _ in out_shape],
        out_shape,
        operands,
        2 * rows * width * mix_out.shape[0],
    )


def plane_order(near, span, size):
    half = size // 2
    places = []
    for down in range(span):
        for across in range(near):
            places.append((across, down, down * size, (down * near + across) * half))
    for across in range(near):
        for down in range(span):
            first = (span * near + across * span + down) * half
            places.append((across, down, down * size + half, first))
    return places


def hidden_kernel(count, near, size, width, *refs):
    pieces, (down_own, down_other, spread), (out, side_out), (rows, side) = (
        refs[: count * near],
        refs[count * near : count * near + 3],
        refs[count * near + 3 : count * near + 5],
        refs[count * near + 5 :],
    )
    step = pl.program_id(0)
    span = pieces[0].shape[0] // size
    plane = near * span * size

    @pl.when(step == 0)
    def _():
        for index in range(count):
            for across, _, source, first in plane_order(near, span, size):
                piece = pieces[index * near + across]
                place = slice(index * plane + first, index * plane + first + size // 2)
                rows[place] = piece[source : source + size // 2, :width]
                side[place] = piece[source : source + size // 2, width:]
        side_out[...] = side[...]

    def emit(down):
        grad = dot_t(rows[...], down[...]) * dot(side[...], spread[...])
        part = out.shape[2]
        for index in range(out.shape[0]):
            out[index] = low(grad[:, index * part : (index + 1) * part])

    half = pl.num_programs(0) // 2

    @pl.when(step < half)
    def _():
        emit(down_own)

    @pl.when(step >= half)
    def _():
        emit(down_other)


def hidden_call(planes, downs, spread, experts, size):
    hidden, width = downs[0].shape
    near = len(planes[0])
    pieces = [piece for plane in planes for piece in plane]
    rows = sum(piece.shape[0] for piece in pieces)
    part = hidden // experts
    side = spread.shape[0]
    pair = 2 * part
    half = experts // 2
    last = half - 1
    return kernel_call(
        functools.partial(hidden_kernel, len(planes), near, size, width),
        (2 * half,),
        [whole(piece) for piece in pieces]
        + [
            pl.BlockSpec((pair, width), lambda n: (jnp.minimum(n, last), 0)),
            pl.BlockSpec((pair, width), lambda n: (jnp.maximum(n - half, 0), 0)),
            pl.BlockSpec((side, pair), lambda n: (0, lax.rem(n, half))),
        ],
        [
            pl.BlockSpec((2, rows, part), lambda n: (n, 0, 0)),
            pl.BlockSpec((rows, side), lambda n: (0, 0)),
        ],
        [((2 * experts, rows, part), jnp.bfloat16), ((rows, side), jnp.bfloat16)],
        [*pieces, *downs, spread],
        4 * rows * hidden * width,
        [pltpu.VMEM((rows, width), jnp.bfloat16), pltpu.VMEM((rows, side), jnp.bfloat16)],
    )


def expert_kernel(count, offset, *refs):
    pieces = refs[:count]
    gate_own, up_own, gate_other, up_other, spread, side, back = refs[count : count + 7]
    outs, hidden_out = refs[count + 7 : 2 * count + 7], refs[2 * count + 7]
    rows, weights, gate_grad, up_grad, hidden, grads, sems, row_sem, back_sem, out_sem = refs[
        2 * count + 8 :
    ]
    step = pl.program_id(0)
    size = pieces[0].shape[0]
    experts, _, part = gate_own.shape
    total_rows = rows.shape[0]
    sources = (gate_own, up_own, gate_other, up_other)

    def load(expert):
        slot = weights.at[expert]
        return [
            pltpu.make_async_copy(
                source.at[expert], slot.at[:, pl.ds(index * part, part)], sems.at[expert]
            )
            for index, source in enumerate(sources)
        ]

    row_copies = [
        pltpu.make_async_copy(piece, rows.at[pl.ds(index * size, size)], row_sem.at[index])
        for index, piece in enumerate(pieces)
    ]
    back_copy = pltpu.make_async_copy(
        back.at[:, pl.ds(offset, total_rows), :], grads, back_sem
    )
    out_copy = pltpu.make_async_copy(hidden, hidden_out, out_sem)

    @pl.when(step == 0)
    def _():
        for copy in row_copies + load(0) + [back_copy] + load(1):
            copy.start()
        for copy in row_copies:
            copy.wait()
        back_copy.wait()

        def work(expert, carry):
            for ahead in range(2, experts):

                @pl.when(expert == ahead - 2)
                def _():
                    for copy in load(ahead):
                        copy.start()

            for copy in load(expert):
                copy.wait()
            values = dot(rows[...], weights[expert])
            weight = dot(side[...], spread[expert])
            for half in range(2):
                gate_value = values[:, 2 * half * part : (2 * half + 1) * part]
                up_value = values[:, (2 * half + 1) * part : (2 * half + 2) * part]
                sigmoid = jax.nn.sigmoid(gate_value)
                silu = gate_value * sigmoid
                place = half * experts + expert
                grad = wide(grads[place])
                gate_grad[place] = low(grad * up_value * (sigmoid + silu * (1.0 - sigmoid)))
                up_grad[place] = low(grad * silu)
                hidden[place] = low(silu * up_value * weight)
            return carry

        lax.fori_loop(0, experts, work, 0)
        out_copy.start()

    tile = outs[0].shape[1]
    columns = pl.ds(pl.multiple_of(step * tile, tile), tile)
    total = None
    for expert in range(experts):
        for half in range(2):
            place = half * experts + expert
            for index, grad in enumerate((gate_grad, up_grad)):
                first = (2 * half + index) * part
                term = dot_t(grad[place], weights[expert, columns, first : first + part])
                total = term if total is None else total + term
    for index, out in enumerate(outs):
        out[...] = low(total[index * size : (index + 1) * size])

    @pl.when(step == pl.num_programs(0) - 1)
    def _():
        out_copy.wait()


def expert_call(pieces, gates, ups, spread, side, back, offset):
    count = len(pieces)
    experts, width, part = gates[0].shape
    size = pieces[0].shape[0]
    rows = size * count
    tile = min(width, 512)
    shape = (2 * experts, rows, part)
    slots = pltpu.VMEM(shape, jnp.bfloat16)
    side_block = pl.BlockSpec((rows, side.shape[1]), lambda n: (offset // rows, 0))
    return kernel_call(
        functools.partial(expert_kernel, count, offset),
        (width // tile,),
        [ANY] * (count + 4) + [whole(spread), side_block, ANY],
        [pl.BlockSpec((size, tile), lambda n: (0, n))] * count + [ANY],
        [((size, width), jnp.bfloat16)] * count + [(shape, jnp.bfloat16)],
        [*pieces, gates[0], ups[0], gates[1], ups[1], spread, side, back],
        16 * rows * experts * part * width,
        [
            pltpu.VMEM((rows, width), jnp.bfloat16),
            pltpu.VMEM((experts, width, 4 * part), jnp.bfloat16),
            slots,
            slots,
            slots,
            slots,
            pltpu.SemaphoreType.DMA((experts,)),
            pltpu.SemaphoreType.DMA((count,)),
            pltpu.SemaphoreType.DMA,
            pltpu.SemaphoreType.DMA,
        ],
    )


def down_kernel(count, span, *refs):
    hiddens, (down_own, down_other), outs = refs[:count], refs[count : count + 2], refs[count + 2 :]
    places, _, part = hiddens[0].shape
    near = len(outs) // count
    size = outs[0].shape[0] // span
    for index, hidden in enumerate(hiddens):
        total = None
        for place in range(places):
            down = down_own if place < places // 2 else down_other
            first = place % (places // 2) * part
            term = dot(hidden[place], down[first : first + part, :])
            total = term if total is None else total + term
        for across, _, target, first in plane_order(near, span, size):
            outs[index * near + across][target : target + size // 2] = low(
                total[first : first + size // 2]
            )


def down_call(hiddens, downs, near, span, size):
    places, rows, part = hiddens[0].shape
    hidden, width = downs[0].shape
    tile = min(width, 512)
    count = len(hiddens)
    down_block = pl.BlockSpec((hidden, tile), lambda n: (0, n))
    outs = kernel_call(
        functools.partial(down_kernel, count, span),
        (width // tile,),
        [whole(array) for array in hiddens] + [down_block] * 2,
        [pl.BlockSpec((span * size, tile), lambda n: (0, n))] * (count * near),
        [((span * size, width), jnp.bfloat16)] * (count * near),
        [*hiddens, *downs],
        4 * count * rows * hidden * width,
    )
    return [outs[index * near : (index + 1) * near] for index in range(count)]


def backward_kernel(width, share, count, scalars, *refs):
    pieces = refs[:count]
    (output_weight, mix_in, mix_out, select, queries, keys, values, attended, query_raw, key_raw,
     query_gain, key_gain, cosine, sine, mask) = refs[count : count + 15]
    (query_out, key_out, value_out, inner_out, mix_in_grad, mix_out_grad) = refs[
        count + 15 : count + 21
    ]
    branch, mixed_grad, grads, inner, sems = refs[count + 21 :]
    head = pl.program_id(0)
    heads = grads.shape[0]
    size = pieces[0].shape[0]
    rows = branch.shape[0]

    @pl.when(head == 0)
    def _():
        copies = []
        for index, piece in enumerate(pieces):
            place = pl.ds(pl.multiple_of(scalars[index] * size, size), size)
            copies.append(pltpu.make_async_copy(piece, branch.at[place], sems.at[index]))
        for copy in copies:
            copy.start()
        for copy in copies:
            copy.wait()
        mixed_grad[...] = low(
            wide(low(dot_t(branch[:, :width], mix_out[...]))) * select[...]
        )
        for index in range(heads):
            part = slice(index * HD, (index + 1) * HD)
            grads[index] = low(
                dot_t(branch[:, :width], output_weight[part, :])
                + dot_t(mixed_grad[...], mix_in[part, :])
            )
        columns = pl.ds(pl.multiple_of(scalars[count] * share, share), share)
        whole_grad = t_dot(branch[:, width:], branch[:, columns])
        mix_out_grad[...] = sliced(whole_grad)
        inner[...] = jnp.zeros_like(inner)

    scale = HD ** (-0.5)
    query, key, value = queries[...], keys[...], values[...]
    grad = grads[head]
    scores = dot_t(query, key) * scale + mask[...]
    raised = jnp.exp(scores - jnp.max(scores, axis=1, keepdims=True))
    weights = raised / jnp.sum(raised, axis=1, keepdims=True)
    value_out[...] = low(t_dot(low(weights), grad))
    weight_grad = dot_t(grad, value)
    center = jnp.sum(weights * weight_grad, axis=1, keepdims=True)
    score_grad = low(weights * (weight_grad - center))
    query_grad = dot(score_grad, key) * scale
    key_grad = t_dot(score_grad, query) * scale
    query_grad = (query_grad * cosine[...] - turned(query_grad) * sine[...]) * wide(query_gain[...])
    key_grad = (key_grad * cosine[...] - turned(key_grad) * sine[...]) * wide(key_gain[...])
    query_out[...] = query_grad
    key_out[...] = key_grad
    query_inner = jnp.sum(query_grad * query_raw[...], axis=1, keepdims=True)
    key_inner = jnp.sum(key_grad * key_raw[...], axis=1, keepdims=True)
    lane = lax.broadcasted_iota(jnp.int32, (rows, 128), 1)
    inner[...] += jnp.where(lane == 0, query_inner, jnp.where(lane == 1, key_inner, 0.0))
    mix_in_grad[...] = sliced(t_dot(mixed_grad[...], attended[...]))

    @pl.when(head == heads - 1)
    def _():
        inner_out[...] = jnp.transpose(inner[...])[:8]


def sliced(values):
    total = values[:RANK]
    for index in range(1, values.shape[0] // RANK):
        total = total + values[index * RANK : (index + 1) * RANK]
    return low(total)


def backward_call(
    scalars, pieces, output_weight, mix_in, mix_out, select, states, raws, gains, tables, mask, share
):
    rows, local = raws[0].shape
    heads = local // HD
    width = output_weight.shape[1]
    block = pl.BlockSpec((rows, HD), lambda head, *_: (0, head))
    gain_block = pl.BlockSpec((1, HD), lambda head, *_: (0, head))
    adapter_block = pl.BlockSpec((RANK, HD), lambda head, *_: (0, head))
    operands = [
        scalars, *pieces, output_weight, mix_in, mix_out, select, *states, *raws, *gains, *tables, mask,
    ]
    wide_out = ((rows, local), jnp.float32)
    return kernel_call(
        functools.partial(backward_kernel, width, share, len(pieces)),
        (heads,),
        [ANY] * len(pieces)
        + [whole(output_weight), whole(mix_in), whole(mix_out), whole(select)]
        + [block] * 6
        + [gain_block] * 2
        + [whole(tables[0]), whole(tables[1]), whole(mask)],
        [block] * 3
        + [
            pl.BlockSpec((8, rows), lambda *_: (0, 0)),
            adapter_block,
            pl.BlockSpec((RANK, share), lambda *_: (0, 0)),
        ],
        [wide_out, wide_out, ((rows, local), jnp.bfloat16), ((8, rows), jnp.float32)]
        + [((RANK, local), jnp.bfloat16), ((RANK, share), jnp.bfloat16)],
        operands,
        14 * rows * rows * local + 2 * rows * local * width,
        [
            pltpu.VMEM((rows, pieces[0].shape[1]), jnp.bfloat16),
            pltpu.VMEM((rows, mix_out.shape[0]), jnp.bfloat16),
            pltpu.VMEM((heads, rows, HD), jnp.bfloat16),
            pltpu.VMEM((rows, 128), jnp.float32),
            pltpu.SemaphoreType.DMA((len(pieces),)),
        ],
        1,
    )


def weight_kernel(
    width, size, scalars, inner, squares, query_grad, key_grad, value_grad, query_raw, key_raw,
    query_weight, key_weight, value_weight, lowrank, adapt_out,
    mine, theirs, lowrank_out, adapt_grad, weights, raw, maps, sems,
):
    copies = []
    for index, source in enumerate((query_weight, key_weight, value_weight)):
        copies.append(pltpu.make_async_copy(source, weights.at[index], sems.at[index]))
    for copy in copies:
        copy.start()
    inverse = lax.rsqrt(spread_columns(squares[...]) / width + EPSILON)
    totals = spread_columns(inner[...]) / width
    for index, (grad, value) in enumerate(((query_grad, query_raw), (key_grad, key_raw))):
        scale = inverse[:, index : index + 1]
        raw[index] = low(
            scale * grad[...]
            - value[...] * scale**3 * totals[:, index : index + 1]
        )
    raw[2] = value_grad[...]
    picked = pl.ds(pl.multiple_of(scalars[1], RANK), RANK)
    maps[...] = jnp.zeros_like(maps)
    lowrank_part = None
    for index in range(3):
        maps[index, index * RANK : (index + 1) * RANK, :] = adapt_out[index, picked, :]
        term = dot_t(raw[index], maps[index])
        lowrank_part = term if lowrank_part is None else lowrank_part + term
        adapt_grad[index * RANK : (index + 1) * RANK, :] = sliced(
            t_dot(lowrank[index], raw[index])
        )
    lowrank_out[...] = low(lowrank_part)
    for copy in copies:
        copy.wait()
    levels = mine.shape[0] // size
    for out, offset in ((theirs, 1 - scalars[0]), (mine, scalars[0])):
        total = None
        for index in range(3):
            taken = [
                raw[index, pl.ds(pl.multiple_of((2 * level + offset) * size, size), size), :]
                for level in range(levels)
            ]
            term = dot_t(jnp.concatenate(taken, axis=0), weights[index])
            total = term if total is None else total + term
        out[...] = total.astype(out.dtype)


def weight_call(scalars, inner, squares, grads, raws, weights, lowrank, adapt_out, size):
    rows, local = raws[0].shape
    width = weights[0].shape[0]
    operands = [scalars, inner, squares, *grads, *raws, *weights, lowrank, adapt_out]
    out_shape = [((rows // 2, width), jnp.float32), ((rows // 2, width), jnp.bfloat16)]
    out_shape += [((rows, 128), jnp.bfloat16), ((3 * RANK, local), jnp.bfloat16)]
    return kernel_call(
        functools.partial(weight_kernel, width, size),
        (1,),
        [whole(array) for array in operands[1:8]] + [ANY] * 3 + [whole(lowrank), whole(adapt_out)],
        [pl.BlockSpec(shape, lambda *_: (0, 0)) for shape, _ in out_shape],
        out_shape,
        operands,
        6 * rows * local * width,
        [
            pltpu.VMEM((3, width, local), jnp.bfloat16),
            pltpu.VMEM((3, rows, local), jnp.bfloat16),
            pltpu.VMEM((3, 128, local), jnp.bfloat16),
            pltpu.SemaphoreType.DMA((3,)),
        ],
        1,
    )


def input_kernel(
    kept, came, lowrank, maps, tokens, gain, resid_grad, out
):
    grad = kept[...] + wide(came[...]) + dot_t(lowrank[...], maps[...])
    scaled = grad * wide(gain[...])
    inputs = wide(tokens[...])
    width = inputs.shape[1]
    inverse = lax.rsqrt(jnp.mean(inputs * inputs, axis=1, keepdims=True) + EPSILON)
    inner = jnp.sum(scaled * inputs, axis=1, keepdims=True)
    out[...] = low(
        resid_grad[...] + norm_back(scaled, inputs, inverse, width, inner)
    )


def input_call(kept, came, lowrank, maps, tokens, gain, resid_grad):
    operands = [kept, came, lowrank, maps, tokens, gain, resid_grad]
    rows, width = tokens.shape
    return kernel_call(
        input_kernel,
        (1,),
        [whole(array) for array in operands],
        [pl.BlockSpec((rows, width), lambda *_: (0, 0))],
        [((rows, width), jnp.bfloat16)],
        operands,
        2 * rows * width * 128,
    )[0]


def compact_kernel(
    scalars, lowrank_grad, normed, mix_out_grad, adapt_grad, mix_in_grad, select, out, held, sem
):
    share = out.shape[1]
    columns = pl.ds(pl.multiple_of(scalars[0] * share, share), share)
    copy = pltpu.make_async_copy(normed.at[:, columns], held, sem)
    copy.start()
    copy.wait()
    first = low(t_dot(lowrank_grad[...], held[...]))[: 3 * RANK]
    out[: 3 * RANK] = first
    out[3 * RANK : 4 * RANK] = mix_out_grad[...]
    out[4 * RANK : 7 * RANK] = adapt_grad[...]
    out[7 * RANK : 8 * RANK] = mix_in_grad[...]
    chosen = low(jnp.broadcast_to(select[...], (RANK, 128)))
    out[8 * RANK :] = jnp.concatenate([chosen] * (share // 128), axis=1)


def compact_call(scalars, lowrank_grad, normed, mix_out_grad, adapt_grad, mix_in_grad, select):
    rows = normed.shape[0]
    share = adapt_grad.shape[1]
    operands = [scalars, lowrank_grad, normed, mix_out_grad, adapt_grad, mix_in_grad, select]
    return kernel_call(
        compact_kernel,
        (1,),
        [whole(lowrank_grad), ANY] + [whole(array) for array in operands[3:]],
        [pl.BlockSpec((9 * RANK, share), lambda *_: (0, 0))],
        [((9 * RANK, share), jnp.bfloat16)],
        operands,
        2 * rows * share * 128,
        [pltpu.VMEM((rows, share), jnp.bfloat16), pltpu.SemaphoreType.DMA],
        1,
    )[0]


def spread_kernel(order, *refs):
    pieces, out = refs[:-1], refs[-1]
    step = pl.program_id(0)
    for index, piece in enumerate(pieces):

        @pl.when(step == index)
        def _():
            out[...] = wide(piece[...])


def spread_call(order, pieces):
    size, width = pieces[0].shape
    count = len(pieces)
    return kernel_call(
        spread_kernel,
        (count,),
        [whole(piece) for piece in pieces],
        [pl.BlockSpec((size, width), lambda step, order: (order[step], 0))],
        [((count * size, width), jnp.float32)],
        [order, *pieces],
        size * width,
        (),
        1,
    )[0]


def assemble_kernel(trees, order, *refs):
    count = len(refs) - 5
    own, pieces = refs[0], refs[1:count]
    in_grad, out_grad, mix_in_grad, mix_out_grad = refs[count : count + 4]
    (choice,) = refs[count + 4 :]
    share = own.shape[1]
    block = own.shape[0] // trees
    row = lax.broadcasted_iota(jnp.int32, (RANK, 128), 0)
    lane = lax.broadcasted_iota(jnp.int32, (RANK, 128), 1)
    same = lax.rem(lane, RANK) == row
    for tree in range(trees):
        chosen = own[tree * block + 8 * RANK : tree * block + 9 * RANK, :128]
        choice[tree * RANK : (tree + 1) * RANK] = low(jnp.where(same, wide(chosen), 0.0))

    def kind(source, stride, index):
        return jnp.concatenate(
            [
                source[tree * stride + index * RANK : tree * stride + (index + 1) * RANK, :]
                for tree in range(trees)
            ],
            axis=0,
        )

    for index in range(3):
        out_grad[index] = t_dot(choice[...], kind(own, block, 4 + index))
    mix_in_grad[...] = t_dot(kind(own, block, 7), choice[...])
    for place, source in enumerate((own, *pieces)):
        stride = block if place == 0 else 4 * RANK
        start = pl.ds(pl.multiple_of(order[place] * share, share), share)
        for index in range(3):
            in_grad[index, start, :] = t_dot(kind(source, stride, index), choice[...])
        mix_out_grad[:, start] = t_dot(choice[...], kind(source, stride, 3))


def assemble_call(order, own, pieces, trees):
    share = own.shape[1]
    count = 1 + len(pieces)
    width = count * share
    out_shape = [((3, width, 128), jnp.float32), ((3, 128, share), jnp.float32)]
    out_shape += [((share, 128), jnp.float32), ((128, width), jnp.float32)]
    operands = [order, own, *pieces]
    return kernel_call(
        functools.partial(assemble_kernel, trees),
        (1,),
        [whole(array) for array in operands[1:]],
        [pl.BlockSpec(shape, lambda *_, size=len(shape): (0,) * size) for shape, _ in out_shape],
        out_shape,
        operands,
        2 * trees * RANK * 128 * width * 4,
        [pltpu.VMEM((trees * RANK, 128), jnp.bfloat16)],
        1,
    )


def body(
    tokens,
    cotangent,
    attn_gain,
    ffn_gain,
    query_gain,
    key_gain,
    query_weight,
    key_weight,
    value_weight,
    output_weight,
    expert_gate,
    expert_up,
    expert_down,
    adapt_in,
    adapt_out,
    adapt_in_out,
    adapt_out_out,
    routes,
    gate_weights,
    block_parent,
    adapter_pick,
):
    rows_here, model_width = tokens.shape
    tensor_rank = lax.axis_index("tensor")
    tensor_count = lax.axis_size("tensor")
    owners = lax.axis_size("expert")
    owner_rank = lax.axis_index("expert")
    axes = divide_axes(owners, tensor_count)
    far, near, span = axes["z"][1], axes["x"][1], axes["y"][1]
    experts_here, _, hidden_here = expert_gate.shape
    experts_all = experts_here * owners
    column_share = model_width // tensor_count
    row_share = rows_here // tensor_count
    hold = lax.optimization_barrier
    level, core = tensor_rank // 2, tensor_rank % 2

    def own_rows(array):
        return lax.dynamic_slice_in_dim(array, tensor_rank * row_share, row_share, 0)

    routes_wide = jnp.swapaxes(routes, 0, 1)
    weights_wide = jnp.swapaxes(gate_weights, 0, 1)
    route_weights = jnp.sum(
        jnp.where(
            routes_wide[:, :, None] == jnp.arange(experts_all, dtype=jnp.int32)[None, None, :],
            weights_wide[:, :, None],
            0.0,
        ),
        axis=0,
    )
    weights_high = low(route_weights)
    weights_low = low(route_weights - wide(weights_high))
    side_width = -(-2 * experts_all // 128) * 128
    side_pad = jnp.zeros((rows_here, side_width - 2 * experts_all), jnp.bfloat16)
    side_rows = jnp.concatenate([weights_high, weights_low, side_pad], axis=1)
    cot_queue = []
    for step in range(span):
        place = ((level + span - step) % span * 2 + core) * row_share
        cot_queue.append(
            jnp.concatenate(
                [
                    lax.dynamic_slice_in_dim(cotangent, place, row_share, 0),
                    lax.dynamic_slice_in_dim(side_rows, place, row_share, 0),
                ],
                axis=1,
            )
        )
    cot_queue = [jnp.concatenate(cot_queue, axis=0)]
    side_index = jnp.arange(side_width, dtype=jnp.int32)
    hidden_owner = (
        owner_rank * experts_here
        + jnp.arange(experts_here * hidden_here, dtype=jnp.int32) // hidden_here
    )
    spread_flat = low(
        (side_index[:, None] % experts_all == hidden_owner[None, :])
        & (side_index[:, None] < 2 * experts_all)
    )
    spread = jnp.swapaxes(spread_flat.reshape(side_width, experts_here, hidden_here), 0, 1)

    cot_planes = [None] * far
    cot_queue.append(turn(cot_queue[0], axes, "z", 1))
    cot_planes[0] = ring(cot_queue[0], axes, "x")
    first_gain, second_gain = attn_gain[None, :], ffn_gain[None, :]
    gains = (query_gain[None, :], key_gain[None, :])
    reached = ancestry(block_parent)
    cosine_table, sine_table = rope_tables(reached, rows_here // block_parent.shape[0], HD)
    signs = jnp.where(jnp.arange(HD) < HD // 2, -1.0, 1.0)[None, :]
    tables = (cosine_table, sine_table * signs)
    mask = jnp.where(token_mask(reached[0], rows_here), 0.0, MASKED_SCORE)
    select = jnp.repeat(wide(adapter_pick), RANK, axis=1)
    picked = jnp.argmax(adapter_pick[0]).astype(jnp.int32) * RANK
    weights = (query_weight, key_weight, value_weight)
    normed_in, lowrank, *raws, squares = project_call(
        tokens, first_gain, weights, adapt_in, adapt_out, select
    )

    squares = lax.psum(squares, "tensor")
    squares, cot_queue[1], cot_planes[0] = hold((squares, cot_queue[1], cot_planes[0]))
    cot_queue.append(turn(cot_queue[1], axes, "z", 1))
    cot_planes[1] = ring(cot_queue[1], axes, "x")
    *states, mine, theirs = attend_call(
        jnp.reshape(core, (1,)).astype(jnp.int32),
        squares,
        raws,
        gains,
        tables,
        mask,
        output_weight,
        adapt_in_out,
        row_share,
    )

    branch_kept, branch_came = scatter_tensor(mine, theirs, axes)
    branch_came, cot_queue[2], cot_planes[1] = hold((branch_came, cot_queue[2], cot_planes[1]))
    cot_queue.append(turn(cot_queue[2], axes, "z", 1))
    cot_planes[2] = ring(cot_queue[2], axes, "x")
    resid_rows, norm_plane, mixed_rows = resid_call(
        branch_kept, branch_came, own_rows(tokens), adapt_out_out, select, second_gain
    )
    gates = (expert_gate, turn(expert_gate, axes, "c", 1))
    ups = (expert_up, turn(expert_up, axes, "c", 1))
    down_tall = expert_down.reshape(-1, model_width)
    downs = (down_tall, turn(down_tall, axes, "c", 1))

    norm_next = turn(norm_plane, axes, "z", 1)
    norm_first = gather_first(norm_plane, axes)
    backs, sides = [None] * far, [None] * far

    def hidden_step(*indices):
        back, side = hidden_call(
            [cot_planes[index] for index in indices], downs, spread_flat, experts_here, row_share
        )
        for order, index in enumerate(indices):
            backs[index], sides[index] = (back, order * side.shape[0] // len(indices)), side
        return back

    back_first = hidden_step(0, 1)

    norm_planes = [None] * far
    norm_next, norm_first, cot_queue[3], cot_planes[2], back_first = hold(
        (norm_next, norm_first, cot_queue[3], cot_planes[2], back_first)
    )
    backs[0], backs[1] = (back_first, backs[0][1]), (back_first, backs[1][1])
    norm_later = turn(norm_next, axes, "z", 1)
    norm_planes[0] = gather_second(norm_first, axes)
    norm_first = gather_first(norm_next, axes)
    cot_planes[3] = ring(cot_queue[3], axes, "x")
    parts, hiddens = [None] * far, [None] * far

    def expert_step(index):
        back, offset = backs[index]
        *parts[index], hiddens[index] = expert_call(
            norm_planes[index], gates, ups, spread, sides[index], back, offset
        )

    back_second = hidden_step(2)

    norm_next, norm_first, norm_planes[0], cot_planes[3], back_second = hold(
        (norm_later, norm_first, norm_planes[0], cot_planes[3], back_second)
    )
    backs[2] = (back_second, 0)
    norm_later = turn(norm_next, axes, "z", 1)
    norm_planes[1] = gather_second(norm_first, axes)
    norm_first = gather_first(norm_next, axes)
    expert_step(0)

    norm_next, norm_first, norm_planes[1], parts[0] = hold(
        (norm_later, norm_first, norm_planes[1], parts[0])
    )
    norm_planes[2] = gather_second(norm_first, axes)
    norm_first = gather_first(norm_next, axes)
    expert_step(1)

    norm_first, norm_planes[2], parts[1] = hold((norm_first, norm_planes[2], parts[1]))
    norm_planes[3] = gather_second(norm_first, axes)
    came = [None] * far
    kept = [None] * far
    came[1] = scatter_first(parts[1], axes)
    expert_step(2)
    hidden_step(3)

    norm_planes[3], came[1], parts[2] = hold((norm_planes[3], came[1], parts[2]))
    kept[1], came[1] = scatter_second(parts[1], came[1], axes)
    came[2] = scatter_first(parts[2], axes)
    came[0] = scatter_first(parts[0], axes)
    expert_step(3)

    kept[1], came[1], came[2], came[0], parts[3] = hold(
        (kept[1], came[1], came[2], came[0], parts[3])
    )
    ring_sum = turn(low(scatter_last(kept[1], came[1])), axes, "z", 1)
    kept[2], came[2] = scatter_second(parts[2], came[2], axes)
    came[3] = scatter_first(parts[3], axes)
    kept[0], came[0] = scatter_second(parts[0], came[0], axes)
    mixes, mix_came = [None] * far, [None] * far

    def down_step(first, second):
        mixes[first], mixes[second] = down_call(
            [hiddens[first], hiddens[second]], downs, near, span, row_share
        )

    down_step(1, 2)

    ring_sum, kept[2], came[2], came[3], mixes[1], mixes[2] = hold(
        (ring_sum, kept[2], came[2], came[3], mixes[1], mixes[2])
    )
    ring_sum = turn(low(wide(ring_sum) + scatter_last(kept[2], came[2])), axes, "z", 1)
    kept[3], came[3] = scatter_second(parts[3], came[3], axes)
    mix_came[1] = send_sum(mixes[1], axes, "x")
    down_step(3, 0)

    ring_sum, kept[3], came[3], kept[0], came[0], mixes[3], mixes[0] = hold(
        (ring_sum, kept[3], came[3], kept[0], came[0], mixes[3], mixes[0])
    )
    ring_sum = turn(low(wide(ring_sum) + scatter_last(kept[3], came[3])), axes, "z", 1)
    ring_sum, mix_came[1] = hold((ring_sum, mix_came[1]))

    mix_sum = turn(low(wide(mixes[1][0]) + wide(mix_came[1])), axes, "z", 1)
    mix_came[2] = send_sum(mixes[2], axes, "x")
    ffn_rows_grad = wide(ring_sum) + scatter_last(kept[0], came[0])
    second_scaled = ffn_rows_grad * wide(second_gain)
    second_inverse = lax.rsqrt(
        jnp.mean(resid_rows * resid_rows, axis=1, keepdims=True) + EPSILON
    )
    resid_grad_rows = wide(own_rows(cotangent)) + norm_back(
        second_scaled,
        resid_rows,
        second_inverse,
        model_width,
        jnp.sum(second_scaled * resid_rows, axis=1, keepdims=True),
    )
    branch_sent = jnp.concatenate([low(resid_grad_rows), mixed_rows], axis=1)
    branch_pieces = gather_tensor(branch_sent, axes)
    order = jnp.stack(
        [
            (level + span - step) % span * 2 + side
            for side in (core, 1 - core)
            for step in range(span)
        ]
    ).astype(jnp.int32)

    branch_pieces, mix_sum, mix_came[2] = hold((branch_pieces, mix_sum, mix_came[2]))
    mix_sum = turn(
        low(wide(mix_sum) + (wide(mixes[2][0]) + wide(mix_came[2]))), axes, "z", 1
    )
    mix_came[3] = send_sum(mixes[3], axes, "x")
    rank_list = jnp.reshape(tensor_rank, (1,)).astype(jnp.int32)
    query_grad, key_grad, value_grad, inner, mix_in_grad, mix_out_grad = backward_call(
        jnp.concatenate([order, rank_list]),
        branch_pieces,
        output_weight,
        adapt_in_out,
        adapt_out_out,
        select,
        states,
        raws[:2],
        gains,
        tables,
        mask,
        column_share,
    )
    inner = lax.psum(inner, "tensor")
    normed_mine, normed_theirs, lowrank_part, adapt_grad = weight_call(
        jnp.stack([core, picked]).astype(jnp.int32),
        inner,
        squares,
        (query_grad, key_grad, value_grad),
        raws[:2],
        weights,
        lowrank,
        adapt_out,
        row_share,
    )

    normed_mine, normed_theirs, lowrank_part, mix_sum, mix_came[3] = hold(
        (normed_mine, normed_theirs, lowrank_part, mix_sum, mix_came[3])
    )
    mix_sum = turn(
        low(wide(mix_sum) + (wide(mixes[3][0]) + wide(mix_came[3]))), axes, "z", 1
    )
    mix_came[0] = send_sum(mixes[0], axes, "x")
    lowrank_grad = low(sum_tensor(lowrank_part, axes))
    normed_kept, normed_came = scatter_tensor(normed_mine, normed_theirs, axes)
    maps = jnp.swapaxes(lax.dynamic_slice_in_dim(adapt_in, picked, RANK, 2), 0, 1)
    maps = maps.reshape(model_width, 3 * RANK)
    maps = jnp.concatenate(
        [maps, jnp.zeros((model_width, 128 - 3 * RANK), jnp.bfloat16)], axis=1
    )
    input_rows = input_call(
        normed_kept,
        normed_came,
        own_rows(lowrank_grad),
        maps,
        own_rows(tokens),
        first_gain,
        resid_grad_rows,
    )
    compact = compact_call(
        rank_list, lowrank_grad, normed_in, mix_out_grad, adapt_grad, mix_in_grad, select
    )
    trees = jnp.concatenate(ring(compact, axes, "x"), axis=0)

    input_rows, trees, mix_sum, mix_came[0] = hold((input_rows, trees, mix_sum, mix_came[0]))
    input_grad = spread_call(order, gather_tensor(input_rows, axes))
    mix_total = wide(mix_sum) + (wide(mixes[0][0]) + wide(mix_came[0]))
    mix_total = jnp.split(mix_total, span, axis=0)
    mix_last = send_sum([low(part) for part in mix_total], axes, "y")
    trees = jnp.concatenate(ring(trees, axes, "z"), axis=0)

    trees, mix_last = hold((trees, mix_last))
    shared = trees.reshape(owners, -1, column_share)[:, : 4 * RANK]
    shared = gather_tensor(shared.reshape(-1, column_share), axes)
    grad_adapt_in, grad_adapt_out, grad_adapt_in_out, grad_adapt_out_out = assemble_call(
        order, trees, shared[1:], owners
    )
    layer_rows = low(resid_rows + mix_total[0] + wide(mix_last))
    layer_out = swap_columns(layer_rows, axes)
    return (
        layer_out,
        input_grad,
        grad_adapt_in,
        grad_adapt_out,
        grad_adapt_in_out,
        grad_adapt_out_out,
    )


def solution(mesh):
    return jax.shard_map(
        body,
        mesh=mesh,
        in_specs=(
            P("expert", None),
            P("expert", None),
            P(),
            P(),
            P("tensor"),
            P("tensor"),
            P(None, "tensor"),
            P(None, "tensor"),
            P(None, "tensor"),
            P("tensor", None),
            P("expert", None, "tensor"),
            P("expert", None, "tensor"),
            P("expert", "tensor", None),
            P(),
            P(None, None, "tensor"),
            P("tensor", None),
            P(),
            P("expert", None),
            P("expert", None),
            P("expert"),
            P("expert", None),
        ),
        out_specs=(
            P("expert", "tensor"),
            P("expert", None),
            P(),
            P(None, None, "tensor"),
            P("tensor", None),
            P(),
        ),
        check_vma=False,
    )
```

```python
import functools

import jax
import jax.numpy as jnp
from jax import lax
from jax.experimental import pallas as pl
from jax.experimental.pallas import tpu as pltpu
from jax.sharding import PartitionSpec as P

HD = 128
RANK = 16


EPSILON = 1e-05
ROPE_BASE = 10000.0
MASKED_SCORE = -1e30
VMEM_LIMIT = 56 * 2**20


def ancestry(parents):
    blocks = parents.shape[0]
    places = jnp.arange(blocks, dtype=jnp.int32)
    walker = places
    reached = walker[:, None] == places[None, :]
    for _ in range(blocks - 1):
        hits = (walker[:, None] == places[None, :]).astype(jnp.int32)
        walker = jnp.sum(hits * parents[None, :], axis=1)
        reached = reached | (walker[:, None] == places[None, :])
    return reached[None]


def rope_tables(reached, block_span, head_size):
    depths = jnp.sum(reached.astype(jnp.int32), axis=2) - 1
    offsets = jnp.arange(block_span, dtype=jnp.int32)
    located = (
        (depths[:, :, None] * block_span + offsets[None, None, :]).reshape(-1).astype(jnp.float32)
    )
    halves = head_size // 2
    speeds = ROPE_BASE ** (-2.0 * jnp.arange(halves, dtype=jnp.float32) / head_size)
    angles = located[:, None] * speeds[None, :]
    angles = jnp.concatenate([angles, angles], axis=1)
    return (jnp.cos(angles), jnp.sin(angles))


def token_mask(reached, total_size):
    blocks = reached.shape[0]
    block_span = total_size // blocks
    widened = jnp.broadcast_to(
        reached[:, None, :, None], (blocks, block_span, blocks, block_span)
    ).reshape(total_size, total_size)
    positions = jnp.arange(total_size, dtype=jnp.int32)
    return widened & (positions[None, :] <= positions[:, None])


def norm_back(scaled_grad, values, inverse, model_width, inner_sum):
    return inverse * scaled_grad - values * inverse**3 * (inner_sum / model_width)


def divide_axes(owners, tensor_count):
    outer = 4
    return {
        "z": ("expert", outer, owners // outer, owners),
        "x": ("expert", owners // outer, 1, owners),
        "y": ("tensor", tensor_count // 2, 2, tensor_count),
        "c": ("tensor", 2, 1, tensor_count),
    }


def turn(array, axes, name, step):
    axis, length, stride, total = axes[name]
    pairs = []
    for index in range(total):
        place = (index // stride) % length
        moved = index + ((place + step) % length - place) * stride
        pairs.append((index, moved))
    return lax.ppermute(array, axis, pairs)


def ring(array, axes, name):
    held = [array]
    for _ in range(axes[name][1] - 1):
        held.append(turn(held[-1], axes, name, 1))
    return held


def wide(array):
    return array.astype(jnp.float32)


def low(array):
    return array.astype(jnp.bfloat16)


def send_sum(parts, axes, name):
    total = parts[-1]
    for part in parts[-2:0:-1]:
        total = low(wide(turn(total, axes, name, -1)) + wide(part))
    return turn(total, axes, name, -1)


def scatter_first(pieces, axes):
    span = axes["y"][1]
    return send_sum(pieces[:span], axes, "y"), send_sum(pieces[span:], axes, "x")


def scatter_second(pieces, came, axes):
    span = axes["y"][1]
    first = wide(pieces[0]) + wide(came[0])
    second = wide(pieces[span]) + wide(came[1])
    first = jnp.split(first, axes["x"][1], axis=0)
    second = jnp.split(second, axes["y"][1], axis=0)
    first_came = send_sum([low(part) for part in first], axes, "x")
    second_came = send_sum([low(part) for part in second], axes, "y")
    return (first[0], second[0]), (first_came, second_came)


def scatter_last(kept, came):
    return jnp.concatenate([kept[0] + wide(came[0]), kept[1] + wide(came[1])], axis=0)


def gather_tensor(rows, axes):
    held = ring(rows, axes, "y")
    return held + [turn(piece, axes, "c", 1) for piece in held]


def scatter_core(mine, came, axes):
    rank = lax.axis_index("tensor")
    span = axes["y"][1]
    size = mine.shape[0] // span
    total = None
    for step in range(span - 1, -1, -1):
        level = (rank // 2 + span - step) % span
        part = wide(lax.dynamic_slice_in_dim(mine, level * size, size, 0)) + wide(
            lax.dynamic_slice_in_dim(came, level * size, size, 0)
        )
        if step == 0:
            return part, total
        total = low(part if total is None else part + wide(turn(total, axes, "y", -1)))


def gather_x(rows, axes):
    return jnp.concatenate(ring(rows, axes, "x"), axis=0)


def swap_columns(rows, axes):
    rank = lax.axis_index("tensor")
    count = lax.axis_size("tensor")
    size, width = rows.shape
    span = axes["y"][1]
    share = width // count
    level, core = rank // 2, rank % 2
    whole = jnp.zeros((count * size, share), rows.dtype)
    for step in range(span):
        toward = (level + step) % span
        piece = lax.dynamic_slice_in_dim(rows, toward * 2 * share, 2 * share, 1)
        if step:
            piece = turn(piece, axes, "y", step)
        mine = lax.dynamic_slice_in_dim(piece, core * share, share, 1)
        theirs = lax.dynamic_slice_in_dim(piece, (1 - core) * share, share, 1)
        theirs = turn(theirs, axes, "c", 1)
        source = (level + span - step) % span
        whole = lax.dynamic_update_slice_in_dim(whole, mine, (source * 2 + core) * size, 0)
        whole = lax.dynamic_update_slice_in_dim(whole, theirs, (source * 2 + 1 - core) * size, 0)
    return whole


def sum_tensor(array, axes):
    total = wide(array) + wide(turn(array, axes, "c", 1))
    moving = total.astype(array.dtype)
    result = total
    for _ in range(axes["y"][1] - 1):
        moving = turn(moving, axes, "y", 1)
        result = result + wide(moving)
    return result


def dot(left, right):
    return jnp.dot(left, right, preferred_element_type=jnp.float32)


def dot_t(left, right):
    return lax.dot_general(
        left, right, (((1,), (1,)), ((), ())), preferred_element_type=jnp.float32
    )


def t_dot(left, right):
    return lax.dot_general(
        left, right, (((0,), (0,)), ((), ())), preferred_element_type=jnp.float32
    )


ANY = pl.BlockSpec(memory_space=pl.ANY)


def whole(array):
    shape = array.shape
    return pl.BlockSpec(shape, lambda *_: (0,) * len(shape))


def kernel_call(kernel, grid, in_specs, out_specs, out_shape, operands, flops, scratch=(), scalars=0):
    moved = sum(array.size * array.dtype.itemsize for array in operands)
    return pl.pallas_call(
        kernel,
        grid_spec=pltpu.PrefetchScalarGridSpec(
            num_scalar_prefetch=scalars,
            grid=grid,
            in_specs=in_specs,
            out_specs=out_specs,
            scratch_shapes=list(scratch),
        ),
        out_shape=[jax.ShapeDtypeStruct(shape, kind) for shape, kind in out_shape],
        compiler_params=pltpu.CompilerParams(vmem_limit_bytes=VMEM_LIMIT),
        cost_estimate=pl.CostEstimate(flops=flops, bytes_accessed=moved, transcendentals=0),
    )(*operands)


def project_kernel(
    tokens, gain, query_weight, key_weight, value_weight, adapt_in, adapt_out, select,
    normed_out, lowrank_out, query_out, key_out, value_out, squares_out,
    weights, maps, sems,
):
    copies = [pltpu.make_async_copy(adapt_in, maps, sems.at[3])]
    for index, source in enumerate((query_weight, key_weight, value_weight)):
        copies.append(pltpu.make_async_copy(source, weights.at[index], sems.at[index]))
    for copy in copies:
        copy.start()
    inputs = wide(tokens[...])
    inverse = lax.rsqrt(jnp.mean(inputs * inputs, axis=1, keepdims=True) + EPSILON)
    normed_out[...] = low(inputs * inverse * wide(gain[...]))
    copies[0].wait()
    for index in range(3):
        lowrank_out[index] = low(dot(normed_out[...], maps[index]) * select[...])
    squares = []
    for index, out in enumerate((query_out, key_out, value_out)):
        copies[index + 1].wait()
        raw = dot(normed_out[...], weights[index]) + dot(lowrank_out[index], adapt_out[index])
        out[...] = raw
        squares.append(jnp.sum(raw * raw, axis=1, keepdims=True))
    lane = lax.broadcasted_iota(jnp.int32, (tokens.shape[0], 128), 1)
    columns = jnp.where(lane == 0, squares[0], jnp.where(lane == 1, squares[1], 0.0))
    squares_out[...] = jnp.transpose(columns)[:8]


def project_call(tokens, gain, weights, adapt_in, adapt_out, select):
    rows, width = tokens.shape
    local = weights[0].shape[1]
    rank = adapt_in.shape[2]
    out_shape = [((rows, width), jnp.bfloat16), ((3, rows, rank), jnp.bfloat16)]
    out_shape += [((rows, local), jnp.float32)] * 3 + [((8, rows), jnp.float32)]
    operands = [tokens, gain, *weights, adapt_in, adapt_out, select]
    return kernel_call(
        project_kernel,
        (1,),
        [whole(tokens), whole(gain), ANY, ANY, ANY, ANY, whole(adapt_out), whole(select)],
        [pl.BlockSpec(shape, lambda *_, size=len(shape): (0,) * size) for shape, _ in out_shape],
        out_shape,
        operands,
        6 * rows * width * local,
        [
            pltpu.VMEM((3, width, local), jnp.bfloat16),
            pltpu.VMEM(adapt_in.shape, jnp.bfloat16),
            pltpu.SemaphoreType.DMA((4,)),
        ],
    )


def spread_columns(rows):
    return jnp.transpose(jnp.concatenate([rows] * (128 // rows.shape[0]), axis=0))


def turned(values):
    half = values.shape[1] // 2
    return jnp.concatenate([values[:, half:], values[:, :half]], axis=1)


def attend_kernel(
    width, size, core, squares, query_raw, key_raw, value_raw, query_gain, key_gain, cosine, sine,
    mask, output_weight, mix_in, queries, keys, values, attended, mine, theirs, held, weight, sem,
):
    head = pl.program_id(0)
    last = pl.num_programs(0) - 1
    copy = pltpu.make_async_copy(output_weight, weight, sem)

    @pl.when(head == 0)
    def _():
        copy.start()

    inverse = lax.rsqrt(spread_columns(squares[...]) / width + EPSILON)
    query = query_raw[...] * inverse[:, 0:1] * wide(query_gain[...])
    key = key_raw[...] * inverse[:, 1:2] * wide(key_gain[...])
    query = low(query * cosine[...] + turned(query) * sine[...])
    key = low(key * cosine[...] + turned(key) * sine[...])
    value = low(value_raw[...])
    queries[...] = query
    keys[...] = key
    values[...] = value
    scores = dot_t(query, key) * HD ** (-0.5) + mask[...]
    raised = jnp.exp(scores - jnp.max(scores, axis=1, keepdims=True))
    weights = low(raised / jnp.sum(raised, axis=1, keepdims=True))
    result = low(dot(weights, value))
    attended[...] = result
    held[head] = result

    @pl.when(head == last)
    def _():
        copy.wait()
        heads = held.shape[0]
        levels = mine.shape[0] // size
        for out, offset in ((mine, core[0]), (theirs, 1 - core[0])):
            taken = []
            for level in range(levels):
                rows = pl.ds(pl.multiple_of((2 * level + offset) * size, size), size)
                taken.append(
                    jnp.concatenate([held[index, rows, :] for index in range(heads)], axis=1)
                )
            taken = jnp.concatenate(taken, axis=0)
            out[:, :width] = dot(taken, weight[...]).astype(out.dtype)
            out[:, width:] = dot(taken, mix_in[...]).astype(out.dtype)


def attend_call(core, squares, raws, gains, tables, mask, output_weight, mix_in, size):
    rows, local = raws[0].shape
    heads = local // HD
    width = output_weight.shape[1]
    wide_width = width + mix_in.shape[1]
    block = pl.BlockSpec((rows, HD), lambda head, *_: (0, head))
    gain_block = pl.BlockSpec((1, HD), lambda head, *_: (0, head))
    fixed = pl.BlockSpec((rows // 2, wide_width), lambda *_: (0, 0))
    operands = [core, squares, *raws, *gains, *tables, mask, output_weight, mix_in]
    return kernel_call(
        functools.partial(attend_kernel, width, size),
        (heads,),
        [whole(squares)] + [block] * 3 + [gain_block] * 2
        + [whole(tables[0]), whole(tables[1]), whole(mask), ANY, whole(mix_in)],
        [block] * 4 + [fixed] * 2,
        [((rows, local), jnp.bfloat16)] * 4
        + [((rows // 2, wide_width), jnp.float32), ((rows // 2, wide_width), jnp.bfloat16)],
        operands,
        4 * rows * rows * local + 2 * rows * local * width,
        [
            pltpu.VMEM((heads, rows, HD), jnp.bfloat16),
            pltpu.VMEM(output_weight.shape, jnp.bfloat16),
            pltpu.SemaphoreType.DMA,
        ],
        1,
    )


def resid_kernel(
    width, kept, came, tokens, mix_out, select, gain, resid_out, norm_out, mixed_out
):
    mixed = low((kept[:, width:] + wide(came[:, width:])) * select[...])
    mixed_out[...] = mixed
    resid = (
        wide(tokens[...])
        + (kept[:, :width] + wide(came[:, :width]))
        + dot(mixed, mix_out[...])
    )
    resid_out[...] = resid
    inverse = lax.rsqrt(jnp.mean(resid * resid, axis=1, keepdims=True) + EPSILON)
    norm_out[...] = low(resid * inverse * wide(gain[...]))


def resid_call(kept, came, tokens, mix_out, select, gain):
    rows, width = tokens.shape
    out_shape = [((rows, width), jnp.float32), ((rows, width), jnp.bfloat16)]
    out_shape += [((rows, mix_out.shape[0]), jnp.bfloat16)]
    operands = [kept, came, tokens, mix_out, select, gain]
    return kernel_call(
        functools.partial(resid_kernel, width),
        (1,),
        [whole(array) for array in operands],
        [pl.BlockSpec(shape, lambda *_: (0, 0)) for shape, _ in out_shape],
        out_shape,
        operands,
        2 * rows * width * mix_out.shape[0],
    )


def plane_order(near, span, size):
    return [
        (across, down * size, (down * near + across) * size)
        for down in range(span)
        for across in range(near)
    ]


def hidden_kernel(places, *refs):
    count = len(places)
    pieces, (down_own, down_other, spread), (out, side_out), (rows, side, row_sems, side_sems) = (
        refs[:count],
        refs[count : count + 3],
        refs[count + 3 : count + 5],
        refs[count + 5 :],
    )
    step = pl.program_id(0)
    width = rows.shape[1]

    @pl.when(step == 0)
    def _():
        copies = []
        for index, (piece, targets) in enumerate(zip(pieces, places)):
            for source, target, size in targets:
                taken = piece.at[pl.ds(source, size)]
                place = pl.ds(target, size)
                slot = len(copies) // 2
                copies.append(
                    pltpu.make_async_copy(
                        taken.at[:, pl.ds(0, width)], rows.at[place], row_sems.at[slot]
                    )
                )
                copies.append(
                    pltpu.make_async_copy(
                        taken.at[:, pl.ds(width, side.shape[1])], side.at[place], side_sems.at[slot]
                    )
                )
        for copy in copies:
            copy.start()
        for copy in copies:
            copy.wait()
        side_out[...] = side[...]

    def emit(down):
        grad = dot_t(rows[...], down[...]) * dot(side[...], spread[...])
        part = out.shape[2]
        for index in range(out.shape[0]):
            out[index] = low(grad[:, index * part : (index + 1) * part])

    half = pl.num_programs(0) // 2

    @pl.when(step < half)
    def _():
        emit(down_own)

    @pl.when(step >= half)
    def _():
        emit(down_other)


def hidden_call(planes, downs, spread, experts, size):
    hidden, width = downs[0].shape
    near = len(planes[0])
    pieces, places, rows = [], [], 0
    for plane in planes:
        for across, column in enumerate(plane):
            down = 0
            for piece in column:
                targets = []
                for source in range(0, piece.shape[0], size):
                    targets.append((source, rows + (down * near + across) * size, size))
                    down += 1
                pieces.append(piece)
                places.append(targets)
        rows += near * down * size
    blocks = rows // size
    part = hidden // experts
    side = spread.shape[0]
    pair = 2 * part
    half = experts // 2
    last = half - 1
    return kernel_call(
        functools.partial(hidden_kernel, places),
        (2 * half,),
        [ANY] * len(pieces)
        + [
            pl.BlockSpec((pair, width), lambda n: (jnp.minimum(n, last), 0)),
            pl.BlockSpec((pair, width), lambda n: (jnp.maximum(n - half, 0), 0)),
            pl.BlockSpec((side, pair), lambda n: (0, lax.rem(n, half))),
        ],
        [
            pl.BlockSpec((2, rows, part), lambda n: (n, 0, 0)),
            pl.BlockSpec((rows, side), lambda n: (0, 0)),
        ],
        [((2 * experts, rows, part), jnp.bfloat16), ((rows, side), jnp.bfloat16)],
        [*pieces, *downs, spread],
        4 * rows * hidden * width,
        [
            pltpu.VMEM((rows, width), jnp.bfloat16),
            pltpu.VMEM((rows, side), jnp.bfloat16),
            pltpu.SemaphoreType.DMA((blocks,)),
            pltpu.SemaphoreType.DMA((blocks,)),
        ],
    )


def expert_kernel(count, near, span, offset, *refs):
    pieces = refs[:count]
    gate_own, up_own, gate_other, up_other, spread, side, back = refs[count : count + 7]
    outs, hidden_out = refs[count + 7 : count + 7 + near + span], refs[count + 7 + near + span]
    rows, weights, gate_grad, up_grad, hidden, grads, sems, row_sem, back_sem, out_sem = refs[
        count + 8 + near + span :
    ]
    step = pl.program_id(0)
    size = pieces[0].shape[0]
    experts, _, part = gate_own.shape
    total_rows = rows.shape[0]
    sources = (gate_own, up_own, gate_other, up_other)

    def load(expert):
        slot = weights.at[expert]
        return [
            pltpu.make_async_copy(
                source.at[expert], slot.at[:, pl.ds(index * part, part)], sems.at[expert]
            )
            for index, source in enumerate(sources)
        ]

    row_copies = [
        pltpu.make_async_copy(piece, rows.at[pl.ds(index * size, size)], row_sem.at[index])
        for index, piece in enumerate(pieces)
    ]
    back_copy = pltpu.make_async_copy(
        back.at[:, pl.ds(offset, total_rows), :], grads, back_sem
    )
    out_copy = pltpu.make_async_copy(hidden, hidden_out, out_sem)

    @pl.when(step == 0)
    def _():
        for copy in row_copies + load(0) + [back_copy] + load(1):
            copy.start()
        for copy in row_copies:
            copy.wait()
        back_copy.wait()

        def work(expert, carry):
            for ahead in range(2, experts):

                @pl.when(expert == ahead - 2)
                def _():
                    for copy in load(ahead):
                        copy.start()

            for copy in load(expert):
                copy.wait()
            values = dot(rows[...], weights[expert])
            weight = dot(side[...], spread[expert])
            for half in range(2):
                gate_value = values[:, 2 * half * part : (2 * half + 1) * part]
                up_value = values[:, (2 * half + 1) * part : (2 * half + 2) * part]
                sigmoid = jax.nn.sigmoid(gate_value)
                silu = gate_value * sigmoid
                place = half * experts + expert
                grad = wide(grads[place])
                gate_grad[place] = low(grad * up_value * (sigmoid + silu * (1.0 - sigmoid)))
                up_grad[place] = low(grad * silu)
                hidden[place] = low(silu * up_value * weight)
            return carry

        lax.fori_loop(0, experts, work, 0)
        out_copy.start()

    tile = outs[0].shape[1]
    columns = pl.ds(pl.multiple_of(step * tile, tile), tile)
    total = None
    for expert in range(experts):
        for half in range(2):
            place = half * experts + expert
            for index, grad in enumerate((gate_grad, up_grad)):
                first = (2 * half + index) * part
                term = dot_t(grad[place], weights[expert, columns, first : first + part])
                total = term if total is None else total + term
    half = total_rows // (2 * near * span)
    for down in range(span):
        for across in range(near):
            first = 2 * (down * near + across) * half
            outs[down][across * half : (across + 1) * half] = low(total[first : first + half])
            outs[span + across][down * half : (down + 1) * half] = low(
                total[first + half : first + 2 * half]
            )

    @pl.when(step == pl.num_programs(0) - 1)
    def _():
        out_copy.wait()


def expert_call(pieces, gates, ups, spread, side, back, offset, near, span):
    count = len(pieces)
    experts, width, part = gates[0].shape
    size = pieces[0].shape[0]
    rows = size * count
    tile = min(width, 512)
    shape = (2 * experts, rows, part)
    slots = pltpu.VMEM(shape, jnp.bfloat16)
    side_block = pl.BlockSpec((rows, side.shape[1]), lambda n: (offset // rows, 0))
    return kernel_call(
        functools.partial(expert_kernel, count, near, span, offset),
        (width // tile,),
        [ANY] * (count + 4) + [whole(spread), side_block, ANY],
        [pl.BlockSpec((rows // (2 * span), tile), lambda n: (0, n))] * span
        + [pl.BlockSpec((rows // (2 * near), tile), lambda n: (0, n))] * near
        + [ANY],
        [((rows // (2 * span), width), jnp.bfloat16)] * span
        + [((rows // (2 * near), width), jnp.bfloat16)] * near
        + [(shape, jnp.bfloat16)],
        [*pieces, gates[0], ups[0], gates[1], ups[1], spread, side, back],
        16 * rows * experts * part * width,
        [
            pltpu.VMEM((rows, width), jnp.bfloat16),
            pltpu.VMEM((experts, width, 4 * part), jnp.bfloat16),
            slots,
            slots,
            slots,
            slots,
            pltpu.SemaphoreType.DMA((experts,)),
            pltpu.SemaphoreType.DMA((count,)),
            pltpu.SemaphoreType.DMA,
            pltpu.SemaphoreType.DMA,
        ],
    )


def down_kernel(count, span, *refs):
    hiddens, (down_own, down_other), outs = refs[:count], refs[count : count + 2], refs[count + 2 :]
    places, _, part = hiddens[0].shape
    near = len(outs) // count
    size = outs[0].shape[0] // span
    for index, hidden in enumerate(hiddens):
        total = None
        for place in range(places):
            down = down_own if place < places // 2 else down_other
            first = place % (places // 2) * part
            term = dot(hidden[place], down[first : first + part, :])
            total = term if total is None else total + term
        for across, target, first in plane_order(near, span, size):
            outs[index * near + across][target : target + size] = low(total[first : first + size])


def down_call(hiddens, downs, near, span, size):
    places, rows, part = hiddens[0].shape
    hidden, width = downs[0].shape
    tile = min(width, 512)
    count = len(hiddens)
    down_block = pl.BlockSpec((hidden, tile), lambda n: (0, n))
    outs = kernel_call(
        functools.partial(down_kernel, count, span),
        (width // tile,),
        [whole(array) for array in hiddens] + [down_block] * 2,
        [pl.BlockSpec((span * size, tile), lambda n: (0, n))] * (count * near),
        [((span * size, width), jnp.bfloat16)] * (count * near),
        [*hiddens, *downs],
        4 * count * rows * hidden * width,
    )
    return [outs[index * near : (index + 1) * near] for index in range(count)]


def backward_kernel(width, share, count, scalars, *refs):
    pieces = refs[:count]
    (output_weight, mix_in, mix_out, select, queries, keys, values, attended, query_raw, key_raw,
     query_gain, key_gain, cosine, sine, mask) = refs[count : count + 15]
    (query_out, key_out, value_out, inner_out, mix_in_grad, mix_out_grad) = refs[
        count + 15 : count + 21
    ]
    branch, mixed_grad, grads, inner, sems = refs[count + 21 :]
    head = pl.program_id(0)
    heads = grads.shape[0]
    size = pieces[0].shape[0]
    rows = branch.shape[0]

    @pl.when(head == 0)
    def _():
        copies = []
        for index, piece in enumerate(pieces):
            place = pl.ds(pl.multiple_of(scalars[index] * size, size), size)
            copies.append(pltpu.make_async_copy(piece, branch.at[place], sems.at[index]))
        for copy in copies:
            copy.start()
        for copy in copies:
            copy.wait()
        mixed_grad[...] = low(
            wide(low(dot_t(branch[:, :width], mix_out[...]))) * select[...]
        )
        for index in range(heads):
            part = slice(index * HD, (index + 1) * HD)
            grads[index] = low(
                dot_t(branch[:, :width], output_weight[part, :])
                + dot_t(mixed_grad[...], mix_in[part, :])
            )
        columns = pl.ds(pl.multiple_of(scalars[count] * share, share), share)
        whole_grad = t_dot(branch[:, width:], branch[:, columns])
        mix_out_grad[...] = sliced(whole_grad)
        inner[...] = jnp.zeros_like(inner)

    scale = HD ** (-0.5)
    query, key, value = queries[...], keys[...], values[...]
    grad = grads[head]
    scores = dot_t(query, key) * scale + mask[...]
    raised = jnp.exp(scores - jnp.max(scores, axis=1, keepdims=True))
    weights = raised / jnp.sum(raised, axis=1, keepdims=True)
    value_out[...] = low(t_dot(low(weights), grad))
    weight_grad = dot_t(grad, value)
    center = jnp.sum(weights * weight_grad, axis=1, keepdims=True)
    score_grad = low(weights * (weight_grad - center))
    query_grad = dot(score_grad, key) * scale
    key_grad = t_dot(score_grad, query) * scale
    query_grad = (query_grad * cosine[...] - turned(query_grad) * sine[...]) * wide(query_gain[...])
    key_grad = (key_grad * cosine[...] - turned(key_grad) * sine[...]) * wide(key_gain[...])
    query_out[...] = query_grad
    key_out[...] = key_grad
    query_inner = jnp.sum(query_grad * query_raw[...], axis=1, keepdims=True)
    key_inner = jnp.sum(key_grad * key_raw[...], axis=1, keepdims=True)
    lane = lax.broadcasted_iota(jnp.int32, (rows, 128), 1)
    inner[...] += jnp.where(lane == 0, query_inner, jnp.where(lane == 1, key_inner, 0.0))
    mix_in_grad[...] = sliced(t_dot(mixed_grad[...], attended[...]))

    @pl.when(head == heads - 1)
    def _():
        inner_out[...] = jnp.transpose(inner[...])[:8]


def sliced(values):
    total = values[:RANK]
    for index in range(1, values.shape[0] // RANK):
        total = total + values[index * RANK : (index + 1) * RANK]
    return low(total)


def backward_call(
    scalars, pieces, output_weight, mix_in, mix_out, select, states, raws, gains, tables, mask, share
):
    rows, local = raws[0].shape
    heads = local // HD
    width = output_weight.shape[1]
    block = pl.BlockSpec((rows, HD), lambda head, *_: (0, head))
    gain_block = pl.BlockSpec((1, HD), lambda head, *_: (0, head))
    adapter_block = pl.BlockSpec((RANK, HD), lambda head, *_: (0, head))
    operands = [
        scalars, *pieces, output_weight, mix_in, mix_out, select, *states, *raws, *gains, *tables, mask,
    ]
    wide_out = ((rows, local), jnp.float32)
    return kernel_call(
        functools.partial(backward_kernel, width, share, len(pieces)),
        (heads,),
        [ANY] * len(pieces)
        + [whole(output_weight), whole(mix_in), whole(mix_out), whole(select)]
        + [block] * 6
        + [gain_block] * 2
        + [whole(tables[0]), whole(tables[1]), whole(mask)],
        [block] * 3
        + [
            pl.BlockSpec((8, rows), lambda *_: (0, 0)),
            adapter_block,
            pl.BlockSpec((RANK, share), lambda *_: (0, 0)),
        ],
        [wide_out, wide_out, ((rows, local), jnp.bfloat16), ((8, rows), jnp.float32)]
        + [((RANK, local), jnp.bfloat16), ((RANK, share), jnp.bfloat16)],
        operands,
        14 * rows * rows * local + 2 * rows * local * width,
        [
            pltpu.VMEM((rows, pieces[0].shape[1]), jnp.bfloat16),
            pltpu.VMEM((rows, mix_out.shape[0]), jnp.bfloat16),
            pltpu.VMEM((heads, rows, HD), jnp.bfloat16),
            pltpu.VMEM((rows, 128), jnp.float32),
            pltpu.SemaphoreType.DMA((len(pieces),)),
        ],
        1,
    )


def raw_kernel(
    width, scalars, inner, squares, query_grad, key_grad, value_grad, query_raw, key_raw, lowrank,
    adapt_out, raw, lowrank_out, adapt_grad, maps,
):
    inverse = lax.rsqrt(spread_columns(squares[...]) / width + EPSILON)
    totals = spread_columns(inner[...]) / width
    for index, (grad, value) in enumerate(((query_grad, query_raw), (key_grad, key_raw))):
        scale = inverse[:, index : index + 1]
        raw[index] = low(
            scale * grad[...]
            - value[...] * scale**3 * totals[:, index : index + 1]
        )
    raw[2] = value_grad[...]
    picked = pl.ds(pl.multiple_of(scalars[0], RANK), RANK)
    maps[...] = jnp.zeros_like(maps)
    lowrank_part = None
    for index in range(3):
        maps[index, index * RANK : (index + 1) * RANK, :] = adapt_out[index, picked, :]
        term = dot_t(raw[index], maps[index])
        lowrank_part = term if lowrank_part is None else lowrank_part + term
        adapt_grad[index * RANK : (index + 1) * RANK, :] = sliced(
            t_dot(lowrank[index], raw[index])
        )
    lowrank_out[...] = low(lowrank_part)


def raw_call(scalars, width, inner, squares, grads, raws, lowrank, adapt_out):
    rows, local = raws[0].shape
    operands = [scalars, inner, squares, *grads, *raws, lowrank, adapt_out]
    out_shape = [((3, rows, local), jnp.bfloat16), ((rows, 128), jnp.bfloat16)]
    out_shape += [((3 * RANK, local), jnp.bfloat16)]
    return kernel_call(
        functools.partial(raw_kernel, width),
        (1,),
        [whole(array) for array in operands[1:]],
        [pl.BlockSpec(shape, lambda *_, size=len(shape): (0,) * size) for shape, _ in out_shape],
        out_shape,
        operands,
        6 * rows * local * 256,
        [pltpu.VMEM((3, 128, local), jnp.bfloat16)],
        1,
    )


def weight_kernel(
    size, scalars, raw, query_weight, key_weight, value_weight, mine, theirs, weights, sems
):
    copies = []
    for index, source in enumerate((query_weight, key_weight, value_weight)):
        copies.append(pltpu.make_async_copy(source, weights.at[index], sems.at[index]))
    for copy in copies:
        copy.start()
    for copy in copies:
        copy.wait()
    levels = mine.shape[0] // size
    for out, offset in ((theirs, 1 - scalars[0]), (mine, scalars[0])):
        total = None
        for index in range(3):
            taken = [
                raw[index, pl.ds(pl.multiple_of((2 * level + offset) * size, size), size), :]
                for level in range(levels)
            ]
            term = dot_t(jnp.concatenate(taken, axis=0), weights[index])
            total = term if total is None else total + term
        out[...] = total.astype(out.dtype)


def weight_call(scalars, raw, weights, size):
    _, rows, local = raw.shape
    width = weights[0].shape[0]
    operands = [scalars, raw, *weights]
    out_shape = [((rows // 2, width), jnp.float32), ((rows // 2, width), jnp.bfloat16)]
    return kernel_call(
        functools.partial(weight_kernel, size),
        (1,),
        [whole(raw)] + [ANY] * 3,
        [pl.BlockSpec(shape, lambda *_: (0, 0)) for shape, _ in out_shape],
        out_shape,
        operands,
        6 * rows * local * width,
        [pltpu.VMEM((3, width, local), jnp.bfloat16), pltpu.SemaphoreType.DMA((3,))],
        1,
    )


def input_kernel(
    kept, came, lowrank, maps, tokens, gain, resid_grad, out
):
    grad = kept[...] + wide(came[...]) + dot_t(lowrank[...], maps[...])
    scaled = grad * wide(gain[...])
    inputs = wide(tokens[...])
    width = inputs.shape[1]
    inverse = lax.rsqrt(jnp.mean(inputs * inputs, axis=1, keepdims=True) + EPSILON)
    inner = jnp.sum(scaled * inputs, axis=1, keepdims=True)
    out[...] = low(
        resid_grad[...] + norm_back(scaled, inputs, inverse, width, inner)
    )


def input_call(kept, came, lowrank, maps, tokens, gain, resid_grad):
    operands = [kept, came, lowrank, maps, tokens, gain, resid_grad]
    rows, width = tokens.shape
    return kernel_call(
        input_kernel,
        (1,),
        [whole(array) for array in operands],
        [pl.BlockSpec((rows, width), lambda *_: (0, 0))],
        [((rows, width), jnp.bfloat16)],
        operands,
        2 * rows * width * 128,
    )[0]


def compact_kernel(
    scalars, lowrank_grad, normed, mix_out_grad, adapt_grad, mix_in_grad, select, out, held, sem
):
    share = out.shape[1]
    columns = pl.ds(pl.multiple_of(scalars[0] * share, share), share)
    copy = pltpu.make_async_copy(normed.at[:, columns], held, sem)
    copy.start()
    copy.wait()
    first = low(t_dot(lowrank_grad[...], held[...]))[: 3 * RANK]
    out[: 3 * RANK] = first
    out[3 * RANK : 4 * RANK] = mix_out_grad[...]
    out[4 * RANK : 7 * RANK] = adapt_grad[...]
    out[7 * RANK : 8 * RANK] = mix_in_grad[...]
    chosen = low(jnp.broadcast_to(select[...], (RANK, 128)))
    out[8 * RANK :] = jnp.concatenate([chosen] * (share // 128), axis=1)


def compact_call(scalars, lowrank_grad, normed, mix_out_grad, adapt_grad, mix_in_grad, select):
    rows = normed.shape[0]
    share = adapt_grad.shape[1]
    operands = [scalars, lowrank_grad, normed, mix_out_grad, adapt_grad, mix_in_grad, select]
    return kernel_call(
        compact_kernel,
        (1,),
        [whole(lowrank_grad), ANY] + [whole(array) for array in operands[3:]],
        [pl.BlockSpec((9 * RANK, share), lambda *_: (0, 0))],
        [((9 * RANK, share), jnp.bfloat16)],
        operands,
        2 * rows * share * 128,
        [pltpu.VMEM((rows, share), jnp.bfloat16), pltpu.SemaphoreType.DMA],
        1,
    )[0]


def spread_kernel(order, *refs):
    pieces, out = refs[:-1], refs[-1]
    step = pl.program_id(0)
    for index, piece in enumerate(pieces):

        @pl.when(step == index)
        def _():
            out[...] = wide(piece[...])


def spread_call(order, pieces):
    size, width = pieces[0].shape
    count = len(pieces)
    return kernel_call(
        spread_kernel,
        (count,),
        [whole(piece) for piece in pieces],
        [pl.BlockSpec((size, width), lambda step, order: (order[step], 0))],
        [((count * size, width), jnp.float32)],
        [order, *pieces],
        size * width,
        (),
        1,
    )[0]


def assemble_kernel(trees, order, *refs):
    count = len(refs) - 5
    own, pieces = refs[0], refs[1:count]
    in_grad, out_grad, mix_in_grad, mix_out_grad = refs[count : count + 4]
    (choice,) = refs[count + 4 :]
    share = own.shape[1]
    block = own.shape[0] // trees
    row = lax.broadcasted_iota(jnp.int32, (RANK, 128), 0)
    lane = lax.broadcasted_iota(jnp.int32, (RANK, 128), 1)
    same = lax.rem(lane, RANK) == row
    for tree in range(trees):
        chosen = own[tree * block + 8 * RANK : tree * block + 9 * RANK, :128]
        choice[tree * RANK : (tree + 1) * RANK] = low(jnp.where(same, wide(chosen), 0.0))

    def kind(source, stride, index):
        return jnp.concatenate(
            [
                source[tree * stride + index * RANK : tree * stride + (index + 1) * RANK, :]
                for tree in range(trees)
            ],
            axis=0,
        )

    for index in range(3):
        out_grad[index] = t_dot(choice[...], kind(own, block, 4 + index))
    mix_in_grad[...] = t_dot(kind(own, block, 7), choice[...])
    for place, source in enumerate((own, *pieces)):
        stride = block if place == 0 else 4 * RANK
        start = pl.ds(pl.multiple_of(order[place] * share, share), share)
        for index in range(3):
            in_grad[index, start, :] = t_dot(kind(source, stride, index), choice[...])
        mix_out_grad[:, start] = t_dot(choice[...], kind(source, stride, 3))


def assemble_call(order, own, pieces, trees):
    share = own.shape[1]
    count = 1 + len(pieces)
    width = count * share
    out_shape = [((3, width, 128), jnp.float32), ((3, 128, share), jnp.float32)]
    out_shape += [((share, 128), jnp.float32), ((128, width), jnp.float32)]
    operands = [order, own, *pieces]
    return kernel_call(
        functools.partial(assemble_kernel, trees),
        (1,),
        [whole(array) for array in operands[1:]],
        [pl.BlockSpec(shape, lambda *_, size=len(shape): (0,) * size) for shape, _ in out_shape],
        out_shape,
        operands,
        2 * trees * RANK * 128 * width * 4,
        [pltpu.VMEM((trees * RANK, 128), jnp.bfloat16)],
        1,
    )


def body(
    tokens,
    cotangent,
    attn_gain,
    ffn_gain,
    query_gain,
    key_gain,
    query_weight,
    key_weight,
    value_weight,
    output_weight,
    expert_gate,
    expert_up,
    expert_down,
    adapt_in,
    adapt_out,
    adapt_in_out,
    adapt_out_out,
    routes,
    gate_weights,
    block_parent,
    adapter_pick,
):
    rows_here, model_width = tokens.shape
    tensor_rank = lax.axis_index("tensor")
    tensor_count = lax.axis_size("tensor")
    owners = lax.axis_size("expert")
    owner_rank = lax.axis_index("expert")
    axes = divide_axes(owners, tensor_count)
    far, near, span = axes["z"][1], axes["x"][1], axes["y"][1]
    experts_here, _, hidden_here = expert_gate.shape
    experts_all = experts_here * owners
    column_share = model_width // tensor_count
    row_share = rows_here // tensor_count
    hold = lax.optimization_barrier
    level, core = tensor_rank // 2, tensor_rank % 2

    def own_rows(array):
        return lax.dynamic_slice_in_dim(array, tensor_rank * row_share, row_share, 0)

    routes_wide = jnp.swapaxes(routes, 0, 1)
    weights_wide = jnp.swapaxes(gate_weights, 0, 1)
    route_weights = jnp.sum(
        jnp.where(
            routes_wide[:, :, None] == jnp.arange(experts_all, dtype=jnp.int32)[None, None, :],
            weights_wide[:, :, None],
            0.0,
        ),
        axis=0,
    )
    weights_high = low(route_weights)
    weights_low = low(route_weights - wide(weights_high))
    side_width = -(-2 * experts_all // 128) * 128
    side_pad = jnp.zeros((rows_here, side_width - 2 * experts_all), jnp.bfloat16)
    side_rows = jnp.concatenate([weights_high, weights_low, side_pad], axis=1)
    cot_queue = []
    for step in range(span):
        place = ((level + span - step) % span * 2 + core) * row_share
        cot_queue.append(
            jnp.concatenate(
                [
                    lax.dynamic_slice_in_dim(cotangent, place, row_share, 0),
                    lax.dynamic_slice_in_dim(side_rows, place, row_share, 0),
                ],
                axis=1,
            )
        )
    cot_queue = [jnp.concatenate(cot_queue, axis=0)]
    side_index = jnp.arange(side_width, dtype=jnp.int32)
    hidden_owner = (
        owner_rank * experts_here
        + jnp.arange(experts_here * hidden_here, dtype=jnp.int32) // hidden_here
    )
    spread_flat = low(
        (side_index[:, None] % experts_all == hidden_owner[None, :])
        & (side_index[:, None] < 2 * experts_all)
    )
    spread = jnp.swapaxes(spread_flat.reshape(side_width, experts_here, hidden_here), 0, 1)

    cot_planes = [None] * far
    cot_queue.append(turn(cot_queue[0], axes, "z", 1))
    cot_planes[0] = ring(cot_queue[0], axes, "x")
    first_gain, second_gain = attn_gain[None, :], ffn_gain[None, :]
    gains = (query_gain[None, :], key_gain[None, :])
    reached = ancestry(block_parent)
    cosine_table, sine_table = rope_tables(reached, rows_here // block_parent.shape[0], HD)
    signs = jnp.where(jnp.arange(HD) < HD // 2, -1.0, 1.0)[None, :]
    tables = (cosine_table, sine_table * signs)
    mask = jnp.where(token_mask(reached[0], rows_here), 0.0, MASKED_SCORE)
    select = jnp.repeat(wide(adapter_pick), RANK, axis=1)
    picked = jnp.argmax(adapter_pick[0]).astype(jnp.int32) * RANK
    weights = (query_weight, key_weight, value_weight)
    normed_in, lowrank, *raws, squares = project_call(
        tokens, first_gain, weights, adapt_in, adapt_out, select
    )

    def halves(rows):
        return [rows[: rows.shape[0] // 2], rows[rows.shape[0] // 2 :]]

    squares = sum_tensor(squares, axes)
    tokens_rows = own_rows(tokens)
    held = (squares, cot_queue[1], cot_planes[0], expert_gate, expert_up, tables, mask, tokens_rows)
    held = hold(held)
    squares, cot_queue[1], cot_planes[0], expert_gate, expert_up, tables, mask, tokens_rows = held
    gates = (expert_gate, turn(expert_gate, axes, "c", 1))
    ups = (expert_up, turn(expert_up, axes, "c", 1))
    cot_queue[1] = halves(cot_queue[1])
    cot_later = turn(cot_queue[1][0], axes, "z", 1)
    cot_across = ring(cot_queue[1][0], axes, "x")[1:]
    *states, mine, theirs = attend_call(
        jnp.reshape(core, (1,)).astype(jnp.int32),
        squares,
        raws,
        gains,
        tables,
        mask,
        output_weight,
        adapt_in_out,
        row_share,
    )
    cot_later, cot_across, mine, theirs = hold((cot_later, cot_across, mine, theirs))

    theirs = turn(theirs, axes, "c", 1)
    branch_kept, branch_sent = scatter_core(mine, theirs, axes)
    branch_sent, cot_queue[1] = hold((branch_sent, cot_queue[1]))
    down_tall = expert_down.reshape(-1, model_width)
    branch_came = turn(branch_sent, axes, "y", -1)
    cot_later = [cot_later, turn(cot_queue[1][1], axes, "z", 1)]
    cot_second = ring(cot_queue[1][1], axes, "x")[1:]
    held = (branch_came, cot_later, cot_second, gates, ups, down_tall)
    branch_came, cot_later, cot_second, gates, ups, down_tall = hold(held)
    downs = (down_tall, turn(down_tall, axes, "c", 1))
    cot_queue.append(cot_later)
    cot_planes[1] = [cot_queue[1]] + [list(pair) for pair in zip(cot_across, cot_second)]
    cot_planes[0] = [[piece] for piece in cot_planes[0]]
    resid_rows, norm_plane, mixed_rows = resid_call(
        branch_kept, branch_came, tokens_rows, adapt_out_out, select, second_gain
    )

    norm_queue = [norm_plane, turn(norm_plane, axes, "z", 1)]
    norm_pairs = [ring(norm_plane, axes, "x")]
    backs, sides = [None] * far, [None] * far
    maps = jnp.swapaxes(lax.dynamic_slice_in_dim(adapt_in, picked, RANK, 2), 0, 1)
    maps = maps.reshape(model_width, 3 * RANK)
    maps = jnp.concatenate(
        [maps, jnp.zeros((model_width, 128 - 3 * RANK), jnp.bfloat16)], axis=1
    )

    def hidden_step(*indices):
        back, side = hidden_call(
            [cot_planes[index] for index in indices], downs, spread_flat, experts_here, row_share
        )
        for order, index in enumerate(indices):
            backs[index], sides[index] = (back, order * side.shape[0] // len(indices)), side
        return back

    def set_back(back, *indices):
        for index in indices:
            backs[index] = (back, backs[index][1])

    norm_planes = [None] * far
    held = (norm_queue[1], norm_pairs[0], maps, downs)
    norm_queue[1], norm_pairs[0], maps, downs = hold(held)
    norm_planes[0] = ring(jnp.concatenate(norm_pairs[0], axis=0), axes, "y")
    norm_queue.append(turn(norm_queue[1], axes, "z", 1))
    norm_pairs.append(ring(norm_queue[1], axes, "x"))
    cot_third = [turn(cot_queue[2][0], axes, "z", 1)]
    cot_across = ring(cot_queue[2][0], axes, "x")[1:]
    back_first = hidden_step(0, 1)
    held = (norm_planes[0], norm_queue[2], norm_pairs[1], cot_third, cot_across, cot_queue[2])
    held, back_first = hold((held, back_first))
    norm_planes[0], norm_queue[2], norm_pairs[1], cot_third, cot_across, cot_queue[2] = held
    set_back(back_first, 0, 1)
    parts, hiddens = [None] * far, [None] * far

    def expert_step(index):
        back, offset = backs[index]
        *parts[index], hiddens[index] = expert_call(
            norm_planes[index], gates, ups, spread, sides[index], back, offset, near, span
        )

    norm_planes[1] = ring(jnp.concatenate(norm_pairs[1], axis=0), axes, "y")
    norm_queue.append(turn(norm_queue[2], axes, "z", 1))
    norm_pairs.append(ring(norm_queue[2], axes, "x"))
    cot_third.append(turn(cot_queue[2][1], axes, "z", 1))
    cot_second = ring(cot_queue[2][1], axes, "x")[1:]
    expert_step(0)

    held = (norm_planes[1], norm_queue[3], norm_pairs[2], cot_third, cot_second, parts[0])
    norm_planes[1], norm_queue[3], norm_pairs[2], cot_third, cot_second, parts[0] = hold(held)
    cot_planes[2] = [cot_queue[2]] + [list(pair) for pair in zip(cot_across, cot_second)]
    cot_queue.append(cot_third)
    norm_planes[2] = ring(jnp.concatenate(norm_pairs[2], axis=0), axes, "y")
    norm_pairs.append(ring(norm_queue[3], axes, "x"))
    cot_across = [ring(rows, axes, "x")[1:] for rows in cot_queue[3]]
    expert_step(1)

    norm_planes[2], norm_pairs[3], parts[1] = hold((norm_planes[2], norm_pairs[3], parts[1]))
    norm_planes[3] = ring(jnp.concatenate(norm_pairs[3], axis=0), axes, "y")
    came = [None] * far
    kept = [None] * far
    came[1] = scatter_first(parts[1], axes)
    back_next = hidden_step(2)
    cot_across, back_next, norm_planes[2] = hold((cot_across, back_next, norm_planes[2]))
    set_back(back_next, 2)
    came[0] = scatter_first(parts[0], axes)
    cot_planes[3] = [cot_queue[3]] + [list(pair) for pair in zip(*cot_across)]
    expert_step(2)
    mixes, mix_came = [None] * far, [None] * far

    def down_step(first, second):
        mixes[first], mixes[second] = down_call(
            [hiddens[first], hiddens[second]], downs, near, span, row_share
        )

    held = (norm_planes[3], came[1], came[0], parts[2], hiddens[1], hiddens[2])
    norm_planes[3], came[1], came[0], parts[2], hiddens[1], hiddens[2] = hold(held)
    kept[1], came[1] = scatter_second(parts[1], came[1], axes)
    came[2] = scatter_first(parts[2], axes)
    down_step(1, 2)
    held = (kept[1], came[1], came[2], mixes[1], mixes[2], cot_planes[3])
    kept[1], came[1], came[2], mixes[1], mixes[2], cot_planes[3] = hold(held)
    kept[2], came[2] = scatter_second(parts[2], came[2], axes)
    ring_sum = turn(low(scatter_last(kept[1], came[1])), axes, "z", 1)
    mix_came[1] = send_sum(mixes[1], axes, "x")
    back_last = hidden_step(3)
    kept[2], came[2], back_last, norm_planes[3] = hold(
        (kept[2], came[2], back_last, norm_planes[3])
    )
    set_back(back_last, 3)
    kept[0], came[0] = scatter_second(parts[0], came[0], axes)
    expert_step(3)

    held = (ring_sum, kept[0], came[0], parts[3], hiddens[3], mix_came[1])
    ring_sum, kept[0], came[0], parts[3], hiddens[3], mix_came[1] = hold(held)
    came[3] = scatter_first(parts[3], axes)
    ring_sum = turn(low(wide(ring_sum) + scatter_last(kept[2], came[2])), axes, "z", 1)
    down_step(3, 0)

    ring_sum, came[3], mixes[3], mixes[0] = hold((ring_sum, came[3], mixes[3], mixes[0]))
    kept[3], came[3] = scatter_second(parts[3], came[3], axes)

    ring_sum, kept[3], came[3], mixes = hold((ring_sum, kept[3], came[3], mixes))
    ring_sum = turn(low(wide(ring_sum) + scatter_last(kept[3], came[3])), axes, "z", 1)
    mix_came[2] = send_sum(mixes[2], axes, "x")

    def mix_down(index):
        total = wide(mixes[index][0]) + wide(mix_came[index])
        total = jnp.split(total, span, axis=0)
        return total[0], send_sum([low(part) for part in total], axes, "y")

    mix_parts = [None] * far
    mix_parts[1] = mix_down(1)

    ring_sum, mix_parts[1] = hold((ring_sum, mix_parts[1]))
    mix_sum = turn(low(mix_parts[1][0] + wide(mix_parts[1][1])), axes, "z", 1)
    ffn_rows_grad = wide(ring_sum) + scatter_last(kept[0], came[0])
    second_scaled = ffn_rows_grad * wide(second_gain)
    second_inverse = lax.rsqrt(
        jnp.mean(resid_rows * resid_rows, axis=1, keepdims=True) + EPSILON
    )
    resid_grad_rows = wide(own_rows(cotangent)) + norm_back(
        second_scaled,
        resid_rows,
        second_inverse,
        model_width,
        jnp.sum(second_scaled * resid_rows, axis=1, keepdims=True),
    )
    branch_sent = jnp.concatenate([low(resid_grad_rows), mixed_rows], axis=1)
    branch_pieces = ring(branch_sent, axes, "y")
    branch_other = turn(branch_pieces[0], axes, "c", 1)
    order = jnp.stack(
        [
            (level + span - step) % span * 2 + side
            for side in (core, 1 - core)
            for step in range(span)
        ]
    ).astype(jnp.int32)

    branch_pieces = hold(branch_pieces)
    branch_others = [turn(piece, axes, "c", 1) for piece in branch_pieces[1:]]
    held = (branch_others, branch_other, mix_sum, mix_came[2], mixes)
    branch_others, branch_other, mix_sum, mix_came[2], mixes = hold(held)
    branch_pieces = branch_pieces + [branch_other] + branch_others
    mix_parts[2] = mix_down(2)
    mix_came[3] = send_sum(mixes[3], axes, "x")
    rank_list = jnp.reshape(tensor_rank, (1,)).astype(jnp.int32)
    query_grad, key_grad, value_grad, inner, mix_in_grad, mix_out_grad = backward_call(
        jnp.concatenate([order, rank_list]),
        branch_pieces,
        output_weight,
        adapt_in_out,
        adapt_out_out,
        select,
        states,
        raws[:2],
        gains,
        tables,
        mask,
        column_share,
    )

    inner = sum_tensor(hold(inner), axes)
    held = (inner, mix_sum, mix_parts[2], mix_came[3], mixes)
    inner, mix_sum, mix_parts[2], mix_came[3], mixes = hold(held)
    mix_came[0] = send_sum(mixes[0], axes, "x")
    mix_sum = turn(
        low(wide(mix_sum) + mix_parts[2][0] + wide(mix_parts[2][1])), axes, "z", 1
    )
    mix_parts[3] = mix_down(3)
    raw_grads, lowrank_part, adapt_grad = raw_call(
        jnp.reshape(picked, (1,)),
        model_width,
        inner,
        squares,
        (query_grad, key_grad, value_grad),
        raws[:2],
        lowrank,
        adapt_out,
    )
    lowrank_came = turn(lowrank_part, axes, "c", 1)
    normed_mine, normed_theirs = weight_call(
        jnp.reshape(core, (1,)).astype(jnp.int32), raw_grads, weights, row_share
    )

    lowrank_part, lowrank_came = hold((lowrank_part, lowrank_came))
    lowrank_part = low(wide(lowrank_part) + wide(lowrank_came))
    lowrank_parts = ring(lowrank_part, axes, "y")

    held = (normed_mine, normed_theirs, lowrank_parts, mix_sum, mix_parts[3], mix_came[0])
    normed_mine, normed_theirs, lowrank_parts, mix_sum, mix_parts[3], mix_came[0] = hold(held)
    normed_theirs = turn(normed_theirs, axes, "c", 1)
    lowrank_grad = low(sum(wide(part) for part in lowrank_parts))
    compact = compact_call(
        rank_list, lowrank_grad, normed_in, mix_out_grad, adapt_grad, mix_in_grad, select
    )
    mix_parts[0] = mix_down(0)
    normed_theirs, compact = hold((normed_theirs, compact))
    trees = ring(compact, axes, "x")
    normed_kept, normed_sent = scatter_core(normed_mine, normed_theirs, axes)
    normed_came = turn(normed_sent, axes, "y", -1)
    mix_sum = turn(
        low(wide(mix_sum) + mix_parts[3][0] + wide(mix_parts[3][1])), axes, "z", 1
    )
    trees = jnp.concatenate(hold(trees), axis=0)
    tree_queue = [trees] + [turn(trees, axes, "z", step) for step in range(1, far)]
    normed_came, mix_parts[0], mix_sum = hold((normed_came, mix_parts[0], mix_sum))

    input_rows = input_call(
        normed_kept,
        normed_came,
        own_rows(lowrank_grad),
        maps,
        tokens_rows,
        first_gain,
        resid_grad_rows,
    )
    input_held = ring(input_rows, axes, "y")
    layer_rows = low(resid_rows + wide(mix_sum) + mix_parts[0][0] + wide(mix_parts[0][1]))

    input_held, layer_rows, tree_queue = hold((input_held, layer_rows, tree_queue))
    input_pieces = input_held + [turn(piece, axes, "c", 1) for piece in input_held]
    layer_out = swap_columns(layer_rows, axes)

    trees = jnp.concatenate(tree_queue, axis=0)
    shared = trees.reshape(owners, -1, column_share)[:, : 4 * RANK]
    shared = gather_tensor(shared.reshape(-1, column_share), axes)
    input_grad = spread_call(order, input_pieces)
    grad_adapt_in, grad_adapt_out, grad_adapt_in_out, grad_adapt_out_out = assemble_call(
        order, trees, shared[1:], owners
    )
    return (
        layer_out,
        input_grad,
        grad_adapt_in,
        grad_adapt_out,
        grad_adapt_in_out,
        grad_adapt_out_out,
    )


def solution(mesh):
    return jax.shard_map(
        body,
        mesh=mesh,
        in_specs=(
            P("expert", None),
            P("expert", None),
            P(),
            P(),
            P("tensor"),
            P("tensor"),
            P(None, "tensor"),
            P(None, "tensor"),
            P(None, "tensor"),
            P("tensor", None),
            P("expert", None, "tensor"),
            P("expert", None, "tensor"),
            P("expert", "tensor", None),
            P(),
            P(None, None, "tensor"),
            P("tensor", None),
            P(),
            P("expert", None),
            P("expert", None),
            P("expert"),
            P("expert", None),
        ),
        out_specs=(
            P("expert", "tensor"),
            P("expert", None),
            P(),
            P(None, None, "tensor"),
            P("tensor", None),
            P(),
        ),
        check_vma=False,
    )
```

```python
import functools

import jax
import jax.numpy as jnp
from jax import lax
from jax.experimental import pallas as pl
from jax.experimental.pallas import tpu as pltpu
from jax.sharding import PartitionSpec as P

HD = 128
RANK = 16


EPSILON = 1e-05
ROPE_BASE = 10000.0
MASKED_SCORE = -1e30
VMEM_LIMIT = 56 * 2**20
CHUNK = 128


def ancestry(parents):
    blocks = parents.shape[0]
    places = jnp.arange(blocks, dtype=jnp.int32)
    walker = places
    reached = walker[:, None] == places[None, :]
    for _ in range(blocks - 1):
        hits = (walker[:, None] == places[None, :]).astype(jnp.int32)
        walker = jnp.sum(hits * parents[None, :], axis=1)
        reached = reached | (walker[:, None] == places[None, :])
    return reached[None]


def rope_tables(reached, block_span, head_size):
    depths = jnp.sum(reached.astype(jnp.int32), axis=2) - 1
    offsets = jnp.arange(block_span, dtype=jnp.int32)
    located = (
        (depths[:, :, None] * block_span + offsets[None, None, :]).reshape(-1).astype(jnp.float32)
    )
    halves = head_size // 2
    speeds = ROPE_BASE ** (-2.0 * jnp.arange(halves, dtype=jnp.float32) / head_size)
    angles = located[:, None] * speeds[None, :]
    angles = jnp.concatenate([angles, angles], axis=1)
    return (jnp.cos(angles), jnp.sin(angles))


def token_mask(reached, total_size):
    blocks = reached.shape[0]
    block_span = total_size // blocks
    widened = jnp.broadcast_to(
        reached[:, None, :, None], (blocks, block_span, blocks, block_span)
    ).reshape(total_size, total_size)
    positions = jnp.arange(total_size, dtype=jnp.int32)
    return widened & (positions[None, :] <= positions[:, None])


def norm_back(scaled_grad, values, inverse, model_width, inner_sum):
    return inverse * scaled_grad - values * inverse**3 * (inner_sum / model_width)


def divide_axes(owners, tensor_count):
    outer = 4
    return {
        "z": ("expert", outer, owners // outer, owners),
        "x": ("expert", owners // outer, 1, owners),
        "y": ("tensor", tensor_count // 2, 2, tensor_count),
        "c": ("tensor", 2, 1, tensor_count),
    }


def turn(array, axes, name, step):
    axis, length, stride, total = axes[name]
    pairs = []
    for index in range(total):
        place = (index // stride) % length
        moved = index + ((place + step) % length - place) * stride
        pairs.append((index, moved))
    return lax.ppermute(array, axis, pairs)


def ring(array, axes, name):
    held = [array]
    for _ in range(axes[name][1] - 1):
        held.append(turn(held[-1], axes, name, 1))
    return held


def wide(array):
    return array.astype(jnp.float32)


def low(array):
    return array.astype(jnp.bfloat16)


def send_sum(parts, axes, name):
    total = parts[-1]
    for part in parts[-2:0:-1]:
        total = low(wide(turn(total, axes, name, -1)) + wide(part))
    return turn(total, axes, name, -1)


def scatter_first(pieces, axes):
    span = axes["y"][1]
    return send_sum(pieces[:span], axes, "y"), send_sum(pieces[span:], axes, "x")


def block(array, index, count):
    size = array.shape[0] // count
    return wide(array[index * size : (index + 1) * size])


def scatter_second(pieces, came, axes):
    near, span = axes["x"][1], axes["y"][1]
    first = [low(block(pieces[0], k, near) + block(came[0], k, near)) for k in range(1, near)]
    second = [low(block(pieces[span], k, span) + block(came[1], k, span)) for k in range(1, span)]
    return send_sum([None] + first, axes, "x"), send_sum([None] + second, axes, "y")


def scatter_last(pieces, came, last, axes):
    near, span = axes["x"][1], axes["y"][1]
    first = block(pieces[0], 0, near) + block(came[0], 0, near) + wide(last[0])
    second = block(pieces[span], 0, span) + block(came[1], 0, span) + wide(last[1])
    return jnp.concatenate([first, second], axis=0)


def gather_tensor(rows, axes):
    held = ring(rows, axes, "y")
    return held + [turn(piece, axes, "c", 1) for piece in held]


def scatter_core(mine, came, axes):
    rank = lax.axis_index("tensor")
    span = axes["y"][1]
    size = mine.shape[0] // span
    total = None
    for step in range(span - 1, -1, -1):
        level = (rank // 2 + span - step) % span
        part = wide(lax.dynamic_slice_in_dim(mine, level * size, size, 0)) + wide(
            lax.dynamic_slice_in_dim(came, level * size, size, 0)
        )
        if step == 0:
            return part, total
        total = low(part if total is None else part + wide(turn(total, axes, "y", -1)))


def gather_x(rows, axes):
    return jnp.concatenate(ring(rows, axes, "x"), axis=0)


def place_columns(rows, axes):
    rank = lax.axis_index("tensor")
    span = axes["y"][1]
    size, share = rows.shape[0] // span, rows.shape[1] // 2
    level, core = rank // 2, rank % 2
    mine = lax.dynamic_slice_in_dim(rows, core * share, share, 1)
    theirs = turn(lax.dynamic_slice_in_dim(rows, (1 - core) * share, share, 1), axes, "c", 1)
    blocks = jnp.zeros((2 * span * size, share), rows.dtype)
    for step in range(span):
        place = (level + span - step) % span * 2
        for part, side in ((mine, core), (theirs, 1 - core)):
            taken = part[step * size : (step + 1) * size]
            blocks = lax.dynamic_update_slice_in_dim(blocks, taken, (place + side) * size, 0)
    return blocks


def sum_tensor(array, axes):
    total = wide(array) + wide(turn(array, axes, "c", 1))
    moving = total.astype(array.dtype)
    result = total
    for _ in range(axes["y"][1] - 1):
        moving = turn(moving, axes, "y", 1)
        result = result + wide(moving)
    return result


def dot(left, right):
    return jnp.dot(left, right, preferred_element_type=jnp.float32)


def dot_t(left, right):
    return lax.dot_general(
        left, right, (((1,), (1,)), ((), ())), preferred_element_type=jnp.float32
    )


def t_dot(left, right):
    return lax.dot_general(
        left, right, (((0,), (0,)), ((), ())), preferred_element_type=jnp.float32
    )


ANY = pl.BlockSpec(memory_space=pl.ANY)


def whole(array):
    shape = array.shape
    return pl.BlockSpec(shape, lambda *_: (0,) * len(shape))


def kernel_call(kernel, grid, in_specs, out_specs, out_shape, operands, flops, scratch=(), scalars=0):
    moved = sum(array.size * array.dtype.itemsize for array in operands)
    return pl.pallas_call(
        kernel,
        grid_spec=pltpu.PrefetchScalarGridSpec(
            num_scalar_prefetch=scalars,
            grid=grid,
            in_specs=in_specs,
            out_specs=out_specs,
            scratch_shapes=list(scratch),
        ),
        out_shape=[jax.ShapeDtypeStruct(shape, kind) for shape, kind in out_shape],
        compiler_params=pltpu.CompilerParams(vmem_limit_bytes=VMEM_LIMIT),
        cost_estimate=pl.CostEstimate(flops=flops, bytes_accessed=moved, transcendentals=0),
    )(*operands)


def normalize_rows(source, gain, target):
    step = 16

    def some(index, carry):
        rows = pl.ds(pl.multiple_of(index * step, step), step)
        values = wide(source[rows, :])
        inverse = lax.rsqrt(jnp.mean(values * values, axis=1, keepdims=True) + EPSILON)
        target[rows, :] = low(values * inverse * gain)
        return carry

    lax.fori_loop(0, source.shape[0] // step, some, 0)


def project_kernel(
    tokens, gain, query_weight, key_weight, value_weight, adapt_in, adapt_out, select,
    normed_out, lowrank_out, query_out, key_out, value_out, squares_out,
    weights, maps, sems,
):
    step = pl.program_id(0)
    rank = adapt_out.shape[1]
    copies = [
        pltpu.make_async_copy(
            adapt_in.at[index], maps.at[:, pl.ds(index * rank, rank)], sems.at[3]
        )
        for index in range(3)
    ]
    for index, source in enumerate((query_weight, key_weight, value_weight)):
        copies.append(pltpu.make_async_copy(source, weights.at[index], sems.at[index]))

    @pl.when(step == 0)
    def _():
        for copy in copies:
            copy.start()

    normalize_rows(tokens, wide(gain[...]), normed_out)

    @pl.when(step == 0)
    def _():
        for copy in copies:
            copy.wait()

    lowrank = dot(normed_out[...], maps[...])
    squares = []
    for index, out in enumerate((query_out, key_out, value_out)):
        lowrank_out[index] = low(lowrank[:, index * rank : (index + 1) * rank] * select[...])
        raw = dot(normed_out[...], weights[index]) + dot(lowrank_out[index], adapt_out[index])
        out[...] = raw
        squares.append(jnp.sum(raw * raw, axis=1, keepdims=True))
    lane = lax.broadcasted_iota(jnp.int32, (tokens.shape[0], 128), 1)
    columns = jnp.where(lane == 0, squares[0], jnp.where(lane == 1, squares[1], 0.0))
    squares_out[...] = jnp.transpose(columns)[:8]


def project_call(tokens, gain, weights, adapt_in, adapt_out, select):
    rows, width = tokens.shape
    local = weights[0].shape[1]
    rank = adapt_in.shape[2]
    tile = rows // 2
    out_shape = [((rows, width), jnp.bfloat16), ((3, rows, rank), jnp.bfloat16)]
    out_shape += [((rows, local), jnp.float32)] * 3 + [((8, rows), jnp.float32)]
    operands = [tokens, gain, *weights, adapt_in, adapt_out, select]
    row_block = pl.BlockSpec((tile, width), lambda n: (n, 0))
    local_block = pl.BlockSpec((tile, local), lambda n: (n, 0))
    return kernel_call(
        project_kernel,
        (2,),
        [row_block, whole(gain), ANY, ANY, ANY, ANY, whole(adapt_out), whole(select)],
        [row_block, pl.BlockSpec((3, tile, rank), lambda n: (0, n, 0))]
        + [local_block] * 3
        + [pl.BlockSpec((8, tile), lambda n: (0, n))],
        out_shape,
        operands,
        6 * rows * width * local,
        [
            pltpu.VMEM((3, width, local), jnp.bfloat16),
            pltpu.VMEM((width, 3 * rank), jnp.bfloat16),
            pltpu.SemaphoreType.DMA((4,)),
        ],
    )


def spread_columns(rows):
    return jnp.transpose(jnp.concatenate([rows] * (128 // rows.shape[0]), axis=0))


def turned(values):
    half = values.shape[1] // 2
    return jnp.concatenate([values[:, half:], values[:, :half]], axis=1)


def attend_kernel(
    width, size, core, squares, query_raw, key_raw, value_raw, query_gain, key_gain, cosine, sine,
    mask, output_weight, mix_in, queries, keys, values, attended, mine, theirs, held, weight, scales, sem,
):
    head = pl.program_id(0)
    last = pl.num_programs(0) - 1
    copy = pltpu.make_async_copy(output_weight, weight, sem)

    @pl.when(head == 0)
    def _():
        copy.start()
        scales[...] = lax.rsqrt(spread_columns(squares[...]) / width + EPSILON)

    inverse = scales[:, :2]
    query = query_raw[...] * inverse[:, 0:1] * wide(query_gain[...])
    key = key_raw[...] * inverse[:, 1:2] * wide(key_gain[...])
    query = low(query * cosine[...] + turned(query) * sine[...])
    key = low(key * cosine[...] + turned(key) * sine[...])
    value = low(value_raw[...])
    queries[...] = query
    keys[...] = key
    values[...] = value
    scores = dot_t(query, key) * HD ** (-0.5) + mask[...]
    raised = jnp.exp(scores - jnp.max(scores, axis=1, keepdims=True))
    weights = low(raised * (1.0 / jnp.sum(raised, axis=1, keepdims=True)))
    result = low(dot(weights, value))
    attended[...] = result
    held[head] = result

    @pl.when(head == last)
    def _():
        copy.wait()
        heads = held.shape[0]
        levels = mine.shape[0] // size
        for out, offset in ((mine, core[0]), (theirs, 1 - core[0])):
            taken = []
            for level in range(levels):
                rows = pl.ds(pl.multiple_of((2 * level + offset) * size, size), size)
                taken.append(
                    jnp.concatenate([held[index, rows, :] for index in range(heads)], axis=1)
                )
            taken = jnp.concatenate(taken, axis=0)
            out[:, :width] = dot(taken, weight[...]).astype(out.dtype)
            out[:, width:] = dot(taken, mix_in[...]).astype(out.dtype)


def attend_call(core, squares, raws, gains, tables, mask, output_weight, mix_in, size):
    rows, local = raws[0].shape
    heads = local // HD
    width = output_weight.shape[1]
    wide_width = width + mix_in.shape[1]
    block = pl.BlockSpec((rows, HD), lambda head, *_: (0, head))
    gain_block = pl.BlockSpec((1, HD), lambda head, *_: (0, head))
    fixed = pl.BlockSpec((rows // 2, wide_width), lambda *_: (0, 0))
    operands = [core, squares, *raws, *gains, *tables, mask, output_weight, mix_in]
    return kernel_call(
        functools.partial(attend_kernel, width, size),
        (heads,),
        [whole(squares)] + [block] * 3 + [gain_block] * 2
        + [whole(tables[0]), whole(tables[1]), whole(mask), ANY, whole(mix_in)],
        [block] * 4 + [fixed] * 2,
        [((rows, local), jnp.bfloat16)] * 4
        + [((rows // 2, wide_width), jnp.float32), ((rows // 2, wide_width), jnp.bfloat16)],
        operands,
        4 * rows * rows * local + 2 * rows * local * width,
        [
            pltpu.VMEM((heads, rows, HD), jnp.bfloat16),
            pltpu.VMEM(output_weight.shape, jnp.bfloat16),
            pltpu.VMEM((rows, 128), jnp.float32),
            pltpu.SemaphoreType.DMA,
        ],
        1,
    )


def resid_kernel(
    width, rank, kept, came, tokens, mix_out, select, gain, resid_out, norm_out, mixed_out
):
    mixed = low((kept[:, width:] + wide(came[:, width:])) * select[...])
    mixed_out[...] = mixed
    resid_out[...] = (
        wide(tokens[...])
        + (kept[:, :width] + wide(came[:, :width]))
        + dot(mixed, mix_out[...])
    )
    normalize_rows(resid_out, wide(gain[...]), norm_out)


def resid_call(rank, kept, came, tokens, mix_out, select, gain):
    rows, width = kept.shape[0], tokens.shape[1]
    out_shape = [((rows, width), jnp.float32), ((rows, width), jnp.bfloat16)]
    out_shape += [((rows, mix_out.shape[0]), jnp.bfloat16)]
    operands = [rank, kept, came, tokens, mix_out, select, gain]
    return kernel_call(
        functools.partial(resid_kernel, width),
        (1,),
        [whole(kept), whole(came), pl.BlockSpec((rows, width), lambda n, rank: (rank[0], 0))]
        + [whole(array) for array in operands[4:]],
        [pl.BlockSpec(shape, lambda *_: (0, 0)) for shape, _ in out_shape],
        out_shape,
        operands,
        2 * rows * width * mix_out.shape[0],
        (),
        1,
    )


def plane_order(near, span, size):
    return [
        (across, down * size, (down * near + across) * size)
        for down in range(span)
        for across in range(near)
    ]


def hidden_kernel(places, *refs):
    count = len(places)
    pieces, (down_own, down_other, spread), (out, side_out), (rows, side, row_sems, side_sems) = (
        refs[:count],
        refs[count : count + 3],
        refs[count + 3 : count + 5],
        refs[count + 5 :],
    )
    step = pl.program_id(0)
    width = rows.shape[1]

    @pl.when(step == 0)
    def _():
        copies = []
        for index, (piece, targets) in enumerate(zip(pieces, places)):
            for source, target, size in targets:
                taken = piece.at[pl.ds(source, size)]
                place = pl.ds(target, size)
                slot = len(copies) // 2
                copies.append(
                    pltpu.make_async_copy(
                        taken.at[:, pl.ds(0, width)], rows.at[place], row_sems.at[slot]
                    )
                )
                copies.append(
                    pltpu.make_async_copy(
                        taken.at[:, pl.ds(width, side.shape[1])], side.at[place], side_sems.at[slot]
                    )
                )
        for copy in copies:
            copy.start()
        for copy in copies:
            copy.wait()
        side_out[...] = side[...]

    def emit(down):
        grad = dot_t(rows[...], down[...]) * dot(side[...], spread[...])
        part = out.shape[2]
        for index in range(out.shape[0]):
            out[index] = low(grad[:, index * part : (index + 1) * part])

    half = pl.num_programs(0) // 2

    @pl.when(step < half)
    def _():
        emit(down_own)

    @pl.when(step >= half)
    def _():
        emit(down_other)


def hidden_call(planes, downs, spread, experts, size):
    hidden, width = downs[0].shape
    near = len(planes[0])
    pieces, places, rows = [], [], 0
    for plane in planes:
        for across, column in enumerate(plane):
            down = 0
            for piece in column:
                targets = []
                for source in range(0, piece.shape[0], size):
                    targets.append((source, rows + (down * near + across) * size, size))
                    down += 1
                pieces.append(piece)
                places.append(targets)
        rows += near * down * size
    blocks = rows // size
    part = hidden // experts
    side = spread.shape[0]
    pair = 2 * part
    half = experts // 2
    last = half - 1
    return kernel_call(
        functools.partial(hidden_kernel, places),
        (2 * half,),
        [ANY] * len(pieces)
        + [
            pl.BlockSpec((pair, width), lambda n: (jnp.minimum(n, last), 0)),
            pl.BlockSpec((pair, width), lambda n: (jnp.maximum(n - half, 0), 0)),
            pl.BlockSpec((side, pair), lambda n: (0, lax.rem(n, half))),
        ],
        [
            pl.BlockSpec((2, rows, part), lambda n: (n, 0, 0)),
            pl.BlockSpec((rows, side), lambda n: (0, 0)),
        ],
        [((2 * experts, rows, part), jnp.bfloat16), ((rows, side), jnp.bfloat16)],
        [*pieces, *downs, spread],
        4 * rows * hidden * width,
        [
            pltpu.VMEM((rows, width), jnp.bfloat16),
            pltpu.VMEM((rows, side), jnp.bfloat16),
            pltpu.SemaphoreType.DMA((blocks,)),
            pltpu.SemaphoreType.DMA((blocks,)),
        ],
    )


def write_rows(total, outs, near, span):
    rows = total.shape[0]
    if not near:
        for down in range(span):
            size = rows // span
            outs[down][...] = low(total[down * size : (down + 1) * size])
        return
    half = rows // (2 * near * span)
    for down in range(span):
        for across in range(near):
            first = 2 * (down * near + across) * half
            outs[down][across * half : (across + 1) * half] = low(total[first : first + half])
            outs[span + across][down * half : (down + 1) * half] = low(
                total[first + half : first + 2 * half]
            )


def expert_kernel(count, near, span, offset, *refs):
    pieces = refs[:count]
    gate_own, up_own, gate_other, up_other, spread, side, back = refs[count : count + 7]
    outs, hidden_out = refs[count + 7 : count + 7 + near + span], refs[count + 7 + near + span]
    rows, weights, gate_grad, up_grad, hidden, grads, sems, row_sem, back_sem, out_sem = refs[
        count + 8 + near + span :
    ]
    step = pl.program_id(0)
    size = pieces[0].shape[0]
    experts, _, part = gate_own.shape
    total_rows = rows.shape[0]
    sources = (gate_own, up_own, gate_other, up_other)

    def load(expert):
        slot = weights.at[expert]
        return [
            pltpu.make_async_copy(
                source.at[expert], slot.at[:, pl.ds(index * part, part)], sems.at[expert]
            )
            for index, source in enumerate(sources)
        ]

    row_copies = [
        pltpu.make_async_copy(piece, rows.at[pl.ds(index * size, size)], row_sem.at[index])
        for index, piece in enumerate(pieces)
    ]
    back_copy = pltpu.make_async_copy(
        back.at[:, pl.ds(offset, total_rows), :], grads, back_sem
    )
    out_copy = pltpu.make_async_copy(hidden, hidden_out, out_sem)

    @pl.when(step == 0)
    def _():
        for copy in row_copies + load(0) + [back_copy] + load(1):
            copy.start()
        for copy in row_copies:
            copy.wait()
        back_copy.wait()

        def work(expert, carry):
            for ahead in range(2, experts):

                @pl.when(expert == ahead - 2)
                def _():
                    for copy in load(ahead):
                        copy.start()

            for copy in load(expert):
                copy.wait()
            values = dot(rows[...], weights[expert])
            weight = dot(side[...], spread[expert])
            for half in range(2):
                gate_value = values[:, 2 * half * part : (2 * half + 1) * part]
                up_value = values[:, (2 * half + 1) * part : (2 * half + 2) * part]
                sigmoid = jax.nn.sigmoid(gate_value)
                silu = gate_value * sigmoid
                place = half * experts + expert
                grad = wide(grads[place])
                gate_grad[place] = low(grad * up_value * (sigmoid + silu * (1.0 - sigmoid)))
                up_grad[place] = low(grad * silu)
                hidden[place] = low(silu * up_value * weight)
            return carry

        lax.fori_loop(0, experts, work, 0)
        out_copy.start()

    tile = outs[0].shape[1]
    columns = pl.ds(pl.multiple_of(step * tile, tile), tile)
    total = None
    for expert in range(experts):
        for half in range(2):
            place = half * experts + expert
            for index, grad in enumerate((gate_grad, up_grad)):
                first = (2 * half + index) * part
                term = dot_t(grad[place], weights[expert, columns, first : first + part])
                total = term if total is None else total + term
    write_rows(total, outs, near, span)

    @pl.when(step == pl.num_programs(0) - 1)
    def _():
        out_copy.wait()


def block_sizes(rows, near, span):
    if not near:
        return [rows // span] * span
    return [rows // (2 * span)] * span + [rows // (2 * near)] * near


def expert_call(pieces, gates, ups, spread, side, back, offset, near, span):
    count = len(pieces)
    experts, width, part = gates[0].shape
    size = pieces[0].shape[0]
    rows = size * count
    tile = min(width, 512)
    shape = (2 * experts, rows, part)
    slots = pltpu.VMEM(shape, jnp.bfloat16)
    sizes = block_sizes(rows, near, span)
    side_block = pl.BlockSpec((rows, side.shape[1]), lambda n: (offset // rows, 0))
    return kernel_call(
        functools.partial(expert_kernel, count, near, span, offset),
        (width // tile,),
        [ANY] * (count + 4) + [whole(spread), side_block, ANY],
        [pl.BlockSpec((size, tile), lambda n: (0, n)) for size in sizes] + [ANY],
        [((size, width), jnp.bfloat16) for size in sizes] + [(shape, jnp.bfloat16)],
        [*pieces, gates[0], ups[0], gates[1], ups[1], spread, side, back],
        16 * rows * experts * part * width,
        [
            pltpu.VMEM((rows, width), jnp.bfloat16),
            pltpu.VMEM((experts, width, 4 * part), jnp.bfloat16),
            slots,
            slots,
            slots,
            slots,
            pltpu.SemaphoreType.DMA((experts,)),
            pltpu.SemaphoreType.DMA((count,)),
            pltpu.SemaphoreType.DMA,
            pltpu.SemaphoreType.DMA,
        ],
    )


def whole_kernel(count, near, span, places, *refs):
    pieces = refs[:count]
    gate_own, up_own, gate_other, up_other, spread, down_own, down_other = refs[count : count + 7]
    refs = refs[count + 7 :]
    cot_pieces, refs = refs[: len(places)], refs[len(places) :]
    outs, hidden_out = refs[: near + span], refs[near + span]
    rows, weights, gate_grad, up_grad, hidden, grads, sems, row_sem, out_sem = refs[
        near + span + 1 : near + span + 10
    ]
    cot_rows, side, downs, cot_sems, side_sems, down_sems = refs[near + span + 10 :]
    step = pl.program_id(0)
    size = pieces[0].shape[0]
    experts, _, part = gate_own.shape
    total_rows = rows.shape[0]
    sources = (gate_own, up_own, gate_other, up_other)

    def load(expert):
        slot = weights.at[expert]
        return [
            pltpu.make_async_copy(
                source.at[expert], slot.at[:, pl.ds(index * part, part)], sems.at[expert]
            )
            for index, source in enumerate(sources)
        ]

    row_copies = [
        pltpu.make_async_copy(piece, rows.at[pl.ds(index * size, size)], row_sem.at[index])
        for index, piece in enumerate(pieces)
    ]
    pairs = experts // 2

    def load_down(chunk):
        source = (down_own, down_other)[chunk // pairs]
        taken = source.at[pl.ds(chunk % pairs * 2 * part, 2 * part)]
        return pltpu.make_async_copy(taken, downs.at[chunk], down_sems.at[chunk])

    out_copy = pltpu.make_async_copy(hidden, hidden_out, out_sem)

    @pl.when(step == 0)
    def _():
        copies = copy_places(cot_pieces, places, cot_rows, side, cot_sems, side_sems)
        for copy in copies + [load_down(0), load_down(1)] + row_copies:
            copy.start()
        for copy in copies:
            copy.wait()

        def back(chunk, carry):
            for ahead in range(2 * pairs):

                @pl.when(chunk == ahead)
                def _():
                    if ahead + 2 < 2 * pairs:
                        load_down(ahead + 2).start()
                    elif ahead + 2 - 2 * pairs < 2:
                        for copy in load(ahead + 2 - 2 * pairs):
                            copy.start()
                    load_down(ahead).wait()

            grad = dot_t(cot_rows[...], downs[chunk])
            place = chunk // pairs * experts + lax.rem(chunk, pairs) * 2
            for index in range(2):
                weight = dot(side[...], spread[lax.rem(chunk, pairs) * 2 + index])
                grads[place + index] = low(grad[:, index * part : (index + 1) * part] * weight)
            return carry

        lax.fori_loop(0, 2 * pairs, back, 0)
        for copy in row_copies:
            copy.wait()

        def work(expert, carry):
            for ahead in range(2, experts):

                @pl.when(expert == ahead - 2)
                def _():
                    for copy in load(ahead):
                        copy.start()

            for copy in load(expert):
                copy.wait()
            values = dot(rows[...], weights[expert])
            weight = dot(side[...], spread[expert])
            for half in range(2):
                gate_value = values[:, 2 * half * part : (2 * half + 1) * part]
                up_value = values[:, (2 * half + 1) * part : (2 * half + 2) * part]
                sigmoid = jax.nn.sigmoid(gate_value)
                silu = gate_value * sigmoid
                place = half * experts + expert
                grad = wide(grads[place])
                gate_grad[place] = low(grad * up_value * (sigmoid + silu * (1.0 - sigmoid)))
                up_grad[place] = low(grad * silu)
                hidden[place] = low(silu * up_value * weight)
            return carry

        lax.fori_loop(0, experts, work, 0)
        out_copy.start()

    tile = outs[0].shape[1]
    columns = pl.ds(pl.multiple_of(step * tile, tile), tile)
    total = None
    for expert in range(experts):
        for half in range(2):
            place = half * experts + expert
            for index, grad in enumerate((gate_grad, up_grad)):
                first = (2 * half + index) * part
                term = dot_t(grad[place], weights[expert, columns, first : first + part])
                total = term if total is None else total + term
    write_rows(total, outs, near, span)

    @pl.when(step == pl.num_programs(0) - 1)
    def _():
        out_copy.wait()


def copy_places(pieces, places, rows, side, row_sems, side_sems):
    width, copies = rows.shape[1], []
    for piece, targets in zip(pieces, places):
        for source, target, size in targets:
            taken, place = piece.at[pl.ds(source, size)], pl.ds(target, size)
            slot = len(copies) // 2
            copies.append(
                pltpu.make_async_copy(
                    taken.at[:, pl.ds(0, width)], rows.at[place], row_sems.at[slot]
                )
            )
            copies.append(
                pltpu.make_async_copy(
                    taken.at[:, pl.ds(width, side.shape[1])], side.at[place], side_sems.at[slot]
                )
            )
    return copies


def whole_call(pieces, cot_plane, gates, ups, downs, spread, near, span, block_rows):
    count = len(pieces)
    experts, width, part = gates[0].shape
    size = pieces[0].shape[0]
    rows = size * count
    tile = min(width, 512)
    shape = (2 * experts, rows, part)
    slots = pltpu.VMEM(shape, jnp.bfloat16)
    places = [
        [
            (down * block_rows, (down * near + across) * block_rows, block_rows)
            for down in range(piece.shape[0] // block_rows)
        ]
        for across, piece in enumerate(cot_plane)
    ]
    blocks = rows // block_rows
    sizes = block_sizes(rows, near, span)
    return kernel_call(
        functools.partial(whole_kernel, count, near, span, places),
        (width // tile,),
        [ANY] * (count + 4) + [whole(spread)] + [ANY] * (2 + len(cot_plane)),
        [pl.BlockSpec((size, tile), lambda n: (0, n)) for size in sizes] + [ANY],
        [((size, width), jnp.bfloat16) for size in sizes] + [(shape, jnp.bfloat16)],
        [*pieces, gates[0], ups[0], gates[1], ups[1], spread, *downs, *cot_plane],
        20 * rows * experts * part * width,
        [
            pltpu.VMEM((rows, width), jnp.bfloat16),
            pltpu.VMEM((experts, width, 4 * part), jnp.bfloat16),
            slots,
            slots,
            slots,
            slots,
            pltpu.SemaphoreType.DMA((experts,)),
            pltpu.SemaphoreType.DMA((count,)),
            pltpu.SemaphoreType.DMA,
            pltpu.VMEM((rows, width), jnp.bfloat16),
            pltpu.VMEM((rows, spread.shape[1]), jnp.bfloat16),
            pltpu.VMEM((experts // 2 * 2, 2 * part, width), jnp.bfloat16),
            pltpu.SemaphoreType.DMA((blocks,)),
            pltpu.SemaphoreType.DMA((blocks,)),
            pltpu.SemaphoreType.DMA((experts // 2 * 2,)),
        ],
    )


def down_kernel(count, span, *refs):
    hiddens, (down_own, down_other), outs = refs[:count], refs[count : count + 2], refs[count + 2 :]
    places, _, part = hiddens[0].shape
    near = len(outs) // (count * span)
    size = outs[0].shape[0]
    for index, hidden in enumerate(hiddens):
        total = None
        for place in range(places):
            down = down_own if place < places // 2 else down_other
            first = place % (places // 2) * part
            term = dot(hidden[place], down[first : first + part, :])
            total = term if total is None else total + term
        for across, target, first in plane_order(near, span, size):
            block = (index * near + across) * span + target // size
            outs[block][...] = low(total[first : first + size])


def down_call(hiddens, downs, near, span, size):
    places, rows, part = hiddens[0].shape
    hidden, width = downs[0].shape
    tile = min(width, 512)
    count = len(hiddens)
    down_block = pl.BlockSpec((hidden, tile), lambda n: (0, n))
    outs = kernel_call(
        functools.partial(down_kernel, count, span),
        (width // tile,),
        [whole(array) for array in hiddens] + [down_block] * 2,
        [pl.BlockSpec((size, tile), lambda n: (0, n))] * (count * near * span),
        [((size, width), jnp.bfloat16)] * (count * near * span),
        [*hiddens, *downs],
        4 * count * rows * hidden * width,
    )
    blocks = [outs[index * span : (index + 1) * span] for index in range(count * near)]
    return [blocks[index * near : (index + 1) * near] for index in range(count)]


def backward_kernel(width, share, count, scalars, *refs):
    pieces = refs[:count]
    (output_weight, mix_in, mix_out, select, queries, keys, values, attended, query_raw, key_raw,
     query_gain, key_gain, cosine, sine, mask) = refs[count : count + 15]
    (query_out, key_out, value_out, inner_out, mix_in_grad, mix_out_grad) = refs[
        count + 15 : count + 21
    ]
    branch, mixed_grad, grads, inner, query_total, key_total, value_total, sems = refs[count + 21 :]
    head = pl.program_id(0)
    heads = grads.shape[0]
    size = pieces[0].shape[0]
    rows = branch.shape[0]

    @pl.when(head == 0)
    def _():
        copies = []
        for index, piece in enumerate(pieces):
            place = pl.ds(pl.multiple_of(scalars[index] * size, size), size)
            copies.append(pltpu.make_async_copy(piece, branch.at[place], sems.at[index]))
        for copy in copies:
            copy.start()
        for copy in copies:
            copy.wait()
        mixed_grad[...] = low(
            wide(low(dot_t(branch[:, :width], mix_out[...]))) * select[...]
        )
        together = dot_t(branch[:, :width], output_weight[...])
        together = low(together + dot_t(mixed_grad[...], mix_in[...]))
        for index in range(heads):
            grads[index] = together[:, index * HD : (index + 1) * HD]
        columns = pl.ds(pl.multiple_of(scalars[count] * share, share), share)
        whole_grad = t_dot(branch[:, width:], branch[:, columns])
        mix_out_grad[...] = sliced(whole_grad)
        inner[...] = jnp.zeros_like(inner)

    scale = HD ** (-0.5)
    query, key, value = queries[...], keys[...], values[...]
    grad = grads[head]
    key_total[...] = jnp.zeros_like(key_total)
    value_total[...] = jnp.zeros_like(value_total)
    for first in range(0, rows, CHUNK):
        last = first + CHUNK
        scores = dot_t(query[first:last], key[:last]) * scale + mask[first:last, :last]
        raised = jnp.exp(scores - jnp.max(scores, axis=1, keepdims=True))
        weights = raised * (1.0 / jnp.sum(raised, axis=1, keepdims=True))
        value_total[:last, :] += t_dot(low(weights), grad[first:last])
        weight_grad = dot_t(grad[first:last], value[:last])
        center = jnp.sum(weights * weight_grad, axis=1, keepdims=True)
        score_grad = low(weights * (weight_grad - center))
        query_total[first:last, :] = dot(score_grad, key[:last]) * scale
        key_total[:last, :] += t_dot(score_grad, query[first:last])
    value_out[...] = low(value_total[...])
    query_grad = query_total[...]
    key_grad = key_total[...] * scale
    query_grad = (query_grad * cosine[...] - turned(query_grad) * sine[...]) * wide(query_gain[...])
    key_grad = (key_grad * cosine[...] - turned(key_grad) * sine[...]) * wide(key_gain[...])
    query_out[...] = query_grad
    key_out[...] = key_grad
    query_inner = jnp.sum(query_grad * query_raw[...], axis=1, keepdims=True)
    key_inner = jnp.sum(key_grad * key_raw[...], axis=1, keepdims=True)
    lane = lax.broadcasted_iota(jnp.int32, (rows, 128), 1)
    inner[...] += jnp.where(lane == 0, query_inner, jnp.where(lane == 1, key_inner, 0.0))
    mix_in_grad[...] = sliced(t_dot(mixed_grad[...], attended[...]))

    @pl.when(head == heads - 1)
    def _():
        inner_out[...] = jnp.transpose(inner[...])[:8]


def sliced(values):
    total = values[:RANK]
    for index in range(1, values.shape[0] // RANK):
        total = total + values[index * RANK : (index + 1) * RANK]
    return low(total)


def backward_call(
    scalars, pieces, output_weight, mix_in, mix_out, select, states, raws, gains, tables, mask, share
):
    rows, local = raws[0].shape
    heads = local // HD
    width = output_weight.shape[1]
    block = pl.BlockSpec((rows, HD), lambda head, *_: (0, head))
    gain_block = pl.BlockSpec((1, HD), lambda head, *_: (0, head))
    adapter_block = pl.BlockSpec((RANK, HD), lambda head, *_: (0, head))
    operands = [
        scalars, *pieces, output_weight, mix_in, mix_out, select, *states, *raws, *gains, *tables, mask,
    ]
    wide_out = ((rows, local), jnp.float32)
    return kernel_call(
        functools.partial(backward_kernel, width, share, len(pieces)),
        (heads,),
        [ANY] * len(pieces)
        + [whole(output_weight), whole(mix_in), whole(mix_out), whole(select)]
        + [block] * 6
        + [gain_block] * 2
        + [whole(tables[0]), whole(tables[1]), whole(mask)],
        [block] * 3
        + [
            pl.BlockSpec((8, rows), lambda *_: (0, 0)),
            adapter_block,
            pl.BlockSpec((RANK, share), lambda *_: (0, 0)),
        ],
        [wide_out, wide_out, ((rows, local), jnp.bfloat16), ((8, rows), jnp.float32)]
        + [((RANK, local), jnp.bfloat16), ((RANK, share), jnp.bfloat16)],
        operands,
        14 * rows * rows * local + 2 * rows * local * width,
        [
            pltpu.VMEM((rows, pieces[0].shape[1]), jnp.bfloat16),
            pltpu.VMEM((rows, mix_out.shape[0]), jnp.bfloat16),
            pltpu.VMEM((heads, rows, HD), jnp.bfloat16),
            pltpu.VMEM((rows, 128), jnp.float32),
            pltpu.VMEM((rows, HD), jnp.float32),
            pltpu.VMEM((rows, HD), jnp.float32),
            pltpu.VMEM((rows, HD), jnp.float32),
            pltpu.SemaphoreType.DMA((len(pieces),)),
        ],
        1,
    )


def adapter_lanes(index, select):
    row = lax.broadcasted_iota(jnp.int32, (128, 128), 0) - index * RANK
    lane = lax.broadcasted_iota(jnp.int32, (128, 128), 1)
    return low(jnp.where(lax.rem(lane, RANK) == row, select, 0.0))


def raw_kernel(
    width, inner, squares, query_grad, key_grad, value_grad, query_raw, key_raw, lowrank,
    adapt_out, select, raw, lowrank_out, adapt_grad,
):
    inverse = lax.rsqrt(spread_columns(squares[...]) / width + EPSILON)
    totals = spread_columns(inner[...]) / width
    for index, (grad, value) in enumerate(((query_grad, query_raw), (key_grad, key_raw))):
        scale = inverse[:, index : index + 1]
        factor = scale**3 * totals[:, index : index + 1]
        raw[index] = low(scale * grad[...] - value[...] * factor)
    raw[2] = value_grad[...]
    lowrank_part = None
    for index in range(3):
        part = low(dot_t(raw[index], adapt_out[index]) * select[...])
        term = dot_t(part, adapter_lanes(index, select[...]))
        lowrank_part = term if lowrank_part is None else lowrank_part + term
        adapt_grad[index * RANK : (index + 1) * RANK, :] = sliced(
            t_dot(lowrank[index], raw[index])
        )
    lowrank_out[...] = low(lowrank_part)


def raw_call(inner, squares, grads, raws, lowrank, adapt_out, select, width):
    rows, local = raws[0].shape
    operands = [inner, squares, *grads, *raws, lowrank, adapt_out, select]
    out_shape = [((3, rows, local), jnp.bfloat16), ((rows, 128), jnp.bfloat16)]
    out_shape += [((3 * RANK, local), jnp.bfloat16)]
    return kernel_call(
        functools.partial(raw_kernel, width),
        (1,),
        [whole(array) for array in operands],
        [pl.BlockSpec(shape, lambda *_, size=len(shape): (0,) * size) for shape, _ in out_shape],
        out_shape,
        operands,
        6 * rows * local * 256,
    )


def weight_kernel(
    size, scalars, raw, query_weight, key_weight, value_weight, mine, theirs, weights, sems
):
    copies = []
    for index, source in enumerate((query_weight, key_weight, value_weight)):
        copies.append(pltpu.make_async_copy(source, weights.at[index], sems.at[index]))
    for copy in copies:
        copy.start()
    for copy in copies:
        copy.wait()
    levels = mine.shape[0] // size
    for out, offset in ((theirs, 1 - scalars[0]), (mine, scalars[0])):
        total = None
        for index in range(3):
            taken = [
                raw[index, pl.ds(pl.multiple_of((2 * level + offset) * size, size), size), :]
                for level in range(levels)
            ]
            term = dot_t(jnp.concatenate(taken, axis=0), weights[index])
            total = term if total is None else total + term
        out[...] = total.astype(out.dtype)


def weight_call(scalars, raw, weights, size):
    _, rows, local = raw.shape
    width = weights[0].shape[0]
    operands = [scalars, raw, *weights]
    out_shape = [((rows // 2, width), jnp.float32), ((rows // 2, width), jnp.bfloat16)]
    return kernel_call(
        functools.partial(weight_kernel, size),
        (1,),
        [whole(raw)] + [ANY] * 3,
        [pl.BlockSpec(shape, lambda *_: (0, 0)) for shape, _ in out_shape],
        out_shape,
        operands,
        6 * rows * local * width,
        [pltpu.VMEM((3, width, local), jnp.bfloat16), pltpu.SemaphoreType.DMA((3,))],
        1,
    )


def input_kernel(
    rank, kept, came, lowrank, adapt_in, select, tokens, gain, resid_grad, out
):
    grad = kept[...] + wide(came[...])
    for index in range(3):
        part = low(dot(lowrank[...], adapter_lanes(index, select[...])))
        grad = grad + dot_t(part, adapt_in[index])
    scaled = grad * wide(gain[...])
    inputs = wide(tokens[...])
    width = inputs.shape[1]
    inverse = lax.rsqrt(jnp.mean(inputs * inputs, axis=1, keepdims=True) + EPSILON)
    inner = jnp.sum(scaled * inputs, axis=1, keepdims=True)
    out[...] = low(
        resid_grad[...] + norm_back(scaled, inputs, inverse, width, inner)
    )


def input_call(rank, kept, came, lowrank, adapt_in, select, tokens, gain, resid_grad):
    operands = [rank, kept, came, lowrank, adapt_in, select, tokens, gain, resid_grad]
    rows, width = kept.shape
    return kernel_call(
        input_kernel,
        (1,),
        [
            whole(kept),
            whole(came),
            pl.BlockSpec((rows, lowrank.shape[1]), lambda n, rank: (rank[0], 0)),
            whole(adapt_in),
            whole(select),
            pl.BlockSpec((rows, width), lambda n, rank: (rank[0], 0)),
            whole(gain),
            whole(resid_grad),
        ],
        [pl.BlockSpec((rows, width), lambda *_: (0, 0))],
        [((rows, width), jnp.bfloat16)],
        operands,
        8 * rows * width * 128,
        (),
        1,
    )[0]


def compact_kernel(
    scalars, lowrank_grad, normed, mix_out_grad, adapt_grad, mix_in_grad, select, out, held, sem
):
    share = out.shape[1]
    columns = pl.ds(pl.multiple_of(scalars[0] * share, share), share)
    copy = pltpu.make_async_copy(normed.at[:, columns], held, sem)
    copy.start()
    copy.wait()
    first = low(t_dot(lowrank_grad[...], held[...]))[: 3 * RANK]
    out[: 3 * RANK] = first
    out[3 * RANK : 4 * RANK] = mix_out_grad[...]
    out[4 * RANK : 7 * RANK] = adapt_grad[...]
    out[7 * RANK : 8 * RANK] = mix_in_grad[...]
    chosen = low(jnp.broadcast_to(select[...], (RANK, 128)))
    out[8 * RANK :] = jnp.concatenate([chosen] * (share // 128), axis=1)


def compact_call(scalars, lowrank_grad, normed, mix_out_grad, adapt_grad, mix_in_grad, select):
    rows = normed.shape[0]
    share = adapt_grad.shape[1]
    operands = [scalars, lowrank_grad, normed, mix_out_grad, adapt_grad, mix_in_grad, select]
    return kernel_call(
        compact_kernel,
        (1,),
        [whole(lowrank_grad), ANY] + [whole(array) for array in operands[3:]],
        [pl.BlockSpec((9 * RANK, share), lambda *_: (0, 0))],
        [((9 * RANK, share), jnp.bfloat16)],
        operands,
        2 * rows * share * 128,
        [pltpu.VMEM((rows, share), jnp.bfloat16), pltpu.SemaphoreType.DMA],
        1,
    )[0]


def spread_kernel(order, *refs):
    pieces, out = refs[:-1], refs[-1]
    step = pl.program_id(0)
    for index, piece in enumerate(pieces):

        @pl.when(step == index)
        def _():
            out[...] = wide(piece[...])


def spread_call(order, pieces):
    size, width = pieces[0].shape
    count = len(pieces)
    return kernel_call(
        spread_kernel,
        (count,),
        [whole(piece) for piece in pieces],
        [pl.BlockSpec((size, width), lambda step, order: (order[step], 0))],
        [((count * size, width), jnp.float32)],
        [order, *pieces],
        size * width,
        (),
        1,
    )[0]


def assemble_kernel(trees, order, *refs):
    count = len(refs) - 5
    own, pieces = refs[0], refs[1:count]
    in_grad, out_grad, mix_in_grad, mix_out_grad = refs[count : count + 4]
    (choice,) = refs[count + 4 :]
    share = own.shape[1]
    block = own.shape[0] // trees
    row = lax.broadcasted_iota(jnp.int32, (RANK, 128), 0)
    lane = lax.broadcasted_iota(jnp.int32, (RANK, 128), 1)
    same = lax.rem(lane, RANK) == row
    for tree in range(trees):
        chosen = own[tree * block + 8 * RANK : tree * block + 9 * RANK, :128]
        choice[tree * RANK : (tree + 1) * RANK] = low(jnp.where(same, wide(chosen), 0.0))

    def kind(source, stride, index):
        return jnp.concatenate(
            [
                source[tree * stride + index * RANK : tree * stride + (index + 1) * RANK, :]
                for tree in range(trees)
            ],
            axis=0,
        )

    for index in range(3):
        out_grad[index] = t_dot(choice[...], kind(own, block, 4 + index))
    mix_in_grad[...] = t_dot(kind(own, block, 7), choice[...])
    for place, source in enumerate((own, *pieces)):
        stride = block if place == 0 else 4 * RANK
        start = pl.ds(pl.multiple_of(order[place] * share, share), share)
        for index in range(3):
            in_grad[index, start, :] = t_dot(kind(source, stride, index), choice[...])
        mix_out_grad[:, start] = t_dot(choice[...], kind(source, stride, 3))


def assemble_call(order, own, pieces, trees):
    share = own.shape[1]
    count = 1 + len(pieces)
    width = count * share
    out_shape = [((3, width, 128), jnp.float32), ((3, 128, share), jnp.float32)]
    out_shape += [((share, 128), jnp.float32), ((128, width), jnp.float32)]
    operands = [order, own, *pieces]
    return kernel_call(
        functools.partial(assemble_kernel, trees),
        (1,),
        [whole(array) for array in operands[1:]],
        [pl.BlockSpec(shape, lambda *_, size=len(shape): (0,) * size) for shape, _ in out_shape],
        out_shape,
        operands,
        2 * trees * RANK * 128 * width * 4,
        [pltpu.VMEM((trees * RANK, 128), jnp.bfloat16)],
        1,
    )


def body(
    tokens,
    cotangent,
    attn_gain,
    ffn_gain,
    query_gain,
    key_gain,
    query_weight,
    key_weight,
    value_weight,
    output_weight,
    expert_gate,
    expert_up,
    expert_down,
    adapt_in,
    adapt_out,
    adapt_in_out,
    adapt_out_out,
    routes,
    gate_weights,
    block_parent,
    adapter_pick,
):
    rows_here, model_width = tokens.shape
    tensor_rank = lax.axis_index("tensor")
    tensor_count = lax.axis_size("tensor")
    owners = lax.axis_size("expert")
    owner_rank = lax.axis_index("expert")
    axes = divide_axes(owners, tensor_count)
    far, near, span = axes["z"][1], axes["x"][1], axes["y"][1]
    experts_here, _, hidden_here = expert_gate.shape
    experts_all = experts_here * owners
    column_share = model_width // tensor_count
    row_share = rows_here // tensor_count
    hold = lax.optimization_barrier
    level, core = tensor_rank // 2, tensor_rank % 2
    rank_list = jnp.reshape(tensor_rank, (1,)).astype(jnp.int32)

    def own_rows(array):
        return lax.dynamic_slice_in_dim(array, tensor_rank * row_share, row_share, 0)

    routes_wide = jnp.swapaxes(routes, 0, 1)
    weights_wide = jnp.swapaxes(gate_weights, 0, 1)
    route_weights = jnp.sum(
        jnp.where(
            routes_wide[:, :, None] == jnp.arange(experts_all, dtype=jnp.int32)[None, None, :],
            weights_wide[:, :, None],
            0.0,
        ),
        axis=0,
    )
    weights_high = low(route_weights)
    weights_low = low(route_weights - wide(weights_high))
    side_width = -(-2 * experts_all // 128) * 128
    side_pad = jnp.zeros((rows_here, side_width - 2 * experts_all), jnp.bfloat16)
    side_rows = jnp.concatenate([weights_high, weights_low, side_pad], axis=1)
    cot_queue = []
    for step in range(span):
        place = ((level + span - step) % span * 2 + core) * row_share
        cot_queue.append(
            jnp.concatenate(
                [
                    lax.dynamic_slice_in_dim(cotangent, place, row_share, 0),
                    lax.dynamic_slice_in_dim(side_rows, place, row_share, 0),
                ],
                axis=1,
            )
        )
    cot_queue = [jnp.concatenate(cot_queue, axis=0)]
    side_index = jnp.arange(side_width, dtype=jnp.int32)
    hidden_owner = (
        owner_rank * experts_here
        + jnp.arange(experts_here * hidden_here, dtype=jnp.int32) // hidden_here
    )
    spread_flat = low(
        (side_index[:, None] % experts_all == hidden_owner[None, :])
        & (side_index[:, None] < 2 * experts_all)
    )
    spread = jnp.swapaxes(spread_flat.reshape(side_width, experts_here, hidden_here), 0, 1)

    cot_planes = [None] * far
    cot_queue.append(turn(cot_queue[0], axes, "z", 1))
    cot_planes[0] = ring(cot_queue[0], axes, "x")
    first_gain, second_gain = attn_gain[None, :], ffn_gain[None, :]
    gains = (query_gain[None, :], key_gain[None, :])
    reached = ancestry(block_parent)
    cosine_table, sine_table = rope_tables(reached, rows_here // block_parent.shape[0], HD)
    signs = jnp.where(jnp.arange(HD) < HD // 2, -1.0, 1.0)[None, :]
    tables = (cosine_table, sine_table * signs)
    mask = jnp.where(token_mask(reached[0], rows_here), 0.0, MASKED_SCORE)
    select = jnp.repeat(wide(adapter_pick), RANK, axis=1)
    weights = (query_weight, key_weight, value_weight)
    normed_in, lowrank, *raws, squares = project_call(
        tokens, first_gain, weights, adapt_in, adapt_out, select
    )

    def halves(rows):
        return [rows[: rows.shape[0] // 2], rows[rows.shape[0] // 2 :]]

    squares = sum_tensor(squares, axes)
    held = (squares, cot_queue[1], cot_planes[0], expert_gate, expert_up, tables, mask)
    squares, cot_queue[1], cot_planes[0], expert_gate, expert_up, tables, mask = hold(held)
    gates = (expert_gate, turn(expert_gate, axes, "c", 1))
    ups = (expert_up, turn(expert_up, axes, "c", 1))
    cot_queue[1] = halves(cot_queue[1])
    cot_later = turn(cot_queue[1][0], axes, "z", 1)
    cot_across = ring(cot_queue[1][0], axes, "x")[1:]
    *states, mine, theirs = attend_call(
        jnp.reshape(core, (1,)).astype(jnp.int32),
        squares,
        raws,
        gains,
        tables,
        mask,
        output_weight,
        adapt_in_out,
        row_share,
    )
    cot_later, cot_across, mine, theirs = hold((cot_later, cot_across, mine, theirs))

    theirs = turn(theirs, axes, "c", 1)
    branch_kept, branch_sent = scatter_core(mine, theirs, axes)
    branch_sent, cot_queue[1] = hold((branch_sent, cot_queue[1]))
    down_tall = expert_down.reshape(-1, model_width)
    branch_came = turn(branch_sent, axes, "y", -1)
    cot_later = [cot_later, turn(cot_queue[1][1], axes, "z", 1)]
    cot_second = ring(cot_queue[1][1], axes, "x")[1:]
    held = (branch_came, cot_later, cot_second, gates, ups, down_tall)
    branch_came, cot_later, cot_second, gates, ups, down_tall = hold(held)
    downs = (down_tall, turn(down_tall, axes, "c", 1))
    cot_queue.append(jnp.concatenate(cot_later, axis=0))
    cot_planes[1] = [cot_queue[1]] + [list(pair) for pair in zip(cot_across, cot_second)]
    cot_planes[0] = [[piece] for piece in cot_planes[0]]
    resid_rows, norm_plane, mixed_rows = resid_call(
        rank_list, branch_kept, branch_came, tokens, adapt_out_out, select, second_gain
    )

    norm_queue = [norm_plane, turn(norm_plane, axes, "z", 1)]
    norm_pairs = [ring(norm_plane, axes, "x")]
    backs, sides = [None] * far, [None] * far

    def hidden_step(*indices):
        back, side = hidden_call(
            [cot_planes[index] for index in indices], downs, spread_flat, experts_here, row_share
        )
        for order, index in enumerate(indices):
            backs[index], sides[index] = (back, order * side.shape[0] // len(indices)), side
        return back

    def set_back(back, *indices):
        for index in indices:
            backs[index] = (back, backs[index][1])

    norm_planes = [None] * far
    held = (norm_queue[1], norm_pairs[0], downs, cot_queue[2])
    norm_queue[1], norm_pairs[0], downs, cot_queue[2] = hold(held)
    norm_planes[0] = ring(jnp.concatenate(norm_pairs[0], axis=0), axes, "y")
    norm_queue.append(turn(norm_queue[1], axes, "z", 1))
    norm_pairs.append(ring(norm_queue[1], axes, "x"))
    back_first = hidden_step(0, 1)
    held = (norm_planes[0], norm_queue[2], norm_pairs[1], cot_queue[2], back_first)
    norm_planes[0], norm_queue[2], norm_pairs[1], cot_queue[2], back_first = hold(held)
    set_back(back_first, 0, 1)
    parts, hiddens = [None] * far, [None] * far

    def expert_step(index):
        back, offset = backs[index]
        *parts[index], hiddens[index] = expert_call(
            norm_planes[index],
            gates,
            ups,
            spread,
            sides[index],
            back,
            offset,
            near if index else 0,
            span,
        )

    def whole_step(index):
        *parts[index], hiddens[index] = whole_call(
            norm_planes[index], cot_planes[index], gates, ups, downs, spread, near, span, row_share
        )

    norm_planes[1] = ring(jnp.concatenate(norm_pairs[1], axis=0), axes, "y")
    norm_queue.append(turn(norm_queue[2], axes, "z", 1))
    norm_pairs.append(ring(norm_queue[2], axes, "x"))
    cot_queue.append(turn(cot_queue[2], axes, "z", 1))
    cot_planes[2] = ring(cot_queue[2], axes, "x")
    expert_step(0)

    held = (norm_planes[1], norm_queue[3], norm_pairs[2], parts[0])
    norm_planes[1], norm_queue[3], norm_pairs[2], parts[0] = hold(held)
    norm_planes[2] = ring(jnp.concatenate(norm_pairs[2], axis=0), axes, "y")
    norm_pairs.append(ring(norm_queue[3], axes, "x"))
    expert_step(1)

    held = (norm_planes[2], norm_pairs[3], parts[1], cot_queue[3], cot_planes[2])
    norm_planes[2], norm_pairs[3], parts[1], cot_queue[3], cot_planes[2] = hold(held)
    norm_planes[3] = ring(jnp.concatenate(norm_pairs[3], axis=0), axes, "y")
    came, last = [None] * far, [None] * far
    came[1] = scatter_first(parts[1], axes)
    cot_across = [turn(piece, axes, "z", 1) for piece in cot_planes[2][1:]]
    whole_step(2)

    held = (norm_planes[3], came[1], parts[2], parts[0], cot_across)
    norm_planes[3], came[1], parts[2], parts[0], cot_across = hold(held)
    cot_planes[3] = [cot_queue[3]] + cot_across
    last[1] = scatter_second(parts[1], came[1], axes)
    came[2] = scatter_first(parts[2], axes)
    came_y = send_sum(parts[0], axes, "y")
    whole_step(3)

    held = (last[1], came[2], came_y, parts[3], hiddens)
    last[1], came[2], came_y, parts[3], hiddens = hold(held)
    came[3] = scatter_first(parts[3], axes)
    last[2] = scatter_second(parts[2], came[2], axes)
    ring_sum = turn(low(scatter_last(parts[1], came[1], last[1], axes)), axes, "z", 1)
    mixes, mix_came = [None] * far, [None] * far

    def down_step(first, second):
        mixes[first], mixes[second] = down_call(
            [hiddens[first], hiddens[second]], downs, near, span, row_share
        )

    down_step(3, 0)

    held = (ring_sum, came[3], last[2], mixes[3], mixes[0], hiddens)
    ring_sum, came[3], last[2], mixes[3], mixes[0], hiddens = hold(held)
    last[3] = scatter_second(parts[3], came[3], axes)
    ring_sum = turn(
        low(wide(ring_sum) + scatter_last(parts[2], came[2], last[2], axes)), axes, "z", 1
    )

    ring_sum, last[3], parts[0], hiddens = hold((ring_sum, last[3], parts[0], hiddens))
    ring_sum = turn(
        low(wide(ring_sum) + scatter_last(parts[3], came[3], last[3], axes)), axes, "z", 1
    )
    own_sums = [
        [block(parts[0][0], k, near), block(came_y, k, near)] for k in range(near)
    ]
    came_x = send_sum([None] + [low(pair[0] + pair[1]) for pair in own_sums[1:]], axes, "x")
    down_step(1, 2)

    half_width = model_width // span

    def column_sum(arrays, owner):
        first = owner * half_width
        return sum(
            wide(lax.dynamic_slice_in_dim(array, first, half_width, 1)) for array in arrays
        )

    def mix_columns(index, owner):
        rows = [column_sum(arrays, owner) for arrays in mix_held[index]]
        return jnp.concatenate(rows, axis=0)

    def mix_down(index):
        came_rows = None
        for step in range(span - 1, 0, -1):
            total = mix_columns(index, (level + span - step) % span)
            if came_rows is not None:
                total = total + rolled(came_rows)
            came_rows = turn(low(total), axes, "y", -1)
        return came_rows

    def rolled(rows):
        size = rows.shape[0] // span
        return wide(jnp.concatenate([rows[size:], rows[:size]], axis=0))

    def mix_total(index):
        return mix_columns(index, level) + rolled(mix_parts[index])

    def mix_send(index, down):
        return send_sum([blocks[down] for blocks in mixes[index]], axes, "x")

    mix_held = [None] * far
    mix_parts = [None] * far

    ring_sum, came_x, mixes = hold((ring_sum, came_x, mixes))
    mix_early = mix_send(3, 0)
    ffn_rows_grad = wide(ring_sum) + (own_sums[0][0] + own_sums[0][1]) + wide(came_x)
    second_scaled = ffn_rows_grad * wide(second_gain)
    second_inverse = lax.rsqrt(
        jnp.mean(resid_rows * resid_rows, axis=1, keepdims=True) + EPSILON
    )
    resid_grad_rows = wide(own_rows(cotangent)) + norm_back(
        second_scaled,
        resid_rows,
        second_inverse,
        model_width,
        jnp.sum(second_scaled * resid_rows, axis=1, keepdims=True),
    )
    branch_sent = jnp.concatenate([low(resid_grad_rows), mixed_rows], axis=1)
    branch_pieces = ring(branch_sent, axes, "y")
    branch_other = turn(branch_pieces[0], axes, "c", 1)
    order = jnp.stack(
        [
            (level + span - step) % span * 2 + side
            for side in (core, 1 - core)
            for step in range(span)
        ]
    ).astype(jnp.int32)

    branch_pieces, mix_early, mixes = hold((branch_pieces, mix_early, mixes))
    branch_others = [turn(piece, axes, "c", 1) for piece in branch_pieces[1:]]
    branch_others, branch_other, mixes = hold((branch_others, branch_other, mixes))
    branch_pieces = branch_pieces + [branch_other] + branch_others
    mix_late = [mix_send(3, down) for down in range(1, span)]
    mix_next = mix_send(2, 0)
    mix_far = [[turn(part, axes, "z", -1) for part in blocks] for blocks in mixes[1][1:]]
    query_grad, key_grad, value_grad, inner, mix_in_grad, mix_out_grad = backward_call(
        jnp.concatenate([order, rank_list]),
        branch_pieces,
        output_weight,
        adapt_in_out,
        adapt_out_out,
        select,
        states,
        raws[:2],
        gains,
        tables,
        mask,
        column_share,
    )

    inner = sum_tensor(hold(inner), axes)
    held = (inner, mix_late, mix_next, mix_far, mixes)
    inner, mix_late, mix_next, mix_far, mixes = hold(held)
    mix_held[3] = list(zip(mixes[3][0], [mix_early] + mix_late))
    mix_parts[3] = mix_down(3)
    mix_last = [mix_send(2, down) for down in range(1, span)]
    mix_near = [turn(mixes[1][0][0], axes, "z", -1)]
    raw_grads, lowrank_part, adapt_grad = raw_call(
        inner,
        squares,
        (query_grad, key_grad, value_grad),
        raws[:2],
        lowrank,
        adapt_out,
        select,
        model_width,
    )
    lowrank_came = turn(lowrank_part, axes, "c", 1)
    lowrank_part, lowrank_came, raw_grads = hold((lowrank_part, lowrank_came, raw_grads))
    lowrank_part = low(wide(lowrank_part) + wide(lowrank_came))
    lowrank_parts = ring(lowrank_part, axes, "y")
    normed_mine, normed_theirs = weight_call(
        jnp.reshape(core, (1,)).astype(jnp.int32), raw_grads, weights, row_share
    )

    held = (normed_mine, normed_theirs, lowrank_parts, mix_parts[3], mix_last, mix_near, mixes)
    held = hold(held)
    normed_mine, normed_theirs, lowrank_parts, mix_parts[3], mix_last, mix_near, mixes = held
    normed_theirs = turn(normed_theirs, axes, "c", 1)
    lowrank_grad = low(sum(wide(part) for part in lowrank_parts))
    mix_held[2] = list(zip(mixes[2][0], [mix_next] + mix_last))
    mix_parts[2] = mix_down(2)
    mix_beside = turn(low(mix_total(3)), axes, "z", 1)
    compact = compact_call(
        rank_list, lowrank_grad, normed_in, mix_out_grad, adapt_grad, mix_in_grad, select
    )
    normed_theirs, compact, mixes = hold((normed_theirs, compact, mixes))
    mix_near = mix_near + [turn(part, axes, "z", -1) for part in mixes[1][0][1:]]
    normed_kept, normed_sent = scatter_core(normed_mine, normed_theirs, axes)
    normed_sent, compact = hold((normed_sent, compact))
    normed_came = turn(normed_sent, axes, "y", -1)
    trees, mix_near, mix_beside = hold((ring(compact, axes, "x"), mix_near, mix_beside))
    trees = jnp.concatenate(trees, axis=0)
    tree_queue = [trees] + [turn(trees, axes, "z", step) for step in range(1, far)]
    normed_came, mix_parts[2], mix_far, mixes = hold((normed_came, mix_parts[2], mix_far, mixes))

    input_rows = input_call(
        rank_list,
        normed_kept,
        normed_came,
        lowrank_grad,
        adapt_in,
        select,
        tokens,
        first_gain,
        resid_grad_rows,
    )
    input_held = ring(input_rows, axes, "y")
    for across in range(1, near):
        pairs = zip(mixes[0][across], mix_far[across - 1])
        mixes[0][across] = [low(wide(mine) + wide(other)) for mine, other in pairs]
    mix_came[0] = [mix_send(0, down) for down in range(span)]
    input_held, tree_queue = hold((input_held, tree_queue))

    trees = jnp.concatenate(tree_queue, axis=0)
    shared = trees.reshape(owners, -1, column_share)[:, : 4 * RANK]
    shared = ring(shared.reshape(-1, column_share), axes, "y")
    mix_across = turn(low(mix_total(2)), axes, "z", -2)
    input_pieces = input_held + [turn(piece, axes, "c", 1) for piece in input_held]
    shared, mix_came[0] = hold((shared, mix_came[0]))
    mix_held[0] = [list(arrays) for arrays in zip(mixes[0][0], mix_came[0], mix_near)]
    mix_held[0][0].append(resid_rows)
    mix_parts[0] = mix_down(0)
    shared = shared + [turn(piece, axes, "c", 1) for piece in shared]
    shared = hold(shared)
    grad_adapt_in, grad_adapt_out, grad_adapt_in_out, grad_adapt_out_out = assemble_call(
        order, trees, shared[1:], owners
    )
    held = (mix_parts[0], mix_across, mix_beside, grad_adapt_in)
    mix_parts[0], mix_across, mix_beside, grad_adapt_in = hold(held)
    layer_columns = low(mix_total(0) + wide(mix_across) + wide(mix_beside))
    layer_out = place_columns(layer_columns, axes)
    input_grad = spread_call(order, input_pieces)
    return (
        layer_out,
        input_grad,
        grad_adapt_in,
        grad_adapt_out,
        grad_adapt_in_out,
        grad_adapt_out_out,
    )


def solution(mesh):
    return jax.shard_map(
        body,
        mesh=mesh,
        in_specs=(
            P("expert", None),
            P("expert", None),
            P(),
            P(),
            P("tensor"),
            P("tensor"),
            P(None, "tensor"),
            P(None, "tensor"),
            P(None, "tensor"),
            P("tensor", None),
            P("expert", None, "tensor"),
            P("expert", None, "tensor"),
            P("expert", "tensor", None),
            P(),
            P(None, None, "tensor"),
            P("tensor", None),
            P(),
            P("expert", None),
            P("expert", None),
            P("expert"),
            P("expert", None),
        ),
        out_specs=(
            P("expert", "tensor"),
            P("expert", None),
            P(),
            P(None, None, "tensor"),
            P("tensor", None),
            P(),
        ),
        check_vma=False,
    )
```

```python
import functools

import jax
import jax.numpy as jnp
from jax import lax
from jax.experimental import pallas as pl
from jax.experimental.pallas import tpu as pltpu
from jax.sharding import PartitionSpec as P

HD = 128
RANK = 16


EPSILON = 1e-05
ROPE_BASE = 10000.0
MASKED_SCORE = -1e30
VMEM_LIMIT = 56 * 2**20
CHUNK = 128


def ancestry(parents):
    blocks = parents.shape[0]
    places = jnp.arange(blocks, dtype=jnp.int32)
    walker = places
    reached = walker[:, None] == places[None, :]
    for _ in range(blocks - 1):
        hits = (walker[:, None] == places[None, :]).astype(jnp.int32)
        walker = jnp.sum(hits * parents[None, :], axis=1)
        reached = reached | (walker[:, None] == places[None, :])
    return reached[None]


def rope_tables(reached, block_span, head_size):
    depths = jnp.sum(reached.astype(jnp.int32), axis=2) - 1
    offsets = jnp.arange(block_span, dtype=jnp.int32)
    located = (
        (depths[:, :, None] * block_span + offsets[None, None, :]).reshape(-1).astype(jnp.float32)
    )
    halves = head_size // 2
    speeds = ROPE_BASE ** (-2.0 * jnp.arange(halves, dtype=jnp.float32) / head_size)
    angles = located[:, None] * speeds[None, :]
    angles = jnp.concatenate([angles, angles], axis=1)
    return (jnp.cos(angles), jnp.sin(angles))


def token_mask(reached, total_size):
    blocks = reached.shape[0]
    block_span = total_size // blocks
    widened = jnp.broadcast_to(
        reached[:, None, :, None], (blocks, block_span, blocks, block_span)
    ).reshape(total_size, total_size)
    positions = jnp.arange(total_size, dtype=jnp.int32)
    return widened & (positions[None, :] <= positions[:, None])


def norm_back(scaled_grad, values, inverse, model_width, inner_sum):
    return inverse * scaled_grad - values * inverse**3 * (inner_sum / model_width)


def divide_axes(owners, tensor_count):
    outer = 4
    return {
        "z": ("expert", outer, owners // outer, owners),
        "x": ("expert", owners // outer, 1, owners),
        "y": ("tensor", tensor_count // 2, 2, tensor_count),
        "c": ("tensor", 2, 1, tensor_count),
    }


def turn(array, axes, name, step):
    axis, length, stride, total = axes[name]
    pairs = []
    for index in range(total):
        place = (index // stride) % length
        moved = index + ((place + step) % length - place) * stride
        pairs.append((index, moved))
    return lax.ppermute(array, axis, pairs)


def ring(array, axes, name):
    held = [array]
    for _ in range(axes[name][1] - 1):
        held.append(turn(held[-1], axes, name, 1))
    return held


def wide(array):
    return array.astype(jnp.float32)


def low(array):
    return array.astype(jnp.bfloat16)


def send_sum(parts, axes, name):
    total = parts[-1]
    for part in parts[-2:0:-1]:
        total = low(wide(turn(total, axes, name, -1)) + wide(part))
    return turn(total, axes, name, -1)


def scatter_first(pieces, axes):
    span = axes["y"][1]
    return send_sum(pieces[:span], axes, "y"), send_sum(pieces[span:], axes, "x")


def block(array, index, count):
    size = array.shape[0] // count
    return wide(array[index * size : (index + 1) * size])


def scatter_second(pieces, came, axes):
    near, span = axes["x"][1], axes["y"][1]
    first = [low(block(pieces[0], k, near) + block(came[0], k, near)) for k in range(1, near)]
    second = [low(block(pieces[span], k, span) + block(came[1], k, span)) for k in range(1, span)]
    return send_sum([None] + first, axes, "x"), send_sum([None] + second, axes, "y")


def scatter_last(pieces, came, last, axes):
    near, span = axes["x"][1], axes["y"][1]
    first = block(pieces[0], 0, near) + block(came[0], 0, near) + wide(last[0])
    second = block(pieces[span], 0, span) + block(came[1], 0, span) + wide(last[1])
    return jnp.concatenate([first, second], axis=0)


def gather_tensor(rows, axes):
    held = ring(rows, axes, "y")
    return held + [turn(piece, axes, "c", 1) for piece in held]


def scatter_core(mine, came, axes):
    rank = lax.axis_index("tensor")
    span = axes["y"][1]
    size = mine.shape[0] // span
    total = None
    for step in range(span - 1, -1, -1):
        level = (rank // 2 + span - step) % span
        part = wide(lax.dynamic_slice_in_dim(mine, level * size, size, 0)) + wide(
            lax.dynamic_slice_in_dim(came, level * size, size, 0)
        )
        if step == 0:
            return part, total
        total = low(part if total is None else part + wide(turn(total, axes, "y", -1)))


def gather_x(rows, axes):
    return jnp.concatenate(ring(rows, axes, "x"), axis=0)


def place_columns(rows, axes):
    rank = lax.axis_index("tensor")
    span = axes["y"][1]
    size, share = rows.shape[0] // span, rows.shape[1] // 2
    level, core = rank // 2, rank % 2
    mine = lax.dynamic_slice_in_dim(rows, core * share, share, 1)
    theirs = turn(lax.dynamic_slice_in_dim(rows, (1 - core) * share, share, 1), axes, "c", 1)
    blocks = jnp.zeros((2 * span * size, share), rows.dtype)
    for step in range(span):
        place = (level + span - step) % span * 2
        for part, side in ((mine, core), (theirs, 1 - core)):
            taken = part[step * size : (step + 1) * size]
            blocks = lax.dynamic_update_slice_in_dim(blocks, taken, (place + side) * size, 0)
    return blocks


def sum_tensor(array, axes):
    total = wide(array) + wide(turn(array, axes, "c", 1))
    moving = total.astype(array.dtype)
    result = total
    for _ in range(axes["y"][1] - 1):
        moving = turn(moving, axes, "y", 1)
        result = result + wide(moving)
    return result


def dot(left, right):
    return jnp.dot(left, right, preferred_element_type=jnp.float32)


def dot_t(left, right):
    return lax.dot_general(
        left, right, (((1,), (1,)), ((), ())), preferred_element_type=jnp.float32
    )


def t_dot(left, right):
    return lax.dot_general(
        left, right, (((0,), (0,)), ((), ())), preferred_element_type=jnp.float32
    )


ANY = pl.BlockSpec(memory_space=pl.ANY)


def whole(array):
    shape = array.shape
    return pl.BlockSpec(shape, lambda *_: (0,) * len(shape))


def kernel_call(kernel, grid, in_specs, out_specs, out_shape, operands, flops, scratch=(), scalars=0):
    moved = sum(array.size * array.dtype.itemsize for array in operands)
    return pl.pallas_call(
        kernel,
        grid_spec=pltpu.PrefetchScalarGridSpec(
            num_scalar_prefetch=scalars,
            grid=grid,
            in_specs=in_specs,
            out_specs=out_specs,
            scratch_shapes=list(scratch),
        ),
        out_shape=[jax.ShapeDtypeStruct(shape, kind) for shape, kind in out_shape],
        compiler_params=pltpu.CompilerParams(vmem_limit_bytes=VMEM_LIMIT),
        cost_estimate=pl.CostEstimate(flops=flops, bytes_accessed=moved, transcendentals=0),
    )(*operands)


def normalize_rows(source, gain, target):
    step = 16

    def some(index, carry):
        rows = pl.ds(pl.multiple_of(index * step, step), step)
        values = wide(source[rows, :])
        inverse = lax.rsqrt(jnp.mean(values * values, axis=1, keepdims=True) + EPSILON)
        target[rows, :] = low(values * inverse * gain)
        return carry

    lax.fori_loop(0, source.shape[0] // step, some, 0)


def project_kernel(
    tokens, gain, query_weight, key_weight, value_weight, adapt_in, adapt_out, select,
    normed_out, lowrank_out, query_out, key_out, value_out, squares_out,
    weights, maps, sems,
):
    step = pl.program_id(0)
    rank = adapt_out.shape[1]
    copies = [
        pltpu.make_async_copy(
            adapt_in.at[index], maps.at[:, pl.ds(index * rank, rank)], sems.at[3]
        )
        for index in range(3)
    ]
    for index, source in enumerate((query_weight, key_weight, value_weight)):
        copies.append(pltpu.make_async_copy(source, weights.at[index], sems.at[index]))

    @pl.when(step == 0)
    def _():
        for copy in copies:
            copy.start()

    normalize_rows(tokens, wide(gain[...]), normed_out)

    @pl.when(step == 0)
    def _():
        for copy in copies:
            copy.wait()

    lowrank = dot(normed_out[...], maps[...])
    squares = []
    for index, out in enumerate((query_out, key_out, value_out)):
        lowrank_out[index] = low(lowrank[:, index * rank : (index + 1) * rank] * select[...])
        raw = dot(normed_out[...], weights[index]) + dot(lowrank_out[index], adapt_out[index])
        out[...] = raw
        squares.append(jnp.sum(raw * raw, axis=1, keepdims=True))
    lane = lax.broadcasted_iota(jnp.int32, (tokens.shape[0], 128), 1)
    columns = jnp.where(lane == 0, squares[0], jnp.where(lane == 1, squares[1], 0.0))
    squares_out[...] = jnp.transpose(columns)[:8]


def project_call(tokens, gain, weights, adapt_in, adapt_out, select):
    rows, width = tokens.shape
    local = weights[0].shape[1]
    rank = adapt_in.shape[2]
    tile = rows // 2
    out_shape = [((rows, width), jnp.bfloat16), ((3, rows, rank), jnp.bfloat16)]
    out_shape += [((rows, local), jnp.float32)] * 3 + [((8, rows), jnp.float32)]
    operands = [tokens, gain, *weights, adapt_in, adapt_out, select]
    row_block = pl.BlockSpec((tile, width), lambda n: (n, 0))
    local_block = pl.BlockSpec((tile, local), lambda n: (n, 0))
    return kernel_call(
        project_kernel,
        (2,),
        [row_block, whole(gain), ANY, ANY, ANY, ANY, whole(adapt_out), whole(select)],
        [row_block, pl.BlockSpec((3, tile, rank), lambda n: (0, n, 0))]
        + [local_block] * 3
        + [pl.BlockSpec((8, tile), lambda n: (0, n))],
        out_shape,
        operands,
        6 * rows * width * local,
        [
            pltpu.VMEM((3, width, local), jnp.bfloat16),
            pltpu.VMEM((width, 3 * rank), jnp.bfloat16),
            pltpu.SemaphoreType.DMA((4,)),
        ],
    )


def spread_columns(rows):
    return jnp.transpose(jnp.concatenate([rows] * (128 // rows.shape[0]), axis=0))


def turned(values):
    half = values.shape[1] // 2
    return jnp.concatenate([values[:, half:], values[:, :half]], axis=1)


def attend_kernel(
    width, size, core, squares, query_raw, key_raw, value_raw, query_gain, key_gain, cosine, sine,
    mask, output_weight, mix_in, queries, keys, values, attended, mine, theirs, held, weight, scales, sem,
):
    head = pl.program_id(0)
    last = pl.num_programs(0) - 1
    copy = pltpu.make_async_copy(output_weight, weight, sem)

    @pl.when(head == 0)
    def _():
        copy.start()
        scales[...] = lax.rsqrt(spread_columns(squares[...]) / width + EPSILON)

    inverse = scales[:, :2]
    query = query_raw[...] * inverse[:, 0:1] * wide(query_gain[...])
    key = key_raw[...] * inverse[:, 1:2] * wide(key_gain[...])
    query = low(query * cosine[...] + turned(query) * sine[...])
    key = low(key * cosine[...] + turned(key) * sine[...])
    value = low(value_raw[...])
    queries[...] = query
    keys[...] = key
    values[...] = value
    scores = dot_t(query, key) * HD ** (-0.5) + mask[...]
    raised = jnp.exp(scores - jnp.max(scores, axis=1, keepdims=True))
    weights = low(raised * (1.0 / jnp.sum(raised, axis=1, keepdims=True)))
    result = low(dot(weights, value))
    attended[...] = result
    held[head] = result

    @pl.when(head == last)
    def _():
        copy.wait()
        heads = held.shape[0]
        levels = mine.shape[0] // size
        for out, offset in ((mine, core[0]), (theirs, 1 - core[0])):
            taken = []
            for level in range(levels):
                rows = pl.ds(pl.multiple_of((2 * level + offset) * size, size), size)
                taken.append(
                    jnp.concatenate([held[index, rows, :] for index in range(heads)], axis=1)
                )
            taken = jnp.concatenate(taken, axis=0)
            out[:, :width] = dot(taken, weight[...]).astype(out.dtype)
            out[:, width:] = dot(taken, mix_in[...]).astype(out.dtype)


def attend_call(core, squares, raws, gains, tables, mask, output_weight, mix_in, size):
    rows, local = raws[0].shape
    heads = local // HD
    width = output_weight.shape[1]
    wide_width = width + mix_in.shape[1]
    block = pl.BlockSpec((rows, HD), lambda head, *_: (0, head))
    gain_block = pl.BlockSpec((1, HD), lambda head, *_: (0, head))
    fixed = pl.BlockSpec((rows // 2, wide_width), lambda *_: (0, 0))
    operands = [core, squares, *raws, *gains, *tables, mask, output_weight, mix_in]
    return kernel_call(
        functools.partial(attend_kernel, width, size),
        (heads,),
        [whole(squares)] + [block] * 3 + [gain_block] * 2
        + [whole(tables[0]), whole(tables[1]), whole(mask), ANY, whole(mix_in)],
        [block] * 4 + [fixed] * 2,
        [((rows, local), jnp.bfloat16)] * 4
        + [((rows // 2, wide_width), jnp.float32), ((rows // 2, wide_width), jnp.bfloat16)],
        operands,
        4 * rows * rows * local + 2 * rows * local * width,
        [
            pltpu.VMEM((heads, rows, HD), jnp.bfloat16),
            pltpu.VMEM(output_weight.shape, jnp.bfloat16),
            pltpu.VMEM((rows, 128), jnp.float32),
            pltpu.SemaphoreType.DMA,
        ],
        1,
    )


def resid_kernel(
    width, rank, kept, came, tokens, mix_out, select, gain, resid_out, norm_out, mixed_out
):
    mixed = low((kept[:, width:] + wide(came[:, width:])) * select[...])
    mixed_out[...] = mixed
    resid_out[...] = (
        wide(tokens[...])
        + (kept[:, :width] + wide(came[:, :width]))
        + dot(mixed, mix_out[...])
    )
    normalize_rows(resid_out, wide(gain[...]), norm_out)


def resid_call(rank, kept, came, tokens, mix_out, select, gain):
    rows, width = kept.shape[0], tokens.shape[1]
    out_shape = [((rows, width), jnp.float32), ((rows, width), jnp.bfloat16)]
    out_shape += [((rows, mix_out.shape[0]), jnp.bfloat16)]
    operands = [rank, kept, came, tokens, mix_out, select, gain]
    return kernel_call(
        functools.partial(resid_kernel, width),
        (1,),
        [whole(kept), whole(came), pl.BlockSpec((rows, width), lambda n, rank: (rank[0], 0))]
        + [whole(array) for array in operands[4:]],
        [pl.BlockSpec(shape, lambda *_: (0, 0)) for shape, _ in out_shape],
        out_shape,
        operands,
        2 * rows * width * mix_out.shape[0],
        (),
        1,
    )


def plane_order(near, span, size):
    return [
        (across, down * size, (down * near + across) * size)
        for down in range(span)
        for across in range(near)
    ]


def hidden_kernel(places, *refs):
    count = len(places)
    pieces, (down_own, down_other, spread), (out, side_out), (rows, side, row_sems, side_sems) = (
        refs[:count],
        refs[count : count + 3],
        refs[count + 3 : count + 5],
        refs[count + 5 :],
    )
    step = pl.program_id(0)
    width = rows.shape[1]

    @pl.when(step == 0)
    def _():
        copies = []
        for index, (piece, targets) in enumerate(zip(pieces, places)):
            for source, target, size in targets:
                taken = piece.at[pl.ds(source, size)]
                place = pl.ds(target, size)
                slot = len(copies) // 2
                copies.append(
                    pltpu.make_async_copy(
                        taken.at[:, pl.ds(0, width)], rows.at[place], row_sems.at[slot]
                    )
                )
                copies.append(
                    pltpu.make_async_copy(
                        taken.at[:, pl.ds(width, side.shape[1])], side.at[place], side_sems.at[slot]
                    )
                )
        for copy in copies:
            copy.start()
        for copy in copies:
            copy.wait()
        side_out[...] = side[...]

    def emit(down):
        grad = dot_t(rows[...], down[...]) * dot(side[...], spread[...])
        part = out.shape[2]
        for index in range(out.shape[0]):
            out[index] = low(grad[:, index * part : (index + 1) * part])

    half = pl.num_programs(0) // 2

    @pl.when(step < half)
    def _():
        emit(down_own)

    @pl.when(step >= half)
    def _():
        emit(down_other)


def hidden_call(planes, downs, spread, experts, size):
    hidden, width = downs[0].shape
    near = len(planes[0])
    pieces, places, rows = [], [], 0
    for plane in planes:
        for across, column in enumerate(plane):
            down = 0
            for piece in column:
                targets = []
                for source in range(0, piece.shape[0], size):
                    targets.append((source, rows + (down * near + across) * size, size))
                    down += 1
                pieces.append(piece)
                places.append(targets)
        rows += near * down * size
    blocks = rows // size
    part = hidden // experts
    side = spread.shape[0]
    pair = 2 * part
    half = experts // 2
    last = half - 1
    return kernel_call(
        functools.partial(hidden_kernel, places),
        (2 * half,),
        [ANY] * len(pieces)
        + [
            pl.BlockSpec((pair, width), lambda n: (jnp.minimum(n, last), 0)),
            pl.BlockSpec((pair, width), lambda n: (jnp.maximum(n - half, 0), 0)),
            pl.BlockSpec((side, pair), lambda n: (0, lax.rem(n, half))),
        ],
        [
            pl.BlockSpec((2, rows, part), lambda n: (n, 0, 0)),
            pl.BlockSpec((rows, side), lambda n: (0, 0)),
        ],
        [((2 * experts, rows, part), jnp.bfloat16), ((rows, side), jnp.bfloat16)],
        [*pieces, *downs, spread],
        4 * rows * hidden * width,
        [
            pltpu.VMEM((rows, width), jnp.bfloat16),
            pltpu.VMEM((rows, side), jnp.bfloat16),
            pltpu.SemaphoreType.DMA((blocks,)),
            pltpu.SemaphoreType.DMA((blocks,)),
        ],
    )


def write_rows(total, outs, near, span, levels):
    rows = total.shape[0]
    if not span:
        block = rows // (near * levels)
        for across in range(near):
            for down in range(levels):
                first = (down * near + across) * block
                outs[across][down * block : (down + 1) * block] = low(total[first : first + block])
        return
    half = rows // (2 * near * span)
    for down in range(span):
        for across in range(near):
            first = 2 * (down * near + across) * half
            outs[down][across * half : (across + 1) * half] = low(total[first : first + half])
            outs[span + across][down * half : (down + 1) * half] = low(
                total[first + half : first + 2 * half]
            )


def expert_kernel(count, near, span, levels, offset, *refs):
    pieces = refs[:count]
    gate_own, up_own, gate_other, up_other, spread, side, back = refs[count : count + 7]
    outs, hidden_out = refs[count + 7 : count + 7 + near + span], refs[count + 7 + near + span]
    rows, weights, gate_grad, up_grad, hidden, grads, sems, row_sem, back_sem, out_sem = refs[
        count + 8 + near + span :
    ]
    step = pl.program_id(0)
    size = pieces[0].shape[0]
    experts, _, part = gate_own.shape
    total_rows = rows.shape[0]
    sources = (gate_own, up_own, gate_other, up_other)

    def load(expert):
        slot = weights.at[expert]
        return [
            pltpu.make_async_copy(
                source.at[expert], slot.at[:, pl.ds(index * part, part)], sems.at[expert]
            )
            for index, source in enumerate(sources)
        ]

    row_copies = [
        pltpu.make_async_copy(piece, rows.at[pl.ds(index * size, size)], row_sem.at[index])
        for index, piece in enumerate(pieces)
    ]
    back_copy = pltpu.make_async_copy(
        back.at[:, pl.ds(offset, total_rows), :], grads, back_sem
    )
    out_copy = pltpu.make_async_copy(hidden, hidden_out, out_sem)

    @pl.when(step == 0)
    def _():
        for copy in row_copies + load(0) + [back_copy] + load(1):
            copy.start()
        for copy in row_copies:
            copy.wait()
        back_copy.wait()

        def work(expert, carry):
            for ahead in range(2, experts):

                @pl.when(expert == ahead - 2)
                def _():
                    for copy in load(ahead):
                        copy.start()

            for copy in load(expert):
                copy.wait()
            values = dot(rows[...], weights[expert])
            weight = dot(side[...], spread[expert])
            for half in range(2):
                gate_value = values[:, 2 * half * part : (2 * half + 1) * part]
                up_value = values[:, (2 * half + 1) * part : (2 * half + 2) * part]
                sigmoid = jax.nn.sigmoid(gate_value)
                silu = gate_value * sigmoid
                place = half * experts + expert
                grad = wide(grads[place])
                gate_grad[place] = low(grad * up_value * (sigmoid + silu * (1.0 - sigmoid)))
                up_grad[place] = low(grad * silu)
                hidden[place] = low(silu * up_value * weight)
            return carry

        lax.fori_loop(0, experts, work, 0)
        out_copy.start()

    tile = outs[0].shape[1]
    columns = pl.ds(pl.multiple_of(step * tile, tile), tile)
    total = None
    for expert in range(experts):
        for half in range(2):
            place = half * experts + expert
            for index, grad in enumerate((gate_grad, up_grad)):
                first = (2 * half + index) * part
                term = dot_t(grad[place], weights[expert, columns, first : first + part])
                total = term if total is None else total + term
    write_rows(total, outs, near, span, levels)

    @pl.when(step == pl.num_programs(0) - 1)
    def _():
        out_copy.wait()


def block_sizes(rows, near, span):
    if not span:
        return [rows // near] * near
    return [rows // (2 * span)] * span + [rows // (2 * near)] * near


def expert_call(pieces, gates, ups, spread, side, back, offset, near, span, levels):
    count = len(pieces)
    experts, width, part = gates[0].shape
    size = pieces[0].shape[0]
    rows = size * count
    tile = min(width, 512)
    shape = (2 * experts, rows, part)
    slots = pltpu.VMEM(shape, jnp.bfloat16)
    sizes = block_sizes(rows, near, span)
    side_block = pl.BlockSpec((rows, side.shape[1]), lambda n: (offset // rows, 0))
    return kernel_call(
        functools.partial(expert_kernel, count, near, span, levels, offset),
        (width // tile,),
        [ANY] * (count + 4) + [whole(spread), side_block, ANY],
        [pl.BlockSpec((size, tile), lambda n: (0, n)) for size in sizes] + [ANY],
        [((size, width), jnp.bfloat16) for size in sizes] + [(shape, jnp.bfloat16)],
        [*pieces, gates[0], ups[0], gates[1], ups[1], spread, side, back],
        16 * rows * experts * part * width,
        [
            pltpu.VMEM((rows, width), jnp.bfloat16),
            pltpu.VMEM((experts, width, 4 * part), jnp.bfloat16),
            slots,
            slots,
            slots,
            slots,
            pltpu.SemaphoreType.DMA((experts,)),
            pltpu.SemaphoreType.DMA((count,)),
            pltpu.SemaphoreType.DMA,
            pltpu.SemaphoreType.DMA,
        ],
    )


def whole_kernel(count, near, span, levels, places, *refs):
    pieces = refs[:count]
    gate_own, up_own, gate_other, up_other, spread, down_own, down_other = refs[count : count + 7]
    refs = refs[count + 7 :]
    cot_pieces, refs = refs[: len(places)], refs[len(places) :]
    outs, hidden_out = refs[: near + span], refs[near + span]
    rows, weights, gate_grad, up_grad, hidden, grads, sems, row_sem, out_sem = refs[
        near + span + 1 : near + span + 10
    ]
    cot_rows, side, downs, cot_sems, side_sems, down_sems = refs[near + span + 10 :]
    step = pl.program_id(0)
    size = pieces[0].shape[0]
    experts, _, part = gate_own.shape
    total_rows = rows.shape[0]
    sources = (gate_own, up_own, gate_other, up_other)

    def load(expert):
        slot = weights.at[expert]
        return [
            pltpu.make_async_copy(
                source.at[expert], slot.at[:, pl.ds(index * part, part)], sems.at[expert]
            )
            for index, source in enumerate(sources)
        ]

    row_copies = [
        pltpu.make_async_copy(piece, rows.at[pl.ds(index * size, size)], row_sem.at[index])
        for index, piece in enumerate(pieces)
    ]
    pairs = experts // 2

    def load_down(chunk):
        source = (down_own, down_other)[chunk // pairs]
        taken = source.at[pl.ds(chunk % pairs * 2 * part, 2 * part)]
        return pltpu.make_async_copy(taken, downs.at[chunk], down_sems.at[chunk])

    out_copy = pltpu.make_async_copy(hidden, hidden_out, out_sem)

    @pl.when(step == 0)
    def _():
        copies = copy_places(cot_pieces, places, cot_rows, side, cot_sems, side_sems)
        for copy in copies + [load_down(0), load_down(1)] + row_copies:
            copy.start()
        for copy in copies:
            copy.wait()

        def back(chunk, carry):
            for ahead in range(2 * pairs):

                @pl.when(chunk == ahead)
                def _():
                    if ahead + 2 < 2 * pairs:
                        load_down(ahead + 2).start()
                    elif ahead + 2 - 2 * pairs < 2:
                        for copy in load(ahead + 2 - 2 * pairs):
                            copy.start()
                    load_down(ahead).wait()

            grad = dot_t(cot_rows[...], downs[chunk])
            place = chunk // pairs * experts + lax.rem(chunk, pairs) * 2
            for index in range(2):
                weight = dot(side[...], spread[lax.rem(chunk, pairs) * 2 + index])
                grads[place + index] = low(grad[:, index * part : (index + 1) * part] * weight)
            return carry

        lax.fori_loop(0, 2 * pairs, back, 0)
        for copy in row_copies:
            copy.wait()

        def work(expert, carry):
            for ahead in range(2, experts):

                @pl.when(expert == ahead - 2)
                def _():
                    for copy in load(ahead):
                        copy.start()

            for copy in load(expert):
                copy.wait()
            values = dot(rows[...], weights[expert])
            weight = dot(side[...], spread[expert])
            for half in range(2):
                gate_value = values[:, 2 * half * part : (2 * half + 1) * part]
                up_value = values[:, (2 * half + 1) * part : (2 * half + 2) * part]
                sigmoid = jax.nn.sigmoid(gate_value)
                silu = gate_value * sigmoid
                place = half * experts + expert
                grad = wide(grads[place])
                gate_grad[place] = low(grad * up_value * (sigmoid + silu * (1.0 - sigmoid)))
                up_grad[place] = low(grad * silu)
                hidden[place] = low(silu * up_value * weight)
            return carry

        lax.fori_loop(0, experts, work, 0)
        out_copy.start()

    tile = outs[0].shape[1]
    columns = pl.ds(pl.multiple_of(step * tile, tile), tile)
    total = None
    for expert in range(experts):
        for half in range(2):
            place = half * experts + expert
            for index, grad in enumerate((gate_grad, up_grad)):
                first = (2 * half + index) * part
                term = dot_t(grad[place], weights[expert, columns, first : first + part])
                total = term if total is None else total + term
    write_rows(total, outs, near, span, levels)

    @pl.when(step == pl.num_programs(0) - 1)
    def _():
        out_copy.wait()


def copy_places(pieces, places, rows, side, row_sems, side_sems):
    width, copies = rows.shape[1], []
    for piece, targets in zip(pieces, places):
        for source, target, size in targets:
            taken, place = piece.at[pl.ds(source, size)], pl.ds(target, size)
            slot = len(copies) // 2
            copies.append(
                pltpu.make_async_copy(
                    taken.at[:, pl.ds(0, width)], rows.at[place], row_sems.at[slot]
                )
            )
            copies.append(
                pltpu.make_async_copy(
                    taken.at[:, pl.ds(width, side.shape[1])], side.at[place], side_sems.at[slot]
                )
            )
    return copies


def whole_call(pieces, cot_plane, gates, ups, downs, spread, near, span, block_rows):
    count = len(pieces)
    experts, width, part = gates[0].shape
    size = pieces[0].shape[0]
    rows = size * count
    tile = min(width, 512)
    shape = (2 * experts, rows, part)
    slots = pltpu.VMEM(shape, jnp.bfloat16)
    cot_pieces, places = [], []
    for across, column in enumerate(cot_plane):
        down = 0
        for piece in column:
            targets = []
            for source in range(0, piece.shape[0], block_rows):
                targets.append((source, (down * near + across) * block_rows, block_rows))
                down += 1
            cot_pieces.append(piece)
            places.append(targets)
    blocks = rows // block_rows
    sizes = block_sizes(rows, near, span)
    return kernel_call(
        functools.partial(whole_kernel, count, near, span, span, places),
        (width // tile,),
        [ANY] * (count + 4) + [whole(spread)] + [ANY] * (2 + len(cot_pieces)),
        [pl.BlockSpec((size, tile), lambda n: (0, n)) for size in sizes] + [ANY],
        [((size, width), jnp.bfloat16) for size in sizes] + [(shape, jnp.bfloat16)],
        [*pieces, gates[0], ups[0], gates[1], ups[1], spread, *downs, *cot_pieces],
        20 * rows * experts * part * width,
        [
            pltpu.VMEM((rows, width), jnp.bfloat16),
            pltpu.VMEM((experts, width, 4 * part), jnp.bfloat16),
            slots,
            slots,
            slots,
            slots,
            pltpu.SemaphoreType.DMA((experts,)),
            pltpu.SemaphoreType.DMA((count,)),
            pltpu.SemaphoreType.DMA,
            pltpu.VMEM((rows, width), jnp.bfloat16),
            pltpu.VMEM((rows, spread.shape[1]), jnp.bfloat16),
            pltpu.VMEM((experts // 2 * 2, 2 * part, width), jnp.bfloat16),
            pltpu.SemaphoreType.DMA((blocks,)),
            pltpu.SemaphoreType.DMA((blocks,)),
            pltpu.SemaphoreType.DMA((experts // 2 * 2,)),
        ],
    )


def down_kernel(count, span, *refs):
    hiddens, (down_own, down_other), outs = refs[:count], refs[count : count + 2], refs[count + 2 :]
    places, _, part = hiddens[0].shape
    near = len(outs) // (count * span)
    size = outs[0].shape[0]
    for index, hidden in enumerate(hiddens):
        total = None
        for place in range(places):
            down = down_own if place < places // 2 else down_other
            first = place % (places // 2) * part
            term = dot(hidden[place], down[first : first + part, :])
            total = term if total is None else total + term
        for across, target, first in plane_order(near, span, size):
            block = (index * near + across) * span + target // size
            outs[block][...] = low(total[first : first + size])


def down_call(hiddens, downs, near, span, size):
    places, rows, part = hiddens[0].shape
    hidden, width = downs[0].shape
    tile = min(width, 512)
    count = len(hiddens)
    down_block = pl.BlockSpec((hidden, tile), lambda n: (0, n))
    outs = kernel_call(
        functools.partial(down_kernel, count, span),
        (width // tile,),
        [whole(array) for array in hiddens] + [down_block] * 2,
        [pl.BlockSpec((size, tile), lambda n: (0, n))] * (count * near * span),
        [((size, width), jnp.bfloat16)] * (count * near * span),
        [*hiddens, *downs],
        4 * count * rows * hidden * width,
    )
    blocks = [list(outs[index * span : (index + 1) * span]) for index in range(count * near)]
    return [blocks[index * near : (index + 1) * near] for index in range(count)]


def backward_kernel(width, share, count, scalars, *refs):
    pieces = refs[:count]
    (output_weight, mix_in, mix_out, select, queries, keys, values, attended, query_raw, key_raw,
     query_gain, key_gain, cosine, sine, mask) = refs[count : count + 15]
    (query_out, key_out, value_out, inner_out, mix_in_grad, mix_out_grad) = refs[
        count + 15 : count + 21
    ]
    branch, mixed_grad, grads, sems = refs[count + 21 :]
    size = pieces[0].shape[0]
    rows, local = grads.shape
    heads = local // HD
    copies = []
    for index, piece in enumerate(pieces):
        place = pl.ds(pl.multiple_of(scalars[index] * size, size), size)
        copies.append(pltpu.make_async_copy(piece, branch.at[place], sems.at[index]))
    for copy in copies:
        copy.start()
    for copy in copies:
        copy.wait()
    mixed_grad[...] = low(wide(low(dot_t(branch[:, :width], mix_out[...]))) * select[...])
    grads[...] = low(
        dot_t(branch[:, :width], output_weight[...]) + dot_t(mixed_grad[...], mix_in[...])
    )
    columns = pl.ds(pl.multiple_of(scalars[count] * share, share), share)
    mix_out_grad[...] = sliced(t_dot(branch[:, width:], branch[:, columns]))
    scale = HD ** (-0.5)
    lane = lax.broadcasted_iota(jnp.int32, (rows, 128), 1)
    sums = jnp.zeros((rows, 128), jnp.float32)
    for head in range(heads):
        part = slice(head * HD, (head + 1) * HD)
        query, key, value = queries[:, part], keys[:, part], values[:, part]
        grad = grads[:, part]
        scores = dot_t(query, key) * scale + mask[...]
        raised = jnp.exp(scores - jnp.max(scores, axis=1, keepdims=True))
        weights = raised * (1.0 / jnp.sum(raised, axis=1, keepdims=True))
        weight_grad = dot_t(grad, value)
        center = jnp.sum(weights * weight_grad, axis=1, keepdims=True)
        score_grad = low(weights * (weight_grad - center))
        value_out[:, part] = low(t_dot(low(weights), grad))
        query_grad = dot(score_grad, key) * scale
        key_grad = t_dot(score_grad, query) * scale
        query_grad = query_grad * cosine[...] - turned(query_grad) * sine[...]
        key_grad = key_grad * cosine[...] - turned(key_grad) * sine[...]
        query_grad = query_grad * wide(query_gain[:, part])
        key_grad = key_grad * wide(key_gain[:, part])
        query_out[:, part] = query_grad
        key_out[:, part] = key_grad
        query_inner = jnp.sum(query_grad * query_raw[:, part], axis=1, keepdims=True)
        key_inner = jnp.sum(key_grad * key_raw[:, part], axis=1, keepdims=True)
        sums = sums + jnp.where(lane == 0, query_inner, jnp.where(lane == 1, key_inner, 0.0))
    mix_in_grad[...] = sliced(t_dot(mixed_grad[...], attended[...]))
    inner_out[...] = jnp.transpose(sums)[:8]


def sliced(values):
    total = values[:RANK]
    for index in range(1, values.shape[0] // RANK):
        total = total + values[index * RANK : (index + 1) * RANK]
    return low(total)


def backward_call(
    scalars, pieces, output_weight, mix_in, mix_out, select, states, raws, gains, tables, mask, share
):
    rows, local = raws[0].shape
    width = output_weight.shape[1]
    operands = [
        scalars, *pieces, output_weight, mix_in, mix_out, select, *states, *raws, *gains, *tables, mask,
    ]
    out_shape = [((rows, local), jnp.float32)] * 2 + [((rows, local), jnp.bfloat16)]
    out_shape += [((8, rows), jnp.float32), ((RANK, local), jnp.bfloat16)]
    out_shape += [((RANK, share), jnp.bfloat16)]
    return kernel_call(
        functools.partial(backward_kernel, width, share, len(pieces)),
        (1,),
        [ANY] * len(pieces) + [whole(array) for array in operands[len(pieces) + 1 :]],
        [pl.BlockSpec(shape, lambda *_: (0, 0)) for shape, _ in out_shape],
        out_shape,
        operands,
        14 * rows * rows * local + 2 * rows * local * width,
        [
            pltpu.VMEM((rows, pieces[0].shape[1]), jnp.bfloat16),
            pltpu.VMEM((rows, mix_out.shape[0]), jnp.bfloat16),
            pltpu.VMEM((rows, local), jnp.bfloat16),
            pltpu.SemaphoreType.DMA((len(pieces),)),
        ],
        1,
    )


def adapter_lanes(index, select):
    row = lax.broadcasted_iota(jnp.int32, (128, 128), 0) - index * RANK
    lane = lax.broadcasted_iota(jnp.int32, (128, 128), 1)
    return low(jnp.where(lax.rem(lane, RANK) == row, select, 0.0))


def raw_kernel(
    width, inner, squares, query_grad, key_grad, value_grad, query_raw, key_raw, lowrank,
    adapt_out, select, raw, lowrank_out, adapt_grad,
):
    inverse = lax.rsqrt(spread_columns(squares[...]) / width + EPSILON)
    totals = spread_columns(inner[...]) / width
    for index, (grad, value) in enumerate(((query_grad, query_raw), (key_grad, key_raw))):
        scale = inverse[:, index : index + 1]
        factor = scale**3 * totals[:, index : index + 1]
        raw[index] = low(scale * grad[...] - value[...] * factor)
    raw[2] = value_grad[...]
    lowrank_part = None
    for index in range(3):
        part = low(dot_t(raw[index], adapt_out[index]) * select[...])
        term = dot_t(part, adapter_lanes(index, select[...]))
        lowrank_part = term if lowrank_part is None else lowrank_part + term
        adapt_grad[index * RANK : (index + 1) * RANK, :] = sliced(
            t_dot(lowrank[index], raw[index])
        )
    lowrank_out[...] = low(lowrank_part)


def raw_call(inner, squares, grads, raws, lowrank, adapt_out, select, width):
    rows, local = raws[0].shape
    operands = [inner, squares, *grads, *raws, lowrank, adapt_out, select]
    out_shape = [((3, rows, local), jnp.bfloat16), ((rows, 128), jnp.bfloat16)]
    out_shape += [((3 * RANK, local), jnp.bfloat16)]
    return kernel_call(
        functools.partial(raw_kernel, width),
        (1,),
        [whole(array) for array in operands],
        [pl.BlockSpec(shape, lambda *_, size=len(shape): (0,) * size) for shape, _ in out_shape],
        out_shape,
        operands,
        6 * rows * local * 256,
    )


def weight_kernel(size, scalars, raw, query_weight, key_weight, value_weight, mine, theirs):
    levels = mine.shape[0] // size
    for out, offset in ((theirs, 1 - scalars[0]), (mine, scalars[0])):
        total = None
        for index, weight in enumerate((query_weight, key_weight, value_weight)):
            taken = [
                raw[index, pl.ds(pl.multiple_of((2 * level + offset) * size, size), size), :]
                for level in range(levels)
            ]
            term = dot_t(jnp.concatenate(taken, axis=0), weight[...])
            total = term if total is None else total + term
        out[...] = total.astype(out.dtype)


def weight_call(scalars, raw, weights, size):
    _, rows, local = raw.shape
    width = weights[0].shape[0]
    tile = min(width, 512)
    operands = [scalars, raw, *weights]
    out_shape = [((rows // 2, width), jnp.float32), ((rows // 2, width), jnp.bfloat16)]
    return kernel_call(
        functools.partial(weight_kernel, size),
        (width // tile,),
        [whole(raw)] + [pl.BlockSpec((tile, local), lambda n, *_: (n, 0))] * 3,
        [pl.BlockSpec((rows // 2, tile), lambda n, *_: (0, n))] * 2,
        out_shape,
        operands,
        6 * rows * local * width,
        (),
        1,
    )


def input_kernel(
    rank, kept, came, lowrank, adapt_in, select, tokens, gain, resid_grad, out
):
    grad = kept[...] + wide(came[...])
    for index in range(3):
        part = low(dot(lowrank[...], adapter_lanes(index, select[...])))
        grad = grad + dot_t(part, adapt_in[index])
    scaled = grad * wide(gain[...])
    inputs = wide(tokens[...])
    width = inputs.shape[1]
    inverse = lax.rsqrt(jnp.mean(inputs * inputs, axis=1, keepdims=True) + EPSILON)
    inner = jnp.sum(scaled * inputs, axis=1, keepdims=True)
    out[...] = low(
        resid_grad[...] + norm_back(scaled, inputs, inverse, width, inner)
    )


def input_call(rank, kept, came, lowrank, adapt_in, select, tokens, gain, resid_grad):
    operands = [rank, kept, came, lowrank, adapt_in, select, tokens, gain, resid_grad]
    rows, width = kept.shape
    return kernel_call(
        input_kernel,
        (1,),
        [
            whole(kept),
            whole(came),
            pl.BlockSpec((rows, lowrank.shape[1]), lambda n, rank: (rank[0], 0)),
            whole(adapt_in),
            whole(select),
            pl.BlockSpec((rows, width), lambda n, rank: (rank[0], 0)),
            whole(gain),
            whole(resid_grad),
        ],
        [pl.BlockSpec((rows, width), lambda *_: (0, 0))],
        [((rows, width), jnp.bfloat16)],
        operands,
        8 * rows * width * 128,
        (),
        1,
    )[0]


def compact_kernel(
    scalars, lowrank_grad, normed, mix_out_grad, adapt_grad, mix_in_grad, select, out, held, sem
):
    share = out.shape[1]
    columns = pl.ds(pl.multiple_of(scalars[0] * share, share), share)
    copy = pltpu.make_async_copy(normed.at[:, columns], held, sem)
    copy.start()
    copy.wait()
    first = low(t_dot(lowrank_grad[...], held[...]))[: 3 * RANK]
    out[: 3 * RANK] = first
    out[3 * RANK : 4 * RANK] = mix_out_grad[...]
    out[4 * RANK : 7 * RANK] = adapt_grad[...]
    out[7 * RANK : 8 * RANK] = mix_in_grad[...]
    chosen = low(jnp.broadcast_to(select[...], (RANK, 128)))
    out[8 * RANK :] = jnp.concatenate([chosen] * (share // 128), axis=1)


def compact_call(scalars, lowrank_grad, normed, mix_out_grad, adapt_grad, mix_in_grad, select):
    rows = normed.shape[0]
    share = adapt_grad.shape[1]
    operands = [scalars, lowrank_grad, normed, mix_out_grad, adapt_grad, mix_in_grad, select]
    return kernel_call(
        compact_kernel,
        (1,),
        [whole(lowrank_grad), ANY] + [whole(array) for array in operands[3:]],
        [pl.BlockSpec((9 * RANK, share), lambda *_: (0, 0))],
        [((9 * RANK, share), jnp.bfloat16)],
        operands,
        2 * rows * share * 128,
        [pltpu.VMEM((rows, share), jnp.bfloat16), pltpu.SemaphoreType.DMA],
        1,
    )[0]


def spread_kernel(order, *refs):
    pieces, out = refs[:-1], refs[-1]
    step = pl.program_id(0)
    for index, piece in enumerate(pieces):

        @pl.when(step == index)
        def _():
            out[...] = wide(piece[...])


def spread_call(order, pieces):
    size, width = pieces[0].shape
    count = len(pieces)
    return kernel_call(
        spread_kernel,
        (count,),
        [whole(piece) for piece in pieces],
        [pl.BlockSpec((size, width), lambda step, order: (order[step], 0))],
        [((count * size, width), jnp.float32)],
        [order, *pieces],
        size * width,
        (),
        1,
    )[0]


def assemble_kernel(trees, order, *refs):
    count = len(refs) - 5
    own, pieces = refs[0], refs[1:count]
    in_grad, out_grad, mix_in_grad, mix_out_grad = refs[count : count + 4]
    (choice,) = refs[count + 4 :]
    share = own.shape[1]
    block = own.shape[0] // trees
    row = lax.broadcasted_iota(jnp.int32, (RANK, 128), 0)
    lane = lax.broadcasted_iota(jnp.int32, (RANK, 128), 1)
    same = lax.rem(lane, RANK) == row
    for tree in range(trees):
        chosen = own[tree * block + 8 * RANK : tree * block + 9 * RANK, :128]
        choice[tree * RANK : (tree + 1) * RANK] = low(jnp.where(same, wide(chosen), 0.0))

    def kind(source, stride, index):
        return jnp.concatenate(
            [
                source[tree * stride + index * RANK : tree * stride + (index + 1) * RANK, :]
                for tree in range(trees)
            ],
            axis=0,
        )

    for index in range(3):
        out_grad[index] = t_dot(choice[...], kind(own, block, 4 + index))
    mix_in_grad[...] = t_dot(kind(own, block, 7), choice[...])
    for place, source in enumerate((own, *pieces)):
        stride = block if place == 0 else 4 * RANK
        start = pl.ds(pl.multiple_of(order[place] * share, share), share)
        for index in range(3):
            in_grad[index, start, :] = t_dot(kind(source, stride, index), choice[...])
        mix_out_grad[:, start] = t_dot(choice[...], kind(source, stride, 3))


def assemble_call(order, own, pieces, trees):
    share = own.shape[1]
    count = 1 + len(pieces)
    width = count * share
    out_shape = [((3, width, 128), jnp.float32), ((3, 128, share), jnp.float32)]
    out_shape += [((share, 128), jnp.float32), ((128, width), jnp.float32)]
    operands = [order, own, *pieces]
    return kernel_call(
        functools.partial(assemble_kernel, trees),
        (1,),
        [whole(array) for array in operands[1:]],
        [pl.BlockSpec(shape, lambda *_, size=len(shape): (0,) * size) for shape, _ in out_shape],
        out_shape,
        operands,
        2 * trees * RANK * 128 * width * 4,
        [pltpu.VMEM((trees * RANK, 128), jnp.bfloat16)],
        1,
    )


def body(
    tokens,
    cotangent,
    attn_gain,
    ffn_gain,
    query_gain,
    key_gain,
    query_weight,
    key_weight,
    value_weight,
    output_weight,
    expert_gate,
    expert_up,
    expert_down,
    adapt_in,
    adapt_out,
    adapt_in_out,
    adapt_out_out,
    routes,
    gate_weights,
    block_parent,
    adapter_pick,
):
    rows_here, model_width = tokens.shape
    tensor_rank = lax.axis_index("tensor")
    tensor_count = lax.axis_size("tensor")
    owners = lax.axis_size("expert")
    owner_rank = lax.axis_index("expert")
    axes = divide_axes(owners, tensor_count)
    far, near, span = axes["z"][1], axes["x"][1], axes["y"][1]
    experts_here, _, hidden_here = expert_gate.shape
    experts_all = experts_here * owners
    column_share = model_width // tensor_count
    row_share = rows_here // tensor_count
    hold = lax.optimization_barrier
    level, core = tensor_rank // 2, tensor_rank % 2
    rank_list = jnp.reshape(tensor_rank, (1,)).astype(jnp.int32)

    def own_rows(array):
        return lax.dynamic_slice_in_dim(array, tensor_rank * row_share, row_share, 0)

    routes_wide = jnp.swapaxes(routes, 0, 1)
    weights_wide = jnp.swapaxes(gate_weights, 0, 1)
    route_weights = jnp.sum(
        jnp.where(
            routes_wide[:, :, None] == jnp.arange(experts_all, dtype=jnp.int32)[None, None, :],
            weights_wide[:, :, None],
            0.0,
        ),
        axis=0,
    )
    weights_high = low(route_weights)
    weights_low = low(route_weights - wide(weights_high))
    side_width = -(-2 * experts_all // 128) * 128
    side_pad = jnp.zeros((rows_here, side_width - 2 * experts_all), jnp.bfloat16)
    side_rows = jnp.concatenate([weights_high, weights_low, side_pad], axis=1)
    cot_queue = []
    for step in range(span):
        place = ((level + span - step) % span * 2 + core) * row_share
        cot_queue.append(
            jnp.concatenate(
                [
                    lax.dynamic_slice_in_dim(cotangent, place, row_share, 0),
                    lax.dynamic_slice_in_dim(side_rows, place, row_share, 0),
                ],
                axis=1,
            )
        )
    cot_queue = [jnp.concatenate(cot_queue, axis=0)]
    side_index = jnp.arange(side_width, dtype=jnp.int32)
    hidden_owner = (
        owner_rank * experts_here
        + jnp.arange(experts_here * hidden_here, dtype=jnp.int32) // hidden_here
    )
    spread_flat = low(
        (side_index[:, None] % experts_all == hidden_owner[None, :])
        & (side_index[:, None] < 2 * experts_all)
    )
    spread = jnp.swapaxes(spread_flat.reshape(side_width, experts_here, hidden_here), 0, 1)

    cot_planes = [None] * far
    cot_queue.append(turn(cot_queue[0], axes, "z", 1))
    cot_planes[0] = ring(cot_queue[0], axes, "x")
    first_gain, second_gain = attn_gain[None, :], ffn_gain[None, :]
    gains = (query_gain[None, :], key_gain[None, :])
    reached = ancestry(block_parent)
    cosine_table, sine_table = rope_tables(reached, rows_here // block_parent.shape[0], HD)
    signs = jnp.where(jnp.arange(HD) < HD // 2, -1.0, 1.0)[None, :]
    tables = (cosine_table, sine_table * signs)
    mask = jnp.where(token_mask(reached[0], rows_here), 0.0, MASKED_SCORE)
    select = jnp.repeat(wide(adapter_pick), RANK, axis=1)
    weights = (query_weight, key_weight, value_weight)
    normed_in, lowrank, *raws, squares = project_call(
        tokens, first_gain, weights, adapt_in, adapt_out, select
    )

    def halves(rows):
        return [rows[: rows.shape[0] // 2], rows[rows.shape[0] // 2 :]]

    squares = sum_tensor(squares, axes)
    held = (squares, cot_queue[1], cot_planes[0], expert_gate, expert_up, tables, mask)
    squares, cot_queue[1], cot_planes[0], expert_gate, expert_up, tables, mask = hold(held)
    gates = (expert_gate, turn(expert_gate, axes, "c", 1))
    ups = (expert_up, turn(expert_up, axes, "c", 1))
    cot_queue[1] = halves(cot_queue[1])
    cot_later = turn(cot_queue[1][0], axes, "z", 1)
    cot_across = ring(cot_queue[1][0], axes, "x")[1:]
    *states, mine, theirs = attend_call(
        jnp.reshape(core, (1,)).astype(jnp.int32),
        squares,
        raws,
        gains,
        tables,
        mask,
        output_weight,
        adapt_in_out,
        row_share,
    )
    cot_later, cot_across, mine, theirs = hold((cot_later, cot_across, mine, theirs))

    theirs = turn(theirs, axes, "c", 1)
    branch_kept, branch_sent = scatter_core(mine, theirs, axes)
    branch_sent, cot_queue[1] = hold((branch_sent, cot_queue[1]))
    down_tall = expert_down.reshape(-1, model_width)
    branch_came = turn(branch_sent, axes, "y", -1)
    cot_later = [cot_later, turn(cot_queue[1][1], axes, "z", 1)]
    cot_second = ring(cot_queue[1][1], axes, "x")[1:]
    held = (branch_came, cot_later, cot_second, gates, ups, down_tall)
    branch_came, cot_later, cot_second, gates, ups, down_tall = hold(held)
    downs = (down_tall, turn(down_tall, axes, "c", 1))
    cot_queue.append(jnp.concatenate(cot_later, axis=0))
    cot_planes[1] = [cot_queue[1]] + [list(pair) for pair in zip(cot_across, cot_second)]
    cot_planes[0] = [[piece] for piece in cot_planes[0]]
    resid_rows, norm_plane, mixed_rows = resid_call(
        rank_list, branch_kept, branch_came, tokens, adapt_out_out, select, second_gain
    )

    norm_queue = [norm_plane, turn(norm_plane, axes, "z", 1)]
    norm_pairs = [ring(norm_plane, axes, "x")]
    backs, sides = [None] * far, [None] * far

    def hidden_step(*indices):
        back, side = hidden_call(
            [cot_planes[index] for index in indices], downs, spread_flat, experts_here, row_share
        )
        for order, index in enumerate(indices):
            backs[index], sides[index] = (back, order * side.shape[0] // len(indices)), side
        return back

    def set_back(back, *indices):
        for index in indices:
            backs[index] = (back, backs[index][1])

    norm_planes = [None] * far
    held = (norm_queue[1], norm_pairs[0], downs, cot_queue[2])
    norm_queue[1], norm_pairs[0], downs, cot_queue[2] = hold(held)
    norm_planes[0] = ring(jnp.concatenate(norm_pairs[0], axis=0), axes, "y")
    norm_queue.append(turn(norm_queue[1], axes, "z", 1))
    norm_pairs.append(ring(norm_queue[1], axes, "x"))
    back_first = hidden_step(0, 1)
    held = (norm_planes[0], norm_queue[2], norm_pairs[1], cot_queue[2], back_first)
    norm_planes[0], norm_queue[2], norm_pairs[1], cot_queue[2], back_first = hold(held)
    set_back(back_first, 0, 1)
    parts, hiddens = [None] * far, [None] * far

    def expert_step(index):
        back, offset = backs[index]
        *parts[index], hiddens[index] = expert_call(
            norm_planes[index],
            gates,
            ups,
            spread,
            sides[index],
            back,
            offset,
            near,
            span if index else 0,
            span,
        )

    def whole_step(index):
        *parts[index], hiddens[index] = whole_call(
            norm_planes[index], cot_planes[index], gates, ups, downs, spread, near, span, row_share
        )

    norm_planes[1] = ring(jnp.concatenate(norm_pairs[1], axis=0), axes, "y")
    norm_queue.append(turn(norm_queue[2], axes, "z", 1))
    norm_pairs.append(ring(norm_queue[2], axes, "x"))
    cot_queue.append(turn(cot_queue[2], axes, "z", 1))
    cot_planes[2] = ring(cot_queue[2], axes, "x")
    expert_step(0)

    held = (norm_planes[1], norm_queue[3], norm_pairs[2], parts[0])
    norm_planes[1], norm_queue[3], norm_pairs[2], parts[0] = hold(held)
    norm_planes[2] = ring(jnp.concatenate(norm_pairs[2], axis=0), axes, "y")
    norm_pairs.append(ring(norm_queue[3], axes, "x"))
    expert_step(1)

    held = (norm_planes[2], norm_pairs[3], parts[1], cot_queue[3], cot_planes[2])
    norm_planes[2], norm_pairs[3], parts[1], cot_queue[3], cot_planes[2] = hold(held)
    norm_planes[3] = ring(jnp.concatenate(norm_pairs[3], axis=0), axes, "y")
    came, last = [None] * far, [None] * far
    came[1] = scatter_first(parts[1], axes)
    came_x = send_sum(parts[0], axes, "x")
    cot_across = [turn(piece, axes, "z", 1) for piece in cot_planes[2][1:]]
    cot_planes[2] = [[piece] for piece in cot_planes[2]]
    whole_step(2)

    held = (norm_planes[3], came[1], parts[2], came_x, cot_across)
    norm_planes[3], came[1], parts[2], came_x, cot_across = hold(held)
    cot_planes[3] = [[piece] for piece in [cot_queue[3]] + cot_across]
    came[2] = scatter_first(parts[2], axes)
    last[1] = scatter_second(parts[1], came[1], axes)
    own_sums = [
        [block(parts[0][0], k, span), block(came_x, k, span)] for k in range(span)
    ]
    came_y = send_sum([None] + [low(pair[0] + pair[1]) for pair in own_sums[1:]], axes, "y")
    whole_step(3)

    held = (last[1], came[2], came_y, parts[3], hiddens)
    last[1], came[2], came_y, parts[3], hiddens = hold(held)
    came[3] = scatter_first(parts[3], axes)
    last[2] = scatter_second(parts[2], came[2], axes)
    ring_sum = turn(low(scatter_last(parts[1], came[1], last[1], axes)), axes, "z", 1)
    mixes, mix_came = [None] * far, [None] * far

    def down_step(*indices):
        done = down_call([hiddens[index] for index in indices], downs, near, span, row_share)
        for index, blocks in zip(indices, done):
            mixes[index] = blocks

    down_step(3, 0)

    held = (ring_sum, came[3], last[2], mixes[3], mixes[0], hiddens)
    ring_sum, came[3], last[2], mixes[3], mixes[0], hiddens = hold(held)
    last[3] = scatter_second(parts[3], came[3], axes)
    ring_sum = turn(
        low(wide(ring_sum) + scatter_last(parts[2], came[2], last[2], axes)), axes, "z", 1
    )
    down_step(2)

    ring_sum, last[3], hiddens, mixes[2] = hold((ring_sum, last[3], hiddens, mixes[2]))
    ring_sum = turn(
        low(wide(ring_sum) + scatter_last(parts[3], came[3], last[3], axes)), axes, "z", 1
    )
    down_step(1)
    half_width = model_width // span

    def column_sum(arrays, owner):
        first = owner * half_width
        return sum(
            wide(lax.dynamic_slice_in_dim(array, first, half_width, 1)) for array in arrays
        )

    def mix_columns(index, owner):
        rows = [column_sum(arrays, owner) for arrays in mix_held[index]]
        return jnp.concatenate(rows, axis=0)

    def mix_sent(index):
        return low(mix_columns(index, (level + 1) % span))

    def mix_down(index, came_rows):
        came_rows = turn(came_rows, axes, "y", -1)
        for step in range(span - 2, 0, -1):
            total = mix_columns(index, (level + span - step) % span) + rolled(came_rows)
            came_rows = turn(low(total), axes, "y", -1)
        return came_rows

    def rolled(rows):
        size = rows.shape[0] // span
        return wide(jnp.concatenate([rows[size:], rows[:size]], axis=0))

    def mix_total(index):
        return mix_columns(index, level) + rolled(mix_parts[index])

    def mix_send(index, down):
        return send_sum([blocks[down] for blocks in mixes[index]], axes, "x")

    mix_held = [None] * far
    mix_parts = [None] * far

    ring_sum, mixes = hold((ring_sum, mixes))
    mix_early = mix_send(3, 0)
    ffn_rows_grad = wide(ring_sum) + (own_sums[0][0] + own_sums[0][1]) + wide(came_y)
    second_scaled = ffn_rows_grad * wide(second_gain)
    second_inverse = lax.rsqrt(
        jnp.mean(resid_rows * resid_rows, axis=1, keepdims=True) + EPSILON
    )
    resid_grad_rows = wide(own_rows(cotangent)) + norm_back(
        second_scaled,
        resid_rows,
        second_inverse,
        model_width,
        jnp.sum(second_scaled * resid_rows, axis=1, keepdims=True),
    )
    branch_sent = jnp.concatenate([low(resid_grad_rows), mixed_rows], axis=1)
    branch_pieces = ring(branch_sent, axes, "y")
    branch_other = turn(branch_pieces[0], axes, "c", 1)
    order = jnp.stack(
        [
            (level + span - step) % span * 2 + side
            for side in (core, 1 - core)
            for step in range(span)
        ]
    ).astype(jnp.int32)

    branch_pieces, mix_early, mixes = hold((branch_pieces, mix_early, mixes))
    branch_others = [turn(piece, axes, "c", 1) for piece in branch_pieces[1:]]
    branch_others, branch_other, mixes = hold((branch_others, branch_other, mixes))
    branch_pieces = branch_pieces + [branch_other] + branch_others
    mix_late = [mix_send(3, down) for down in range(1, span)]
    mix_next = mix_send(2, 0)
    mix_far = [[turn(part, axes, "z", -1) for part in blocks] for blocks in mixes[1][1:]]
    query_grad, key_grad, value_grad, inner, mix_in_grad, mix_out_grad = backward_call(
        jnp.concatenate([order, rank_list]),
        branch_pieces,
        output_weight,
        adapt_in_out,
        adapt_out_out,
        select,
        states,
        raws[:2],
        gains,
        tables,
        mask,
        column_share,
    )

    held = (inner, mix_late, mix_next, mix_far, mixes)
    inner, mix_late, mix_next, mix_far, mixes = hold(held)
    mix_held[3] = list(zip(mixes[3][0], [mix_early] + mix_late))
    mix_ready = mix_sent(3)
    inner = sum_tensor(inner, axes)
    inner, mix_ready, mixes = hold((inner, mix_ready, mixes))
    mix_parts[3] = mix_down(3, mix_ready)
    mix_last = [mix_send(2, down) for down in range(1, span)]
    mix_near = [turn(mixes[1][0][0], axes, "z", -1)]
    raw_grads, lowrank_part, adapt_grad = raw_call(
        inner,
        squares,
        (query_grad, key_grad, value_grad),
        raws[:2],
        lowrank,
        adapt_out,
        select,
        model_width,
    )
    lowrank_came = turn(lowrank_part, axes, "c", 1)
    lowrank_part, lowrank_came, raw_grads = hold((lowrank_part, lowrank_came, raw_grads))
    lowrank_part = low(wide(lowrank_part) + wide(lowrank_came))
    lowrank_parts = ring(lowrank_part, axes, "y")
    normed_mine, normed_theirs = weight_call(
        jnp.reshape(core, (1,)).astype(jnp.int32), raw_grads, weights, row_share
    )

    held = (normed_mine, normed_theirs, lowrank_parts, mix_parts[3], mix_last, mix_near, mixes)
    held = hold(held)
    normed_mine, normed_theirs, lowrank_parts, mix_parts[3], mix_last, mix_near, mixes = held
    normed_theirs = hold(turn(normed_theirs, axes, "c", 1))
    normed_kept, normed_sent = scatter_core(normed_mine, normed_theirs, axes)
    held = (normed_sent, lowrank_parts, mixes, mix_last)
    normed_sent, lowrank_parts, mixes, mix_last = hold(held)
    normed_came = turn(normed_sent, axes, "y", -1)
    lowrank_grad = low(sum(wide(part) for part in lowrank_parts))
    mix_near = mix_near + [turn(part, axes, "z", -1) for part in mixes[1][0][1:]]
    compact = compact_call(
        rank_list, lowrank_grad, normed_in, mix_out_grad, adapt_grad, mix_in_grad, select
    )
    trees = ring(compact, axes, "x")
    mix_held[2] = list(zip(mixes[2][0], [mix_next] + mix_last))
    mix_ready = mix_sent(2)
    trees, mix_near, mix_ready, normed_came = hold((trees, mix_near, mix_ready, normed_came))

    tree_queue = [jnp.concatenate(trees, axis=0)]
    tree_queue.append(turn(tree_queue[-1], axes, "z", 1))
    input_rows = input_call(
        rank_list,
        normed_kept,
        normed_came,
        lowrank_grad,
        adapt_in,
        select,
        tokens,
        first_gain,
        resid_grad_rows,
    )
    input_rows, tree_queue = hold((input_rows, tree_queue))
    input_held = ring(input_rows, axes, "y")
    tree_queue.append(turn(tree_queue[-1], axes, "z", 1))
    for across in range(1, near):
        pairs = zip(mixes[0][across], mix_far[across - 1])
        mixes[0][across] = [low(wide(mine) + wide(other)) for mine, other in pairs]
    whole_blocks = [jnp.concatenate(blocks, axis=0) for blocks in mixes[0][1:]]
    mix_came[0] = send_sum([None] + whole_blocks, axes, "x")
    mix_parts[2] = mix_down(2, mix_ready)
    tree_queue, mixes, input_held = hold((tree_queue, mixes, input_held))
    tree_queue.append(turn(tree_queue[-1], axes, "z", 1))
    input_pieces = input_held + [turn(piece, axes, "c", 1) for piece in input_held]
    mix_parts[2], tree_queue = hold((mix_parts[2], tree_queue))

    trees = jnp.concatenate(tree_queue, axis=0)
    shared = trees.reshape(owners, -1, column_share)[:, : 4 * RANK]
    shared = ring(shared.reshape(-1, column_share), axes, "y")
    mix_sum = turn(low(mix_total(2)), axes, "z", 1)
    shared, mix_came[0] = hold((shared, mix_came[0]))
    arrived = [mix_came[0][down * row_share : (down + 1) * row_share] for down in range(span)]
    mix_held[0] = [list(arrays) for arrays in zip(mixes[0][0], arrived, mix_near)]
    mix_held[0][0].append(resid_rows)
    shared = shared + [turn(piece, axes, "c", 1) for piece in shared]
    mix_parts[0] = mix_down(0, mix_sent(0))
    shared, mix_sum = hold((shared, mix_sum))
    mix_sum = turn(low(wide(mix_sum) + mix_total(3)), axes, "z", 1)
    grad_adapt_in, grad_adapt_out, grad_adapt_in_out, grad_adapt_out_out = assemble_call(
        order, trees, shared[1:], owners
    )
    input_grad = spread_call(order, input_pieces)
    held = (mix_parts[0], mix_sum, grad_adapt_in, input_grad)
    mix_parts[0], mix_sum, grad_adapt_in, input_grad = hold(held)
    layer_columns = low(mix_total(0) + wide(mix_sum))
    layer_out = place_columns(layer_columns, axes)
    return (
        layer_out,
        input_grad,
        grad_adapt_in,
        grad_adapt_out,
        grad_adapt_in_out,
        grad_adapt_out_out,
    )


def solution(mesh):
    return jax.shard_map(
        body,
        mesh=mesh,
        in_specs=(
            P("expert", None),
            P("expert", None),
            P(),
            P(),
            P("tensor"),
            P("tensor"),
            P(None, "tensor"),
            P(None, "tensor"),
            P(None, "tensor"),
            P("tensor", None),
            P("expert", None, "tensor"),
            P("expert", None, "tensor"),
            P("expert", "tensor", None),
            P(),
            P(None, None, "tensor"),
            P("tensor", None),
            P(),
            P("expert", None),
            P("expert", None),
            P("expert"),
            P("expert", None),
        ),
        out_specs=(
            P("expert", "tensor"),
            P("expert", None),
            P(),
            P(None, None, "tensor"),
            P("tensor", None),
            P(),
        ),
        check_vma=False,
    )
```

```python
import functools

import jax
import jax.numpy as jnp
from jax import lax
from jax.experimental import pallas as pl
from jax.experimental.pallas import tpu as pltpu
from jax.sharding import PartitionSpec as P

HD = 128
RANK = 16


EPSILON = 1e-05
ROPE_BASE = 10000.0
MASKED_SCORE = -1e30
VMEM_LIMIT = 56 * 2**20
CHUNK = 128


def ancestry(parents):
    blocks = parents.shape[0]
    places = jnp.arange(blocks, dtype=jnp.int32)
    walker = places
    reached = walker[:, None] == places[None, :]
    for _ in range(blocks - 1):
        hits = (walker[:, None] == places[None, :]).astype(jnp.int32)
        walker = jnp.sum(hits * parents[None, :], axis=1)
        reached = reached | (walker[:, None] == places[None, :])
    return reached[None]


def rope_tables(reached, block_span, head_size):
    depths = jnp.sum(reached.astype(jnp.int32), axis=2) - 1
    offsets = jnp.arange(block_span, dtype=jnp.int32)
    located = (
        (depths[:, :, None] * block_span + offsets[None, None, :]).reshape(-1).astype(jnp.float32)
    )
    halves = head_size // 2
    speeds = ROPE_BASE ** (-2.0 * jnp.arange(halves, dtype=jnp.float32) / head_size)
    angles = located[:, None] * speeds[None, :]
    angles = jnp.concatenate([angles, angles], axis=1)
    return (jnp.cos(angles), jnp.sin(angles))


def token_mask(reached, total_size):
    blocks = reached.shape[0]
    block_span = total_size // blocks
    widened = jnp.broadcast_to(
        reached[:, None, :, None], (blocks, block_span, blocks, block_span)
    ).reshape(total_size, total_size)
    positions = jnp.arange(total_size, dtype=jnp.int32)
    return widened & (positions[None, :] <= positions[:, None])


def norm_back(scaled_grad, values, inverse, model_width, inner_sum):
    return inverse * scaled_grad - values * inverse**3 * (inner_sum / model_width)


def divide_axes(owners, tensor_count):
    outer = 4
    return {
        "z": ("expert", outer, owners // outer, owners),
        "x": ("expert", owners // outer, 1, owners),
        "y": ("tensor", tensor_count // 2, 2, tensor_count),
        "c": ("tensor", 2, 1, tensor_count),
    }


def turn(array, axes, name, step):
    axis, length, stride, total = axes[name]
    pairs = []
    for index in range(total):
        place = (index // stride) % length
        moved = index + ((place + step) % length - place) * stride
        pairs.append((index, moved))
    return lax.ppermute(array, axis, pairs)


def ring(array, axes, name):
    held = [array]
    for _ in range(axes[name][1] - 1):
        held.append(turn(held[-1], axes, name, 1))
    return held


def wide(array):
    return array.astype(jnp.float32)


def low(array):
    return array.astype(jnp.bfloat16)


def send_sum(parts, axes, name):
    total = parts[-1]
    for part in parts[-2:0:-1]:
        total = low(wide(turn(total, axes, name, -1)) + wide(part))
    return turn(total, axes, name, -1)


def scatter_first(pieces, axes):
    span = axes["y"][1]
    return send_sum(pieces[:span], axes, "y"), send_sum(pieces[span:], axes, "x")


def block(array, index, count):
    size = array.shape[0] // count
    return wide(array[index * size : (index + 1) * size])


def scatter_second(pieces, came, axes):
    near, span = axes["x"][1], axes["y"][1]
    first = [low(block(pieces[0], k, near) + block(came[0], k, near)) for k in range(1, near)]
    second = [low(block(pieces[span], k, span) + block(came[1], k, span)) for k in range(1, span)]
    return send_sum([None] + first, axes, "x"), send_sum([None] + second, axes, "y")


def scatter_last(pieces, came, last, axes):
    near, span = axes["x"][1], axes["y"][1]
    first = block(pieces[0], 0, near) + block(came[0], 0, near) + wide(last[0])
    second = block(pieces[span], 0, span) + block(came[1], 0, span) + wide(last[1])
    return jnp.concatenate([first, second], axis=0)


def gather_tensor(rows, axes):
    held = ring(rows, axes, "y")
    return held + [turn(piece, axes, "c", 1) for piece in held]


def scatter_core(mine, came, axes):
    rank = lax.axis_index("tensor")
    span = axes["y"][1]
    size = mine.shape[0] // span
    total = None
    for step in range(span - 1, -1, -1):
        level = (rank // 2 + span - step) % span
        part = wide(lax.dynamic_slice_in_dim(mine, level * size, size, 0)) + wide(
            lax.dynamic_slice_in_dim(came, level * size, size, 0)
        )
        if step == 0:
            return part, total
        total = low(part if total is None else part + wide(turn(total, axes, "y", -1)))


def gather_x(rows, axes):
    return jnp.concatenate(ring(rows, axes, "x"), axis=0)


def place_columns(rows, axes):
    rank = lax.axis_index("tensor")
    span = axes["y"][1]
    size, share = rows.shape[0] // span, rows.shape[1] // 2
    level, core = rank // 2, rank % 2
    mine = lax.dynamic_slice_in_dim(rows, core * share, share, 1)
    theirs = turn(lax.dynamic_slice_in_dim(rows, (1 - core) * share, share, 1), axes, "c", 1)
    blocks = jnp.zeros((2 * span * size, share), rows.dtype)
    for step in range(span):
        place = (level + span - step) % span * 2
        for part, side in ((mine, core), (theirs, 1 - core)):
            taken = part[step * size : (step + 1) * size]
            blocks = lax.dynamic_update_slice_in_dim(blocks, taken, (place + side) * size, 0)
    return blocks


def sum_tensor(array, axes):
    total = wide(array) + wide(turn(array, axes, "c", 1))
    moving = total.astype(array.dtype)
    result = total
    for _ in range(axes["y"][1] - 1):
        moving = turn(moving, axes, "y", 1)
        result = result + wide(moving)
    return result


def dot(left, right):
    return jnp.dot(left, right, preferred_element_type=jnp.float32)


def dot_t(left, right):
    return lax.dot_general(
        left, right, (((1,), (1,)), ((), ())), preferred_element_type=jnp.float32
    )


def t_dot(left, right):
    return lax.dot_general(
        left, right, (((0,), (0,)), ((), ())), preferred_element_type=jnp.float32
    )


ANY = pl.BlockSpec(memory_space=pl.ANY)


def whole(array):
    shape = array.shape
    return pl.BlockSpec(shape, lambda *_: (0,) * len(shape))


def kernel_call(kernel, grid, in_specs, out_specs, out_shape, operands, flops, scratch=(), scalars=0):
    moved = sum(array.size * array.dtype.itemsize for array in operands) if flops else 0
    return pl.pallas_call(
        kernel,
        grid_spec=pltpu.PrefetchScalarGridSpec(
            num_scalar_prefetch=scalars,
            grid=grid,
            in_specs=in_specs,
            out_specs=out_specs,
            scratch_shapes=list(scratch),
        ),
        out_shape=[jax.ShapeDtypeStruct(shape, kind) for shape, kind in out_shape],
        compiler_params=pltpu.CompilerParams(vmem_limit_bytes=VMEM_LIMIT),
        cost_estimate=pl.CostEstimate(flops=flops, bytes_accessed=moved, transcendentals=0),
    )(*operands)


def normalize_rows(source, gain, target):
    step = 16

    def some(index, carry):
        rows = pl.ds(pl.multiple_of(index * step, step), step)
        values = wide(source[rows, :])
        inverse = lax.rsqrt(jnp.mean(values * values, axis=1, keepdims=True) + EPSILON)
        target[rows, :] = low(values * inverse * gain)
        return carry

    lax.fori_loop(0, source.shape[0] // step, some, 0)


def project_kernel(
    tokens, gain, query_weight, key_weight, value_weight, adapt_in, adapt_out, select,
    normed_out, lowrank_out, query_out, key_out, value_out, squares_out,
    weights, maps, sems,
):
    step = pl.program_id(0)
    rank = adapt_out.shape[1]
    copies = [
        pltpu.make_async_copy(
            adapt_in.at[index], maps.at[:, pl.ds(index * rank, rank)], sems.at[3]
        )
        for index in range(3)
    ]
    for index, source in enumerate((query_weight, key_weight, value_weight)):
        copies.append(pltpu.make_async_copy(source, weights.at[index], sems.at[index]))

    @pl.when(step == 0)
    def _():
        for copy in copies:
            copy.start()

    normalize_rows(tokens, wide(gain[...]), normed_out)

    @pl.when(step == 0)
    def _():
        for copy in copies:
            copy.wait()

    lowrank = dot(normed_out[...], maps[...])
    squares = []
    for index, out in enumerate((query_out, key_out, value_out)):
        lowrank_out[index] = low(lowrank[:, index * rank : (index + 1) * rank] * select[...])
        raw = dot(normed_out[...], weights[index]) + dot(lowrank_out[index], adapt_out[index])
        out[...] = raw
        squares.append(jnp.sum(raw * raw, axis=1, keepdims=True))
    lane = lax.broadcasted_iota(jnp.int32, (tokens.shape[0], 128), 1)
    columns = jnp.where(lane == 0, squares[0], jnp.where(lane == 1, squares[1], 0.0))
    squares_out[...] = jnp.transpose(columns)[:8]


def project_call(tokens, gain, weights, adapt_in, adapt_out, select):
    rows, width = tokens.shape
    local = weights[0].shape[1]
    rank = adapt_in.shape[2]
    tile = rows // 2
    out_shape = [((rows, width), jnp.bfloat16), ((3, rows, rank), jnp.bfloat16)]
    out_shape += [((rows, local), jnp.float32)] * 3 + [((8, rows), jnp.float32)]
    operands = [tokens, gain, *weights, adapt_in, adapt_out, select]
    row_block = pl.BlockSpec((tile, width), lambda n: (n, 0))
    local_block = pl.BlockSpec((tile, local), lambda n: (n, 0))
    return kernel_call(
        project_kernel,
        (2,),
        [row_block, whole(gain), ANY, ANY, ANY, ANY, whole(adapt_out), whole(select)],
        [row_block, pl.BlockSpec((3, tile, rank), lambda n: (0, n, 0))]
        + [local_block] * 3
        + [pl.BlockSpec((8, tile), lambda n: (0, n))],
        out_shape,
        operands,
        6 * rows * width * local,
        [
            pltpu.VMEM((3, width, local), jnp.bfloat16),
            pltpu.VMEM((width, 3 * rank), jnp.bfloat16),
            pltpu.SemaphoreType.DMA((4,)),
        ],
    )


def spread_columns(rows):
    return jnp.transpose(jnp.concatenate([rows] * (128 // rows.shape[0]), axis=0))


def turned(values):
    half = values.shape[1] // 2
    return jnp.concatenate([values[:, half:], values[:, :half]], axis=1)


def attend_kernel(
    width, size, core, squares, query_raw, key_raw, value_raw, query_gain, key_gain, cosine, sine,
    mask, output_weight, mix_in, queries, keys, values, attended, mine, theirs, held, weight, sem,
):
    copy = pltpu.make_async_copy(output_weight, weight, sem)
    copy.start()
    inverse = lax.rsqrt(spread_columns(squares[...]) / width + EPSILON)
    heads = query_raw.shape[1] // HD
    for head in range(heads):
        part = slice(head * HD, (head + 1) * HD)
        query = query_raw[:, part] * inverse[:, 0:1] * wide(query_gain[:, part])
        key = key_raw[:, part] * inverse[:, 1:2] * wide(key_gain[:, part])
        query = low(query * cosine[...] + turned(query) * sine[...])
        key = low(key * cosine[...] + turned(key) * sine[...])
        value = low(value_raw[:, part])
        queries[:, part] = query
        keys[:, part] = key
        values[:, part] = value
        scores = dot_t(query, key) * HD ** (-0.5) + mask[...]
        raised = jnp.exp(scores - jnp.max(scores, axis=1, keepdims=True))
        weights = low(raised * (1.0 / jnp.sum(raised, axis=1, keepdims=True)))
        result = low(dot(weights, value))
        attended[:, part] = result
        held[:, part] = result
    copy.wait()
    levels = mine.shape[0] // size
    for out, offset in ((theirs, 1 - core[0]), (mine, core[0])):
        taken = [
            held[pl.ds(pl.multiple_of((2 * level + offset) * size, size), size), :]
            for level in range(levels)
        ]
        taken = jnp.concatenate(taken, axis=0)
        out[:, :width] = dot(taken, weight[...]).astype(out.dtype)
        out[:, width:] = dot(taken, mix_in[...]).astype(out.dtype)


def attend_call(core, squares, raws, gains, tables, mask, output_weight, mix_in, size):
    rows, local = raws[0].shape
    width = output_weight.shape[1]
    wide_width = width + mix_in.shape[1]
    operands = [core, squares, *raws, *gains, *tables, mask, output_weight, mix_in]
    out_shape = [((rows, local), jnp.bfloat16)] * 4
    out_shape += [((rows // 2, wide_width), jnp.float32), ((rows // 2, wide_width), jnp.bfloat16)]
    return kernel_call(
        functools.partial(attend_kernel, width, size),
        (1,),
        [whole(array) for array in operands[1:-2]] + [ANY, whole(mix_in)],
        [pl.BlockSpec(shape, lambda *_: (0, 0)) for shape, _ in out_shape],
        out_shape,
        operands,
        4 * rows * rows * local + 2 * rows * local * width,
        [
            pltpu.VMEM((rows, local), jnp.bfloat16),
            pltpu.VMEM(output_weight.shape, jnp.bfloat16),
            pltpu.SemaphoreType.DMA,
        ],
        1,
    )


def resid_kernel(
    width, rank, kept, came, tokens, mix_out, select, gain, resid_out, norm_out, mixed_out
):
    mixed = low((kept[:, width:] + wide(came[:, width:])) * select[...])
    mixed_out[...] = mixed
    resid_out[...] = (
        wide(tokens[...])
        + (kept[:, :width] + wide(came[:, :width]))
        + dot(mixed, mix_out[...])
    )
    normalize_rows(resid_out, wide(gain[...]), norm_out)


def resid_call(rank, kept, came, tokens, mix_out, select, gain):
    rows, width = kept.shape[0], tokens.shape[1]
    out_shape = [((rows, width), jnp.float32), ((rows, width), jnp.bfloat16)]
    out_shape += [((rows, mix_out.shape[0]), jnp.bfloat16)]
    operands = [rank, kept, came, tokens, mix_out, select, gain]
    return kernel_call(
        functools.partial(resid_kernel, width),
        (1,),
        [whole(kept), whole(came), pl.BlockSpec((rows, width), lambda n, rank: (rank[0], 0))]
        + [whole(array) for array in operands[4:]],
        [pl.BlockSpec(shape, lambda *_: (0, 0)) for shape, _ in out_shape],
        out_shape,
        operands,
        0,
        (),
        1,
    )


def plane_order(near, span, size):
    return [
        (across, down * size, (down * near + across) * size)
        for down in range(span)
        for across in range(near)
    ]


def hidden_kernel(places, *refs):
    count = len(places)
    pieces, (down_own, down_other, spread), (out, side_out), (rows, side, row_sems, side_sems) = (
        refs[:count],
        refs[count : count + 3],
        refs[count + 3 : count + 5],
        refs[count + 5 :],
    )
    step = pl.program_id(0)
    width = rows.shape[1]

    @pl.when(step == 0)
    def _():
        copies = []
        for index, (piece, targets) in enumerate(zip(pieces, places)):
            for source, target, size in targets:
                taken = piece.at[pl.ds(source, size)]
                place = pl.ds(target, size)
                slot = len(copies) // 2
                copies.append(
                    pltpu.make_async_copy(
                        taken.at[:, pl.ds(0, width)], rows.at[place], row_sems.at[slot]
                    )
                )
                copies.append(
                    pltpu.make_async_copy(
                        taken.at[:, pl.ds(width, side.shape[1])], side.at[place], side_sems.at[slot]
                    )
                )
        for copy in copies:
            copy.start()
        for copy in copies:
            copy.wait()
        side_out[...] = side[...]

    def emit(down):
        grad = dot_t(rows[...], down[...]) * dot(side[...], spread[...])
        part = out.shape[2]
        for index in range(out.shape[0]):
            out[index] = low(grad[:, index * part : (index + 1) * part])

    half = pl.num_programs(0) // 2

    @pl.when(step < half)
    def _():
        emit(down_own)

    @pl.when(step >= half)
    def _():
        emit(down_other)


def hidden_call(planes, downs, spread, experts, size):
    hidden, width = downs[0].shape
    near = len(planes[0])
    pieces, places, rows = [], [], 0
    for plane in planes:
        for across, column in enumerate(plane):
            down = 0
            for piece in column:
                targets = []
                for source in range(0, piece.shape[0], size):
                    targets.append((source, rows + (down * near + across) * size, size))
                    down += 1
                pieces.append(piece)
                places.append(targets)
        rows += near * down * size
    blocks = rows // size
    part = hidden // experts
    side = spread.shape[0]
    pair = 2 * part
    half = experts // 2
    last = half - 1
    return kernel_call(
        functools.partial(hidden_kernel, places),
        (2 * half,),
        [ANY] * len(pieces)
        + [
            pl.BlockSpec((pair, width), lambda n: (jnp.minimum(n, last), 0)),
            pl.BlockSpec((pair, width), lambda n: (jnp.maximum(n - half, 0), 0)),
            pl.BlockSpec((side, pair), lambda n: (0, lax.rem(n, half))),
        ],
        [
            pl.BlockSpec((2, rows, part), lambda n: (n, 0, 0)),
            pl.BlockSpec((rows, side), lambda n: (0, 0)),
        ],
        [((2 * experts, rows, part), jnp.bfloat16), ((rows, side), jnp.bfloat16)],
        [*pieces, *downs, spread],
        4 * rows * hidden * width,
        [
            pltpu.VMEM((rows, width), jnp.bfloat16),
            pltpu.VMEM((rows, side), jnp.bfloat16),
            pltpu.SemaphoreType.DMA((blocks,)),
            pltpu.SemaphoreType.DMA((blocks,)),
        ],
    )


def write_rows(total, outs, near, span, levels):
    rows = total.shape[0]
    if not span:
        block = rows // (near * levels)
        for across in range(near):
            for down in range(levels):
                first = (down * near + across) * block
                outs[across][down * block : (down + 1) * block] = low(total[first : first + block])
        return
    half = rows // (2 * near * span)
    for down in range(span):
        for across in range(near):
            first = 2 * (down * near + across) * half
            outs[down][across * half : (across + 1) * half] = low(total[first : first + half])
            outs[span + across][down * half : (down + 1) * half] = low(
                total[first + half : first + 2 * half]
            )


def expert_kernel(count, near, span, levels, offset, *refs):
    pieces = refs[:count]
    gate_own, up_own, gate_other, up_other, spread, side, back = refs[count : count + 7]
    outs, hidden_out = refs[count + 7 : count + 7 + near + span], refs[count + 7 + near + span]
    rows, weights, gate_grad, up_grad, hidden, grads, sems, row_sem, back_sem, out_sem = refs[
        count + 8 + near + span :
    ]
    step = pl.program_id(0)
    size = pieces[0].shape[0]
    experts, _, part = gate_own.shape
    total_rows = rows.shape[0]
    sources = (gate_own, up_own, gate_other, up_other)

    def load(expert):
        slot = weights.at[expert]
        return [
            pltpu.make_async_copy(
                source.at[expert], slot.at[:, pl.ds(index * part, part)], sems.at[expert]
            )
            for index, source in enumerate(sources)
        ]

    row_copies = [
        pltpu.make_async_copy(piece, rows.at[pl.ds(index * size, size)], row_sem.at[index])
        for index, piece in enumerate(pieces)
    ]
    back_copy = pltpu.make_async_copy(
        back.at[:, pl.ds(offset, total_rows), :], grads, back_sem
    )
    out_copy = pltpu.make_async_copy(hidden, hidden_out, out_sem)

    @pl.when(step == 0)
    def _():
        for copy in row_copies + load(0) + [back_copy] + load(1):
            copy.start()
        for copy in row_copies:
            copy.wait()
        back_copy.wait()

        def work(expert, carry):
            for ahead in range(2, experts):

                @pl.when(expert == ahead - 2)
                def _():
                    for copy in load(ahead):
                        copy.start()

            for copy in load(expert):
                copy.wait()
            values = dot(rows[...], weights[expert])
            weight = dot(side[...], spread[expert])
            for half in range(2):
                gate_value = values[:, 2 * half * part : (2 * half + 1) * part]
                up_value = values[:, (2 * half + 1) * part : (2 * half + 2) * part]
                sigmoid = jax.nn.sigmoid(gate_value)
                silu = gate_value * sigmoid
                place = half * experts + expert
                grad = wide(grads[place])
                gate_grad[place] = low(grad * up_value * (sigmoid + silu * (1.0 - sigmoid)))
                up_grad[place] = low(grad * silu)
                hidden[place] = low(silu * up_value * weight)
            return carry

        lax.fori_loop(0, experts, work, 0)
        out_copy.start()

    tile = outs[0].shape[1]
    columns = pl.ds(pl.multiple_of(step * tile, tile), tile)
    total = None
    for expert in range(experts):
        for half in range(2):
            place = half * experts + expert
            for index, grad in enumerate((gate_grad, up_grad)):
                first = (2 * half + index) * part
                term = dot_t(grad[place], weights[expert, columns, first : first + part])
                total = term if total is None else total + term
    write_rows(total, outs, near, span, levels)

    @pl.when(step == pl.num_programs(0) - 1)
    def _():
        out_copy.wait()


def block_sizes(rows, near, span):
    if not span:
        return [rows // near] * near
    return [rows // (2 * span)] * span + [rows // (2 * near)] * near


def expert_call(pieces, gates, ups, spread, side, back, offset, near, span, levels):
    count = len(pieces)
    experts, width, part = gates[0].shape
    size = pieces[0].shape[0]
    rows = size * count
    tile = min(width, 512)
    shape = (2 * experts, rows, part)
    slots = pltpu.VMEM(shape, jnp.bfloat16)
    sizes = block_sizes(rows, near, span)
    side_block = pl.BlockSpec((rows, side.shape[1]), lambda n: (offset // rows, 0))
    return kernel_call(
        functools.partial(expert_kernel, count, near, span, levels, offset),
        (width // tile,),
        [ANY] * (count + 4) + [whole(spread), side_block, ANY],
        [pl.BlockSpec((size, tile), lambda n: (0, n)) for size in sizes] + [ANY],
        [((size, width), jnp.bfloat16) for size in sizes] + [(shape, jnp.bfloat16)],
        [*pieces, gates[0], ups[0], gates[1], ups[1], spread, side, back],
        16 * rows * experts * part * width,
        [
            pltpu.VMEM((rows, width), jnp.bfloat16),
            pltpu.VMEM((experts, width, 4 * part), jnp.bfloat16),
            slots,
            slots,
            slots,
            slots,
            pltpu.SemaphoreType.DMA((experts,)),
            pltpu.SemaphoreType.DMA((count,)),
            pltpu.SemaphoreType.DMA,
            pltpu.SemaphoreType.DMA,
        ],
    )


def whole_kernel(count, near, span, levels, places, *refs):
    pieces = refs[:count]
    gate_own, up_own, gate_other, up_other, spread, down_own, down_other = refs[count : count + 7]
    refs = refs[count + 7 :]
    cot_pieces, refs = refs[: len(places)], refs[len(places) :]
    outs, hidden_out = refs[: near + span], refs[near + span]
    rows, weights, gate_grad, up_grad, hidden, grads, sems, row_sem, out_sem = refs[
        near + span + 1 : near + span + 10
    ]
    cot_rows, side, downs, cot_sems, side_sems, down_sems = refs[near + span + 10 :]
    step = pl.program_id(0)
    size = pieces[0].shape[0]
    experts, _, part = gate_own.shape
    total_rows = rows.shape[0]
    sources = (gate_own, up_own, gate_other, up_other)

    def load(expert):
        slot = weights.at[expert]
        return [
            pltpu.make_async_copy(
                source.at[expert], slot.at[:, pl.ds(index * part, part)], sems.at[expert]
            )
            for index, source in enumerate(sources)
        ]

    row_copies = [
        pltpu.make_async_copy(piece, rows.at[pl.ds(index * size, size)], row_sem.at[index])
        for index, piece in enumerate(pieces)
    ]
    pairs = experts // 2

    def load_down(chunk):
        source = (down_own, down_other)[chunk // pairs]
        taken = source.at[pl.ds(chunk % pairs * 2 * part, 2 * part)]
        return pltpu.make_async_copy(taken, downs.at[chunk], down_sems.at[chunk])

    out_copy = pltpu.make_async_copy(hidden, hidden_out, out_sem)

    @pl.when(step == 0)
    def _():
        copies = copy_places(cot_pieces, places, cot_rows, side, cot_sems, side_sems)
        for copy in copies + [load_down(0), load_down(1)] + row_copies:
            copy.start()
        for copy in copies:
            copy.wait()

        def back(chunk, carry):
            for ahead in range(2 * pairs):

                @pl.when(chunk == ahead)
                def _():
                    if ahead + 2 < 2 * pairs:
                        load_down(ahead + 2).start()
                    elif ahead + 2 - 2 * pairs < 2:
                        for copy in load(ahead + 2 - 2 * pairs):
                            copy.start()
                    load_down(ahead).wait()

            grad = dot_t(cot_rows[...], downs[chunk])
            place = chunk // pairs * experts + lax.rem(chunk, pairs) * 2
            for index in range(2):
                weight = dot(side[...], spread[lax.rem(chunk, pairs) * 2 + index])
                grads[place + index] = low(grad[:, index * part : (index + 1) * part] * weight)
            return carry

        lax.fori_loop(0, 2 * pairs, back, 0)
        for copy in row_copies:
            copy.wait()

        def work(expert, carry):
            for ahead in range(2, experts):

                @pl.when(expert == ahead - 2)
                def _():
                    for copy in load(ahead):
                        copy.start()

            for copy in load(expert):
                copy.wait()
            values = dot(rows[...], weights[expert])
            weight = dot(side[...], spread[expert])
            for half in range(2):
                gate_value = values[:, 2 * half * part : (2 * half + 1) * part]
                up_value = values[:, (2 * half + 1) * part : (2 * half + 2) * part]
                sigmoid = jax.nn.sigmoid(gate_value)
                silu = gate_value * sigmoid
                place = half * experts + expert
                grad = wide(grads[place])
                gate_grad[place] = low(grad * up_value * (sigmoid + silu * (1.0 - sigmoid)))
                up_grad[place] = low(grad * silu)
                hidden[place] = low(silu * up_value * weight)
            return carry

        lax.fori_loop(0, experts, work, 0)
        out_copy.start()

    tile = outs[0].shape[1]
    columns = pl.ds(pl.multiple_of(step * tile, tile), tile)
    total = None
    for expert in range(experts):
        for half in range(2):
            place = half * experts + expert
            for index, grad in enumerate((gate_grad, up_grad)):
                first = (2 * half + index) * part
                term = dot_t(grad[place], weights[expert, columns, first : first + part])
                total = term if total is None else total + term
    write_rows(total, outs, near, span, levels)

    @pl.when(step == pl.num_programs(0) - 1)
    def _():
        out_copy.wait()


def copy_places(pieces, places, rows, side, row_sems, side_sems):
    width, copies = rows.shape[1], []
    for piece, targets in zip(pieces, places):
        for source, target, size in targets:
            taken, place = piece.at[pl.ds(source, size)], pl.ds(target, size)
            slot = len(copies) // 2
            copies.append(
                pltpu.make_async_copy(
                    taken.at[:, pl.ds(0, width)], rows.at[place], row_sems.at[slot]
                )
            )
            copies.append(
                pltpu.make_async_copy(
                    taken.at[:, pl.ds(width, side.shape[1])], side.at[place], side_sems.at[slot]
                )
            )
    return copies


def whole_call(pieces, cot_plane, gates, ups, downs, spread, near, span, block_rows):
    count = len(pieces)
    experts, width, part = gates[0].shape
    size = pieces[0].shape[0]
    rows = size * count
    tile = min(width, 512)
    shape = (2 * experts, rows, part)
    slots = pltpu.VMEM(shape, jnp.bfloat16)
    cot_pieces, places = [], []
    for across, column in enumerate(cot_plane):
        down = 0
        for piece in column:
            targets = []
            for source in range(0, piece.shape[0], block_rows):
                targets.append((source, (down * near + across) * block_rows, block_rows))
                down += 1
            cot_pieces.append(piece)
            places.append(targets)
    blocks = rows // block_rows
    sizes = block_sizes(rows, near, span)
    return kernel_call(
        functools.partial(whole_kernel, count, near, span, span, places),
        (width // tile,),
        [ANY] * (count + 4) + [whole(spread)] + [ANY] * (2 + len(cot_pieces)),
        [pl.BlockSpec((size, tile), lambda n: (0, n)) for size in sizes] + [ANY],
        [((size, width), jnp.bfloat16) for size in sizes] + [(shape, jnp.bfloat16)],
        [*pieces, gates[0], ups[0], gates[1], ups[1], spread, *downs, *cot_pieces],
        20 * rows * experts * part * width,
        [
            pltpu.VMEM((rows, width), jnp.bfloat16),
            pltpu.VMEM((experts, width, 4 * part), jnp.bfloat16),
            slots,
            slots,
            slots,
            slots,
            pltpu.SemaphoreType.DMA((experts,)),
            pltpu.SemaphoreType.DMA((count,)),
            pltpu.SemaphoreType.DMA,
            pltpu.VMEM((rows, width), jnp.bfloat16),
            pltpu.VMEM((rows, spread.shape[1]), jnp.bfloat16),
            pltpu.VMEM((experts // 2 * 2, 2 * part, width), jnp.bfloat16),
            pltpu.SemaphoreType.DMA((blocks,)),
            pltpu.SemaphoreType.DMA((blocks,)),
            pltpu.SemaphoreType.DMA((experts // 2 * 2,)),
        ],
    )


def down_kernel(count, span, *refs):
    hiddens, (down_own, down_other), outs = refs[:count], refs[count : count + 2], refs[count + 2 :]
    places, _, part = hiddens[0].shape
    near = len(outs) // (count * span)
    size = outs[0].shape[0]
    for index, hidden in enumerate(hiddens):
        total = None
        for place in range(places):
            down = down_own if place < places // 2 else down_other
            first = place % (places // 2) * part
            term = dot(hidden[place], down[first : first + part, :])
            total = term if total is None else total + term
        for across, target, first in plane_order(near, span, size):
            block = (index * near + across) * span + target // size
            outs[block][...] = low(total[first : first + size])


def down_call(hiddens, downs, near, span, size):
    places, rows, part = hiddens[0].shape
    hidden, width = downs[0].shape
    tile = min(width, 512)
    count = len(hiddens)
    down_block = pl.BlockSpec((hidden, tile), lambda n: (0, n))
    outs = kernel_call(
        functools.partial(down_kernel, count, span),
        (width // tile,),
        [whole(array) for array in hiddens] + [down_block] * 2,
        [pl.BlockSpec((size, tile), lambda n: (0, n))] * (count * near * span),
        [((size, width), jnp.bfloat16)] * (count * near * span),
        [*hiddens, *downs],
        0,
    )
    blocks = [list(outs[index * span : (index + 1) * span]) for index in range(count * near)]
    return [blocks[index * near : (index + 1) * near] for index in range(count)]


def backward_kernel(width, share, count, scalars, *refs):
    pieces = refs[:count]
    (output_weight, mix_in, mix_out, select, queries, keys, values, attended, query_raw, key_raw,
     query_gain, key_gain, cosine, sine, mask) = refs[count : count + 15]
    (query_out, key_out, value_out, inner_out, mix_in_grad, mix_out_grad) = refs[
        count + 15 : count + 21
    ]
    branch, mixed_grad, grads, sems = refs[count + 21 :]
    size = pieces[0].shape[0]
    rows, local = grads.shape
    heads = local // HD
    copies = []
    for index, piece in enumerate(pieces):
        place = pl.ds(pl.multiple_of(scalars[index] * size, size), size)
        copies.append(pltpu.make_async_copy(piece, branch.at[place], sems.at[index]))
    for copy in copies:
        copy.start()
    for copy in copies:
        copy.wait()
    mixed_grad[...] = low(wide(low(dot_t(branch[:, :width], mix_out[...]))) * select[...])
    grads[...] = low(
        dot_t(branch[:, :width], output_weight[...]) + dot_t(mixed_grad[...], mix_in[...])
    )
    columns = pl.ds(pl.multiple_of(scalars[count] * share, share), share)
    mix_out_grad[...] = sliced(t_dot(branch[:, width:], branch[:, columns]))
    scale = HD ** (-0.5)
    lane = lax.broadcasted_iota(jnp.int32, (rows, 128), 1)
    sums = jnp.zeros((rows, 128), jnp.float32)
    for head in range(heads):
        part = slice(head * HD, (head + 1) * HD)
        query, key, value = queries[:, part], keys[:, part], values[:, part]
        grad = grads[:, part]
        scores = dot_t(query, key) * scale + mask[...]
        raised = jnp.exp(scores - jnp.max(scores, axis=1, keepdims=True))
        weights = raised * (1.0 / jnp.sum(raised, axis=1, keepdims=True))
        weight_grad = dot_t(grad, value)
        center = jnp.sum(weights * weight_grad, axis=1, keepdims=True)
        score_grad = low(weights * (weight_grad - center))
        value_out[:, part] = low(t_dot(low(weights), grad))
        query_grad = dot(score_grad, key) * scale
        key_grad = t_dot(score_grad, query) * scale
        query_grad = query_grad * cosine[...] - turned(query_grad) * sine[...]
        key_grad = key_grad * cosine[...] - turned(key_grad) * sine[...]
        query_grad = query_grad * wide(query_gain[:, part])
        key_grad = key_grad * wide(key_gain[:, part])
        query_out[:, part] = query_grad
        key_out[:, part] = key_grad
        query_inner = jnp.sum(query_grad * query_raw[:, part], axis=1, keepdims=True)
        key_inner = jnp.sum(key_grad * key_raw[:, part], axis=1, keepdims=True)
        sums = sums + jnp.where(lane == 0, query_inner, jnp.where(lane == 1, key_inner, 0.0))
    mix_in_grad[...] = sliced(t_dot(mixed_grad[...], attended[...]))
    inner_out[...] = jnp.transpose(sums)[:8]


def sliced(values):
    total = values[:RANK]
    for index in range(1, values.shape[0] // RANK):
        total = total + values[index * RANK : (index + 1) * RANK]
    return low(total)


def backward_call(
    scalars, pieces, output_weight, mix_in, mix_out, select, states, raws, gains, tables, mask, share
):
    rows, local = raws[0].shape
    width = output_weight.shape[1]
    operands = [
        scalars, *pieces, output_weight, mix_in, mix_out, select, *states, *raws, *gains, *tables, mask,
    ]
    out_shape = [((rows, local), jnp.float32)] * 2 + [((rows, local), jnp.bfloat16)]
    out_shape += [((8, rows), jnp.float32), ((RANK, local), jnp.bfloat16)]
    out_shape += [((RANK, share), jnp.bfloat16)]
    return kernel_call(
        functools.partial(backward_kernel, width, share, len(pieces)),
        (1,),
        [ANY] * len(pieces) + [whole(array) for array in operands[len(pieces) + 1 :]],
        [pl.BlockSpec(shape, lambda *_: (0, 0)) for shape, _ in out_shape],
        out_shape,
        operands,
        14 * rows * rows * local + 2 * rows * local * width,
        [
            pltpu.VMEM((rows, pieces[0].shape[1]), jnp.bfloat16),
            pltpu.VMEM((rows, mix_out.shape[0]), jnp.bfloat16),
            pltpu.VMEM((rows, local), jnp.bfloat16),
            pltpu.SemaphoreType.DMA((len(pieces),)),
        ],
        1,
    )


def adapter_lanes(index, select):
    row = lax.broadcasted_iota(jnp.int32, (128, 128), 0) - index * RANK
    lane = lax.broadcasted_iota(jnp.int32, (128, 128), 1)
    return low(jnp.where(lax.rem(lane, RANK) == row, select, 0.0))


def raw_kernel(
    width, inner, squares, query_grad, key_grad, value_grad, query_raw, key_raw, lowrank,
    adapt_out, select, raw, lowrank_out, adapt_grad,
):
    inverse = lax.rsqrt(spread_columns(squares[...]) / width + EPSILON)
    totals = spread_columns(inner[...]) / width
    for index, (grad, value) in enumerate(((query_grad, query_raw), (key_grad, key_raw))):
        scale = inverse[:, index : index + 1]
        factor = scale**3 * totals[:, index : index + 1]
        raw[index] = low(scale * grad[...] - value[...] * factor)
    raw[2] = value_grad[...]
    lowrank_part = None
    for index in range(3):
        part = low(dot_t(raw[index], adapt_out[index]) * select[...])
        term = dot_t(part, adapter_lanes(index, select[...]))
        lowrank_part = term if lowrank_part is None else lowrank_part + term
        adapt_grad[index * RANK : (index + 1) * RANK, :] = sliced(
            t_dot(lowrank[index], raw[index])
        )
    lowrank_out[...] = low(lowrank_part)


def raw_call(inner, squares, grads, raws, lowrank, adapt_out, select, width):
    rows, local = raws[0].shape
    operands = [inner, squares, *grads, *raws, lowrank, adapt_out, select]
    out_shape = [((3, rows, local), jnp.bfloat16), ((rows, 128), jnp.bfloat16)]
    out_shape += [((3 * RANK, local), jnp.bfloat16)]
    return kernel_call(
        functools.partial(raw_kernel, width),
        (1,),
        [whole(array) for array in operands],
        [pl.BlockSpec(shape, lambda *_, size=len(shape): (0,) * size) for shape, _ in out_shape],
        out_shape,
        operands,
        0,
    )


def weight_kernel(size, scalars, raw, query_weight, key_weight, value_weight, mine, theirs):
    levels = mine.shape[0] // size
    for out, offset in ((theirs, 1 - scalars[0]), (mine, scalars[0])):
        total = None
        for index, weight in enumerate((query_weight, key_weight, value_weight)):
            taken = [
                raw[index, pl.ds(pl.multiple_of((2 * level + offset) * size, size), size), :]
                for level in range(levels)
            ]
            term = dot_t(jnp.concatenate(taken, axis=0), weight[...])
            total = term if total is None else total + term
        out[...] = total.astype(out.dtype)


def weight_call(scalars, raw, weights, size):
    _, rows, local = raw.shape
    width = weights[0].shape[0]
    tile = min(width, 512)
    operands = [scalars, raw, *weights]
    out_shape = [((rows // 2, width), jnp.float32), ((rows // 2, width), jnp.bfloat16)]
    return kernel_call(
        functools.partial(weight_kernel, size),
        (width // tile,),
        [whole(raw)] + [pl.BlockSpec((tile, local), lambda n, *_: (n, 0))] * 3,
        [pl.BlockSpec((rows // 2, tile), lambda n, *_: (0, n))] * 2,
        out_shape,
        operands,
        0,
        (),
        1,
    )


def input_kernel(
    rank, kept, came, lowrank, adapt_in, select, tokens, gain, resid_grad, out
):
    grad = kept[...] + wide(came[...])
    for index in range(3):
        part = low(dot(lowrank[...], adapter_lanes(index, select[...])))
        grad = grad + dot_t(part, adapt_in[index])
    scaled = grad * wide(gain[...])
    inputs = wide(tokens[...])
    width = inputs.shape[1]
    inverse = lax.rsqrt(jnp.mean(inputs * inputs, axis=1, keepdims=True) + EPSILON)
    inner = jnp.sum(scaled * inputs, axis=1, keepdims=True)
    out[...] = low(
        resid_grad[...] + norm_back(scaled, inputs, inverse, width, inner)
    )


def input_call(rank, kept, came, lowrank, adapt_in, select, tokens, gain, resid_grad):
    operands = [rank, kept, came, lowrank, adapt_in, select, tokens, gain, resid_grad]
    rows, width = kept.shape
    return kernel_call(
        input_kernel,
        (1,),
        [
            whole(kept),
            whole(came),
            pl.BlockSpec((rows, lowrank.shape[1]), lambda n, rank: (rank[0], 0)),
            whole(adapt_in),
            whole(select),
            pl.BlockSpec((rows, width), lambda n, rank: (rank[0], 0)),
            whole(gain),
            whole(resid_grad),
        ],
        [pl.BlockSpec((rows, width), lambda *_: (0, 0))],
        [((rows, width), jnp.bfloat16)],
        operands,
        0,
        (),
        1,
    )[0]


def compact_kernel(
    scalars, lowrank_grad, normed, mix_out_grad, adapt_grad, mix_in_grad, select, out, held, sem
):
    share = out.shape[1]
    columns = pl.ds(pl.multiple_of(scalars[0] * share, share), share)
    copy = pltpu.make_async_copy(normed.at[:, columns], held, sem)
    copy.start()
    copy.wait()
    first = low(t_dot(lowrank_grad[...], held[...]))[: 3 * RANK]
    out[: 3 * RANK] = first
    out[3 * RANK : 4 * RANK] = mix_out_grad[...]
    out[4 * RANK : 7 * RANK] = adapt_grad[...]
    out[7 * RANK : 8 * RANK] = mix_in_grad[...]
    chosen = low(jnp.broadcast_to(select[...], (RANK, 128)))
    out[8 * RANK :] = jnp.concatenate([chosen] * (share // 128), axis=1)


def compact_call(scalars, lowrank_grad, normed, mix_out_grad, adapt_grad, mix_in_grad, select):
    rows = normed.shape[0]
    share = adapt_grad.shape[1]
    operands = [scalars, lowrank_grad, normed, mix_out_grad, adapt_grad, mix_in_grad, select]
    return kernel_call(
        compact_kernel,
        (1,),
        [whole(lowrank_grad), ANY] + [whole(array) for array in operands[3:]],
        [pl.BlockSpec((9 * RANK, share), lambda *_: (0, 0))],
        [((9 * RANK, share), jnp.bfloat16)],
        operands,
        0,
        [pltpu.VMEM((rows, share), jnp.bfloat16), pltpu.SemaphoreType.DMA],
        1,
    )[0]


def spread_kernel(order, *refs):
    pieces, out = refs[:-1], refs[-1]
    step = pl.program_id(0)
    for index, piece in enumerate(pieces):

        @pl.when(step == index)
        def _():
            out[...] = wide(piece[...])


def spread_call(order, pieces):
    size, width = pieces[0].shape
    count = len(pieces)
    return kernel_call(
        spread_kernel,
        (count,),
        [whole(piece) for piece in pieces],
        [pl.BlockSpec((size, width), lambda step, order: (order[step], 0))],
        [((count * size, width), jnp.float32)],
        [order, *pieces],
        0,
        (),
        1,
    )[0]


def assemble_kernel(trees, order, *refs):
    count = len(refs) - 5
    own, pieces = refs[0], refs[1:count]
    in_grad, out_grad, mix_in_grad, mix_out_grad = refs[count : count + 4]
    (choice,) = refs[count + 4 :]
    share = own.shape[1]
    block = own.shape[0] // trees
    row = lax.broadcasted_iota(jnp.int32, (RANK, 128), 0)
    lane = lax.broadcasted_iota(jnp.int32, (RANK, 128), 1)
    same = lax.rem(lane, RANK) == row
    for tree in range(trees):
        chosen = own[tree * block + 8 * RANK : tree * block + 9 * RANK, :128]
        choice[tree * RANK : (tree + 1) * RANK] = low(jnp.where(same, wide(chosen), 0.0))

    def kind(source, stride, index):
        return jnp.concatenate(
            [
                source[tree * stride + index * RANK : tree * stride + (index + 1) * RANK, :]
                for tree in range(trees)
            ],
            axis=0,
        )

    for index in range(3):
        out_grad[index] = t_dot(choice[...], kind(own, block, 4 + index))
    mix_in_grad[...] = t_dot(kind(own, block, 7), choice[...])
    for place, source in enumerate((own, *pieces)):
        stride = block if place == 0 else 4 * RANK
        start = pl.ds(pl.multiple_of(order[place] * share, share), share)
        for index in range(3):
            in_grad[index, start, :] = t_dot(kind(source, stride, index), choice[...])
        mix_out_grad[:, start] = t_dot(choice[...], kind(source, stride, 3))


def assemble_call(order, own, pieces, trees):
    share = own.shape[1]
    count = 1 + len(pieces)
    width = count * share
    out_shape = [((3, width, 128), jnp.float32), ((3, 128, share), jnp.float32)]
    out_shape += [((share, 128), jnp.float32), ((128, width), jnp.float32)]
    operands = [order, own, *pieces]
    return kernel_call(
        functools.partial(assemble_kernel, trees),
        (1,),
        [whole(array) for array in operands[1:]],
        [pl.BlockSpec(shape, lambda *_, size=len(shape): (0,) * size) for shape, _ in out_shape],
        out_shape,
        operands,
        0,
        [pltpu.VMEM((trees * RANK, 128), jnp.bfloat16)],
        1,
    )


def body(
    tokens,
    cotangent,
    attn_gain,
    ffn_gain,
    query_gain,
    key_gain,
    query_weight,
    key_weight,
    value_weight,
    output_weight,
    expert_gate,
    expert_up,
    expert_down,
    adapt_in,
    adapt_out,
    adapt_in_out,
    adapt_out_out,
    routes,
    gate_weights,
    block_parent,
    adapter_pick,
):
    rows_here, model_width = tokens.shape
    tensor_rank = lax.axis_index("tensor")
    tensor_count = lax.axis_size("tensor")
    owners = lax.axis_size("expert")
    owner_rank = lax.axis_index("expert")
    axes = divide_axes(owners, tensor_count)
    far, near, span = axes["z"][1], axes["x"][1], axes["y"][1]
    experts_here, _, hidden_here = expert_gate.shape
    experts_all = experts_here * owners
    column_share = model_width // tensor_count
    row_share = rows_here // tensor_count
    hold = lax.optimization_barrier
    level, core = tensor_rank // 2, tensor_rank % 2
    rank_list = jnp.reshape(tensor_rank, (1,)).astype(jnp.int32)

    def own_rows(array):
        return lax.dynamic_slice_in_dim(array, tensor_rank * row_share, row_share, 0)

    routes_wide = jnp.swapaxes(routes, 0, 1)
    weights_wide = jnp.swapaxes(gate_weights, 0, 1)
    route_weights = jnp.sum(
        jnp.where(
            routes_wide[:, :, None] == jnp.arange(experts_all, dtype=jnp.int32)[None, None, :],
            weights_wide[:, :, None],
            0.0,
        ),
        axis=0,
    )
    weights_high = low(route_weights)
    weights_low = low(route_weights - wide(weights_high))
    side_width = -(-2 * experts_all // 128) * 128
    side_pad = jnp.zeros((rows_here, side_width - 2 * experts_all), jnp.bfloat16)
    side_rows = jnp.concatenate([weights_high, weights_low, side_pad], axis=1)
    cot_queue = []
    for step in range(span):
        place = ((level + span - step) % span * 2 + core) * row_share
        cot_queue.append(
            jnp.concatenate(
                [
                    lax.dynamic_slice_in_dim(cotangent, place, row_share, 0),
                    lax.dynamic_slice_in_dim(side_rows, place, row_share, 0),
                ],
                axis=1,
            )
        )
    cot_queue = [jnp.concatenate(cot_queue, axis=0)]
    side_index = jnp.arange(side_width, dtype=jnp.int32)
    hidden_owner = (
        owner_rank * experts_here
        + jnp.arange(experts_here * hidden_here, dtype=jnp.int32) // hidden_here
    )
    spread_flat = low(
        (side_index[:, None] % experts_all == hidden_owner[None, :])
        & (side_index[:, None] < 2 * experts_all)
    )
    spread = jnp.swapaxes(spread_flat.reshape(side_width, experts_here, hidden_here), 0, 1)

    cot_planes = [None] * far
    cot_queue.append(turn(cot_queue[0], axes, "z", 1))
    cot_planes[0] = ring(cot_queue[0], axes, "x")
    first_gain, second_gain = attn_gain[None, :], ffn_gain[None, :]
    gains = (query_gain[None, :], key_gain[None, :])
    reached = ancestry(block_parent)
    cosine_table, sine_table = rope_tables(reached, rows_here // block_parent.shape[0], HD)
    signs = jnp.where(jnp.arange(HD) < HD // 2, -1.0, 1.0)[None, :]
    tables = (cosine_table, sine_table * signs)
    mask = jnp.where(token_mask(reached[0], rows_here), 0.0, MASKED_SCORE)
    select = jnp.repeat(wide(adapter_pick), RANK, axis=1)
    weights = (query_weight, key_weight, value_weight)
    normed_in, lowrank, *raws, squares = project_call(
        tokens, first_gain, weights, adapt_in, adapt_out, select
    )

    def halves(rows):
        return [rows[: rows.shape[0] // 2], rows[rows.shape[0] // 2 :]]

    squares = sum_tensor(squares, axes)
    held = (squares, cot_queue[1], cot_planes[0], expert_gate, expert_up, tables, mask)
    squares, cot_queue[1], cot_planes[0], expert_gate, expert_up, tables, mask = hold(held)
    gates = (expert_gate, turn(expert_gate, axes, "c", 1))
    ups = (expert_up, turn(expert_up, axes, "c", 1))
    cot_queue[1] = halves(cot_queue[1])
    cot_later = turn(cot_queue[1][0], axes, "z", 1)
    cot_across = ring(cot_queue[1][0], axes, "x")[1:]
    *states, mine, theirs = attend_call(
        jnp.reshape(core, (1,)).astype(jnp.int32),
        squares,
        raws,
        gains,
        tables,
        mask,
        output_weight,
        adapt_in_out,
        row_share,
    )
    cot_later, cot_across, mine, theirs = hold((cot_later, cot_across, mine, theirs))

    theirs = turn(theirs, axes, "c", 1)
    branch_kept, branch_sent = scatter_core(mine, theirs, axes)
    branch_sent, cot_queue[1] = hold((branch_sent, cot_queue[1]))
    down_tall = expert_down.reshape(-1, model_width)
    branch_came = turn(branch_sent, axes, "y", -1)
    cot_later = [cot_later, turn(cot_queue[1][1], axes, "z", 1)]
    cot_second = ring(cot_queue[1][1], axes, "x")[1:]
    held = (branch_came, cot_later, cot_second, gates, ups, down_tall)
    branch_came, cot_later, cot_second, gates, ups, down_tall = hold(held)
    downs = (down_tall, turn(down_tall, axes, "c", 1))
    cot_queue.append(jnp.concatenate(cot_later, axis=0))
    cot_planes[1] = [cot_queue[1]] + [list(pair) for pair in zip(cot_across, cot_second)]
    cot_planes[0] = [[piece] for piece in cot_planes[0]]
    resid_rows, norm_plane, mixed_rows = resid_call(
        rank_list, branch_kept, branch_came, tokens, adapt_out_out, select, second_gain
    )

    norm_queue = [norm_plane, turn(norm_plane, axes, "z", 1)]
    norm_pairs = [ring(norm_plane, axes, "x")]
    backs, sides = [None] * far, [None] * far

    def hidden_step(*indices):
        back, side = hidden_call(
            [cot_planes[index] for index in indices], downs, spread_flat, experts_here, row_share
        )
        for order, index in enumerate(indices):
            backs[index], sides[index] = (back, order * side.shape[0] // len(indices)), side
        return back

    def set_back(back, *indices):
        for index in indices:
            backs[index] = (back, backs[index][1])

    norm_planes = [None] * far
    held = (norm_queue[1], norm_pairs[0], downs, cot_queue[2])
    norm_queue[1], norm_pairs[0], downs, cot_queue[2] = hold(held)
    norm_planes[0] = ring(jnp.concatenate(norm_pairs[0], axis=0), axes, "y")
    norm_queue.append(turn(norm_queue[1], axes, "z", 1))
    norm_pairs.append(ring(norm_queue[1], axes, "x"))
    back_first = hidden_step(0, 1)
    held = (norm_planes[0], norm_queue[2], norm_pairs[1], cot_queue[2], back_first)
    norm_planes[0], norm_queue[2], norm_pairs[1], cot_queue[2], back_first = hold(held)
    set_back(back_first, 0, 1)
    parts, hiddens = [None] * far, [None] * far

    def expert_step(index):
        back, offset = backs[index]
        *parts[index], hiddens[index] = expert_call(
            norm_planes[index],
            gates,
            ups,
            spread,
            sides[index],
            back,
            offset,
            near,
            span if index else 0,
            span,
        )

    def whole_step(index):
        *parts[index], hiddens[index] = whole_call(
            norm_planes[index], cot_planes[index], gates, ups, downs, spread, near, span, row_share
        )

    norm_planes[1] = ring(jnp.concatenate(norm_pairs[1], axis=0), axes, "y")
    norm_queue.append(turn(norm_queue[2], axes, "z", 1))
    norm_pairs.append(ring(norm_queue[2], axes, "x"))
    cot_queue.append(turn(cot_queue[2], axes, "z", 1))
    cot_planes[2] = ring(cot_queue[2], axes, "x")
    expert_step(0)

    held = (norm_planes[1], norm_queue[3], norm_pairs[2], parts[0])
    norm_planes[1], norm_queue[3], norm_pairs[2], parts[0] = hold(held)
    norm_planes[2] = ring(jnp.concatenate(norm_pairs[2], axis=0), axes, "y")
    norm_pairs.append(ring(norm_queue[3], axes, "x"))
    expert_step(1)

    held = (norm_planes[2], norm_pairs[3], parts[1], cot_queue[3], cot_planes[2])
    norm_planes[2], norm_pairs[3], parts[1], cot_queue[3], cot_planes[2] = hold(held)
    norm_planes[3] = ring(jnp.concatenate(norm_pairs[3], axis=0), axes, "y")
    came, last = [None] * far, [None] * far
    came[1] = scatter_first(parts[1], axes)
    came_x = send_sum(parts[0], axes, "x")
    cot_across = [turn(piece, axes, "z", 1) for piece in cot_planes[2][1:]]
    cot_planes[2] = [[piece] for piece in cot_planes[2]]
    whole_step(2)

    held = (norm_planes[3], came[1], parts[2], came_x, cot_across)
    norm_planes[3], came[1], parts[2], came_x, cot_across = hold(held)
    cot_planes[3] = [[piece] for piece in [cot_queue[3]] + cot_across]
    came[2] = scatter_first(parts[2], axes)
    last[1] = scatter_second(parts[1], came[1], axes)
    own_sums = [
        [block(parts[0][0], k, span), block(came_x, k, span)] for k in range(span)
    ]
    came_y = send_sum([None] + [low(pair[0] + pair[1]) for pair in own_sums[1:]], axes, "y")
    whole_step(3)

    held = (last[1], came[2], came_y, parts[3], hiddens)
    last[1], came[2], came_y, parts[3], hiddens = hold(held)
    came[3] = scatter_first(parts[3], axes)
    last[2] = scatter_second(parts[2], came[2], axes)
    ring_sum = turn(low(scatter_last(parts[1], came[1], last[1], axes)), axes, "z", 1)
    mixes, mix_came = [None] * far, [None] * far

    def down_step(*indices):
        done = down_call([hiddens[index] for index in indices], downs, near, span, row_share)
        for index, blocks in zip(indices, done):
            mixes[index] = blocks

    down_step(3, 0)

    held = (ring_sum, came[3], last[2], mixes[3], mixes[0], hiddens)
    ring_sum, came[3], last[2], mixes[3], mixes[0], hiddens = hold(held)
    last[3] = scatter_second(parts[3], came[3], axes)
    ring_sum = turn(
        low(wide(ring_sum) + scatter_last(parts[2], came[2], last[2], axes)), axes, "z", 1
    )
    down_step(2)

    ring_sum, last[3], hiddens, mixes[2] = hold((ring_sum, last[3], hiddens, mixes[2]))
    ring_sum = turn(
        low(wide(ring_sum) + scatter_last(parts[3], came[3], last[3], axes)), axes, "z", 1
    )
    down_step(1)
    half_width = model_width // span

    def column_sum(arrays, owner):
        first = owner * half_width
        return sum(
            wide(lax.dynamic_slice_in_dim(array, first, half_width, 1)) for array in arrays
        )

    def mix_columns(index, owner):
        rows = [column_sum(arrays, owner) for arrays in mix_held[index]]
        return jnp.concatenate(rows, axis=0)

    def mix_sent(index):
        return low(mix_columns(index, (level + 1) % span))

    def mix_down(index, came_rows):
        came_rows = turn(came_rows, axes, "y", -1)
        for step in range(span - 2, 0, -1):
            total = mix_columns(index, (level + span - step) % span) + rolled(came_rows)
            came_rows = turn(low(total), axes, "y", -1)
        return came_rows

    def rolled(rows):
        size = rows.shape[0] // span
        return wide(jnp.concatenate([rows[size:], rows[:size]], axis=0))

    def mix_total(index):
        return mix_columns(index, level) + rolled(mix_parts[index])

    def mix_send(index, down):
        return send_sum([blocks[down] for blocks in mixes[index]], axes, "x")

    mix_held = [None] * far
    mix_parts = [None] * far

    ring_sum, mixes = hold((ring_sum, mixes))
    mix_early = mix_send(3, 0)
    ffn_rows_grad = wide(ring_sum) + (own_sums[0][0] + own_sums[0][1]) + wide(came_y)
    second_scaled = ffn_rows_grad * wide(second_gain)
    second_inverse = lax.rsqrt(
        jnp.mean(resid_rows * resid_rows, axis=1, keepdims=True) + EPSILON
    )
    resid_grad_rows = wide(own_rows(cotangent)) + norm_back(
        second_scaled,
        resid_rows,
        second_inverse,
        model_width,
        jnp.sum(second_scaled * resid_rows, axis=1, keepdims=True),
    )
    branch_sent = jnp.concatenate([low(resid_grad_rows), mixed_rows], axis=1)
    branch_pieces = ring(branch_sent, axes, "y")
    branch_other = turn(branch_pieces[0], axes, "c", 1)
    order = jnp.stack(
        [
            (level + span - step) % span * 2 + side
            for side in (core, 1 - core)
            for step in range(span)
        ]
    ).astype(jnp.int32)

    branch_pieces, mix_early, mixes = hold((branch_pieces, mix_early, mixes))
    branch_others = [turn(piece, axes, "c", 1) for piece in branch_pieces[1:]]
    branch_others, branch_other, mixes = hold((branch_others, branch_other, mixes))
    branch_pieces = branch_pieces + [branch_other] + branch_others
    mix_late = [mix_send(3, down) for down in range(1, span)]
    mix_next = mix_send(2, 0)
    mix_far = [[turn(part, axes, "z", -1) for part in blocks] for blocks in mixes[1][1:]]
    query_grad, key_grad, value_grad, inner, mix_in_grad, mix_out_grad = backward_call(
        jnp.concatenate([order, rank_list]),
        branch_pieces,
        output_weight,
        adapt_in_out,
        adapt_out_out,
        select,
        states,
        raws[:2],
        gains,
        tables,
        mask,
        column_share,
    )

    held = (inner, mix_late, mix_next, mix_far, mixes)
    inner, mix_late, mix_next, mix_far, mixes = hold(held)
    mix_held[3] = list(zip(mixes[3][0], [mix_early] + mix_late))
    mix_ready = mix_sent(3)
    inner = sum_tensor(inner, axes)
    inner, mix_ready, mixes = hold((inner, mix_ready, mixes))
    mix_parts[3] = mix_down(3, mix_ready)
    mix_last = [mix_send(2, down) for down in range(1, span)]
    mix_near = [turn(mixes[1][0][0], axes, "z", -1)]
    raw_grads, lowrank_part, adapt_grad = raw_call(
        inner,
        squares,
        (query_grad, key_grad, value_grad),
        raws[:2],
        lowrank,
        adapt_out,
        select,
        model_width,
    )
    lowrank_came = turn(lowrank_part, axes, "c", 1)
    lowrank_part, lowrank_came, raw_grads = hold((lowrank_part, lowrank_came, raw_grads))
    lowrank_part = low(wide(lowrank_part) + wide(lowrank_came))
    lowrank_parts = ring(lowrank_part, axes, "y")
    normed_mine, normed_theirs = weight_call(
        jnp.reshape(core, (1,)).astype(jnp.int32), raw_grads, weights, row_share
    )

    held = (normed_mine, normed_theirs, lowrank_parts, mix_parts[3], mix_last, mix_near, mixes)
    held = hold(held)
    normed_mine, normed_theirs, lowrank_parts, mix_parts[3], mix_last, mix_near, mixes = held
    for across in range(1, near):
        pairs = zip(mixes[0][across], mix_far[across - 1])
        mixes[0][across] = [low(wide(mine) + wide(other)) for mine, other in pairs]
    normed_theirs, mixes = hold((turn(normed_theirs, axes, "c", 1), mixes))
    normed_kept, normed_sent = scatter_core(normed_mine, normed_theirs, axes)
    held = (normed_sent, lowrank_parts, mixes, mix_last)
    normed_sent, lowrank_parts, mixes, mix_last = hold(held)
    normed_came = turn(normed_sent, axes, "y", -1)
    lowrank_grad = low(sum(wide(part) for part in lowrank_parts))
    mix_came[0] = [mix_send(0, 0)]
    compact = compact_call(
        rank_list, lowrank_grad, normed_in, mix_out_grad, adapt_grad, mix_in_grad, select
    )
    tree_queue = [compact, turn(compact, axes, "z", 1)]
    mix_near = mix_near + [turn(part, axes, "z", -1) for part in mixes[1][0][1:]]
    mix_held[2] = list(zip(mixes[2][0], [mix_next] + mix_last))
    mix_ready = mix_sent(2)
    held = (tree_queue, mix_ready, normed_came, mix_came[0], mix_near, mixes)
    tree_queue, mix_ready, normed_came, mix_came[0], mix_near, mixes = hold(held)

    tree_queue.append(turn(tree_queue[-1], axes, "z", 1))
    mix_parts[2] = mix_down(2, mix_ready)
    mix_came[0] = mix_came[0] + [mix_send(0, down) for down in range(1, span)]
    input_rows = input_call(
        rank_list,
        normed_kept,
        normed_came,
        lowrank_grad,
        adapt_in,
        select,
        tokens,
        first_gain,
        resid_grad_rows,
    )
    input_rows, tree_queue = hold((input_rows, tree_queue))
    input_held = ring(input_rows, axes, "y")
    tree_queue.append(turn(tree_queue[-1], axes, "z", 1))
    held = (tree_queue, mix_came[0], mix_parts[2])
    tree_queue, mix_came[0], mix_parts[2] = hold(held)

    trees = ring(jnp.concatenate(tree_queue, axis=0), axes, "x")
    mix_sum = turn(low(mix_total(2)), axes, "z", 1)
    mix_held[0] = [list(arrays) for arrays in zip(mixes[0][0], mix_came[0], mix_near)]
    mix_held[0][0].append(resid_rows)
    mix_parts[0] = mix_down(0, mix_sent(0))
    held = (trees, mix_sum, mix_parts[0], input_held)
    trees, mix_sum, mix_parts[0], input_held = hold(held)
    input_pieces = input_held + [turn(piece, axes, "c", 1) for piece in input_held]
    trees = jnp.concatenate(trees, axis=0)
    shared = trees.reshape(owners, -1, column_share)[:, : 4 * RANK]
    shared = ring(shared.reshape(-1, column_share), axes, "y")
    mix_sum = turn(low(wide(mix_sum) + mix_total(3)), axes, "z", 1)
    input_grad = spread_call(order, input_pieces)
    shared, mix_sum, input_grad = hold((shared, mix_sum, input_grad))
    shared = shared + [turn(piece, axes, "c", 1) for piece in shared]
    layer_columns = low(mix_total(0) + wide(mix_sum))
    layer_out = place_columns(layer_columns, axes)
    grad_adapt_in, grad_adapt_out, grad_adapt_in_out, grad_adapt_out_out = assemble_call(
        order, trees, shared[1:], owners
    )
    return (
        layer_out,
        input_grad,
        grad_adapt_in,
        grad_adapt_out,
        grad_adapt_in_out,
        grad_adapt_out_out,
    )


def solution(mesh):
    return jax.shard_map(
        body,
        mesh=mesh,
        in_specs=(
            P("expert", None),
            P("expert", None),
            P(),
            P(),
            P("tensor"),
            P("tensor"),
            P(None, "tensor"),
            P(None, "tensor"),
            P(None, "tensor"),
            P("tensor", None),
            P("expert", None, "tensor"),
            P("expert", None, "tensor"),
            P("expert", "tensor", None),
            P(),
            P(None, None, "tensor"),
            P("tensor", None),
            P(),
            P("expert", None),
            P("expert", None),
            P("expert"),
            P("expert", None),
        ),
        out_specs=(
            P("expert", "tensor"),
            P("expert", None),
            P(),
            P(None, None, "tensor"),
            P("tensor", None),
            P(),
        ),
        check_vma=False,
    )
```

```python
import functools

import jax
import jax.numpy as jnp
from jax import lax
from jax.experimental import pallas as pl
from jax.experimental.pallas import tpu as pltpu
from jax.sharding import PartitionSpec as P

HD = 128
RANK = 16


EPSILON = 1e-05
ROPE_BASE = 10000.0
MASKED_SCORE = -1e30
VMEM_LIMIT = 56 * 2**20
CHUNK = 128


def ancestry(parents):
    blocks = parents.shape[0]
    places = jnp.arange(blocks, dtype=jnp.int32)
    walker = places
    reached = walker[:, None] == places[None, :]
    for _ in range(blocks - 1):
        hits = (walker[:, None] == places[None, :]).astype(jnp.int32)
        walker = jnp.sum(hits * parents[None, :], axis=1)
        reached = reached | (walker[:, None] == places[None, :])
    return reached[None]


def rope_tables(reached, block_span, head_size):
    depths = jnp.sum(reached.astype(jnp.int32), axis=2) - 1
    offsets = jnp.arange(block_span, dtype=jnp.int32)
    located = (
        (depths[:, :, None] * block_span + offsets[None, None, :]).reshape(-1).astype(jnp.float32)
    )
    halves = head_size // 2
    speeds = ROPE_BASE ** (-2.0 * jnp.arange(halves, dtype=jnp.float32) / head_size)
    angles = located[:, None] * speeds[None, :]
    angles = jnp.concatenate([angles, angles], axis=1)
    return (jnp.cos(angles), jnp.sin(angles))


def token_mask(reached, total_size):
    blocks = reached.shape[0]
    block_span = total_size // blocks
    widened = jnp.broadcast_to(
        reached[:, None, :, None], (blocks, block_span, blocks, block_span)
    ).reshape(total_size, total_size)
    positions = jnp.arange(total_size, dtype=jnp.int32)
    return widened & (positions[None, :] <= positions[:, None])


def norm_back(scaled_grad, values, inverse, model_width, inner_sum):
    return inverse * scaled_grad - values * inverse**3 * (inner_sum / model_width)


def divide_axes(owners, tensor_count):
    outer = 4
    return {
        "z": ("expert", outer, owners // outer, owners),
        "x": ("expert", owners // outer, 1, owners),
        "y": ("tensor", tensor_count // 2, 2, tensor_count),
        "c": ("tensor", 2, 1, tensor_count),
    }


def turn(array, axes, name, step):
    axis, length, stride, total = axes[name]
    pairs = []
    for index in range(total):
        place = (index // stride) % length
        moved = index + ((place + step) % length - place) * stride
        pairs.append((index, moved))
    return lax.ppermute(array, axis, pairs)


def ring(array, axes, name):
    held = [array]
    for _ in range(axes[name][1] - 1):
        held.append(turn(held[-1], axes, name, 1))
    return held


def wide(array):
    return array.astype(jnp.float32)


def low(array):
    return array.astype(jnp.bfloat16)


def send_sum(parts, axes, name):
    total = parts[-1]
    for part in parts[-2:0:-1]:
        total = low(wide(turn(total, axes, name, -1)) + wide(part))
    return turn(total, axes, name, -1)


def scatter_first(pieces, axes):
    span = axes["y"][1]
    return send_sum(pieces[:span], axes, "y"), send_sum(pieces[span:], axes, "x")


def block(array, index, count):
    size = array.shape[0] // count
    return wide(array[index * size : (index + 1) * size])


def scatter_second(pieces, came, axes):
    near, span = axes["x"][1], axes["y"][1]
    first = [low(block(pieces[0], k, near) + block(came[0], k, near)) for k in range(1, near)]
    second = [low(block(pieces[span], k, span) + block(came[1], k, span)) for k in range(1, span)]
    return send_sum([None] + first, axes, "x"), send_sum([None] + second, axes, "y")


def scatter_last(pieces, came, last, axes):
    near, span = axes["x"][1], axes["y"][1]
    first = block(pieces[0], 0, near) + block(came[0], 0, near) + wide(last[0])
    second = block(pieces[span], 0, span) + block(came[1], 0, span) + wide(last[1])
    return jnp.concatenate([first, second], axis=0)


def gather_tensor(rows, axes):
    held = ring(rows, axes, "y")
    return held + [turn(piece, axes, "c", 1) for piece in held]


def scatter_core(mine, came, axes):
    rank = lax.axis_index("tensor")
    span = axes["y"][1]
    size = mine.shape[0] // span
    total = None
    for step in range(span - 1, -1, -1):
        level = (rank // 2 + span - step) % span
        part = wide(lax.dynamic_slice_in_dim(mine, level * size, size, 0)) + wide(
            lax.dynamic_slice_in_dim(came, level * size, size, 0)
        )
        if step == 0:
            return part, total
        total = low(part if total is None else part + wide(turn(total, axes, "y", -1)))


def gather_x(rows, axes):
    return jnp.concatenate(ring(rows, axes, "x"), axis=0)


def place_columns(rows, axes):
    rank = lax.axis_index("tensor")
    span = axes["y"][1]
    size, share = rows.shape[0] // span, rows.shape[1] // 2
    level, core = rank // 2, rank % 2
    mine = lax.dynamic_slice_in_dim(rows, core * share, share, 1)
    theirs = turn(lax.dynamic_slice_in_dim(rows, (1 - core) * share, share, 1), axes, "c", 1)
    blocks = jnp.zeros((2 * span * size, share), rows.dtype)
    for step in range(span):
        place = (level + span - step) % span * 2
        for part, side in ((mine, core), (theirs, 1 - core)):
            taken = part[step * size : (step + 1) * size]
            blocks = lax.dynamic_update_slice_in_dim(blocks, taken, (place + side) * size, 0)
    return blocks


def sum_tensor(array, axes):
    total = wide(array) + wide(turn(array, axes, "c", 1))
    moving = total.astype(array.dtype)
    result = total
    for _ in range(axes["y"][1] - 1):
        moving = turn(moving, axes, "y", 1)
        result = result + wide(moving)
    return result


def dot(left, right):
    return jnp.dot(left, right, preferred_element_type=jnp.float32)


def dot_t(left, right):
    return lax.dot_general(
        left, right, (((1,), (1,)), ((), ())), preferred_element_type=jnp.float32
    )


def t_dot(left, right):
    return lax.dot_general(
        left, right, (((0,), (0,)), ((), ())), preferred_element_type=jnp.float32
    )


ANY = pl.BlockSpec(memory_space=pl.ANY)


def whole(array):
    shape = array.shape
    return pl.BlockSpec(shape, lambda *_: (0,) * len(shape))


def kernel_call(kernel, grid, in_specs, out_specs, out_shape, operands, flops, scratch=(), scalars=0):
    moved = sum(array.size * array.dtype.itemsize for array in operands) if flops else 0
    return pl.pallas_call(
        kernel,
        grid_spec=pltpu.PrefetchScalarGridSpec(
            num_scalar_prefetch=scalars,
            grid=grid,
            in_specs=in_specs,
            out_specs=out_specs,
            scratch_shapes=list(scratch),
        ),
        out_shape=[jax.ShapeDtypeStruct(shape, kind) for shape, kind in out_shape],
        compiler_params=pltpu.CompilerParams(vmem_limit_bytes=VMEM_LIMIT),
        cost_estimate=pl.CostEstimate(flops=flops, bytes_accessed=moved, transcendentals=0),
    )(*operands)


def normalize_rows(source, gain, target):
    step = 16

    def some(index, carry):
        for part in range(4):
            rows = pl.ds(pl.multiple_of((index * 4 + part) * step, step), step)
            values = wide(source[rows, :])
            inverse = lax.rsqrt(jnp.mean(values * values, axis=1, keepdims=True) + EPSILON)
            target[rows, :] = low(values * inverse * gain)
        return carry

    lax.fori_loop(0, source.shape[0] // (4 * step), some, 0)


def project_kernel(
    tokens, gain, query_weight, key_weight, value_weight, adapt_in, adapt_out, select,
    normed_out, lowrank_out, query_out, key_out, value_out, squares_out,
    weights, maps, sems,
):
    step = pl.program_id(0)
    rank = adapt_out.shape[1]
    copies = [
        pltpu.make_async_copy(
            adapt_in.at[index], maps.at[:, pl.ds(index * rank, rank)], sems.at[3]
        )
        for index in range(3)
    ]
    for index, source in enumerate((query_weight, key_weight, value_weight)):
        copies.append(pltpu.make_async_copy(source, weights.at[index], sems.at[index]))

    @pl.when(step == 0)
    def _():
        for copy in copies:
            copy.start()

    normalize_rows(tokens, wide(gain[...]), normed_out)

    @pl.when(step == 0)
    def _():
        for copy in copies:
            copy.wait()

    lowrank = dot(normed_out[...], maps[...])
    squares = []
    for index, out in enumerate((query_out, key_out, value_out)):
        lowrank_out[index] = low(lowrank[:, index * rank : (index + 1) * rank] * select[...])
        raw = dot(normed_out[...], weights[index]) + dot(lowrank_out[index], adapt_out[index])
        out[...] = raw
        squares.append(jnp.sum(raw * raw, axis=1, keepdims=True))
    lane = lax.broadcasted_iota(jnp.int32, (tokens.shape[0], 128), 1)
    columns = jnp.where(lane == 0, squares[0], jnp.where(lane == 1, squares[1], 0.0))
    squares_out[...] = jnp.transpose(columns)[:8]


def project_call(tokens, gain, weights, adapt_in, adapt_out, select):
    rows, width = tokens.shape
    local = weights[0].shape[1]
    rank = adapt_in.shape[2]
    tile = rows // 2
    out_shape = [((rows, width), jnp.bfloat16), ((3, rows, rank), jnp.bfloat16)]
    out_shape += [((rows, local), jnp.float32)] * 3 + [((8, rows), jnp.float32)]
    operands = [tokens, gain, *weights, adapt_in, adapt_out, select]
    row_block = pl.BlockSpec((tile, width), lambda n: (n, 0))
    local_block = pl.BlockSpec((tile, local), lambda n: (n, 0))
    return kernel_call(
        project_kernel,
        (2,),
        [row_block, whole(gain), ANY, ANY, ANY, ANY, whole(adapt_out), whole(select)],
        [row_block, pl.BlockSpec((3, tile, rank), lambda n: (0, n, 0))]
        + [local_block] * 3
        + [pl.BlockSpec((8, tile), lambda n: (0, n))],
        out_shape,
        operands,
        6 * rows * width * local,
        [
            pltpu.VMEM((3, width, local), jnp.bfloat16),
            pltpu.VMEM((width, 3 * rank), jnp.bfloat16),
            pltpu.SemaphoreType.DMA((4,)),
        ],
    )


def spread_columns(rows):
    return jnp.transpose(jnp.concatenate([rows] * (128 // rows.shape[0]), axis=0))


def turned(values):
    half = values.shape[1] // 2
    return jnp.concatenate([values[:, half:], values[:, :half]], axis=1)


def attend_kernel(
    width, size, core, squares, query_raw, key_raw, value_raw, query_gain, key_gain, cosine, sine,
    mask, output_weight, mix_in, queries, keys, values, attended, mine, theirs, held, weight, sem,
):
    copy = pltpu.make_async_copy(output_weight, weight, sem)
    copy.start()
    inverse = lax.rsqrt(spread_columns(squares[...]) / width + EPSILON)
    heads = query_raw.shape[1] // HD
    for head in range(heads):
        part = slice(head * HD, (head + 1) * HD)
        query = query_raw[:, part] * inverse[:, 0:1] * wide(query_gain[:, part])
        key = key_raw[:, part] * inverse[:, 1:2] * wide(key_gain[:, part])
        query = low(query * cosine[...] + turned(query) * sine[...])
        key = low(key * cosine[...] + turned(key) * sine[...])
        value = low(value_raw[:, part])
        queries[:, part] = query
        keys[:, part] = key
        values[:, part] = value
        scores = dot_t(query, key) * HD ** (-0.5) + mask[...]
        raised = jnp.exp(scores - jnp.max(scores, axis=1, keepdims=True))
        weights = low(raised * (1.0 / jnp.sum(raised, axis=1, keepdims=True)))
        result = low(dot(weights, value))
        attended[:, part] = result
        held[:, part] = result
    copy.wait()
    levels = mine.shape[0] // size
    for out, offset in ((theirs, 1 - core[0]), (mine, core[0])):
        taken = [
            held[pl.ds(pl.multiple_of((2 * level + offset) * size, size), size), :]
            for level in range(levels)
        ]
        taken = jnp.concatenate(taken, axis=0)
        out[:, :width] = dot(taken, weight[...]).astype(out.dtype)
        out[:, width:] = dot(taken, mix_in[...]).astype(out.dtype)


def attend_call(core, squares, raws, gains, tables, mask, output_weight, mix_in, size):
    rows, local = raws[0].shape
    width = output_weight.shape[1]
    wide_width = width + mix_in.shape[1]
    operands = [core, squares, *raws, *gains, *tables, mask, output_weight, mix_in]
    out_shape = [((rows, local), jnp.bfloat16)] * 4
    out_shape += [((rows // 2, wide_width), jnp.float32), ((rows // 2, wide_width), jnp.bfloat16)]
    return kernel_call(
        functools.partial(attend_kernel, width, size),
        (1,),
        [whole(array) for array in operands[1:-2]] + [ANY, whole(mix_in)],
        [pl.BlockSpec(shape, lambda *_: (0, 0)) for shape, _ in out_shape],
        out_shape,
        operands,
        4 * rows * rows * local + 2 * rows * local * width,
        [
            pltpu.VMEM((rows, local), jnp.bfloat16),
            pltpu.VMEM(output_weight.shape, jnp.bfloat16),
            pltpu.SemaphoreType.DMA,
        ],
        1,
    )


def resid_kernel(
    width, rank, kept, came, tokens, mix_out, select, gain, resid_out, norm_out, mixed_out
):
    mixed = low((kept[:, width:] + wide(came[:, width:])) * select[...])
    mixed_out[...] = mixed
    resid_out[...] = (
        wide(tokens[...])
        + (kept[:, :width] + wide(came[:, :width]))
        + dot(mixed, mix_out[...])
    )
    normalize_rows(resid_out, wide(gain[...]), norm_out)


def resid_call(rank, kept, came, tokens, mix_out, select, gain):
    rows, width = kept.shape[0], tokens.shape[1]
    out_shape = [((rows, width), jnp.float32), ((rows, width), jnp.bfloat16)]
    out_shape += [((rows, mix_out.shape[0]), jnp.bfloat16)]
    operands = [rank, kept, came, tokens, mix_out, select, gain]
    return kernel_call(
        functools.partial(resid_kernel, width),
        (1,),
        [whole(kept), whole(came), pl.BlockSpec((rows, width), lambda n, rank: (rank[0], 0))]
        + [whole(array) for array in operands[4:]],
        [pl.BlockSpec(shape, lambda *_: (0, 0)) for shape, _ in out_shape],
        out_shape,
        operands,
        0,
        (),
        1,
    )


def plane_order(near, span, size):
    return [
        (across, down * size, (down * near + across) * size)
        for down in range(span)
        for across in range(near)
    ]


def hidden_kernel(places, *refs):
    count = len(places)
    pieces, (down_own, down_other, spread), (out, side_out), (rows, side, row_sems, side_sems) = (
        refs[:count],
        refs[count : count + 3],
        refs[count + 3 : count + 5],
        refs[count + 5 :],
    )
    step = pl.program_id(0)
    width = rows.shape[1]

    @pl.when(step == 0)
    def _():
        copies = []
        for index, (piece, targets) in enumerate(zip(pieces, places)):
            for source, target, size in targets:
                taken = piece.at[pl.ds(source, size)]
                place = pl.ds(target, size)
                slot = len(copies) // 2
                copies.append(
                    pltpu.make_async_copy(
                        taken.at[:, pl.ds(0, width)], rows.at[place], row_sems.at[slot]
                    )
                )
                copies.append(
                    pltpu.make_async_copy(
                        taken.at[:, pl.ds(width, side.shape[1])], side.at[place], side_sems.at[slot]
                    )
                )
        for copy in copies:
            copy.start()
        for copy in copies:
            copy.wait()
        side_out[...] = side[...]

    def emit(down):
        grad = dot_t(rows[...], down[...]) * dot(side[...], spread[...])
        part = out.shape[2]
        for index in range(out.shape[0]):
            out[index] = low(grad[:, index * part : (index + 1) * part])

    half = pl.num_programs(0) // 2

    @pl.when(step < half)
    def _():
        emit(down_own)

    @pl.when(step >= half)
    def _():
        emit(down_other)


def hidden_call(planes, downs, spread, experts, size):
    hidden, width = downs[0].shape
    near = len(planes[0])
    pieces, places, rows = [], [], 0
    for plane in planes:
        for across, column in enumerate(plane):
            down = 0
            for piece in column:
                targets = []
                for source in range(0, piece.shape[0], size):
                    targets.append((source, rows + (down * near + across) * size, size))
                    down += 1
                pieces.append(piece)
                places.append(targets)
        rows += near * down * size
    blocks = rows // size
    part = hidden // experts
    side = spread.shape[0]
    pair = 2 * part
    half = experts // 2
    last = half - 1
    return kernel_call(
        functools.partial(hidden_kernel, places),
        (2 * half,),
        [ANY] * len(pieces)
        + [
            pl.BlockSpec((pair, width), lambda n: (jnp.minimum(n, last), 0)),
            pl.BlockSpec((pair, width), lambda n: (jnp.maximum(n - half, 0), 0)),
            pl.BlockSpec((side, pair), lambda n: (0, lax.rem(n, half))),
        ],
        [
            pl.BlockSpec((2, rows, part), lambda n: (n, 0, 0)),
            pl.BlockSpec((rows, side), lambda n: (0, 0)),
        ],
        [((2 * experts, rows, part), jnp.bfloat16), ((rows, side), jnp.bfloat16)],
        [*pieces, *downs, spread],
        0,
        [
            pltpu.VMEM((rows, width), jnp.bfloat16),
            pltpu.VMEM((rows, side), jnp.bfloat16),
            pltpu.SemaphoreType.DMA((blocks,)),
            pltpu.SemaphoreType.DMA((blocks,)),
        ],
    )


def write_rows(total, outs, near, span, levels):
    rows = total.shape[0]
    if not span:
        block = rows // (near * levels)
        for across in range(near):
            for down in range(levels):
                first = (down * near + across) * block
                outs[across][down * block : (down + 1) * block] = low(total[first : first + block])
        return
    half = rows // (2 * near * span)
    for down in range(span):
        for across in range(near):
            first = 2 * (down * near + across) * half
            outs[down][across * half : (across + 1) * half] = low(total[first : first + half])
            outs[span + across][down * half : (down + 1) * half] = low(
                total[first + half : first + 2 * half]
            )


def expert_kernel(count, near, span, levels, offset, *refs):
    pieces = refs[:count]
    gate_own, up_own, gate_other, up_other, spread, side, back = refs[count : count + 7]
    outs, hidden_out = refs[count + 7 : count + 7 + near + span], refs[count + 7 + near + span]
    rows, weights, gate_grad, up_grad, hidden, grads, sems, row_sem, back_sem, out_sem = refs[
        count + 8 + near + span :
    ]
    step = pl.program_id(0)
    size = pieces[0].shape[0]
    experts, _, part = gate_own.shape
    total_rows = rows.shape[0]
    sources = (gate_own, up_own, gate_other, up_other)

    def load(expert):
        slot = weights.at[expert]
        return [
            pltpu.make_async_copy(
                source.at[expert], slot.at[:, pl.ds(index * part, part)], sems.at[expert]
            )
            for index, source in enumerate(sources)
        ]

    row_copies = [
        pltpu.make_async_copy(piece, rows.at[pl.ds(index * size, size)], row_sem.at[index])
        for index, piece in enumerate(pieces)
    ]
    back_copy = pltpu.make_async_copy(
        back.at[:, pl.ds(offset, total_rows), :], grads, back_sem
    )
    out_copy = pltpu.make_async_copy(hidden, hidden_out, out_sem)

    @pl.when(step == 0)
    def _():
        for copy in row_copies + load(0) + [back_copy] + load(1):
            copy.start()
        for copy in row_copies:
            copy.wait()
        back_copy.wait()

        def work(expert, carry):
            for ahead in range(2, experts):

                @pl.when(expert == ahead - 2)
                def _():
                    for copy in load(ahead):
                        copy.start()

            for copy in load(expert):
                copy.wait()
            values = dot(rows[...], weights[expert])
            weight = dot(side[...], spread[expert])
            for half in range(2):
                gate_value = values[:, 2 * half * part : (2 * half + 1) * part]
                up_value = values[:, (2 * half + 1) * part : (2 * half + 2) * part]
                sigmoid = jax.nn.sigmoid(gate_value)
                silu = gate_value * sigmoid
                place = half * experts + expert
                grad = wide(grads[place])
                gate_grad[place] = low(grad * up_value * (sigmoid + silu * (1.0 - sigmoid)))
                up_grad[place] = low(grad * silu)
                hidden[place] = low(silu * up_value * weight)
            return carry

        lax.fori_loop(0, experts, work, 0)
        out_copy.start()

    tile = outs[0].shape[1]
    columns = pl.ds(pl.multiple_of(step * tile, tile), tile)
    total = None
    for expert in range(experts):
        for half in range(2):
            place = half * experts + expert
            for index, grad in enumerate((gate_grad, up_grad)):
                first = (2 * half + index) * part
                term = dot_t(grad[place], weights[expert, columns, first : first + part])
                total = term if total is None else total + term
    write_rows(total, outs, near, span, levels)

    @pl.when(step == pl.num_programs(0) - 1)
    def _():
        out_copy.wait()


def block_sizes(rows, near, span):
    if not span:
        return [rows // near] * near
    return [rows // (2 * span)] * span + [rows // (2 * near)] * near


def expert_call(pieces, gates, ups, spread, side, back, offset, near, span, levels):
    count = len(pieces)
    experts, width, part = gates[0].shape
    size = pieces[0].shape[0]
    rows = size * count
    tile = min(width, 1024)
    shape = (2 * experts, rows, part)
    slots = pltpu.VMEM(shape, jnp.bfloat16)
    sizes = block_sizes(rows, near, span)
    side_block = pl.BlockSpec((rows, side.shape[1]), lambda n: (offset // rows, 0))
    return kernel_call(
        functools.partial(expert_kernel, count, near, span, levels, offset),
        (width // tile,),
        [ANY] * (count + 4) + [whole(spread), side_block, ANY],
        [pl.BlockSpec((size, tile), lambda n: (0, n)) for size in sizes] + [ANY],
        [((size, width), jnp.bfloat16) for size in sizes] + [(shape, jnp.bfloat16)],
        [*pieces, gates[0], ups[0], gates[1], ups[1], spread, side, back],
        16 * rows * experts * part * width,
        [
            pltpu.VMEM((rows, width), jnp.bfloat16),
            pltpu.VMEM((experts, width, 4 * part), jnp.bfloat16),
            slots,
            slots,
            slots,
            slots,
            pltpu.SemaphoreType.DMA((experts,)),
            pltpu.SemaphoreType.DMA((count,)),
            pltpu.SemaphoreType.DMA,
            pltpu.SemaphoreType.DMA,
        ],
    )


def whole_kernel(count, near, span, levels, places, *refs):
    pieces = refs[:count]
    gate_own, up_own, gate_other, up_other, spread, down_own, down_other = refs[count : count + 7]
    refs = refs[count + 7 :]
    cot_pieces, refs = refs[: len(places)], refs[len(places) :]
    outs, hidden_out = refs[: near + span], refs[near + span]
    rows, weights, gate_grad, up_grad, hidden, grads, sems, row_sem, out_sem = refs[
        near + span + 1 : near + span + 10
    ]
    cot_rows, side, downs, cot_sems, side_sems, down_sems = refs[near + span + 10 :]
    step = pl.program_id(0)
    size = pieces[0].shape[0]
    experts, _, part = gate_own.shape
    total_rows = rows.shape[0]
    sources = (gate_own, up_own, gate_other, up_other)

    def load(expert):
        slot = weights.at[expert]
        return [
            pltpu.make_async_copy(
                source.at[expert], slot.at[:, pl.ds(index * part, part)], sems.at[expert]
            )
            for index, source in enumerate(sources)
        ]

    row_copies = [
        pltpu.make_async_copy(piece, rows.at[pl.ds(index * size, size)], row_sem.at[index])
        for index, piece in enumerate(pieces)
    ]
    pairs = experts // 2

    def load_down(chunk):
        source = (down_own, down_other)[chunk // pairs]
        taken = source.at[pl.ds(chunk % pairs * 2 * part, 2 * part)]
        return pltpu.make_async_copy(taken, downs.at[chunk], down_sems.at[chunk])

    out_copy = pltpu.make_async_copy(hidden, hidden_out, out_sem)

    @pl.when(step == 0)
    def _():
        copies = copy_places(cot_pieces, places, cot_rows, side, cot_sems, side_sems)
        for copy in copies + [load_down(0), load_down(1)] + row_copies:
            copy.start()
        for copy in copies:
            copy.wait()

        def back(chunk, carry):
            for ahead in range(2 * pairs):

                @pl.when(chunk == ahead)
                def _():
                    if ahead + 2 < 2 * pairs:
                        load_down(ahead + 2).start()
                    elif ahead + 2 - 2 * pairs < 2:
                        for copy in load(ahead + 2 - 2 * pairs):
                            copy.start()
                    load_down(ahead).wait()

            grad = dot_t(cot_rows[...], downs[chunk])
            place = chunk // pairs * experts + lax.rem(chunk, pairs) * 2
            for index in range(2):
                weight = dot(side[...], spread[lax.rem(chunk, pairs) * 2 + index])
                grads[place + index] = low(grad[:, index * part : (index + 1) * part] * weight)
            return carry

        lax.fori_loop(0, 2 * pairs, back, 0)
        for copy in row_copies:
            copy.wait()

        def work(expert, carry):
            for ahead in range(2, experts):

                @pl.when(expert == ahead - 2)
                def _():
                    for copy in load(ahead):
                        copy.start()

            for copy in load(expert):
                copy.wait()
            values = dot(rows[...], weights[expert])
            weight = dot(side[...], spread[expert])
            for half in range(2):
                gate_value = values[:, 2 * half * part : (2 * half + 1) * part]
                up_value = values[:, (2 * half + 1) * part : (2 * half + 2) * part]
                sigmoid = jax.nn.sigmoid(gate_value)
                silu = gate_value * sigmoid
                place = half * experts + expert
                grad = wide(grads[place])
                gate_grad[place] = low(grad * up_value * (sigmoid + silu * (1.0 - sigmoid)))
                up_grad[place] = low(grad * silu)
                hidden[place] = low(silu * up_value * weight)
            return carry

        lax.fori_loop(0, experts, work, 0)
        out_copy.start()

    tile = outs[0].shape[1]
    columns = pl.ds(pl.multiple_of(step * tile, tile), tile)
    total = None
    for expert in range(experts):
        for half in range(2):
            place = half * experts + expert
            for index, grad in enumerate((gate_grad, up_grad)):
                first = (2 * half + index) * part
                term = dot_t(grad[place], weights[expert, columns, first : first + part])
                total = term if total is None else total + term
    write_rows(total, outs, near, span, levels)

    @pl.when(step == pl.num_programs(0) - 1)
    def _():
        out_copy.wait()


def copy_places(pieces, places, rows, side, row_sems, side_sems):
    width, copies = rows.shape[1], []
    for piece, targets in zip(pieces, places):
        for source, target, size in targets:
            taken, place = piece.at[pl.ds(source, size)], pl.ds(target, size)
            slot = len(copies) // 2
            copies.append(
                pltpu.make_async_copy(
                    taken.at[:, pl.ds(0, width)], rows.at[place], row_sems.at[slot]
                )
            )
            copies.append(
                pltpu.make_async_copy(
                    taken.at[:, pl.ds(width, side.shape[1])], side.at[place], side_sems.at[slot]
                )
            )
    return copies


def whole_call(pieces, cot_plane, gates, ups, downs, spread, near, span, block_rows):
    count = len(pieces)
    experts, width, part = gates[0].shape
    size = pieces[0].shape[0]
    rows = size * count
    tile = min(width, 1024)
    shape = (2 * experts, rows, part)
    slots = pltpu.VMEM(shape, jnp.bfloat16)
    cot_pieces, places = [], []
    for across, column in enumerate(cot_plane):
        down = 0
        for piece in column:
            targets = []
            for source in range(0, piece.shape[0], block_rows):
                targets.append((source, (down * near + across) * block_rows, block_rows))
                down += 1
            cot_pieces.append(piece)
            places.append(targets)
    blocks = rows // block_rows
    sizes = block_sizes(rows, near, span)
    return kernel_call(
        functools.partial(whole_kernel, count, near, span, span, places),
        (width // tile,),
        [ANY] * (count + 4) + [whole(spread)] + [ANY] * (2 + len(cot_pieces)),
        [pl.BlockSpec((size, tile), lambda n: (0, n)) for size in sizes] + [ANY],
        [((size, width), jnp.bfloat16) for size in sizes] + [(shape, jnp.bfloat16)],
        [*pieces, gates[0], ups[0], gates[1], ups[1], spread, *downs, *cot_pieces],
        20 * rows * experts * part * width,
        [
            pltpu.VMEM((rows, width), jnp.bfloat16),
            pltpu.VMEM((experts, width, 4 * part), jnp.bfloat16),
            slots,
            slots,
            slots,
            slots,
            pltpu.SemaphoreType.DMA((experts,)),
            pltpu.SemaphoreType.DMA((count,)),
            pltpu.SemaphoreType.DMA,
            pltpu.VMEM((rows, width), jnp.bfloat16),
            pltpu.VMEM((rows, spread.shape[1]), jnp.bfloat16),
            pltpu.VMEM((experts // 2 * 2, 2 * part, width), jnp.bfloat16),
            pltpu.SemaphoreType.DMA((blocks,)),
            pltpu.SemaphoreType.DMA((blocks,)),
            pltpu.SemaphoreType.DMA((experts // 2 * 2,)),
        ],
    )


def down_kernel(count, span, *refs):
    hiddens, (down_own, down_other), outs = refs[:count], refs[count : count + 2], refs[count + 2 :]
    places, _, part = hiddens[0].shape
    near = len(outs) // (count * span)
    size = outs[0].shape[0]
    for index, hidden in enumerate(hiddens):
        total = None
        for place in range(places):
            down = down_own if place < places // 2 else down_other
            first = place % (places // 2) * part
            term = dot(hidden[place], down[first : first + part, :])
            total = term if total is None else total + term
        for across, target, first in plane_order(near, span, size):
            block = (index * near + across) * span + target // size
            outs[block][...] = low(total[first : first + size])


def down_call(hiddens, downs, near, span, size):
    places, rows, part = hiddens[0].shape
    hidden, width = downs[0].shape
    tile = min(width, 512)
    count = len(hiddens)
    down_block = pl.BlockSpec((hidden, tile), lambda n: (0, n))
    outs = kernel_call(
        functools.partial(down_kernel, count, span),
        (width // tile,),
        [whole(array) for array in hiddens] + [down_block] * 2,
        [pl.BlockSpec((size, tile), lambda n: (0, n))] * (count * near * span),
        [((size, width), jnp.bfloat16)] * (count * near * span),
        [*hiddens, *downs],
        0,
    )
    blocks = [list(outs[index * span : (index + 1) * span]) for index in range(count * near)]
    return [blocks[index * near : (index + 1) * near] for index in range(count)]


def backward_kernel(width, share, count, scalars, *refs):
    pieces = refs[:count]
    (output_weight, mix_in, mix_out, select, queries, keys, values, attended, query_raw, key_raw,
     query_gain, key_gain, cosine, sine, mask) = refs[count : count + 15]
    (query_out, key_out, value_out, inner_out, mix_in_grad, mix_out_grad) = refs[
        count + 15 : count + 21
    ]
    branch, mixed_grad, grads, sems = refs[count + 21 :]
    size = pieces[0].shape[0]
    rows, local = grads.shape
    heads = local // HD
    copies = []
    for index, piece in enumerate(pieces):
        place = pl.ds(pl.multiple_of(scalars[index] * size, size), size)
        copies.append(pltpu.make_async_copy(piece, branch.at[place], sems.at[index]))
    for copy in copies:
        copy.start()
    for copy in copies:
        copy.wait()
    mixed_grad[...] = low(wide(low(dot_t(branch[:, :width], mix_out[...]))) * select[...])
    grads[...] = low(
        dot_t(branch[:, :width], output_weight[...]) + dot_t(mixed_grad[...], mix_in[...])
    )
    columns = pl.ds(pl.multiple_of(scalars[count] * share, share), share)
    mix_out_grad[...] = sliced(t_dot(branch[:, width:], branch[:, columns]))
    scale = HD ** (-0.5)
    lane = lax.broadcasted_iota(jnp.int32, (rows, 128), 1)
    sums = jnp.zeros((rows, 128), jnp.float32)
    for head in range(heads):
        part = slice(head * HD, (head + 1) * HD)
        query, key, value = queries[:, part], keys[:, part], values[:, part]
        grad = grads[:, part]
        scores = dot_t(query, key) * scale + mask[...]
        raised = jnp.exp(scores - jnp.max(scores, axis=1, keepdims=True))
        weights = raised * (1.0 / jnp.sum(raised, axis=1, keepdims=True))
        weight_grad = dot_t(grad, value)
        center = jnp.sum(weights * weight_grad, axis=1, keepdims=True)
        score_grad = low(weights * (weight_grad - center))
        value_out[:, part] = low(t_dot(low(weights), grad))
        query_grad = dot(score_grad, key) * scale
        key_grad = t_dot(score_grad, query) * scale
        query_grad = query_grad * cosine[...] - turned(query_grad) * sine[...]
        key_grad = key_grad * cosine[...] - turned(key_grad) * sine[...]
        query_grad = query_grad * wide(query_gain[:, part])
        key_grad = key_grad * wide(key_gain[:, part])
        query_out[:, part] = query_grad
        key_out[:, part] = key_grad
        query_inner = jnp.sum(query_grad * query_raw[:, part], axis=1, keepdims=True)
        key_inner = jnp.sum(key_grad * key_raw[:, part], axis=1, keepdims=True)
        sums = sums + jnp.where(lane == 0, query_inner, jnp.where(lane == 1, key_inner, 0.0))
    mix_in_grad[...] = sliced(t_dot(mixed_grad[...], attended[...]))
    inner_out[...] = jnp.transpose(sums)[:8]


def sliced(values):
    total = values[:RANK]
    for index in range(1, values.shape[0] // RANK):
        total = total + values[index * RANK : (index + 1) * RANK]
    return low(total)


def backward_call(
    scalars, pieces, output_weight, mix_in, mix_out, select, states, raws, gains, tables, mask, share
):
    rows, local = raws[0].shape
    width = output_weight.shape[1]
    operands = [
        scalars, *pieces, output_weight, mix_in, mix_out, select, *states, *raws, *gains, *tables, mask,
    ]
    out_shape = [((rows, local), jnp.float32)] * 2 + [((rows, local), jnp.bfloat16)]
    out_shape += [((8, rows), jnp.float32), ((RANK, local), jnp.bfloat16)]
    out_shape += [((RANK, share), jnp.bfloat16)]
    return kernel_call(
        functools.partial(backward_kernel, width, share, len(pieces)),
        (1,),
        [ANY] * len(pieces) + [whole(array) for array in operands[len(pieces) + 1 :]],
        [pl.BlockSpec(shape, lambda *_: (0, 0)) for shape, _ in out_shape],
        out_shape,
        operands,
        14 * rows * rows * local + 2 * rows * local * width,
        [
            pltpu.VMEM((rows, pieces[0].shape[1]), jnp.bfloat16),
            pltpu.VMEM((rows, mix_out.shape[0]), jnp.bfloat16),
            pltpu.VMEM((rows, local), jnp.bfloat16),
            pltpu.SemaphoreType.DMA((len(pieces),)),
        ],
        1,
    )


def adapter_lanes(index, select):
    row = lax.broadcasted_iota(jnp.int32, (128, 128), 0) - index * RANK
    lane = lax.broadcasted_iota(jnp.int32, (128, 128), 1)
    return low(jnp.where(lax.rem(lane, RANK) == row, select, 0.0))


def resid_grad_kernel(
    rank, arrived, own, own_x, own_y, cotangent, resid, mixed, gain, grad_out, sent_out
):
    width = resid.shape[1]
    step = 16

    for first in range(0, resid.shape[0], step):
        rows = pl.ds(first, step)
        total = wide(arrived[rows, :]) + wide(own_y[rows, :])
        total = total + wide(own[rows, :]) + wide(own_x[rows, :])
        scaled = total * wide(gain[...])
        values = resid[rows, :]
        inverse = lax.rsqrt(jnp.mean(values * values, axis=1, keepdims=True) + EPSILON)
        inner = jnp.sum(scaled * values, axis=1, keepdims=True)
        grad = wide(cotangent[rows, :]) + norm_back(scaled, values, inverse, width, inner)
        grad_out[rows, :] = grad
        sent_out[rows, pl.ds(0, width)] = low(grad)
    sent_out[:, width:] = mixed[...]


def resid_grad_call(rank, arrived, own, own_x, own_y, cotangent, resid, mixed, gain):
    rows, width = resid.shape
    wide_width = width + mixed.shape[1]
    first = pl.BlockSpec((rows, width), lambda n, rank: (0, 0))
    return kernel_call(
        resid_grad_kernel,
        (1,),
        [first] * 4
        + [pl.BlockSpec((rows, width), lambda n, rank: (rank[0], 0))]
        + [whole(resid), whole(mixed), whole(gain)],
        [first, pl.BlockSpec((rows, wide_width), lambda n, rank: (0, 0))],
        [((rows, width), jnp.float32), ((rows, wide_width), jnp.bfloat16)],
        [rank, arrived, own, own_x, own_y, cotangent, resid, mixed, gain],
        0,
        (),
        1,
    )


def raw_kernel(
    width, inner, squares, query_grad, key_grad, value_grad, query_raw, key_raw, lowrank,
    adapt_out, select, raw, lowrank_out, adapt_grad,
):
    inverse = lax.rsqrt(spread_columns(squares[...]) / width + EPSILON)
    totals = spread_columns(inner[...]) / width
    for index, (grad, value) in enumerate(((query_grad, query_raw), (key_grad, key_raw))):
        scale = inverse[:, index : index + 1]
        factor = scale**3 * totals[:, index : index + 1]
        raw[index] = low(scale * grad[...] - value[...] * factor)
    raw[2] = value_grad[...]
    lowrank_part = None
    for index in range(3):
        part = low(dot_t(raw[index], adapt_out[index]) * select[...])
        term = dot_t(part, adapter_lanes(index, select[...]))
        lowrank_part = term if lowrank_part is None else lowrank_part + term
        adapt_grad[index * RANK : (index + 1) * RANK, :] = sliced(
            t_dot(lowrank[index], raw[index])
        )
    lowrank_out[...] = low(lowrank_part)


def raw_call(inner, squares, grads, raws, lowrank, adapt_out, select, width):
    rows, local = raws[0].shape
    operands = [inner, squares, *grads, *raws, lowrank, adapt_out, select]
    out_shape = [((3, rows, local), jnp.bfloat16), ((rows, 128), jnp.bfloat16)]
    out_shape += [((3 * RANK, local), jnp.bfloat16)]
    return kernel_call(
        functools.partial(raw_kernel, width),
        (1,),
        [whole(array) for array in operands],
        [pl.BlockSpec(shape, lambda *_, size=len(shape): (0,) * size) for shape, _ in out_shape],
        out_shape,
        operands,
        0,
    )


def weight_kernel(size, scalars, raw, query_weight, key_weight, value_weight, mine, theirs):
    levels = mine.shape[0] // size
    for out, offset in ((theirs, 1 - scalars[0]), (mine, scalars[0])):
        total = None
        for index, weight in enumerate((query_weight, key_weight, value_weight)):
            taken = [
                raw[index, pl.ds(pl.multiple_of((2 * level + offset) * size, size), size), :]
                for level in range(levels)
            ]
            term = dot_t(jnp.concatenate(taken, axis=0), weight[...])
            total = term if total is None else total + term
        out[...] = total.astype(out.dtype)


def weight_call(scalars, raw, weights, size):
    _, rows, local = raw.shape
    width = weights[0].shape[0]
    tile = min(width, 512)
    operands = [scalars, raw, *weights]
    out_shape = [((rows // 2, width), jnp.float32), ((rows // 2, width), jnp.bfloat16)]
    return kernel_call(
        functools.partial(weight_kernel, size),
        (width // tile,),
        [whole(raw)] + [pl.BlockSpec((tile, local), lambda n, *_: (n, 0))] * 3,
        [pl.BlockSpec((rows // 2, tile), lambda n, *_: (0, n))] * 2,
        out_shape,
        operands,
        0,
        (),
        1,
    )


def input_kernel(
    rank, kept, came, lowrank, adapt_in, select, tokens, gain, resid_grad, out
):
    grad = kept[...] + wide(came[...])
    for index in range(3):
        part = low(dot(lowrank[...], adapter_lanes(index, select[...])))
        grad = grad + dot_t(part, adapt_in[index])
    scaled = grad * wide(gain[...])
    inputs = wide(tokens[...])
    width = inputs.shape[1]
    inverse = lax.rsqrt(jnp.mean(inputs * inputs, axis=1, keepdims=True) + EPSILON)
    inner = jnp.sum(scaled * inputs, axis=1, keepdims=True)
    out[...] = low(
        resid_grad[...] + norm_back(scaled, inputs, inverse, width, inner)
    )


def input_call(rank, kept, came, lowrank, adapt_in, select, tokens, gain, resid_grad):
    operands = [rank, kept, came, lowrank, adapt_in, select, tokens, gain, resid_grad]
    rows, width = kept.shape
    return kernel_call(
        input_kernel,
        (1,),
        [
            whole(kept),
            whole(came),
            pl.BlockSpec((rows, lowrank.shape[1]), lambda n, rank: (rank[0], 0)),
            whole(adapt_in),
            whole(select),
            pl.BlockSpec((rows, width), lambda n, rank: (rank[0], 0)),
            whole(gain),
            whole(resid_grad),
        ],
        [pl.BlockSpec((rows, width), lambda *_: (0, 0))],
        [((rows, width), jnp.bfloat16)],
        operands,
        0,
        (),
        1,
    )[0]


def compact_kernel(
    scalars, lowrank_grad, normed, mix_out_grad, adapt_grad, mix_in_grad, select, out, held, sem
):
    share = out.shape[1]
    columns = pl.ds(pl.multiple_of(scalars[0] * share, share), share)
    copy = pltpu.make_async_copy(normed.at[:, columns], held, sem)
    copy.start()
    copy.wait()
    first = low(t_dot(lowrank_grad[...], held[...]))[: 3 * RANK]
    out[: 3 * RANK] = first
    out[3 * RANK : 4 * RANK] = mix_out_grad[...]
    out[4 * RANK : 7 * RANK] = adapt_grad[...]
    out[7 * RANK : 8 * RANK] = mix_in_grad[...]
    chosen = low(jnp.broadcast_to(select[...], (RANK, 128)))
    out[8 * RANK :] = jnp.concatenate([chosen] * (share // 128), axis=1)


def compact_call(scalars, lowrank_grad, normed, mix_out_grad, adapt_grad, mix_in_grad, select):
    rows = normed.shape[0]
    share = adapt_grad.shape[1]
    operands = [scalars, lowrank_grad, normed, mix_out_grad, adapt_grad, mix_in_grad, select]
    return kernel_call(
        compact_kernel,
        (1,),
        [whole(lowrank_grad), ANY] + [whole(array) for array in operands[3:]],
        [pl.BlockSpec((9 * RANK, share), lambda *_: (0, 0))],
        [((9 * RANK, share), jnp.bfloat16)],
        operands,
        0,
        [pltpu.VMEM((rows, share), jnp.bfloat16), pltpu.SemaphoreType.DMA],
        1,
    )[0]


def spread_kernel(order, *refs):
    pieces, out = refs[:-1], refs[-1]
    step = pl.program_id(0)
    for index, piece in enumerate(pieces):

        @pl.when(step == index)
        def _():
            out[...] = wide(piece[...])


def spread_call(order, pieces):
    size, width = pieces[0].shape
    count = len(pieces)
    return kernel_call(
        spread_kernel,
        (count,),
        [whole(piece) for piece in pieces],
        [pl.BlockSpec((size, width), lambda step, order: (order[step], 0))],
        [((count * size, width), jnp.float32)],
        [order, *pieces],
        0,
        (),
        1,
    )[0]


def assemble_kernel(trees, order, *refs):
    count = len(refs) - 5
    own, pieces = refs[0], refs[1:count]
    in_grad, out_grad, mix_in_grad, mix_out_grad = refs[count : count + 4]
    (choice,) = refs[count + 4 :]
    share = own.shape[1]
    block = own.shape[0] // trees
    row = lax.broadcasted_iota(jnp.int32, (RANK, 128), 0)
    lane = lax.broadcasted_iota(jnp.int32, (RANK, 128), 1)
    same = lax.rem(lane, RANK) == row
    for tree in range(trees):
        chosen = own[tree * block + 8 * RANK : tree * block + 9 * RANK, :128]
        choice[tree * RANK : (tree + 1) * RANK] = low(jnp.where(same, wide(chosen), 0.0))

    def kind(source, stride, index):
        return jnp.concatenate(
            [
                source[tree * stride + index * RANK : tree * stride + (index + 1) * RANK, :]
                for tree in range(trees)
            ],
            axis=0,
        )

    for index in range(3):
        out_grad[index] = t_dot(choice[...], kind(own, block, 4 + index))
    mix_in_grad[...] = t_dot(kind(own, block, 7), choice[...])
    for place, source in enumerate((own, *pieces)):
        stride = block if place == 0 else 4 * RANK
        start = pl.ds(pl.multiple_of(order[place] * share, share), share)
        for index in range(3):
            in_grad[index, start, :] = t_dot(kind(source, stride, index), choice[...])
        mix_out_grad[:, start] = t_dot(choice[...], kind(source, stride, 3))


def assemble_call(order, own, pieces, trees):
    share = own.shape[1]
    count = 1 + len(pieces)
    width = count * share
    out_shape = [((3, width, 128), jnp.float32), ((3, 128, share), jnp.float32)]
    out_shape += [((share, 128), jnp.float32), ((128, width), jnp.float32)]
    operands = [order, own, *pieces]
    return kernel_call(
        functools.partial(assemble_kernel, trees),
        (1,),
        [whole(array) for array in operands[1:]],
        [pl.BlockSpec(shape, lambda *_, size=len(shape): (0,) * size) for shape, _ in out_shape],
        out_shape,
        operands,
        0,
        [pltpu.VMEM((trees * RANK, 128), jnp.bfloat16)],
        1,
    )


def body(
    tokens,
    cotangent,
    attn_gain,
    ffn_gain,
    query_gain,
    key_gain,
    query_weight,
    key_weight,
    value_weight,
    output_weight,
    expert_gate,
    expert_up,
    expert_down,
    adapt_in,
    adapt_out,
    adapt_in_out,
    adapt_out_out,
    routes,
    gate_weights,
    block_parent,
    adapter_pick,
):
    rows_here, model_width = tokens.shape
    tensor_rank = lax.axis_index("tensor")
    tensor_count = lax.axis_size("tensor")
    owners = lax.axis_size("expert")
    owner_rank = lax.axis_index("expert")
    axes = divide_axes(owners, tensor_count)
    far, near, span = axes["z"][1], axes["x"][1], axes["y"][1]
    experts_here, _, hidden_here = expert_gate.shape
    experts_all = experts_here * owners
    column_share = model_width // tensor_count
    row_share = rows_here // tensor_count
    hold = lax.optimization_barrier
    level, core = tensor_rank // 2, tensor_rank % 2
    rank_list = jnp.reshape(tensor_rank, (1,)).astype(jnp.int32)

    def own_rows(array):
        return lax.dynamic_slice_in_dim(array, tensor_rank * row_share, row_share, 0)

    routes_wide = jnp.swapaxes(routes, 0, 1)
    weights_wide = jnp.swapaxes(gate_weights, 0, 1)
    route_weights = jnp.sum(
        jnp.where(
            routes_wide[:, :, None] == jnp.arange(experts_all, dtype=jnp.int32)[None, None, :],
            weights_wide[:, :, None],
            0.0,
        ),
        axis=0,
    )
    weights_high = low(route_weights)
    weights_low = low(route_weights - wide(weights_high))
    side_width = -(-2 * experts_all // 128) * 128
    side_pad = jnp.zeros((rows_here, side_width - 2 * experts_all), jnp.bfloat16)
    side_rows = jnp.concatenate([weights_high, weights_low, side_pad], axis=1)
    cot_queue = []
    for step in range(span):
        place = ((level + span - step) % span * 2 + core) * row_share
        cot_queue.append(
            jnp.concatenate(
                [
                    lax.dynamic_slice_in_dim(cotangent, place, row_share, 0),
                    lax.dynamic_slice_in_dim(side_rows, place, row_share, 0),
                ],
                axis=1,
            )
        )
    cot_queue = [jnp.concatenate(cot_queue, axis=0)]
    side_index = jnp.arange(side_width, dtype=jnp.int32)
    hidden_owner = (
        owner_rank * experts_here
        + jnp.arange(experts_here * hidden_here, dtype=jnp.int32) // hidden_here
    )
    spread_flat = low(
        (side_index[:, None] % experts_all == hidden_owner[None, :])
        & (side_index[:, None] < 2 * experts_all)
    )
    spread = jnp.swapaxes(spread_flat.reshape(side_width, experts_here, hidden_here), 0, 1)

    cot_planes = [None] * far
    cot_queue.append(turn(cot_queue[0], axes, "z", 1))
    cot_planes[0] = ring(cot_queue[0], axes, "x")
    first_gain, second_gain = attn_gain[None, :], ffn_gain[None, :]
    gains = (query_gain[None, :], key_gain[None, :])
    reached = ancestry(block_parent)
    cosine_table, sine_table = rope_tables(reached, rows_here // block_parent.shape[0], HD)
    signs = jnp.where(jnp.arange(HD) < HD // 2, -1.0, 1.0)[None, :]
    tables = (cosine_table, sine_table * signs)
    mask = jnp.where(token_mask(reached[0], rows_here), 0.0, MASKED_SCORE)
    select = jnp.repeat(wide(adapter_pick), RANK, axis=1)
    weights = (query_weight, key_weight, value_weight)
    normed_in, lowrank, *raws, squares = project_call(
        tokens, first_gain, weights, adapt_in, adapt_out, select
    )

    def halves(rows):
        return [rows[: rows.shape[0] // 2], rows[rows.shape[0] // 2 :]]

    squares = sum_tensor(squares, axes)
    held = (squares, cot_queue[1], cot_planes[0], expert_gate, expert_up, tables, mask)
    squares, cot_queue[1], cot_planes[0], expert_gate, expert_up, tables, mask = hold(held)
    gates = (expert_gate, turn(expert_gate, axes, "c", 1))
    ups = (expert_up, turn(expert_up, axes, "c", 1))
    cot_queue[1] = halves(cot_queue[1])
    cot_later = turn(cot_queue[1][0], axes, "z", 1)
    cot_across = ring(cot_queue[1][0], axes, "x")[1:]
    *states, mine, theirs = attend_call(
        jnp.reshape(core, (1,)).astype(jnp.int32),
        squares,
        raws,
        gains,
        tables,
        mask,
        output_weight,
        adapt_in_out,
        row_share,
    )
    cot_later, cot_across, mine, theirs = hold((cot_later, cot_across, mine, theirs))

    theirs = turn(theirs, axes, "c", 1)
    branch_kept, branch_sent = scatter_core(mine, theirs, axes)
    branch_sent, cot_queue[1] = hold((branch_sent, cot_queue[1]))
    down_tall = expert_down.reshape(-1, model_width)
    branch_came = turn(branch_sent, axes, "y", -1)
    cot_later = [cot_later, turn(cot_queue[1][1], axes, "z", 1)]
    cot_second = ring(cot_queue[1][1], axes, "x")[1:]
    held = (branch_came, cot_later, cot_second, gates, ups, down_tall)
    branch_came, cot_later, cot_second, gates, ups, down_tall = hold(held)
    downs = (down_tall, turn(down_tall, axes, "c", 1))
    cot_queue.append(jnp.concatenate(cot_later, axis=0))
    cot_planes[1] = [cot_queue[1]] + [list(pair) for pair in zip(cot_across, cot_second)]
    cot_planes[0] = [[piece] for piece in cot_planes[0]]
    resid_rows, norm_plane, mixed_rows = resid_call(
        rank_list, branch_kept, branch_came, tokens, adapt_out_out, select, second_gain
    )

    norm_queue = [norm_plane, turn(norm_plane, axes, "z", 1)]
    norm_pairs = [ring(norm_plane, axes, "x")]
    backs, sides = [None] * far, [None] * far

    def hidden_step(*indices):
        back, side = hidden_call(
            [cot_planes[index] for index in indices], downs, spread_flat, experts_here, row_share
        )
        for order, index in enumerate(indices):
            backs[index], sides[index] = (back, order * side.shape[0] // len(indices)), side
        return back

    def set_back(back, *indices):
        for index in indices:
            backs[index] = (back, backs[index][1])

    norm_planes = [None] * far
    held = (norm_queue[1], norm_pairs[0], downs, cot_queue[2])
    norm_queue[1], norm_pairs[0], downs, cot_queue[2] = hold(held)
    norm_planes[0] = ring(jnp.concatenate(norm_pairs[0], axis=0), axes, "y")
    norm_queue.append(turn(norm_queue[1], axes, "z", 1))
    norm_pairs.append(ring(norm_queue[1], axes, "x"))
    back_first = hidden_step(0, 1)
    held = (norm_planes[0], norm_queue[2], norm_pairs[1], cot_queue[2], back_first)
    norm_planes[0], norm_queue[2], norm_pairs[1], cot_queue[2], back_first = hold(held)
    set_back(back_first, 0, 1)
    parts, hiddens = [None] * far, [None] * far

    def expert_step(index):
        back, offset = backs[index]
        *parts[index], hiddens[index] = expert_call(
            norm_planes[index],
            gates,
            ups,
            spread,
            sides[index],
            back,
            offset,
            near,
            span if index else 0,
            span,
        )

    def whole_step(index):
        *parts[index], hiddens[index] = whole_call(
            norm_planes[index], cot_planes[index], gates, ups, downs, spread, near, span, row_share
        )

    norm_planes[1] = ring(jnp.concatenate(norm_pairs[1], axis=0), axes, "y")
    norm_queue.append(turn(norm_queue[2], axes, "z", 1))
    norm_pairs.append(ring(norm_queue[2], axes, "x"))
    cot_queue.append(turn(cot_queue[2], axes, "z", 1))
    cot_planes[2] = ring(cot_queue[2], axes, "x")
    expert_step(0)

    held = (norm_planes[1], norm_queue[3], norm_pairs[2], parts[0])
    norm_planes[1], norm_queue[3], norm_pairs[2], parts[0] = hold(held)
    norm_planes[2] = ring(jnp.concatenate(norm_pairs[2], axis=0), axes, "y")
    norm_pairs.append(ring(norm_queue[3], axes, "x"))
    expert_step(1)

    held = (norm_planes[2], norm_pairs[3], parts[1], cot_queue[3], cot_planes[2])
    norm_planes[2], norm_pairs[3], parts[1], cot_queue[3], cot_planes[2] = hold(held)
    norm_planes[3] = ring(jnp.concatenate(norm_pairs[3], axis=0), axes, "y")
    came, last = [None] * far, [None] * far
    came[1] = scatter_first(parts[1], axes)
    came_x = send_sum(parts[0], axes, "x")
    cot_across = [turn(piece, axes, "z", 1) for piece in cot_planes[2][1:]]
    cot_planes[2] = [[piece] for piece in cot_planes[2]]
    whole_step(2)

    held = (norm_planes[3], came[1], parts[2], came_x, cot_across)
    norm_planes[3], came[1], parts[2], came_x, cot_across = hold(held)
    cot_planes[3] = [[piece] for piece in [cot_queue[3]] + cot_across]
    came[2] = scatter_first(parts[2], axes)
    last[1] = scatter_second(parts[1], came[1], axes)
    own_sums = [
        [block(parts[0][0], k, span), block(came_x, k, span)] for k in range(span)
    ]
    came_y = send_sum([None] + [low(pair[0] + pair[1]) for pair in own_sums[1:]], axes, "y")
    whole_step(3)

    held = (last[1], came[2], came_y, parts[3], hiddens)
    last[1], came[2], came_y, parts[3], hiddens = hold(held)
    came[3] = scatter_first(parts[3], axes)
    last[2] = scatter_second(parts[2], came[2], axes)
    ring_sum = turn(low(scatter_last(parts[1], came[1], last[1], axes)), axes, "z", 1)
    mixes, mix_came = [None] * far, [None] * far

    def down_step(*indices):
        done = down_call([hiddens[index] for index in indices], downs, near, span, row_share)
        for index, blocks in zip(indices, done):
            mixes[index] = blocks

    down_step(3, 0)

    held = (ring_sum, came[3], last[2], mixes[3], mixes[0], hiddens)
    ring_sum, came[3], last[2], mixes[3], mixes[0], hiddens = hold(held)
    last[3] = scatter_second(parts[3], came[3], axes)
    ring_sum = turn(
        low(wide(ring_sum) + scatter_last(parts[2], came[2], last[2], axes)), axes, "z", 1
    )
    down_step(2)

    ring_sum, last[3], hiddens, mixes[2] = hold((ring_sum, last[3], hiddens, mixes[2]))
    ring_sum = turn(
        low(wide(ring_sum) + scatter_last(parts[3], came[3], last[3], axes)), axes, "z", 1
    )
    down_step(1)
    half_width = model_width // span

    def column_sum(arrays, owner):
        first = owner * half_width
        return sum(
            wide(lax.dynamic_slice_in_dim(array, first, half_width, 1)) for array in arrays
        )

    def mix_columns(index, owner):
        rows = [column_sum(arrays, owner) for arrays in mix_held[index]]
        return jnp.concatenate(rows, axis=0)

    def mix_sent(index):
        return low(mix_columns(index, (level + 1) % span))

    def mix_down(index, came_rows):
        came_rows = turn(came_rows, axes, "y", -1)
        for step in range(span - 2, 0, -1):
            total = mix_columns(index, (level + span - step) % span) + rolled(came_rows)
            came_rows = turn(low(total), axes, "y", -1)
        return came_rows

    def rolled(rows):
        size = rows.shape[0] // span
        return wide(jnp.concatenate([rows[size:], rows[:size]], axis=0))

    def mix_total(index):
        return mix_columns(index, level) + rolled(mix_parts[index])

    def mix_send(index, down):
        return send_sum([blocks[down] for blocks in mixes[index]], axes, "x")

    mix_held = [None] * far
    mix_parts = [None] * far

    ring_sum, mixes = hold((ring_sum, mixes))
    mix_early = mix_send(3, 0)
    resid_grad_rows, branch_sent = resid_grad_call(
        rank_list,
        ring_sum,
        parts[0][0],
        came_x,
        came_y,
        cotangent,
        resid_rows,
        mixed_rows,
        second_gain,
    )
    branch_pieces = ring(branch_sent, axes, "y")
    branch_other = turn(branch_pieces[0], axes, "c", 1)
    order = jnp.stack(
        [
            (level + span - step) % span * 2 + side
            for side in (core, 1 - core)
            for step in range(span)
        ]
    ).astype(jnp.int32)

    branch_pieces, mix_early, mixes = hold((branch_pieces, mix_early, mixes))
    branch_others = [turn(piece, axes, "c", 1) for piece in branch_pieces[1:]]
    branch_others, branch_other, mixes = hold((branch_others, branch_other, mixes))
    branch_pieces = branch_pieces + [branch_other] + branch_others
    mix_late = [mix_send(3, down) for down in range(1, span)]
    mix_next = mix_send(2, 0)
    mix_far = [[turn(part, axes, "z", -1) for part in blocks] for blocks in mixes[1][1:]]
    query_grad, key_grad, value_grad, inner, mix_in_grad, mix_out_grad = backward_call(
        jnp.concatenate([order, rank_list]),
        branch_pieces,
        output_weight,
        adapt_in_out,
        adapt_out_out,
        select,
        states,
        raws[:2],
        gains,
        tables,
        mask,
        column_share,
    )

    held = (inner, mix_late, mix_next, mix_far, mixes)
    inner, mix_late, mix_next, mix_far, mixes = hold(held)
    mix_held[3] = list(zip(mixes[3][0], [mix_early] + mix_late))
    mix_ready = mix_sent(3)
    inner = sum_tensor(inner, axes)
    inner, mix_ready, mixes = hold((inner, mix_ready, mixes))
    mix_parts[3] = mix_down(3, mix_ready)
    mix_last = [mix_send(2, down) for down in range(1, span)]
    mix_near = [turn(mixes[1][0][0], axes, "z", -1)]
    raw_grads, lowrank_part, adapt_grad = raw_call(
        inner,
        squares,
        (query_grad, key_grad, value_grad),
        raws[:2],
        lowrank,
        adapt_out,
        select,
        model_width,
    )
    lowrank_came = turn(lowrank_part, axes, "c", 1)
    lowrank_part, lowrank_came, raw_grads = hold((lowrank_part, lowrank_came, raw_grads))
    lowrank_part = low(wide(lowrank_part) + wide(lowrank_came))
    lowrank_parts = ring(lowrank_part, axes, "y")
    normed_mine, normed_theirs = weight_call(
        jnp.reshape(core, (1,)).astype(jnp.int32), raw_grads, weights, row_share
    )

    held = (normed_mine, normed_theirs, lowrank_parts, mix_parts[3], mix_last, mix_near, mixes)
    held = hold(held)
    normed_mine, normed_theirs, lowrank_parts, mix_parts[3], mix_last, mix_near, mixes = held
    for across in range(1, near):
        pairs = zip(mixes[0][across], mix_far[across - 1])
        mixes[0][across] = [low(wide(mine) + wide(other)) for mine, other in pairs]
    normed_theirs, mixes = hold((turn(normed_theirs, axes, "c", 1), mixes))
    normed_kept, normed_sent = scatter_core(normed_mine, normed_theirs, axes)
    held = (normed_sent, lowrank_parts, mixes, mix_last)
    normed_sent, lowrank_parts, mixes, mix_last = hold(held)
    normed_came = turn(normed_sent, axes, "y", -1)
    lowrank_grad = low(sum(wide(part) for part in lowrank_parts))
    mix_came[0] = [mix_send(0, 0)]
    compact = compact_call(
        rank_list, lowrank_grad, normed_in, mix_out_grad, adapt_grad, mix_in_grad, select
    )
    tree_queue = [compact, turn(compact, axes, "z", 1)]
    mix_near = mix_near + [turn(part, axes, "z", -1) for part in mixes[1][0][1:]]
    mix_held[2] = list(zip(mixes[2][0], [mix_next] + mix_last))
    mix_ready = mix_sent(2)
    held = (tree_queue, mix_ready, normed_came, mix_came[0], mix_near, mixes)
    tree_queue, mix_ready, normed_came, mix_came[0], mix_near, mixes = hold(held)

    tree_queue.append(turn(tree_queue[-1], axes, "z", 1))
    mix_parts[2] = mix_down(2, mix_ready)
    mix_came[0] = mix_came[0] + [mix_send(0, down) for down in range(1, span)]
    input_rows = input_call(
        rank_list,
        normed_kept,
        normed_came,
        lowrank_grad,
        adapt_in,
        select,
        tokens,
        first_gain,
        resid_grad_rows,
    )
    input_rows, tree_queue = hold((input_rows, tree_queue))
    input_held = ring(input_rows, axes, "y")
    tree_queue.append(turn(tree_queue[-1], axes, "z", 1))
    held = (tree_queue, mix_came[0], mix_parts[2])
    tree_queue, mix_came[0], mix_parts[2] = hold(held)

    trees = ring(jnp.concatenate(tree_queue, axis=0), axes, "x")
    mix_sum = turn(low(mix_total(2)), axes, "z", 1)
    mix_held[0] = [list(arrays) for arrays in zip(mixes[0][0], mix_came[0], mix_near)]
    mix_held[0][0].append(resid_rows)
    mix_parts[0] = mix_down(0, mix_sent(0))
    held = (trees, mix_sum, mix_parts[0], input_held)
    trees, mix_sum, mix_parts[0], input_held = hold(held)
    input_pieces = input_held + [turn(piece, axes, "c", 1) for piece in input_held]
    trees = jnp.concatenate(trees, axis=0)
    shared = trees.reshape(owners, -1, column_share)[:, : 4 * RANK]
    shared = ring(shared.reshape(-1, column_share), axes, "y")
    mix_sum = turn(low(wide(mix_sum) + mix_total(3)), axes, "z", 1)
    input_grad = spread_call(order, input_pieces)
    shared, mix_sum, input_grad = hold((shared, mix_sum, input_grad))
    shared = shared + [turn(piece, axes, "c", 1) for piece in shared]
    layer_columns = low(mix_total(0) + wide(mix_sum))
    layer_out = place_columns(layer_columns, axes)
    grad_adapt_in, grad_adapt_out, grad_adapt_in_out, grad_adapt_out_out = assemble_call(
        order, trees, shared[1:], owners
    )
    return (
        layer_out,
        input_grad,
        grad_adapt_in,
        grad_adapt_out,
        grad_adapt_in_out,
        grad_adapt_out_out,
    )


def solution(mesh):
    return jax.shard_map(
        body,
        mesh=mesh,
        in_specs=(
            P("expert", None),
            P("expert", None),
            P(),
            P(),
            P("tensor"),
            P("tensor"),
            P(None, "tensor"),
            P(None, "tensor"),
            P(None, "tensor"),
            P("tensor", None),
            P("expert", None, "tensor"),
            P("expert", None, "tensor"),
            P("expert", "tensor", None),
            P(),
            P(None, None, "tensor"),
            P("tensor", None),
            P(),
            P("expert", None),
            P("expert", None),
            P("expert"),
            P("expert", None),
        ),
        out_specs=(
            P("expert", "tensor"),
            P("expert", None),
            P(),
            P(None, None, "tensor"),
            P("tensor", None),
            P(),
        ),
        check_vma=False,
    )
```
